32 devices in a mesh: fsdp: 32 (over z, y, x, core).
Axes of the slice: x: 2, y: 2, z: 4, core: 2. Of those that a mesh axis runs over, the one named last changes fastest.
Arguments:
- activations: bfloat16 [4096, 768], P('fsdp'), may hold values from -6 to 6
- query_weight: bfloat16 [2, 768, 768], P(None, 'fsdp'), may hold values from -0.21875 to 0.21875
- query_bias: bfloat16 [2, 768], P(None, 'fsdp'), may hold values from -4 to 4
- key_weight: bfloat16 [2, 768, 768], P(None, 'fsdp'), may hold values from -0.21875 to 0.21875
- value_weight: bfloat16 [2, 768, 768], P(None, 'fsdp'), may hold values from -0.21875 to 0.21875
- value_bias: bfloat16 [2, 768], P(None, 'fsdp'), may hold values from -0.4375 to 0.4375
- output_weight: bfloat16 [2, 768, 768], P(None, 'fsdp'), may hold values from -3.5 to 3.5
- output_bias: bfloat16 [2, 768], P(None, 'fsdp'), may hold values from -4 to 4
- first_gain: bfloat16 [2, 768], P(None, 'fsdp'), may hold values from 0.5 to 1.5
- first_shift: bfloat16 [2, 768], P(None, 'fsdp'), may hold values from -4 to 4
- inner_weight: bfloat16 [2, 768, 3072], P(None, 'fsdp'), may hold values from -0.21875 to 0.21875
- inner_bias: bfloat16 [2, 3072], P(None, 'fsdp'), may hold values from -4 to 4
- outer_weight: bfloat16 [2, 3072, 768], P(None, 'fsdp'), may hold values from -0.109375 to 0.109375
- outer_bias: bfloat16 [2, 768], P(None, 'fsdp'), may hold values from -4 to 4
- second_gain: bfloat16 [2, 768], P(None, 'fsdp'), may hold values from 0.5 to 1.5
- second_shift: bfloat16 [2, 768], P(None, 'fsdp'), may hold values from -4 to 4
- cotangent: bfloat16 [4096, 768], P('fsdp'), may hold values from -6 to 6
- parents: int32 [13], replicated, may hold values from 0 to 12, as said below
- segments: int32 [4096], P('fsdp'), may hold values from 0 to 12, as said below
Outputs:
- result: bfloat16 [4096, 768], P('fsdp')
- input_grad: bfloat16 [4096, 768], P('fsdp')
- query_weight_grad: float32 [2, 768, 768], P(None, 'fsdp')
- query_bias_grad: float32 [2, 768], P(None, 'fsdp')
- key_weight_grad: float32 [2, 768, 768], P(None, 'fsdp')
- value_weight_grad: float32 [2, 768, 768], P(None, 'fsdp')
- value_bias_grad: float32 [2, 768], P(None, 'fsdp')
- output_weight_grad: float32 [2, 768, 768], P(None, 'fsdp')
- output_bias_grad: float32 [2, 768], P(None, 'fsdp')
- first_gain_grad: float32 [2, 768], P(None, 'fsdp')
- first_shift_grad: float32 [2, 768], P(None, 'fsdp')
- inner_weight_grad: float32 [2, 768, 3072], P(None, 'fsdp')
- inner_bias_grad: float32 [2, 3072], P(None, 'fsdp')
- outer_weight_grad: float32 [2, 3072, 768], P(None, 'fsdp')
- outer_bias_grad: float32 [2, 768], P(None, 'fsdp')
- second_gain_grad: float32 [2, 768], P(None, 'fsdp')
- second_shift_grad: float32 [2, 768], P(None, 'fsdp')
The draws below stay inside these ranges and needn't reach their ends.
Inputs may be any that keep to these rules, and one draw needn't show every extreme that they name: `parents`: every tree is one trunk, four branches whose parent is the trunk, and eight leaves, two with each branch as parent; a trunk is its own parent. Segment numbers are spread over the trees in a drawn order. `segments`: tree t fills tokens t * 4096 to (t + 1) * 4096 - 1: its trunk's 1024 tokens first, then its twelve branches and leaves, 256 tokens each, in an order drawn per tree.
All inputs are finite; a program needn't handle non-finite values.
Results may differ from the reference program's by a relative error of at most 0.023.
Values may be sent and summed in bfloat16 or wider, within the bound.
A program may use at most 256 MiB of HBM per device.

```python
import jax
import jax.numpy as jnp
from jax import lax

D = 768
HEADS = 12
HEAD_DIM = 64
FF = 3072
LAYERS = 2
TRUNK = 1024
SEG = 256
TREE_LEN = 4096
TOKENS = 4096
TREES = 1


def tree_layout(key):
    labels = jax.random.permutation(jax.random.fold_in(key, 17), 13 * TREES).astype(jnp.int32)
    tree_keys = jax.random.split(jax.random.fold_in(key, 29), TREES)
    orders = jax.vmap(lambda k: jax.random.permutation(k, 12))(tree_keys).astype(jnp.int32)
    slot_parent = jnp.array([0, 0, 0, 0, 0, 1, 1, 2, 2, 3, 3, 4, 4], dtype=jnp.int32)
    offsets = 13 * jnp.arange(TREES, dtype=jnp.int32)[:, None]
    places = jnp.arange(TREE_LEN, dtype=jnp.int32)
    blocks = jnp.maximum(places - TRUNK, 0) // SEG
    slots = jnp.where(places[None, :] < TRUNK, 0, 1 + orders[:, blocks])
    segment_ids = labels[offsets + slots].reshape(-1).astype(jnp.int32)
    parent_ids = jnp.zeros((13 * TREES,), jnp.int32).at[labels].set(labels[offsets + slot_parent[None, :]].reshape(-1))
    return (segment_ids, parent_ids)


def draw_parents(key, part):
    return tree_layout(key)[1]


def draw_segments(key, part):
    return tree_layout(key)[0]


def block_scale(stream_key, dims, cuts, low, high):
    def one(axis_at, shards_of):
        heights = jax.random.uniform(jax.random.fold_in(jax.random.fold_in(stream_key, 6), axis_at), (shards_of,), jnp.float32, low / len(cuts), high / len(cuts))
        return jnp.repeat(jnp.exp(heights), dims[axis_at] // shards_of).reshape((-1,) + (1,) * (len(dims) - axis_at - 1))

    loudness = one(*cuts[0])
    for cut in cuts[1:]:
        loudness = loudness * one(*cut)
    return loudness


def normal_values(own_key, dims, deviation, bound, shards=(), kind=jnp.bfloat16):
    values = jax.random.normal(own_key, dims, jnp.float32) * deviation
    if len(shards) > 0:
        values = block_scale(own_key, dims, shards, -0.22, 0.18) * values
    return jnp.clip(values, min=-bound, max=bound).astype(kind)


def setup_inputs(seed: int = 0) -> dict:
    key_list = jax.random.split(jax.random.key(seed), 20)
    activations = normal_values(key_list[0], (TOKENS, D), 1.0, 6.0, ((0, 32),))
    query_weight = normal_values(key_list[1], (LAYERS, D, D), D ** -0.5, 0.21875, ((1, 32),))
    query_bias = normal_values(key_list[2], (LAYERS, D), 0.3, 4.0, ((1, 32),))
    key_weight = normal_values(key_list[3], (LAYERS, D, D), D ** -0.5, 0.21875, ((1, 32),))
    value_weight = normal_values(key_list[4], (LAYERS, D, D), D ** -0.5, 0.21875, ((1, 32),))
    value_bias = normal_values(key_list[5], (LAYERS, D), 0.03, 0.4375, ((1, 32),))
    output_weight = normal_values(key_list[6], (LAYERS, D, D), (max(D // 256, 1)) ** -0.5, 3.5, ((1, 32),))
    output_bias = normal_values(key_list[7], (LAYERS, D), 0.3, 4.0, ((1, 32),))
    first_gain = jnp.clip(1.0 + 0.1 * jax.random.normal(key_list[8], (LAYERS, D), jnp.float32), 0.5, 1.5).astype(jnp.bfloat16)
    first_shift = normal_values(key_list[9], (LAYERS, D), 0.3, 4.0, ((1, 32),))
    inner_weight = normal_values(key_list[10], (LAYERS, D, FF), D ** -0.5, 0.21875, ((1, 32),))
    inner_bias = normal_values(key_list[11], (LAYERS, FF), 0.3, 4.0, ((1, 32),))
    outer_weight = normal_values(key_list[12], (LAYERS, FF, D), FF ** -0.5, 0.109375, ((1, 32),))
    outer_bias = normal_values(key_list[13], (LAYERS, D), 0.3, 4.0, ((1, 32),))
    second_gain = jnp.clip(1.0 + 0.1 * jax.random.normal(key_list[14], (LAYERS, D), jnp.float32), 0.5, 1.5).astype(jnp.bfloat16)
    second_shift = normal_values(key_list[15], (LAYERS, D), 0.3, 4.0, ((1, 32),))
    cotangent = normal_values(key_list[16], (TOKENS, D), 1.0, 6.0, ((0, 32),))
    parents = draw_parents(jax.random.fold_in(key_list[19], 71), 0)
    segments = draw_segments(jax.random.fold_in(key_list[19], 71), 0)
    return dict(activations=activations, query_weight=query_weight, query_bias=query_bias, key_weight=key_weight, value_weight=value_weight, value_bias=value_bias, output_weight=output_weight, output_bias=output_bias, first_gain=first_gain, first_shift=first_shift, inner_weight=inner_weight, inner_bias=inner_bias, outer_weight=outer_weight, outer_bias=outer_bias, second_gain=second_gain, second_shift=second_shift, cotangent=cotangent, parents=parents, segments=segments)


@jax.custom_vjp
def low(v):
    return lax.optimization_barrier(v.astype(jnp.bfloat16)).astype(jnp.float32)

@jax.custom_vjp
def low_back(v):
    return v

def low_keep(v):
    return (low(v), None)

def low_pass(kept, grad):
    return (grad,)

def back_keep(v):
    return (v, None)

def back_low(kept, grad):
    return (low(grad),)
low.defvjp(low_keep, low_pass)
low_back.defvjp(back_keep, back_low)
EPSILON = 1e-06
MASKED = -1000000000.0

def round_both(v):
    return low_back(low(v))

def matmul_high(a, b):
    return jnp.dot(a, b, precision=lax.Precision.HIGHEST)

def layer_norm(z, gain_vec, shift_vec):
    centre = z - lax.optimization_barrier(jnp.mean(z, axis=-1, keepdims=True))
    scaled = centre * lax.rsqrt(lax.optimization_barrier(jnp.mean(centre * centre, axis=-1, keepdims=True)) + EPSILON)
    return scaled * gain_vec + shift_vec

def head_attend(q, k, v, allowed):
    s = low_back(matmul_high(q, k.T) * HEAD_DIM ** (-0.5))
    s = jnp.where(allowed, s, MASKED)
    e = jnp.exp(s - lax.optimization_barrier(jnp.max(s, axis=-1, keepdims=True)))
    p = e / lax.optimization_barrier(jnp.sum(e, axis=-1, keepdims=True))
    return matmul_high(low(p), v)

def one_layer(x, weights, allowed):
    q_weight, q_bias, k_weight, v_weight, v_bias, o_weight, o_bias, gain_one, shift_one, up_weight, up_bias, down_weight, down_bias, gain_two, shift_two = weights
    n = x.shape[0]
    inputs = low(x)
    q = round_both(matmul_high(inputs, q_weight) + q_bias)
    k = round_both(matmul_high(inputs, k_weight))
    v = round_both(matmul_high(inputs, v_weight) + v_bias)

    def split_heads(t):
        return t.reshape(n, HEADS, HEAD_DIM).transpose(1, 0, 2)

    def per_head(triple):
        return head_attend(triple[0], triple[1], triple[2], allowed)
    heads_out = lax.map(jax.checkpoint(per_head), (split_heads(q), split_heads(k), split_heads(v)))
    context = round_both(heads_out.transpose(1, 0, 2).reshape(n, HEADS * HEAD_DIM))
    attn_out = low_back(matmul_high(context, o_weight) + o_bias)
    hidden = layer_norm(x + attn_out, gain_one, shift_one)
    pre_act = low_back(matmul_high(low(hidden), up_weight) + up_bias)
    gelu_out = low(jax.nn.gelu(pre_act, approximate=False))
    ffn_out = low_back(matmul_high(gelu_out, down_weight) + down_bias)
    return layer_norm(hidden + ffn_out, gain_two, shift_two)

def tree_forward(x, weights, labels, parents):
    parent_one = parents[labels]
    parent_two = parents[parent_one]
    allowed = (labels[None, :] == labels[:, None]) | (labels[None, :] == parent_one[:, None]) | (labels[None, :] == parent_two[:, None])
    for i in range(LAYERS):
        x = one_layer(x, tuple((w[i] for w in weights)), allowed)
    return x

def forward(start, weights, segments, parents):
    trees = start.reshape(TREES, TREE_LEN, D)
    labels = segments.reshape(TREES, TREE_LEN)

    def per_tree(pair):
        return tree_forward(pair[0], weights, pair[1], parents)
    return lax.map(jax.checkpoint(per_tree), (trees, labels)).reshape(TREES * TREE_LEN, D)

def reference(activations, query_weight, query_bias, key_weight, value_weight, value_bias, output_weight, output_bias, first_gain, first_shift, inner_weight, inner_bias, outer_weight, outer_bias, second_gain, second_shift, cotangent, parents, segments):
    weights = tuple((w.astype(jnp.float32) for w in (query_weight, query_bias, key_weight, value_weight, value_bias, output_weight, output_bias, first_gain, first_shift, inner_weight, inner_bias, outer_weight, outer_bias, second_gain, second_shift)))
    start = activations.astype(jnp.float32)

    def whole(s, w):
        return forward(s, w, segments, parents)
    outcome, pullback = jax.vjp(whole, start, weights)
    grads = pullback(cotangent.astype(jnp.float32))
    g = grads[1]
    return (outcome.astype(jnp.bfloat16), grads[0].astype(jnp.bfloat16), g[0], g[1], g[2], g[3], g[4], g[5], g[6], g[7], g[8], g[9], g[10], g[11], g[12], g[13], g[14])
```

```python
import jax
import jax.numpy as jnp
from jax import lax
from jax.experimental import pallas as pl
from jax.experimental.pallas import tpu as pltpu
from jax.sharding import PartitionSpec as P

HEADS = 12
HEAD_DIM = 64
LAYERS = 2
TREE_LEN = 4096


EPSILON = 1e-06
MASKED = -1000000000.0


def partner_2(shard, axis, stride):
    return lax.ppermute(shard, axis, [(i, i ^ 1 << stride) for i in range(lax.axis_size(axis))])


def as_sent(shard):
    return jax.tree.map(lambda a: a.astype(jnp.bfloat16) if a.dtype == jnp.float32 else a, shard)


def product(a, b):
    return jnp.dot(a, b, preferred_element_type=jnp.float32)


def product_tn(a, b):
    return lax.dot_general(a, b, (((0,), (0,)), ((), ())), preferred_element_type=jnp.float32)


def product_nt(a, b):
    return lax.dot_general(a, b, (((1,), (1,)), ((), ())), preferred_element_type=jnp.float32)


def exact_gelu(u):
    return jax.nn.gelu(u, approximate=False)


def layer_norm(z, gain_vec, shift_vec):
    centre = z - jnp.mean(z, axis=-1, keepdims=True)
    scaled = centre * lax.rsqrt(jnp.mean(centre * centre, axis=-1, keepdims=True) + EPSILON)
    return scaled * gain_vec.astype(jnp.float32) + shift_vec.astype(jnp.float32)


def norm_backward(z, gain_vec, upstream):
    centre = z - jnp.mean(z, axis=-1, keepdims=True)
    invert = lax.rsqrt(jnp.mean(centre * centre, axis=-1, keepdims=True) + EPSILON)
    scaled = centre * invert
    weighted = upstream * gain_vec.astype(jnp.float32)
    inner = invert * (
        weighted
        - jnp.mean(weighted, axis=-1, keepdims=True)
        - scaled * jnp.mean(weighted * scaled, axis=-1, keepdims=True)
    )
    return (inner, jnp.sum(upstream * scaled, axis=0), jnp.sum(upstream, axis=0))


def lookup_rows(ids, parents):
    table = jnp.arange(parents.shape[0], dtype=jnp.int32)
    return jnp.sum(jnp.where(ids[:, None] == table[None, :], parents[None, :], 0), axis=1)


def join_heads(stacked):
    return stacked.transpose(1, 0, 2).reshape(stacked.shape[1], -1)


def gather_group(key_rows, value_rows, labels, position, bit_count):
    for b in range(bit_count):
        partner = partner_2((key_rows, value_rows, labels), "fsdp", b)
        upper_side = position >> b & 1 == 1
        key_rows = jnp.where(
            upper_side,
            jnp.concatenate([partner[0], key_rows]),
            jnp.concatenate([key_rows, partner[0]]),
        )
        value_rows = jnp.where(
            upper_side,
            jnp.concatenate([partner[1], value_rows]),
            jnp.concatenate([value_rows, partner[1]]),
        )
        labels = jnp.where(
            upper_side, jnp.concatenate([partner[2], labels]), jnp.concatenate([labels, partner[2]])
        )
    return (key_rows, value_rows, labels)


def sum_group(key_grad, value_grad, position, bit_count):
    for b in reversed(range(bit_count)):
        halfway = key_grad.shape[0] // 2
        upper_side = position >> b & 1 == 1
        outgoing = (
            jnp.where(upper_side, key_grad[:halfway], key_grad[halfway:]),
            jnp.where(upper_side, value_grad[:halfway], value_grad[halfway:]),
        )
        partner = partner_2((as_sent(outgoing[0]), as_sent(outgoing[1])), "fsdp", b)
        key_grad = jnp.where(upper_side, key_grad[halfway:], key_grad[:halfway]) + partner[0]
        value_grad = jnp.where(upper_side, value_grad[halfway:], value_grad[:halfway]) + partner[1]
    return (key_grad, value_grad)


def attend_forward(queries, key_rows, value_rows, allowed):
    factor = HEAD_DIM ** (-0.5)

    def one_head(j):
        start = j * HEAD_DIM
        q = lax.dynamic_slice_in_dim(queries, start, HEAD_DIM, 1)
        k = lax.dynamic_slice_in_dim(key_rows, start, HEAD_DIM, 1)
        v = lax.dynamic_slice_in_dim(value_rows, start, HEAD_DIM, 1)
        s = jnp.where(allowed, product_nt(q, k) * factor, MASKED)
        maxima = jnp.max(s, axis=1, keepdims=True)
        e = jnp.exp(s - maxima)
        totals = jnp.sum(e, axis=1, keepdims=True)
        p = (e / totals).astype(jnp.bfloat16)
        return (product(p, v), (maxima + jnp.log(totals))[:, 0])

    stacked, log_total = lax.map(one_head, jnp.arange(HEADS))
    return (join_heads(stacked), log_total)


def attend_backward(queries, key_rows, value_rows, allowed, log_total, grad_context):
    factor = HEAD_DIM ** (-0.5)

    def one_head(j):
        start = j * HEAD_DIM
        q = lax.dynamic_slice_in_dim(queries, start, HEAD_DIM, 1)
        k = lax.dynamic_slice_in_dim(key_rows, start, HEAD_DIM, 1)
        v = lax.dynamic_slice_in_dim(value_rows, start, HEAD_DIM, 1)
        g = lax.dynamic_slice_in_dim(grad_context, start, HEAD_DIM, 1)
        s = jnp.where(allowed, product_nt(q, k) * factor, MASKED)
        p = jnp.where(allowed, jnp.exp(s - log_total[j][:, None]), 0.0)
        grad_p = product_nt(g, v)
        grad_v = product_tn(p.astype(jnp.bfloat16), g)
        grad_s = (p * (grad_p - jnp.sum(p * grad_p, axis=1, keepdims=True))).astype(jnp.bfloat16)
        grad_q = product(grad_s, k) * factor
        grad_k = product_tn(grad_s, q) * factor
        return (grad_q, grad_k, grad_v)

    grad_q, grad_k, grad_v = lax.map(one_head, jnp.arange(HEADS))
    return (join_heads(grad_q), join_heads(grad_k), join_heads(grad_v))


def layer_forward(state, full, segments, parent_one, parent_two, position, bit_count):
    (
        q_weight,
        q_bias,
        k_weight,
        v_weight,
        v_bias,
        o_weight,
        o_bias,
        gain_one,
        shift_one,
        up_weight,
        up_bias,
        down_weight,
        down_bias,
        gain_two,
        shift_two,
    ) = full
    inputs = state.astype(jnp.bfloat16)
    queries = (product(inputs, q_weight) + q_bias).astype(jnp.bfloat16)
    key_local = product(inputs, k_weight).astype(jnp.bfloat16)
    value_local = (product(inputs, v_weight) + v_bias).astype(jnp.bfloat16)
    key_rows, value_rows, labels = gather_group(
        key_local, value_local, segments, position, bit_count
    )
    allowed = (
        (labels[None, :] == segments[:, None])
        | (labels[None, :] == parent_one[:, None])
        | (labels[None, :] == parent_two[:, None])
    )
    context_wide, log_total = attend_forward(queries, key_rows, value_rows, allowed)
    context = context_wide.astype(jnp.bfloat16)
    first_sum = state + product(context, o_weight) + o_bias
    hidden = layer_norm(first_sum, gain_one, shift_one)
    hidden_low = hidden.astype(jnp.bfloat16)
    pre_act = product(hidden_low, up_weight) + up_bias
    gelu_out = exact_gelu(pre_act).astype(jnp.bfloat16)
    second_sum = hidden + product(gelu_out, down_weight) + down_bias
    record = (
        inputs,
        queries,
        key_rows,
        value_rows,
        allowed,
        log_total,
        context,
        first_sum,
        hidden_low,
        pre_act,
        gelu_out,
        second_sum,
    )
    return (record, layer_norm(second_sum, gain_two, shift_two))


def layer_backward(upstream, full, record, position, bit_count):
    (
        q_weight,
        q_bias,
        k_weight,
        v_weight,
        v_bias,
        o_weight,
        o_bias,
        gain_one,
        shift_one,
        up_weight,
        up_bias,
        down_weight,
        down_bias,
        gain_two,
        shift_two,
    ) = full
    (
        inputs,
        queries,
        key_rows,
        value_rows,
        allowed,
        log_total,
        context,
        first_sum,
        hidden_low,
        pre_act,
        gelu_out,
        second_sum,
    ) = record
    grad_z2, grad_gain_two, grad_shift_two = norm_backward(second_sum, gain_two, upstream)
    grad_f = grad_z2.astype(jnp.bfloat16)
    grad_down_bias = jnp.sum(grad_f.astype(jnp.float32), axis=0)
    grad_down = product_tn(gelu_out, grad_f)
    grad_gelu = product_nt(grad_f, down_weight)
    unused_value, gelu_back = jax.vjp(exact_gelu, pre_act)
    grad_u = gelu_back(grad_gelu)[0].astype(jnp.bfloat16)
    grad_up_bias = jnp.sum(grad_u.astype(jnp.float32), axis=0)
    grad_up = product_tn(hidden_low, grad_u)
    grad_h = grad_z2 + product_nt(grad_u, up_weight)
    grad_z1, grad_gain_one, grad_shift_one = norm_backward(first_sum, gain_one, grad_h)
    grad_a = grad_z1.astype(jnp.bfloat16)
    grad_o_bias = jnp.sum(grad_a.astype(jnp.float32), axis=0)
    grad_o = product_tn(context, grad_a)
    grad_context = product_nt(grad_a, o_weight).astype(jnp.bfloat16)
    grad_q, key_grad, value_grad = attend_backward(
        queries, key_rows, value_rows, allowed, log_total, grad_context
    )
    key_grad, value_grad = sum_group(key_grad, value_grad, position, bit_count)
    q_low = grad_q.astype(jnp.bfloat16)
    k_low = key_grad.astype(jnp.bfloat16)
    v_low = value_grad.astype(jnp.bfloat16)
    grad_x = (
        grad_z1
        + product_nt(q_low, q_weight)
        + product_nt(k_low, k_weight)
        + product_nt(v_low, v_weight)
    )
    terms = (
        product_tn(inputs, q_low),
        jnp.sum(q_low.astype(jnp.float32), axis=0),
        product_tn(inputs, k_low),
        product_tn(inputs, v_low),
        jnp.sum(v_low.astype(jnp.float32), axis=0),
        grad_o,
        grad_o_bias,
        grad_gain_one,
        grad_shift_one,
        grad_up,
        grad_up_bias,
        grad_down,
        grad_down_bias,
        grad_gain_two,
        grad_shift_two,
    )
    return (grad_x, terms)


def stack_layers(groups, n):
    return jnp.stack([g[n] for g in groups])


def body(
    activations,
    query_weight,
    query_bias,
    key_weight,
    value_weight,
    value_bias,
    output_weight,
    output_bias,
    first_gain,
    first_shift,
    inner_weight,
    inner_bias,
    outer_weight,
    outer_bias,
    second_gain,
    second_shift,
    cotangent,
    parents,
    segments,
):
    position = lax.axis_index("fsdp")
    bit_count = (TREE_LEN // activations.shape[0]).bit_length() - 1
    parent_one = lookup_rows(segments, parents)
    parent_two = lookup_rows(parent_one, parents)
    state = activations.astype(jnp.float32)
    saved = []
    kept_weights = []
    for i in range(LAYERS):
        full = (
            lax.all_gather(query_weight[i], "fsdp", axis=0, tiled=True),
            lax.all_gather(query_bias[i], "fsdp", axis=0, tiled=True),
            lax.all_gather(key_weight[i], "fsdp", axis=0, tiled=True),
            lax.all_gather(value_weight[i], "fsdp", axis=0, tiled=True),
            lax.all_gather(value_bias[i], "fsdp", axis=0, tiled=True),
            lax.all_gather(output_weight[i], "fsdp", axis=0, tiled=True),
            lax.all_gather(output_bias[i], "fsdp", axis=0, tiled=True),
            lax.all_gather(first_gain[i], "fsdp", axis=0, tiled=True),
            lax.all_gather(first_shift[i], "fsdp", axis=0, tiled=True),
            lax.all_gather(inner_weight[i], "fsdp", axis=0, tiled=True),
            lax.all_gather(inner_bias[i], "fsdp", axis=0, tiled=True),
            lax.all_gather(outer_weight[i], "fsdp", axis=0, tiled=True),
            lax.all_gather(outer_bias[i], "fsdp", axis=0, tiled=True),
            lax.all_gather(second_gain[i], "fsdp", axis=0, tiled=True),
            lax.all_gather(second_shift[i], "fsdp", axis=0, tiled=True),
        )
        kept_weights.append(full)
        record, state = layer_forward(
            state, full, segments, parent_one, parent_two, position, bit_count
        )
        saved.append(record)
    outcome = state.astype(jnp.bfloat16)
    upstream = cotangent.astype(jnp.float32)
    layer_grads = [None] * LAYERS
    for i in reversed(range(LAYERS)):
        full = (
            lax.all_gather(query_weight[i], "fsdp", axis=0, tiled=True),
            lax.all_gather(query_bias[i], "fsdp", axis=0, tiled=True),
            lax.all_gather(key_weight[i], "fsdp", axis=0, tiled=True),
            lax.all_gather(value_weight[i], "fsdp", axis=0, tiled=True),
            lax.all_gather(value_bias[i], "fsdp", axis=0, tiled=True),
            lax.all_gather(output_weight[i], "fsdp", axis=0, tiled=True),
            lax.all_gather(output_bias[i], "fsdp", axis=0, tiled=True),
            lax.all_gather(first_gain[i], "fsdp", axis=0, tiled=True),
            lax.all_gather(first_shift[i], "fsdp", axis=0, tiled=True),
            lax.all_gather(inner_weight[i], "fsdp", axis=0, tiled=True),
            lax.all_gather(inner_bias[i], "fsdp", axis=0, tiled=True),
            lax.all_gather(outer_weight[i], "fsdp", axis=0, tiled=True),
            lax.all_gather(outer_bias[i], "fsdp", axis=0, tiled=True),
            lax.all_gather(second_gain[i], "fsdp", axis=0, tiled=True),
            lax.all_gather(second_shift[i], "fsdp", axis=0, tiled=True),
        )
        upstream, terms = layer_backward(upstream, full, saved[i], position, bit_count)
        layer_grads[i] = (
            lax.psum_scatter(terms[0], "fsdp", scatter_dimension=0, tiled=True),
            lax.psum_scatter(terms[1], "fsdp", scatter_dimension=0, tiled=True),
            lax.psum_scatter(terms[2], "fsdp", scatter_dimension=0, tiled=True),
            lax.psum_scatter(terms[3], "fsdp", scatter_dimension=0, tiled=True),
            lax.psum_scatter(terms[4], "fsdp", scatter_dimension=0, tiled=True),
            lax.psum_scatter(terms[5], "fsdp", scatter_dimension=0, tiled=True),
            lax.psum_scatter(terms[6], "fsdp", scatter_dimension=0, tiled=True),
            lax.psum_scatter(terms[7], "fsdp", scatter_dimension=0, tiled=True),
            lax.psum_scatter(terms[8], "fsdp", scatter_dimension=0, tiled=True),
            lax.psum_scatter(terms[9], "fsdp", scatter_dimension=0, tiled=True),
            lax.psum_scatter(terms[10], "fsdp", scatter_dimension=0, tiled=True),
            lax.psum_scatter(terms[11], "fsdp", scatter_dimension=0, tiled=True),
            lax.psum_scatter(terms[12], "fsdp", scatter_dimension=0, tiled=True),
            lax.psum_scatter(terms[13], "fsdp", scatter_dimension=0, tiled=True),
            lax.psum_scatter(terms[14], "fsdp", scatter_dimension=0, tiled=True),
        )
    shares = tuple((stack_layers(layer_grads, n) for n in range(15)))
    return (outcome, upstream.astype(jnp.bfloat16)) + tuple(shares)


MESH = pl.DeviceIdType.MESH
BF = jnp.bfloat16
F32 = jnp.float32
WIDE = 768
SLICE = 384
PACKED = 640
ROWS = 128
NKEYS = 1536


class Pool:
    def __init__(self, ref):
        self.ref = ref
        self.used = 0

    def take(self):
        self.used += 1
        return self.ref.at[self.used - 1]

    def block(self, n):
        first = self.used
        self.used += n
        return lambda i: self.ref.at[first + i]


class Place:
    def __init__(self):
        me = lax.axis_index("fsdp")
        p = lax.rem(me, 32)
        self.base = me - p
        self.z = p // 8
        self.f = lax.rem(p // 2, 4)
        self.c = lax.rem(p, 2)

    def at(self, z, f, c):
        return self.base + 8 * z + 2 * f + c

    def f_at(self, k):
        return lax.rem(self.f + k + 4, 4)

    def z_at(self, k):
        return lax.rem(self.z + k + 4, 4)

    def plane(self, k):
        return self.at(self.z, self.f_at(k), self.c)

    def column(self, k):
        return self.at(self.z_at(k), self.f, self.c)

    def sibling(self):
        return self.at(self.z, self.f, 1 - self.c)


def greet(place):
    barrier = pltpu.get_barrier_semaphore()
    for dev in [place.plane(k) for k in (1, 2, 3)] + [place.column(k) for k in (1, 2, 3)] + [place.sibling()]:
        pl.semaphore_signal(barrier, inc=1, device_id=(dev,), device_id_type=MESH)
    pl.semaphore_wait(barrier, 7)


def remote(src, dst, sems, device):
    return pltpu.make_async_remote_copy(
        src_ref=src, dst_ref=dst, send_sem=sems[0], recv_sem=sems[1], device_id=(device,), device_id_type=MESH
    )


def norm_rows(z, gain, shift):
    centre = z - jnp.mean(z, axis=-1, keepdims=True)
    inv = lax.rsqrt(jnp.mean(centre * centre, axis=-1, keepdims=True) + EPSILON)
    return centre * inv * gain + shift


def norm_rows_back(z, gain, upstream):
    centre = z - jnp.mean(z, axis=-1, keepdims=True)
    inv = lax.rsqrt(jnp.mean(centre * centre, axis=-1, keepdims=True) + EPSILON)
    scaled = centre * inv
    weighted = upstream * gain
    inner = inv * (
        weighted
        - jnp.mean(weighted, axis=-1, keepdims=True)
        - scaled * jnp.mean(weighted * scaled, axis=-1, keepdims=True)
    )
    return inner, jnp.sum(upstream * scaled, axis=0, keepdims=True), jnp.sum(upstream, axis=0, keepdims=True)


def weights_kernel(
    col, rows_out, rows_o, small, colg, outg, og, smallg, send_sems, recv_sems, local_sems
):
    place = Place()
    z, f, c = place.z, place.f, place.c
    sends, recvs, locs = Pool(send_sems), Pool(recv_sems), Pool(local_sems)

    def pair():
        return sends.take(), recvs.take()

    mine = [
        pltpu.make_async_copy(col.at[f], colg.at[z, c, f], locs.take()),
        pltpu.make_async_copy(small, smallg.at[z, c, f], locs.take()),
        pltpu.make_async_copy(rows_out, outg.at[z, c], locs.take()),
    ]
    o_copy = pltpu.make_async_copy(rows_o, og.at[c, f], locs.take())
    for m in mine:
        m.start()

    @pl.when(f == z)
    def _():
        o_copy.start()

    greet(place)
    flying = []
    first = []
    for k in (1, 2, 3):
        a = remote(col.at[place.f_at(k)], colg.at[z, c, f], pair(), place.plane(k))
        b = remote(small, smallg.at[z, c, f], pair(), place.plane(k))
        a.start()
        b.start()
        first += [a, b]
        flying += [a, b]
    o_send, o_recv = sends.take(), recvs.block(4)
    o_index = lax.rem(z - f + 4, 4)
    o_first = remote(rows_o, og.at[c, f], (o_send, o_recv(o_index)), place.at(z, z, c))

    @pl.when(f != z)
    def _():
        o_first.start()

    out_moves = []
    for k in (1, 2, 3):
        a = remote(rows_out, outg.at[z, c], pair(), place.column(k))
        a.start()
        out_moves.append(a)
    flying += out_moves
    for m in mine:
        m.wait()
    for a in first:
        a.wait_recv()
    moves = []
    for k in (1, 2, 3):
        a = remote(colg.at[z, c], colg.at[z, c], pair(), place.column(k))
        b = remote(smallg.at[z, c], smallg.at[z, c], pair(), place.column(k))
        a.start()
        b.start()
        moves.append((a, b))
        flying += [a, b]
    o_sends, o_arrive = sends.block(4), recvs.take()
    o_moves = [
        remote(og.at[c], og.at[c], (o_sends(k), o_arrive), place.column(k)) for k in (1, 2, 3)
    ]

    @pl.when(f == z)
    def _():
        o_copy.wait()
        for k in (1, 2, 3):
            remote(rows_o, og.at[c, f], (o_send, o_recv(k)), place.at(z, z, c)).wait_recv()
        for m in o_moves:
            m.start()

    side = []

    def hand_over(zz):
        for ref in (colg, outg, smallg):
            a = remote(ref.at[zz, c], ref.at[zz, c], pair(), place.sibling())
            a.start()
            side.append(a)

    hand_over(z)
    for k in (1, 2, 3):
        moves[k - 1][0].wait_recv()
        moves[k - 1][1].wait_recv()
        out_moves[k - 1].wait_recv()
        hand_over(place.z_at(-k))

    @pl.when(f != z)
    def _():
        o_moves[0].wait_recv()

    a = remote(og.at[c], og.at[c], pair(), place.sibling())
    a.start()
    side.append(a)
    for a in side:
        a.wait_recv()
    for a in flying + side:
        a.wait_send()

    @pl.when(f != z)
    def _():
        o_first.wait_send()

    @pl.when(f == z)
    def _():
        for m in o_moves:
            m.wait_send()


def pick_parents(kp, kv, route, zz, cc):
    def one(b, carry):
        total = kp[b, cc]
        for ft in range(4):
            total = total + kv[zz, cc, ft * ROWS : (ft + 1) * ROWS, :] * route[b, 4 * zz + ft].astype(BF)
        kp[b, cc] = total
        return carry

    lax.fori_loop(0, 4, one, 0)


def all_keys(kv, kp, z, b, lanes):
    rows = pl.ds(pl.multiple_of(b * ROWS, ROWS), ROWS)
    return jnp.concatenate(
        [
            kv[0, 0, :, lanes], kv[0, 1, :, lanes], kv[z, 0, rows, lanes], kv[z, 1, rows, lanes],
            kp[b, 0, :, lanes], kp[b, 1, :, lanes],
        ],
        axis=0,
    )


def forward_kernel(
    x_ref, wqkv, wo, win, wout, vec, route, pen,
    xn_ref, xb_o, qp_o, kv_o, kp_o, p_o, ctx_o, z1_o, hb_o, gp_o, gl_o, z2_o,
    xb, qp, kv, kp, p, ctx, hb, gp, gl, z1, z2, own, rs1_s, rs1_r, rs2_s, rs2_r,
    send_sems, recv_sems, local_sems,
):
    place = Place()
    z, f, c = place.z, place.f, place.c
    sends, recvs, locs = Pool(send_sems), Pool(recv_sems), Pool(local_sems)
    flying, saving = [], []

    def launch(src, dst, device):
        a = remote(src, dst, (sends.take(), recvs.take()), device)
        a.start()
        flying.append(a)
        return a

    def save(src, dst):
        a = pltpu.make_async_copy(src, dst, locs.take())
        a.start()
        saving.append(a)

    xb[f] = x_ref[...].astype(BF)
    greet(place)
    came = [None] + [launch(xb.at[f], xb.at[f], place.plane(k)) for k in (1, 2, 3)]
    lane = lax.broadcasted_iota(jnp.int32, (ROWS, 128), 1)
    for k in range(4):
        g = place.f_at(-k)
        if k:
            came[k].wait_recv()
        qkv = product(xb[g], wqkv[...]) + vec[0:1, :PACKED]
        rows = pl.ds(pl.multiple_of(g * ROWS, ROWS), ROWS)
        kv[z, c, rows, :] = qkv[:, 256:].astype(BF)
        scaled = qkv[:, :256] * (HEAD_DIM ** (-0.5))
        front = scaled[:, :128]
        qp[rows, 0:128] = jnp.where(lane < 64, front, 0.0).astype(BF)
        qp[rows, 128:256] = jnp.where(lane < 64, pltpu.roll(front, 64, 1), 0.0).astype(BF)
        qp[rows, 256:384] = scaled[:, 128:].astype(BF)
    move = [launch(kv.at[z, c], kv.at[z, c], place.column(k)) for k in (1, 2, 3)]
    side = [launch(kv.at[z, c], kv.at[z, c], place.sibling())]
    save(xb, xb_o)
    save(qp, qp_o)
    kp[...] = jnp.zeros_like(kp)
    pick_parents(kp, kv, route, z, c)
    for k in (1, 2, 3):
        move[k - 1].wait_recv()
        there = place.z_at(-k)
        side.append(launch(kv.at[there, c], kv.at[there, c], place.sibling()))
        pick_parents(kp, kv, route, there, c)
    for k in range(4):
        side[k].wait_recv()
        pick_parents(kp, kv, route, place.z_at(-k), 1 - c)
    save(kp, kp_o)
    save(kv, kv_o)

    def attend(i, carry):
        h, b = i // 4, lax.rem(i, 4)
        lanes = pl.ds(pl.multiple_of(h * 128, 128), 128)
        rows = pl.ds(pl.multiple_of(b * ROWS, ROWS), ROWS)
        keys = all_keys(kv, kp, z, b, lanes)
        s = product_nt(qp[rows, lanes], keys)
        s = jnp.concatenate(
            [s[:, :1024], s[:, 1024:1280] + pen[4 + b], s[:, 1280:] + pen[b]], axis=1
        )
        e = jnp.exp(s - jnp.max(s, axis=1, keepdims=True))
        pb = (e / jnp.sum(e, axis=1, keepdims=True)).astype(BF)
        p[h, b] = pb
        ctx[rows, lanes] = product(pb, keys).astype(BF)
        return carry

    lax.fori_loop(0, 12, attend, 0)
    save(p, p_o)
    save(ctx, ctx_o)
    back = [None]
    for k in (1, 2, 3, 0):
        g = place.f_at(-k)
        rows = pl.ds(pl.multiple_of(g * ROWS, ROWS), ROWS)
        part = product(ctx[rows, :], wo[...])
        if k:
            rs1_s[k - 1] = part.astype(BF)
            back.append(launch(rs1_s.at[k - 1], rs1_r.at[k - 1], place.plane(-k)))
        else:
            own[...] = part
    for k in (1, 2, 3):
        back[k].wait_recv()
    total = own[...] + rs1_r[0].astype(F32) + rs1_r[1].astype(F32) + rs1_r[2].astype(F32)
    zz = x_ref[...] + total + vec[1:2, :]
    z1[...] = zz
    save(z1, z1_o)
    hidden = norm_rows(zz, vec[2:3, :], vec[3:4, :])
    hb[f] = hidden.astype(BF)
    came = [None] + [launch(hb.at[f], hb.at[f], place.plane(k)) for k in (1, 2, 3)]
    back = [None]
    for k in range(4):
        g = place.f_at(-k)
        if k:
            came[k].wait_recv()
        u = product(hb[g], win[...]) + vec[4:5, :]
        cdf = 0.5 * (1.0 + lax.erf(u * (0.5 ** 0.5)))
        gp[g] = cdf + u * jnp.exp(-0.5 * u * u) * 0.3989422804014327
        low = (u * cdf).astype(BF)
        gl[g] = low
        part = product(low, wout[...])
        if k:
            rs2_s[k - 1] = part.astype(BF)
            back.append(launch(rs2_s.at[k - 1], rs2_r.at[k - 1], place.plane(-k)))
        else:
            own[...] = part
    save(hb, hb_o)
    save(gp, gp_o)
    save(gl, gl_o)
    for k in (1, 2, 3):
        back[k].wait_recv()
    total = own[...] + rs2_r[0].astype(F32) + rs2_r[1].astype(F32) + rs2_r[2].astype(F32)
    zz = norm_rows(z1[...], vec[2:3, :], vec[3:4, :]) + total + vec[5:6, :]
    z2[...] = zz
    save(z2, z2_o)
    xn_ref[...] = norm_rows(zz, vec[6:7, :], vec[7:8, :])
    for a in saving:
        a.wait()
    for a in flying:
        a.wait_send()


def backward_kernel(
    dy_ref, wqkv, wo, win, wout, vec, route, xb, qp, kv, kp, p, ctx, z1, hb, gp, gl, z2,
    dx_ref, dqkv_o, din_o, dout_o, do_o, dvec_o,
    df, du, da, dctx, dqf, dqkv, dz, dz1, dkt, dself, dpar, tgt, tgt_r, summed, summed_r,
    own, rs1_s, rs1_r, rs2_s, rs2_r, send_sems, recv_sems,
):
    place = Place()
    z, f, c = place.z, place.f, place.c
    sends, recvs = Pool(send_sems), Pool(recv_sems)
    flying = []

    def launch(src, dst, device):
        a = remote(src, dst, (sends.take(), recvs.take()), device)
        a.start()
        flying.append(a)
        return a

    def whole(ref):
        return ref[...].reshape(4 * ROWS, ref.shape[-1])

    grad, dgain, dshift = norm_rows_back(z2[...], vec[6:7, :], dy_ref[...])
    dvec_o[6:7, :] = dgain
    dvec_o[7:8, :] = dshift
    dz[...] = grad
    low = grad.astype(BF)
    df[f] = low
    dvec_o[5:6, :] = jnp.sum(low.astype(F32), axis=0, keepdims=True)
    greet(place)
    came = [None] + [launch(df.at[f], df.at[f], place.plane(k)) for k in (1, 2, 3)]
    back = [None]
    bias = jnp.zeros((1, WIDE), F32)
    for k in range(4):
        g = place.f_at(-k)
        if k:
            came[k].wait_recv()
        low = (product_nt(df[g], wout[...]) * gp[g]).astype(BF)
        du[g] = low
        bias = bias + jnp.sum(low.astype(F32), axis=0, keepdims=True)
        part = product_nt(low, win[...])
        if k:
            rs1_s[k - 1] = part.astype(BF)
            back.append(launch(rs1_s.at[k - 1], rs1_r.at[k - 1], place.plane(-k)))
        else:
            own[...] = part
    dvec_o[4:5, :] = bias

    def ffn_grads(i, carry):
        lanes = pl.ds(pl.multiple_of(i * 256, 256), 256)
        dout_o[lanes, :] = product_tn(gl[:, :, lanes].reshape(512, 256), whole(df)).astype(BF)
        din_o[lanes, :] = product_tn(hb[:, :, lanes].reshape(512, 256), whole(du)).astype(BF)
        return carry

    lax.fori_loop(0, 3, ffn_grads, 0)
    for k in (1, 2, 3):
        back[k].wait_recv()
    up = dz[...] + own[...] + rs1_r[0].astype(F32) + rs1_r[1].astype(F32) + rs1_r[2].astype(F32)
    grad, dgain, dshift = norm_rows_back(z1[...], vec[2:3, :], up)
    dvec_o[2:3, :] = dgain
    dvec_o[3:4, :] = dshift
    dz1[...] = grad
    low = grad.astype(BF)
    da[f] = low
    dvec_o[1:2, :] = jnp.sum(low.astype(F32), axis=0, keepdims=True)
    came = [None] + [launch(da.at[f], da.at[f], place.plane(k)) for k in (1, 2, 3)]
    dkt[...] = jnp.zeros_like(dkt)
    for k in range(4):
        g = place.f_at(-k)
        rows = pl.ds(pl.multiple_of(g * ROWS, ROWS), ROWS)
        if k:
            came[k].wait_recv()
        dctx[rows, :] = product_nt(da[g], wo[...]).astype(BF)

    def attend(i, carry):
        h, b = i // 4, lax.rem(i, 4)
        lanes = pl.ds(pl.multiple_of(h * 128, 128), 128)
        rows = pl.ds(pl.multiple_of(b * ROWS, ROWS), ROWS)
        keys = all_keys(kv, kp, z, b, lanes)
        q, g = qp[rows, lanes], dctx[rows, lanes]
        low = p[h, b]
        pf = low.astype(F32)
        dp = product_nt(g, keys)
        t = pf * dp
        ds = (t - pf * jnp.sum(t, axis=1, keepdims=True)).astype(BF)
        dqf[h, rows, :] = product(ds, keys) * (HEAD_DIM ** (-0.5))
        dkv = product_tn(jnp.concatenate([ds, low], axis=0), jnp.concatenate([q, g], axis=0))
        dkt[:, lanes] += dkv[:1024]
        dself[b, :, lanes] = dkv[1024:1280]
        dpar[b, :, lanes] = dkv[1280:]
        return carry

    lax.fori_loop(0, 12, attend, 0)
    for cc in range(2):
        tgt[cc, 0] = dkt[cc * 512 : (cc + 1) * 512, :].astype(BF)

    def scatter(i, carry):
        zt, ft = 1 + i // 4, lax.rem(i, 4)
        rows = pl.ds(pl.multiple_of(ft * ROWS, ROWS), ROWS)
        here = jnp.where(zt == z, 1.0, 0.0)
        for cc in range(2):
            half = slice(cc * ROWS, (cc + 1) * ROWS)
            total = dself[ft, half, :] * here
            for b in range(4):
                total = total + dpar[b, half, :] * route[b, 4 * zt + ft]
            tgt[cc, zt, rows, :] = total.astype(BF)
        return carry

    lax.fori_loop(0, 12, scatter, 0)
    near = launch(tgt.at[1 - c], tgt_r, place.sibling())
    lane = lax.broadcasted_iota(jnp.int32, (ROWS, 128), 1)
    for g in range(4):
        rows = slice(g * ROWS, (g + 1) * ROWS)
        first = jnp.where(lane < 64, dqf[0, rows, :], pltpu.roll(dqf[1, rows, :], 64, 1))
        dqkv[g, :, 0:128] = first.astype(BF)
        dqkv[g, :, 128:256] = jnp.where(lane < 64, dqf[2, rows, :], 0.0).astype(BF)
    near.wait_recv()
    for zt in range(4):
        summed[zt] = (tgt[c, zt].astype(F32) + tgt_r[zt].astype(F32)).astype(BF)
    far = [launch(summed.at[place.z_at(k)], summed_r.at[k - 1], place.column(k)) for k in (1, 2, 3)]
    do_o[...] = product_tn(ctx[...], whole(da)).astype(BF)
    for a in far:
        a.wait_recv()
    total = summed[z].astype(F32) + summed_r[0].astype(F32) + summed_r[1].astype(F32) + summed_r[2].astype(F32)
    for g in range(4):
        dqkv[g, :, 256:] = total[g * ROWS : (g + 1) * ROWS, :].astype(BF)
    back = [None]
    for k in (1, 2, 3, 0):
        g = place.f_at(-k)
        part = product_nt(dqkv[g], wqkv[...])
        if k:
            rs2_s[k - 1] = part.astype(BF)
            back.append(launch(rs2_s.at[k - 1], rs2_r.at[k - 1], place.plane(-k)))
        else:
            own[...] = part

    def qkv_grads(i, carry):
        lanes = pl.ds(pl.multiple_of(i * 256, 256), 256)
        dqkv_o[lanes, :] = product_tn(xb[:, :, lanes].reshape(512, 256), whole(dqkv)).astype(BF)
        return carry

    lax.fori_loop(0, 3, qkv_grads, 0)
    sums = jnp.sum(whole(dqkv).astype(F32), axis=0, keepdims=True)
    dvec_o[0:1, :] = jnp.concatenate([sums, jnp.zeros((1, WIDE - PACKED), F32)], axis=1)
    for k in (1, 2, 3):
        back[k].wait_recv()
    dx_ref[...] = dz1[...] + own[...] + rs2_r[0].astype(F32) + rs2_r[1].astype(F32) + rs2_r[2].astype(F32)
    for a in flying:
        a.wait_send()


def reduce_kernel(
    gcol, gout, go, gsm, col_o, out_o, o_o, sm_o,
    col_a, out_a, o_a, sm_a, col_u, out_u, o_u, sm_u, col_b, out_b, o_b, sm_b, col_v, o_v, sm_v,
    send_sems, recv_sems,
):
    place = Place()
    z, f, c = place.z, place.f, place.c
    sends, recvs = Pool(send_sems), Pool(recv_sems)
    flying = []

    def launch(src, dst, device):
        a = remote(src, dst, (sends.take(), recvs.take()), device)
        a.start()
        flying.append(a)
        return a

    greet(place)
    sib = place.sibling()
    near = [
        launch(gcol.at[1 - c], col_a, sib),
        launch(gout.at[1 - c], out_a, sib),
        launch(go.at[1 - c], o_a, sib),
        launch(gsm, sm_a, sib),
    ]
    for a in near:
        a.wait_recv()
    sm_u[...] = gsm[...] + sm_a[...]
    o_u[...] = (go[c].astype(F32) + o_a[...].astype(F32)).astype(BF)

    def chip_sum(i, carry):
        col_u[i] = (gcol[c, i].astype(F32) + col_a[i].astype(F32)).astype(BF)
        out_u[i] = (gout[c, i].astype(F32) + out_a[i].astype(F32)).astype(BF)
        return carry

    lax.fori_loop(0, 4, chip_sum, 0)
    far = []
    for k in (1, 2, 3):
        there = place.z_at(k)
        far.append(launch(col_u.at[there], col_b.at[k - 1], place.column(k)))
        far.append(launch(out_u.at[there], out_b.at[k - 1], place.column(k)))
        far.append(launch(sm_u, sm_b.at[k - 1], place.column(k)))
    o_send, o_recv = sends.take(), recvs.block(4)
    shift = lax.rem(f - z + 4, 4)
    o_far = remote(o_u, o_b.at[shift], (o_send, o_recv(shift)), place.at(f, f, c))

    @pl.when(f != z)
    def _():
        o_far.start()

    @pl.when(f == z)
    def _():
        for k in (1, 2, 3):
            remote(o_u, o_b.at[k], (o_send, o_recv(k)), place.at(f, f, c)).wait_recv()
        for g in range(4):
            rows = slice(g * 48, (g + 1) * 48)
            o_v[g] = (
                o_u[rows, :].astype(F32)
                + o_b[1, rows, :].astype(F32)
                + o_b[2, rows, :].astype(F32)
                + o_b[3, rows, :].astype(F32)
            ).astype(BF)

    for a in far:
        a.wait_recv()
    sm_v[...] = sm_u[...] + sm_b[0] + sm_b[1] + sm_b[2]
    out_o[...] = out_u[z].astype(F32) + out_b[0].astype(F32) + out_b[1].astype(F32) + out_b[2].astype(F32)
    for g in range(4):
        rows = slice(g * 48, (g + 1) * 48)
        col_v[g] = (
            col_u[z, rows, :].astype(F32)
            + col_b[0, rows, :].astype(F32)
            + col_b[1, rows, :].astype(F32)
            + col_b[2, rows, :].astype(F32)
        ).astype(BF)
    last = []
    for k in (1, 2, 3):
        last.append(launch(col_v.at[place.f_at(k)], col_o.at[f], place.plane(k)))
        last.append(launch(sm_v, sm_o.at[f], place.plane(k)))
    col_o[f] = col_v[f]
    sm_o[f] = sm_v[...]
    o_sends, o_last = sends.block(4), recvs.take()
    moves = [
        remote(o_v.at[place.f_at(k)], o_o, (o_sends(k), o_last), place.plane(k)) for k in (1, 2, 3)
    ]

    @pl.when(f == z)
    def _():
        for m in moves:
            m.start()
        o_o[...] = o_v[f]

    @pl.when(f != z)
    def _():
        moves[0].wait_recv()

    for a in last:
        a.wait_recv()
    for a in flying:
        a.wait_send()

    @pl.when(f != z)
    def _():
        o_far.wait_send()

    @pl.when(f == z)
    def _():
        for m in moves:
            m.wait_send()


ANY = pl.BlockSpec(memory_space=pl.ANY)
VM = pl.BlockSpec(memory_space=pltpu.VMEM)
SM = pl.BlockSpec(memory_space=pltpu.SMEM)
LIMIT = 60 * 1024 * 1024


def shape(*dims, dtype=BF):
    return jax.ShapeDtypeStruct(dims, dtype)


def call(kernel, number, outs, out_specs, in_specs, scratch, sems, args, flops):
    return pl.pallas_call(
        kernel,
        out_shape=outs,
        in_specs=in_specs,
        out_specs=out_specs,
        scratch_shapes=[pltpu.VMEM(s.shape, s.dtype) for s in scratch]
        + [pltpu.SemaphoreType.DMA((n,)) for n in sems],
        compiler_params=pltpu.CompilerParams(
            collective_id=number, has_side_effects=True, vmem_limit_bytes=LIMIT
        ),
        cost_estimate=pl.CostEstimate(flops=flops, bytes_accessed=20000000, transcendentals=0),
    )(*args)


def column_parts(query, key, value, inner):
    n = query.shape[0] * query.shape[1]
    q = query.reshape(n, 4, 3, 64)
    q = jnp.pad(q, ((0, 0), (0, 0), (0, 1), (0, 0))).reshape(n, 4, 256)
    kv = jnp.stack([key.reshape(n, 4, 3, 64), value.reshape(n, 4, 3, 64)], axis=3).reshape(n, 4, 384)
    up = inner.reshape(n, 4, 4, 192).transpose(0, 2, 1, 3).reshape(n, 4, WIDE)
    return jnp.concatenate([q, kv, up], axis=2).transpose(1, 0, 2)


def gather_weights(col, rows_out, rows_o, small):
    return call(
        weights_kernel, 0,
        (shape(4, 2, 4, 48, 1408), shape(4, 2, 192, WIDE), shape(2, 4, 48, WIDE), shape(4, 2, 4, 16, 128)),
        (ANY,) * 4, [ANY] * 4, [], (64, 64, 8), (col, rows_out, rows_o, small), 1000,
    )


def forward_layer(state, weights, vec, route, pen):
    wqkv, wo, win, wout = weights
    saved = (
        shape(4, ROWS, WIDE), shape(512, SLICE), shape(4, 2, 512, SLICE), shape(4, 2, ROWS, SLICE), shape(3, 4, ROWS, NKEYS),
        shape(512, SLICE), shape(ROWS, WIDE, dtype=F32), shape(4, ROWS, WIDE), shape(4, ROWS, WIDE, dtype=F32),
        shape(4, ROWS, WIDE), shape(ROWS, WIDE, dtype=F32),
    )
    xb, qp, kv, kp, p, ctx, z1, hb, gp, gl, z2 = saved
    piece = shape(3, ROWS, WIDE)
    outs = call(
        forward_kernel, 1, (shape(ROWS, WIDE, dtype=F32),) + saved, (VM,) + (ANY,) * 11,
        [VM] * 6 + [SM] * 2,
        [xb, qp, kv, kp, p, ctx, hb, gp, gl, z1, z2, shape(ROWS, WIDE, dtype=F32)] + [piece] * 4,
        (48, 48, 16), (state, wqkv, wo, win, wout, vec, route, pen), 3 * 10**9,
    )
    return outs[0], outs[1:]


def backward_layer(upstream, weights, vec, route, saved):
    wqkv, wo, win, wout = weights
    local = shape(ROWS, WIDE, dtype=F32)
    full = shape(4, ROWS, WIDE)
    piece = shape(3, ROWS, WIDE)
    keys = shape(4, 256, SLICE, dtype=F32)
    return call(
        backward_kernel, 2,
        (local, shape(WIDE, PACKED), shape(WIDE, WIDE), shape(WIDE, WIDE), shape(SLICE, WIDE), shape(8, WIDE, dtype=F32)),
        (VM,) * 6, [VM] * 6 + [SM] + [VM] * 11,
        [full, full, full, shape(512, SLICE), shape(3, 512, 128, dtype=F32), shape(4, ROWS, PACKED), local, local,
         shape(1024, SLICE, dtype=F32), keys, keys, shape(2, 4, 512, SLICE), shape(4, 512, SLICE),
         shape(4, 512, SLICE), shape(3, 512, SLICE), local, piece, piece, piece, piece],
        (48, 48), (upstream, wqkv, wo, win, wout, vec, route) + tuple(saved), 6 * 10**9,
    )


def reduce_grads(gcol, gout, go, gsm):
    half = [shape(4, 192, 1408), shape(4, 192, WIDE), shape(192, WIDE), shape(16, WIDE, dtype=F32)]
    far = [shape(3, 192, 1408), shape(3, 192, WIDE), shape(4, 192, WIDE), shape(3, 16, WIDE, dtype=F32)]
    return call(
        reduce_kernel, 3,
        (shape(4, 48, 1408), shape(192, WIDE, dtype=F32), shape(48, WIDE), shape(4, 16, WIDE, dtype=F32)),
        (VM,) * 4, [VM] * 4,
        half + half + far + [shape(4, 48, 1408), shape(4, 48, WIDE), shape(16, WIDE, dtype=F32)],
        (64, 64), (gcol, gout, go, gsm), 1000,
    )


def slice_body(
    activations, query_weight, query_bias, key_weight, value_weight, value_bias, output_weight, output_bias,
    first_gain, first_shift, inner_weight, inner_bias, outer_weight, outer_bias, second_gain, second_shift,
    cotangent, parents, segments,
):
    place = Place()
    z, f, c = place.z, place.f, place.c
    col = column_parts(query_weight, key_weight, value_weight, inner_weight)
    vectors = (query_bias, value_bias, output_bias, first_gain, first_shift, outer_bias, second_gain, second_shift)
    small = jnp.concatenate([v.reshape(-1) for v in vectors] + [inner_bias.reshape(-1), segments[:1].astype(BF)])
    small = jnp.pad(small, (0, 2048 - small.shape[0])).reshape(16, 128)
    colg, outg, og, smallg = gather_weights(
        col, outer_weight.reshape(192, WIDE), output_weight.reshape(48, WIDE), small
    )
    wide = colg.reshape(4, 2, 4, 2, 24, 1408).transpose(3, 0, 2, 1, 4, 5).reshape(2, WIDE, 1408)
    outer = outg.reshape(4, 2, 2, 96, WIDE).transpose(2, 0, 1, 3, 4).reshape(2, WIDE, WIDE)
    o_rows = og.reshape(2, 4, 2, 24, WIDE).transpose(2, 1, 0, 3, 4).reshape(2, 3, 64, WIDE)
    o_rows = jnp.pad(o_rows, ((0, 0), (0, 0), (64, 0), (0, 0))).reshape(2, SLICE, WIDE)
    flat = smallg.transpose(0, 2, 1, 3, 4).reshape(32, 2048).astype(F32)
    parts = [flat[:, i * 48 : (i + 1) * 48].reshape(32, 2, 24).transpose(1, 0, 2).reshape(2, WIDE) for i in range(8)]
    q_all, v_all, o_all, g1, s1, out_all, g2, s2 = parts
    in_all = flat[:, 384:576].reshape(4, 4, 2, 2, 96)
    in_mine = lax.dynamic_index_in_dim(in_all, f, 1, keepdims=False).transpose(2, 0, 1, 3).reshape(2, WIDE)
    q_mine = lax.dynamic_slice_in_dim(q_all, 192 * f, 192, 1)
    v_mine = lax.dynamic_slice_in_dim(v_all, 192 * f, 192, 1).reshape(2, 3, 64)
    kv_mine = jnp.pad(v_mine, ((0, 0), (0, 0), (64, 0))).reshape(2, SLICE)
    qkv_mine = jnp.pad(jnp.concatenate([q_mine, jnp.zeros((2, 64), F32), kv_mine], axis=1), ((0, 0), (0, WIDE - PACKED)))
    vecs = jnp.stack([qkv_mine, o_all, g1, s1, in_mine, out_all, g2, s2], axis=1)

    labels = flat[:, 576].reshape(16, 2)[:, 0].astype(jnp.int32)
    mine = lax.dynamic_slice_in_dim(labels, 4 * z, 4, 0)
    parent = lookup_rows(mine, parents)
    match = (parent[:, None] == labels[None, :]).astype(jnp.int32)
    branch = parent != labels[0]
    pen = jnp.concatenate(
        [jnp.where(branch, 0.0, MASKED), jnp.where(z > 0, jnp.zeros((4,), F32), MASKED)]
    ).astype(F32)
    route = jnp.where(branch[:, None], match, 0).astype(F32)

    state = activations.astype(F32)
    saved = []
    weights = []
    for i in range(LAYERS):
        weights.append((wide[i, :, :PACKED], o_rows[i], wide[i, :, PACKED:], outer[i]))
        state, kept = forward_layer(state, weights[i], vecs[i], route, pen)
        saved.append(kept)
    outcome = state.astype(BF)
    upstream = cotangent.astype(F32)
    grads = [None] * LAYERS
    for i in reversed(range(LAYERS)):
        upstream, *grads[i] = backward_layer(upstream, weights[i], vecs[i], route, saved[i])

    dqkv, din, dout, do, dvec = (jnp.stack([grads[0][j], grads[1][j]]) for j in range(5))
    gcol = jnp.concatenate([dqkv, din], axis=2).reshape(2, 4, 4, 2, 24, 1408)
    gcol = gcol.transpose(3, 1, 2, 0, 4, 5).reshape(2, 4, 192, 1408)
    gout = dout.reshape(2, 4, 2, 96, WIDE).transpose(2, 1, 0, 3, 4).reshape(2, 4, 192, WIDE)
    go = do.reshape(2, 3, 2, 64, WIDE)[:, :, 1].reshape(2, 4, 2, 24, WIDE)
    go = go.transpose(2, 1, 0, 3, 4).reshape(2, 192, WIDE)
    rcol, rout, ro, rsm = reduce_grads(gcol, gout, go, dvec.reshape(16, WIDE))
    rcol = rcol.astype(F32).reshape(4, 2, 24, 1408).transpose(1, 2, 0, 3)
    dq = rcol[..., :192].reshape(2, 24, WIDE)
    dkv = rcol[..., 256:640].reshape(2, 24, 4, 3, 2, 64)
    dk = dkv[..., 0, :].reshape(2, 24, WIDE)
    dv = dkv[..., 1, :].reshape(2, 24, WIDE)
    dinner = rcol[..., 640:].reshape(2, 24, 4, 4, 192).transpose(0, 1, 3, 2, 4).reshape(2, 24, 3072)
    rsm = rsm.reshape(4, 2, 8, WIDE)
    sums = jnp.sum(rsm, axis=0)
    at = 24 * (8 * z + 2 * f + c)

    def own_part(v):
        return lax.dynamic_slice_in_dim(v, at, 24, 1)

    dqb = rsm[:, :, 0, :192].transpose(1, 0, 2).reshape(2, WIDE)
    dvb = rsm[:, :, 0, 256:640].reshape(4, 2, 3, 2, 64)[:, :, :, 1].transpose(1, 0, 2, 3).reshape(2, WIDE)
    dib = lax.dynamic_index_in_dim(rsm[:, :, 4], f, 0, keepdims=False)
    dib = lax.dynamic_slice_in_dim(dib, 96 * (2 * z + c), 96, 1)
    return (
        outcome, upstream.astype(BF), dq, own_part(dqb), dk, dv, own_part(dvb),
        ro.astype(F32).reshape(2, 24, WIDE), own_part(sums[:, 1]), own_part(sums[:, 2]), own_part(sums[:, 3]),
        dinner, dib, rout.reshape(2, 96, WIDE), own_part(sums[:, 5]), own_part(sums[:, 6]), own_part(sums[:, 7]),
    )


def solution(mesh):
    placed = (
        P("fsdp", None),
        P(None, "fsdp", None),
        P(None, "fsdp"),
        P(None, "fsdp", None),
        P(None, "fsdp", None),
        P(None, "fsdp"),
        P(None, "fsdp", None),
        P(None, "fsdp"),
        P(None, "fsdp"),
        P(None, "fsdp"),
        P(None, "fsdp", None),
        P(None, "fsdp"),
        P(None, "fsdp", None),
        P(None, "fsdp"),
        P(None, "fsdp"),
        P(None, "fsdp"),
        P("fsdp", None),
        P(),
        P("fsdp"),
    )
    return jax.shard_map(
        slice_body if mesh.shape["fsdp"] == 32 else body,
        mesh=mesh,
        in_specs=placed,
        out_specs=(
            P("fsdp", None),
            P("fsdp", None),
            P(None, "fsdp", None),
            P(None, "fsdp"),
            P(None, "fsdp", None),
            P(None, "fsdp", None),
            P(None, "fsdp"),
            P(None, "fsdp", None),
            P(None, "fsdp"),
            P(None, "fsdp"),
            P(None, "fsdp"),
            P(None, "fsdp", None),
            P(None, "fsdp"),
            P(None, "fsdp", None),
            P(None, "fsdp"),
            P(None, "fsdp"),
            P(None, "fsdp"),
        ),
        check_vma=False,
    )
```

```python
import jax
import jax.numpy as jnp
from jax import lax
from jax.experimental import pallas as pl
from jax.experimental.pallas import tpu as pltpu
from jax.sharding import PartitionSpec as P

HEADS = 12
HEAD_DIM = 64
LAYERS = 2
TREE_LEN = 4096


EPSILON = 1e-06
MASKED = -1000000000.0


def partner_2(shard, axis, stride):
    return lax.ppermute(shard, axis, [(i, i ^ 1 << stride) for i in range(lax.axis_size(axis))])


def as_sent(shard):
    return jax.tree.map(lambda a: a.astype(jnp.bfloat16) if a.dtype == jnp.float32 else a, shard)


def product(a, b):
    return jnp.dot(a, b, preferred_element_type=jnp.float32)


def product_tn(a, b):
    return lax.dot_general(a, b, (((0,), (0,)), ((), ())), preferred_element_type=jnp.float32)


def product_nt(a, b):
    return lax.dot_general(a, b, (((1,), (1,)), ((), ())), preferred_element_type=jnp.float32)


def exact_gelu(u):
    return jax.nn.gelu(u, approximate=False)


def layer_norm(z, gain_vec, shift_vec):
    centre = z - jnp.mean(z, axis=-1, keepdims=True)
    scaled = centre * lax.rsqrt(jnp.mean(centre * centre, axis=-1, keepdims=True) + EPSILON)
    return scaled * gain_vec.astype(jnp.float32) + shift_vec.astype(jnp.float32)


def norm_backward(z, gain_vec, upstream):
    centre = z - jnp.mean(z, axis=-1, keepdims=True)
    invert = lax.rsqrt(jnp.mean(centre * centre, axis=-1, keepdims=True) + EPSILON)
    scaled = centre * invert
    weighted = upstream * gain_vec.astype(jnp.float32)
    inner = invert * (
        weighted
        - jnp.mean(weighted, axis=-1, keepdims=True)
        - scaled * jnp.mean(weighted * scaled, axis=-1, keepdims=True)
    )
    return (inner, jnp.sum(upstream * scaled, axis=0), jnp.sum(upstream, axis=0))


def lookup_rows(ids, parents):
    table = jnp.arange(parents.shape[0], dtype=jnp.int32)
    return jnp.sum(jnp.where(ids[:, None] == table[None, :], parents[None, :], 0), axis=1)


def join_heads(stacked):
    return stacked.transpose(1, 0, 2).reshape(stacked.shape[1], -1)


def gather_group(key_rows, value_rows, labels, position, bit_count):
    for b in range(bit_count):
        partner = partner_2((key_rows, value_rows, labels), "fsdp", b)
        upper_side = position >> b & 1 == 1
        key_rows = jnp.where(
            upper_side,
            jnp.concatenate([partner[0], key_rows]),
            jnp.concatenate([key_rows, partner[0]]),
        )
        value_rows = jnp.where(
            upper_side,
            jnp.concatenate([partner[1], value_rows]),
            jnp.concatenate([value_rows, partner[1]]),
        )
        labels = jnp.where(
            upper_side, jnp.concatenate([partner[2], labels]), jnp.concatenate([labels, partner[2]])
        )
    return (key_rows, value_rows, labels)


def sum_group(key_grad, value_grad, position, bit_count):
    for b in reversed(range(bit_count)):
        halfway = key_grad.shape[0] // 2
        upper_side = position >> b & 1 == 1
        outgoing = (
            jnp.where(upper_side, key_grad[:halfway], key_grad[halfway:]),
            jnp.where(upper_side, value_grad[:halfway], value_grad[halfway:]),
        )
        partner = partner_2((as_sent(outgoing[0]), as_sent(outgoing[1])), "fsdp", b)
        key_grad = jnp.where(upper_side, key_grad[halfway:], key_grad[:halfway]) + partner[0]
        value_grad = jnp.where(upper_side, value_grad[halfway:], value_grad[:halfway]) + partner[1]
    return (key_grad, value_grad)


def attend_forward(queries, key_rows, value_rows, allowed):
    factor = HEAD_DIM ** (-0.5)

    def one_head(j):
        start = j * HEAD_DIM
        q = lax.dynamic_slice_in_dim(queries, start, HEAD_DIM, 1)
        k = lax.dynamic_slice_in_dim(key_rows, start, HEAD_DIM, 1)
        v = lax.dynamic_slice_in_dim(value_rows, start, HEAD_DIM, 1)
        s = jnp.where(allowed, product_nt(q, k) * factor, MASKED)
        maxima = jnp.max(s, axis=1, keepdims=True)
        e = jnp.exp(s - maxima)
        totals = jnp.sum(e, axis=1, keepdims=True)
        p = (e / totals).astype(jnp.bfloat16)
        return (product(p, v), (maxima + jnp.log(totals))[:, 0])

    stacked, log_total = lax.map(one_head, jnp.arange(HEADS))
    return (join_heads(stacked), log_total)


def attend_backward(queries, key_rows, value_rows, allowed, log_total, grad_context):
    factor = HEAD_DIM ** (-0.5)

    def one_head(j):
        start = j * HEAD_DIM
        q = lax.dynamic_slice_in_dim(queries, start, HEAD_DIM, 1)
        k = lax.dynamic_slice_in_dim(key_rows, start, HEAD_DIM, 1)
        v = lax.dynamic_slice_in_dim(value_rows, start, HEAD_DIM, 1)
        g = lax.dynamic_slice_in_dim(grad_context, start, HEAD_DIM, 1)
        s = jnp.where(allowed, product_nt(q, k) * factor, MASKED)
        p = jnp.where(allowed, jnp.exp(s - log_total[j][:, None]), 0.0)
        grad_p = product_nt(g, v)
        grad_v = product_tn(p.astype(jnp.bfloat16), g)
        grad_s = (p * (grad_p - jnp.sum(p * grad_p, axis=1, keepdims=True))).astype(jnp.bfloat16)
        grad_q = product(grad_s, k) * factor
        grad_k = product_tn(grad_s, q) * factor
        return (grad_q, grad_k, grad_v)

    grad_q, grad_k, grad_v = lax.map(one_head, jnp.arange(HEADS))
    return (join_heads(grad_q), join_heads(grad_k), join_heads(grad_v))


def layer_forward(state, full, segments, parent_one, parent_two, position, bit_count):
    (
        q_weight,
        q_bias,
        k_weight,
        v_weight,
        v_bias,
        o_weight,
        o_bias,
        gain_one,
        shift_one,
        up_weight,
        up_bias,
        down_weight,
        down_bias,
        gain_two,
        shift_two,
    ) = full
    inputs = state.astype(jnp.bfloat16)
    queries = (product(inputs, q_weight) + q_bias).astype(jnp.bfloat16)
    key_local = product(inputs, k_weight).astype(jnp.bfloat16)
    value_local = (product(inputs, v_weight) + v_bias).astype(jnp.bfloat16)
    key_rows, value_rows, labels = gather_group(
        key_local, value_local, segments, position, bit_count
    )
    allowed = (
        (labels[None, :] == segments[:, None])
        | (labels[None, :] == parent_one[:, None])
        | (labels[None, :] == parent_two[:, None])
    )
    context_wide, log_total = attend_forward(queries, key_rows, value_rows, allowed)
    context = context_wide.astype(jnp.bfloat16)
    first_sum = state + product(context, o_weight) + o_bias
    hidden = layer_norm(first_sum, gain_one, shift_one)
    hidden_low = hidden.astype(jnp.bfloat16)
    pre_act = product(hidden_low, up_weight) + up_bias
    gelu_out = exact_gelu(pre_act).astype(jnp.bfloat16)
    second_sum = hidden + product(gelu_out, down_weight) + down_bias
    record = (
        inputs,
        queries,
        key_rows,
        value_rows,
        allowed,
        log_total,
        context,
        first_sum,
        hidden_low,
        pre_act,
        gelu_out,
        second_sum,
    )
    return (record, layer_norm(second_sum, gain_two, shift_two))


def layer_backward(upstream, full, record, position, bit_count):
    (
        q_weight,
        q_bias,
        k_weight,
        v_weight,
        v_bias,
        o_weight,
        o_bias,
        gain_one,
        shift_one,
        up_weight,
        up_bias,
        down_weight,
        down_bias,
        gain_two,
        shift_two,
    ) = full
    (
        inputs,
        queries,
        key_rows,
        value_rows,
        allowed,
        log_total,
        context,
        first_sum,
        hidden_low,
        pre_act,
        gelu_out,
        second_sum,
    ) = record
    grad_z2, grad_gain_two, grad_shift_two = norm_backward(second_sum, gain_two, upstream)
    grad_f = grad_z2.astype(jnp.bfloat16)
    grad_down_bias = jnp.sum(grad_f.astype(jnp.float32), axis=0)
    grad_down = product_tn(gelu_out, grad_f)
    grad_gelu = product_nt(grad_f, down_weight)
    unused_value, gelu_back = jax.vjp(exact_gelu, pre_act)
    grad_u = gelu_back(grad_gelu)[0].astype(jnp.bfloat16)
    grad_up_bias = jnp.sum(grad_u.astype(jnp.float32), axis=0)
    grad_up = product_tn(hidden_low, grad_u)
    grad_h = grad_z2 + product_nt(grad_u, up_weight)
    grad_z1, grad_gain_one, grad_shift_one = norm_backward(first_sum, gain_one, grad_h)
    grad_a = grad_z1.astype(jnp.bfloat16)
    grad_o_bias = jnp.sum(grad_a.astype(jnp.float32), axis=0)
    grad_o = product_tn(context, grad_a)
    grad_context = product_nt(grad_a, o_weight).astype(jnp.bfloat16)
    grad_q, key_grad, value_grad = attend_backward(
        queries, key_rows, value_rows, allowed, log_total, grad_context
    )
    key_grad, value_grad = sum_group(key_grad, value_grad, position, bit_count)
    q_low = grad_q.astype(jnp.bfloat16)
    k_low = key_grad.astype(jnp.bfloat16)
    v_low = value_grad.astype(jnp.bfloat16)
    grad_x = (
        grad_z1
        + product_nt(q_low, q_weight)
        + product_nt(k_low, k_weight)
        + product_nt(v_low, v_weight)
    )
    terms = (
        product_tn(inputs, q_low),
        jnp.sum(q_low.astype(jnp.float32), axis=0),
        product_tn(inputs, k_low),
        product_tn(inputs, v_low),
        jnp.sum(v_low.astype(jnp.float32), axis=0),
        grad_o,
        grad_o_bias,
        grad_gain_one,
        grad_shift_one,
        grad_up,
        grad_up_bias,
        grad_down,
        grad_down_bias,
        grad_gain_two,
        grad_shift_two,
    )
    return (grad_x, terms)


def stack_layers(groups, n):
    return jnp.stack([g[n] for g in groups])


def body(
    activations,
    query_weight,
    query_bias,
    key_weight,
    value_weight,
    value_bias,
    output_weight,
    output_bias,
    first_gain,
    first_shift,
    inner_weight,
    inner_bias,
    outer_weight,
    outer_bias,
    second_gain,
    second_shift,
    cotangent,
    parents,
    segments,
):
    position = lax.axis_index("fsdp")
    bit_count = (TREE_LEN // activations.shape[0]).bit_length() - 1
    parent_one = lookup_rows(segments, parents)
    parent_two = lookup_rows(parent_one, parents)
    state = activations.astype(jnp.float32)
    saved = []
    kept_weights = []
    for i in range(LAYERS):
        full = (
            lax.all_gather(query_weight[i], "fsdp", axis=0, tiled=True),
            lax.all_gather(query_bias[i], "fsdp", axis=0, tiled=True),
            lax.all_gather(key_weight[i], "fsdp", axis=0, tiled=True),
            lax.all_gather(value_weight[i], "fsdp", axis=0, tiled=True),
            lax.all_gather(value_bias[i], "fsdp", axis=0, tiled=True),
            lax.all_gather(output_weight[i], "fsdp", axis=0, tiled=True),
            lax.all_gather(output_bias[i], "fsdp", axis=0, tiled=True),
            lax.all_gather(first_gain[i], "fsdp", axis=0, tiled=True),
            lax.all_gather(first_shift[i], "fsdp", axis=0, tiled=True),
            lax.all_gather(inner_weight[i], "fsdp", axis=0, tiled=True),
            lax.all_gather(inner_bias[i], "fsdp", axis=0, tiled=True),
            lax.all_gather(outer_weight[i], "fsdp", axis=0, tiled=True),
            lax.all_gather(outer_bias[i], "fsdp", axis=0, tiled=True),
            lax.all_gather(second_gain[i], "fsdp", axis=0, tiled=True),
            lax.all_gather(second_shift[i], "fsdp", axis=0, tiled=True),
        )
        kept_weights.append(full)
        record, state = layer_forward(
            state, full, segments, parent_one, parent_two, position, bit_count
        )
        saved.append(record)
    outcome = state.astype(jnp.bfloat16)
    upstream = cotangent.astype(jnp.float32)
    layer_grads = [None] * LAYERS
    for i in reversed(range(LAYERS)):
        full = (
            lax.all_gather(query_weight[i], "fsdp", axis=0, tiled=True),
            lax.all_gather(query_bias[i], "fsdp", axis=0, tiled=True),
            lax.all_gather(key_weight[i], "fsdp", axis=0, tiled=True),
            lax.all_gather(value_weight[i], "fsdp", axis=0, tiled=True),
            lax.all_gather(value_bias[i], "fsdp", axis=0, tiled=True),
            lax.all_gather(output_weight[i], "fsdp", axis=0, tiled=True),
            lax.all_gather(output_bias[i], "fsdp", axis=0, tiled=True),
            lax.all_gather(first_gain[i], "fsdp", axis=0, tiled=True),
            lax.all_gather(first_shift[i], "fsdp", axis=0, tiled=True),
            lax.all_gather(inner_weight[i], "fsdp", axis=0, tiled=True),
            lax.all_gather(inner_bias[i], "fsdp", axis=0, tiled=True),
            lax.all_gather(outer_weight[i], "fsdp", axis=0, tiled=True),
            lax.all_gather(outer_bias[i], "fsdp", axis=0, tiled=True),
            lax.all_gather(second_gain[i], "fsdp", axis=0, tiled=True),
            lax.all_gather(second_shift[i], "fsdp", axis=0, tiled=True),
        )
        upstream, terms = layer_backward(upstream, full, saved[i], position, bit_count)
        layer_grads[i] = (
            lax.psum_scatter(terms[0], "fsdp", scatter_dimension=0, tiled=True),
            lax.psum_scatter(terms[1], "fsdp", scatter_dimension=0, tiled=True),
            lax.psum_scatter(terms[2], "fsdp", scatter_dimension=0, tiled=True),
            lax.psum_scatter(terms[3], "fsdp", scatter_dimension=0, tiled=True),
            lax.psum_scatter(terms[4], "fsdp", scatter_dimension=0, tiled=True),
            lax.psum_scatter(terms[5], "fsdp", scatter_dimension=0, tiled=True),
            lax.psum_scatter(terms[6], "fsdp", scatter_dimension=0, tiled=True),
            lax.psum_scatter(terms[7], "fsdp", scatter_dimension=0, tiled=True),
            lax.psum_scatter(terms[8], "fsdp", scatter_dimension=0, tiled=True),
            lax.psum_scatter(terms[9], "fsdp", scatter_dimension=0, tiled=True),
            lax.psum_scatter(terms[10], "fsdp", scatter_dimension=0, tiled=True),
            lax.psum_scatter(terms[11], "fsdp", scatter_dimension=0, tiled=True),
            lax.psum_scatter(terms[12], "fsdp", scatter_dimension=0, tiled=True),
            lax.psum_scatter(terms[13], "fsdp", scatter_dimension=0, tiled=True),
            lax.psum_scatter(terms[14], "fsdp", scatter_dimension=0, tiled=True),
        )
    shares = tuple((stack_layers(layer_grads, n) for n in range(15)))
    return (outcome, upstream.astype(jnp.bfloat16)) + tuple(shares)


MESH = pl.DeviceIdType.MESH
BF = jnp.bfloat16
F32 = jnp.float32
WIDE = 768
SLICE = 384
PACKED = 640
ROWS = 128
NKEYS = 1536


class Pool:
    def __init__(self, ref):
        self.ref = ref
        self.used = 0

    def take(self):
        self.used += 1
        return self.ref.at[self.used - 1]

    def block(self, n):
        first = self.used
        self.used += n
        return lambda i: self.ref.at[first + i]


class Place:
    def __init__(self):
        me = lax.axis_index("fsdp")
        p = lax.rem(me, 32)
        self.base = me - p
        self.z = p // 8
        self.f = lax.rem(p // 2, 4)
        self.c = lax.rem(p, 2)

    def at(self, z, f, c):
        return self.base + 8 * z + 2 * f + c

    def f_at(self, k):
        return lax.rem(self.f + k + 4, 4)

    def z_at(self, k):
        return lax.rem(self.z + k + 4, 4)

    def plane(self, k):
        return self.at(self.z, self.f_at(k), self.c)

    def across(self, k):
        return self.at(self.z, self.f_at(k), 1 - self.c)

    def column(self, k):
        return self.at(self.z_at(k), self.f, self.c)

    def sibling(self):
        return self.at(self.z, self.f, 1 - self.c)


def remote(src, dst, sems, device):
    return pltpu.make_async_remote_copy(
        src_ref=src, dst_ref=dst, send_sem=sems[0], recv_sem=sems[1], device_id=(device,), device_id_type=MESH
    )


class Run:
    def __init__(self, send_sems, recv_sems, local_sems):
        self.place = Place()
        self.sends, self.recvs, self.locals = Pool(send_sems), Pool(recv_sems), Pool(local_sems)
        self.flying, self.saving = [], []

    def greet(self, wide):
        place = self.place
        there = [place.plane(k) for k in (1, 2, 3)] + [place.column(k) for k in (1, 2, 3)] + [place.sibling()]
        if wide:
            there += [place.across(k) for k in (1, 2, 3)]
        barrier = pltpu.get_barrier_semaphore()
        for dev in there:
            pl.semaphore_signal(barrier, inc=1, device_id=(dev,), device_id_type=MESH)
        pl.semaphore_wait(barrier, len(there))

    def launch(self, src, dst, device):
        a = remote(src, dst, (self.sends.take(), self.recvs.take()), device)
        a.start()
        self.flying.append((None, a))
        return a

    def launch_if(self, cond, src, dst, sems, device):
        a = remote(src, dst, sems, device)

        @pl.when(cond)
        def _():
            a.start()

        self.flying.append((cond, a))
        return a

    def local(self, src, dst):
        a = pltpu.make_async_copy(src, dst, self.locals.take())
        a.start()
        return a

    def save(self, src, dst):
        self.saving.append(self.local(src, dst))

    def close(self):
        for a in self.saving:
            a.wait()
        for cond, a in self.flying:
            if cond is None:
                a.wait_send()
            else:

                @pl.when(cond)
                def _(a=a):
                    a.wait_send()


class Spread:
    def __init__(self, run, chunk, full):
        self.run, self.chunk, self.full = run, chunk, full

    def start(self):
        run, place = self.run, self.run.place
        mine = self.full.at[place.z, place.c]
        self.own = run.local(self.chunk, mine)
        self.far = [run.launch(self.chunk, mine, place.column(k)) for k in (1, 2, 3)]
        self.near = [run.launch(self.chunk, mine, place.sibling())]

    def relay(self):
        run, place = self.run, self.run.place
        for k in (1, 2, 3):
            self.far[k - 1].wait_recv()
            there = self.full.at[place.z_at(-k), place.c]
            self.near.append(run.launch(there, there, place.sibling()))

    def finish(self):
        self.own.wait()
        for a in self.near:
            a.wait_recv()


class SpreadOutput:
    def __init__(self, run, chunk, full):
        self.run, self.chunk = run, chunk
        self.part = full.at[pl.ds(pl.multiple_of(run.place.c * 96, 96), 96)]

    def start(self):
        run, place = self.run, self.run.place
        self.copy = pltpu.make_async_copy(self.chunk, self.part, run.locals.take())

        @pl.when(place.f == place.z)
        def _():
            self.copy.start()

        arrive = run.recvs.take()
        for k in (1, 2, 3):
            self.far = run.launch_if(
                place.f == place.z, self.chunk, self.part, (run.sends.take(), arrive), place.column(k)
            )

    def relay(self):
        run, place = self.run, self.run.place

        @pl.when(place.f == place.z)
        def _():
            self.copy.wait()

        @pl.when(place.f != place.z)
        def _():
            self.far.wait_recv()

        self.near = run.launch(self.part, self.part, place.sibling())

    def finish(self):
        self.near.wait_recv()


class Collect:
    def __init__(self, run, part, near, far, total, out):
        self.run, self.part, self.near, self.far, self.total, self.out = run, part, near, far, total, out

    def start(self):
        place = self.run.place
        self.a = self.run.launch(self.part.at[1 - place.c], self.near, place.sibling())

    def middle(self):
        run, place = self.run, self.run.place
        self.a.wait_recv()

        def add(i, carry):
            self.near[i] = (self.part[place.c, i].astype(F32) + self.near[i].astype(F32)).astype(BF)
            return carry

        lax.fori_loop(0, 4, add, 0)
        self.moves = [
            run.launch(self.near.at[place.z_at(k)], self.far.at[k - 1], place.column(k)) for k in (1, 2, 3)
        ]

    def end(self):
        run, place = self.run, self.run.place
        for a in self.moves:
            a.wait_recv()
        result = self.near[place.z].astype(F32)
        for k in range(3):
            result = result + self.far[k].astype(F32)
        if self.total is None:
            self.out[...] = result
            return
        self.total[...] = result
        scatter_rows(self, self.total, self.out.at[place.f], None)

    def last(self):
        if self.total is None:
            return
        place = self.run.place
        for k in (1, 2, 3):
            g = place.f_at(k)
            remote(
                self.out.at[g], self.out.at[g], (self.send, self.arrive(g)), place.plane(k)
            ).wait_recv()

        @pl.when(place.c != place.f // 2)
        def _():
            remote(
                self.out.at[place.f], self.out.at[place.f], (self.send, self.arrive(place.f)), place.sibling()
            ).wait_recv()


def scatter_rows(task, total, landing, cond):
    run, place = task.run, task.run.place
    arrive = run.recvs.block(4)
    for j in range(4):
        there = place.at(place.z, 2 * place.c + j // 2, j % 2)
        here = jnp.logical_and(place.f == 2 * place.c + j // 2, place.c == j % 2)
        away = jnp.logical_not(here)
        if cond is not None:
            here, away = jnp.logical_and(here, cond), jnp.logical_and(away, cond)
        task.send = run.sends.take()
        slot = arrive(place.f) if cond is None else arrive(0)
        run.launch_if(away, total.at[pl.ds(24 * j, 24)], landing, (task.send, slot), there)

        @pl.when(here)
        def _(j=j):
            landing[...] = total[24 * j : 24 * (j + 1), :]

    task.arrive = arrive


class CollectOutput:
    def __init__(self, run, part, near, far, total, out):
        self.run, self.part, self.near, self.far, self.total, self.out = run, part, near, far, total, out

    def start(self):
        place = self.run.place
        self.a = self.run.launch(self.part.at[1 - place.c], self.near, place.sibling())

    def middle(self):
        run, place = self.run, self.run.place
        self.a.wait_recv()
        self.near[...] = (self.part[place.c].astype(F32) + self.near[...].astype(F32)).astype(BF)
        self.slot = run.recvs.block(4)
        self.one = run.sends.take()
        shift = lax.rem(place.f - place.z + 4, 4)
        run.launch_if(
            place.f != place.z, self.near, self.far.at[shift], (self.one, self.slot(shift)),
            place.at(place.f, place.f, place.c),
        )

    def end(self):
        place = self.run.place

        @pl.when(place.f == place.z)
        def _():
            result = self.near[...].astype(F32)
            for k in (1, 2, 3):
                remote(
                    self.near, self.far.at[k], (self.one, self.slot(k)), place.column(k)
                ).wait_recv()
                result = result + self.far[k].astype(F32)
            self.total[...] = result

        scatter_rows(self, self.total, self.out, place.f == place.z)

    def last(self):
        place = self.run.place
        mine = jnp.logical_and(place.f == place.z, place.c == place.f // 2)

        @pl.when(jnp.logical_not(mine))
        def _():
            remote(self.out, self.out, (self.send, self.arrive(0)), place.sibling()).wait_recv()


def norm_rows(z, gain, shift):
    centre = z - jnp.mean(z, axis=-1, keepdims=True)
    inv = lax.rsqrt(jnp.mean(centre * centre, axis=-1, keepdims=True) + EPSILON)
    return centre * inv * gain + shift


def norm_rows_back(z, gain, upstream):
    centre = z - jnp.mean(z, axis=-1, keepdims=True)
    inv = lax.rsqrt(jnp.mean(centre * centre, axis=-1, keepdims=True) + EPSILON)
    scaled = centre * inv
    weighted = upstream * gain
    inner = inv * (
        weighted
        - jnp.mean(weighted, axis=-1, keepdims=True)
        - scaled * jnp.mean(weighted * scaled, axis=-1, keepdims=True)
    )
    return inner, jnp.sum(upstream * scaled, axis=0, keepdims=True), jnp.sum(upstream, axis=0, keepdims=True)


def exchange_kernel(col, rows_o, small, colp, op, smallg, send_sems, recv_sems, local_sems):
    run = Run(send_sems, recv_sems, local_sems)
    place = run.place
    z, f, c = place.z, place.f, place.c
    mine = c == f // 2
    slot = 2 * lax.rem(f, 2) + c
    own = pltpu.make_async_copy(col.at[f], colp.at[slot], run.locals.take())
    own_o = pltpu.make_async_copy(rows_o, op.at[slot], run.locals.take())
    keep = jnp.logical_and(mine, f == z)

    @pl.when(mine)
    def _():
        own.start()

    @pl.when(keep)
    def _():
        own_o.start()

    own_small = run.local(small, smallg.at[z, c, f])
    run.greet(True)
    first = [run.launch(small, smallg.at[z, c, f], place.plane(k)) for k in (1, 2, 3)]
    arrive, arrive_o = run.recvs.block(4), run.recvs.block(4)
    for k in (1, 2, 3):
        run.launch_if(
            f >= 0, col.at[place.f_at(k)], colp.at[slot], (run.sends.take(), arrive(slot)),
            place.at(z, place.f_at(k), f // 2),
        )
    one = run.sends.take()
    run.launch_if(
        jnp.logical_not(mine), col.at[f], colp.at[slot], (one, arrive(slot)), place.sibling()
    )
    run.launch_if(
        jnp.logical_not(keep), rows_o, op.at[slot], (run.sends.take(), arrive_o(slot)), place.at(z, z, f // 2)
    )
    own_small.wait()
    for a in first:
        a.wait_recv()
    block = smallg.at[z, c]
    far = [run.launch(block, block, place.column(k)) for k in (1, 2, 3)]
    near = [run.launch(block, block, place.sibling())]
    for k in (1, 2, 3):
        far[k - 1].wait_recv()
        there = smallg.at[place.z_at(-k), c]
        near.append(run.launch(there, there, place.sibling()))

    for j in range(4):
        me = jnp.logical_and(f == 2 * c + j // 2, c == j % 2)
        other = jnp.logical_not(me)

        @pl.when(other)
        def _(j=j):
            remote(col.at[0], colp.at[j], (one, arrive(j)), place.sibling()).wait_recv()

        @pl.when(jnp.logical_and(other, f == z))
        def _(j=j):
            remote(rows_o, op.at[j], (one, arrive_o(j)), place.sibling()).wait_recv()

    for a in near:
        a.wait_recv()

    @pl.when(mine)
    def _():
        own.wait()

    @pl.when(keep)
    def _():
        own_o.wait()

    run.close()


def pick_parents(kp, kv, route, zz, cc):
    def one(b, carry):
        total = kp[b, cc]
        for ft in range(4):
            total = total + kv[zz, cc, ft * ROWS : (ft + 1) * ROWS, :] * route[b, 4 * zz + ft].astype(BF)
        kp[b, cc] = total
        return carry

    lax.fori_loop(0, 4, one, 0)


def all_keys(kv, kp, z, b, lanes):
    rows = pl.ds(pl.multiple_of(b * ROWS, ROWS), ROWS)
    return jnp.concatenate(
        [
            kv[0, 0, :, lanes], kv[0, 1, :, lanes], kv[z, 0, rows, lanes], kv[z, 1, rows, lanes],
            kp[b, 0, :, lanes], kp[b, 1, :, lanes],
        ],
        axis=0,
    )


def flat(ref):
    return ref[...].reshape(-1, ref.shape[-1])


def forward_kernel(first, *refs):
    refs = list(refs)

    def take(n):
        out = refs[:n]
        del refs[:n]
        return out

    x_ref, qkv_in, o_in, in_c, out_c, vec, route, pen = take(8)
    if first:
        qkv_next, o_next = take(2)
    xn_ref, xb_o, qp_o, kv_o, kp_o, p_o, ctx_o, z1_o, hb_o, gp_o, gl_o, z2_o, win_o, wout_o = take(14)
    if first:
        wqkv_o, wo_o, wqkv_n, wo_n = take(4)
    xb, qp, kv, kp, p, ctx, z1, hb, gp, gl, z2, win, wout, wqkv, wo, heads, own, rs1_s, rs1_r, rs2_s, rs2_r = take(21)
    run = Run(*refs)
    place = run.place
    z, f, c = place.z, place.f, place.c
    launch = run.launch

    xb[f] = x_ref[...].astype(BF)
    wo[192:256, :] = jnp.zeros((64, WIDE), BF)
    if not first:
        loads = [run.local(qkv_in, wqkv), run.local(o_in, wo.at[pl.ds(0, 192)])]
    run.greet(False)
    came = [None] + [launch(xb.at[f], xb.at[f], place.plane(k)) for k in (1, 2, 3)]
    if first:
        a_tasks = [Spread(run, qkv_in, wqkv), SpreadOutput(run, o_in, wo)]
        for t in a_tasks:
            t.start()
        a_tasks[0].relay()
        a_tasks[0].finish()
    else:
        for a in loads:
            a.wait()
    lane = lax.broadcasted_iota(jnp.int32, (ROWS, 128), 1)
    for k in range(4):
        g = place.f_at(-k)
        if k:
            came[k].wait_recv()
        qkv = product(xb[g], flat(wqkv)) + vec[0:1, :PACKED]
        rows = pl.ds(pl.multiple_of(g * ROWS, ROWS), ROWS)
        kv[z, c, rows, :] = qkv[:, 256:].astype(BF)
        scaled = qkv[:, :256] * (HEAD_DIM ** (-0.5))
        front = scaled[:, :128]
        qp[rows, 0:128] = jnp.where(lane < 64, front, 0.0).astype(BF)
        qp[rows, 128:256] = jnp.where(lane < 64, pltpu.roll(front, 64, 1), 0.0).astype(BF)
        qp[rows, 256:384] = scaled[:, 128:].astype(BF)
    move = [launch(kv.at[z, c], kv.at[z, c], place.column(k)) for k in (1, 2, 3)]
    side = [launch(kv.at[z, c], kv.at[z, c], place.sibling())]
    m_tasks = [Spread(run, in_c, win), Spread(run, out_c, wout)]
    for t in m_tasks:
        t.start()
    run.save(xb, xb_o)
    run.save(qp, qp_o)
    kp[...] = jnp.zeros_like(kp)
    pick_parents(kp, kv, route, z, c)
    for k in (1, 2, 3):
        move[k - 1].wait_recv()
        there = place.z_at(-k)
        side.append(launch(kv.at[there, c], kv.at[there, c], place.sibling()))
        pick_parents(kp, kv, route, there, c)
    for k in range(4):
        side[k].wait_recv()
        pick_parents(kp, kv, route, place.z_at(-k), 1 - c)
    run.save(kp, kp_o)
    run.save(kv, kv_o)
    if first:
        a_tasks[1].relay()
        n_tasks = [Spread(run, qkv_next, wqkv_n), SpreadOutput(run, o_next, wo_n)]
        for t in n_tasks:
            t.start()

    def attend(i, carry):
        h, b = i // 4, lax.rem(i, 4)
        lanes = pl.ds(pl.multiple_of(h * 128, 128), 128)
        rows = pl.ds(pl.multiple_of(b * ROWS, ROWS), ROWS)
        keys = all_keys(kv, kp, z, b, lanes)
        s = product_nt(qp[rows, lanes], keys)
        s = jnp.concatenate(
            [s[:, :1024], s[:, 1024:1280] + pen[4 + b], s[:, 1280:] + pen[b]], axis=1
        )
        e = jnp.exp(s - jnp.max(s, axis=1, keepdims=True))
        pb = (e / jnp.sum(e, axis=1, keepdims=True)).astype(BF)
        p[h, b] = pb
        heads[h, b] = product(pb, keys)
        return carry

    lax.fori_loop(0, 12, attend, 0)
    run.save(p, p_o)
    if first:
        a_tasks[1].finish()
    back = [None]
    for k in (1, 2, 3, 0):
        g = place.f_at(-k)
        ctx[g, :, 0:128] = jnp.where(lane < 64, pltpu.roll(heads[0, g], 64, 1), heads[1, g]).astype(BF)
        ctx[g, :, 128:256] = jnp.where(lane < 64, pltpu.roll(heads[2, g], 64, 1), 0.0).astype(BF)
        part = product(ctx[g], wo[...])
        if k:
            rs1_s[k - 1] = part.astype(BF)
            back.append(launch(rs1_s.at[k - 1], rs1_r.at[k - 1], place.plane(-k)))
        else:
            own[...] = part
    run.save(ctx, ctx_o)
    for t in m_tasks:
        t.relay()
    for k in (1, 2, 3):
        back[k].wait_recv()
    total = own[...] + rs1_r[0].astype(F32) + rs1_r[1].astype(F32) + rs1_r[2].astype(F32)
    zz = x_ref[...] + total + vec[1:2, :]
    z1[...] = zz
    run.save(z1, z1_o)
    hidden = norm_rows(zz, vec[2:3, :], vec[3:4, :])
    hb[f] = hidden.astype(BF)
    came = [None] + [launch(hb.at[f], hb.at[f], place.plane(k)) for k in (1, 2, 3)]
    back = [None]
    for t in m_tasks:
        t.finish()
    for k in range(4):
        g = place.f_at(-k)
        if k:
            came[k].wait_recv()
        u = product(hb[g], flat(win)) + vec[4:5, :]
        cdf = 0.5 * (1.0 + lax.erf(u * (0.5 ** 0.5)))
        gp[g] = cdf + u * jnp.exp(-0.5 * u * u) * 0.3989422804014327
        low = (u * cdf).astype(BF)
        gl[g] = low
        part = product(low, flat(wout))
        if k:
            rs2_s[k - 1] = part.astype(BF)
            back.append(launch(rs2_s.at[k - 1], rs2_r.at[k - 1], place.plane(-k)))
        else:
            own[...] = part
    run.save(hb, hb_o)
    run.save(gp, gp_o)
    run.save(gl, gl_o)
    run.save(win, win_o)
    run.save(wout, wout_o)
    if first:
        run.save(wqkv, wqkv_o)
        run.save(wo.at[pl.ds(0, 192)], wo_o)
        for t in n_tasks:
            t.relay()
    for k in (1, 2, 3):
        back[k].wait_recv()
    total = own[...] + rs2_r[0].astype(F32) + rs2_r[1].astype(F32) + rs2_r[2].astype(F32)
    zz = norm_rows(z1[...], vec[2:3, :], vec[3:4, :]) + total + vec[5:6, :]
    z2[...] = zz
    run.save(z2, z2_o)
    xn_ref[...] = norm_rows(zz, vec[6:7, :], vec[7:8, :])
    if first:
        for t in n_tasks:
            t.finish()
    run.close()


def backward_kernel(extra, *refs):
    refs = list(refs)

    def take(n):
        out = refs[:n]
        del refs[:n]
        return out

    dy_ref, win, wout, vec, route, z1, hb, gp, gl, z2 = take(10)
    late_in = take(8)
    if extra:
        pq_in, po_in = take(2)
    dx_ref, pq, po, din_o, dout_o, dvec_o = take(6)
    if extra:
        dqkv_o, do_o = take(2)
    late = take(8)
    wqkv, wo, xb, qp, kv, kp, p, ctx = late
    (
        df, du, da, dctx, dqf, dqkv, dz, dz1, dkt, dself, dpar, tgt, tgt_r, summed, summed_r,
        own, rs1_s, rs1_r, rs2_s, rs2_r,
    ) = take(20)
    pin, nin, fin, tin, pout, nout, fout = take(7)
    if extra:
        nq, fq, tq, no, fo, to = take(6)
    run = Run(*refs)
    place = run.place
    z, f, c = place.z, place.f, place.c
    launch = run.launch
    loads = []
    for n, (src, dst) in enumerate(zip(late_in, late)):
        loads.append(run.local(src, dst.at[pl.ds(0, 192)] if n == 1 else dst))
    wo[192:256, :] = jnp.zeros((64, WIDE), BF)

    grad, dgain, dshift = norm_rows_back(z2[...], vec[6:7, :], dy_ref[...])
    dvec_o[6:7, :] = dgain
    dvec_o[7:8, :] = dshift
    dz[...] = grad
    low = grad.astype(BF)
    df[f] = low
    dvec_o[5:6, :] = jnp.sum(low.astype(F32), axis=0, keepdims=True)
    run.greet(True)
    came = [None] + [launch(df.at[f], df.at[f], place.plane(k)) for k in (1, 2, 3)]
    a_tasks = []
    if extra:
        a_tasks = [Collect(run, pq_in, nq, fq, tq, dqkv_o), CollectOutput(run, po_in, no, fo, to, do_o)]
    for t in a_tasks:
        t.start()
    back = [None]
    bias = jnp.zeros((1, WIDE), F32)
    for k in range(4):
        g = place.f_at(-k)
        if k:
            came[k].wait_recv()
        low = (product_nt(df[g], flat(wout)) * gp[g]).astype(BF)
        du[g] = low
        bias = bias + jnp.sum(low.astype(F32), axis=0, keepdims=True)
        part = product_nt(low, flat(win))
        if k:
            rs1_s[k - 1] = part.astype(BF)
            back.append(launch(rs1_s.at[k - 1], rs1_r.at[k - 1], place.plane(-k)))
        else:
            own[...] = part
            for t in a_tasks:
                t.middle()
    dvec_o[4:5, :] = bias
    m_tasks = [Collect(run, pin, nin, fin, tin, din_o), Collect(run, pout, nout, fout, None, dout_o)]

    def split_rows(dst, left, right, i):
        lanes = pl.ds(pl.multiple_of(i * 384, 128), 384)
        value = product_tn(left[:, :, lanes].reshape(512, 384), flat(right)).astype(BF)
        for zz in range(2):
            for cc in range(2):
                at = (2 * zz + cc) * 96
                dst[cc, 2 * i + zz] = value[at : at + 96, :]

    def ffn_grads(i, carry):
        split_rows(pout, gl, df, i)
        split_rows(pin, hb, du, i)
        return carry

    lax.fori_loop(0, 2, ffn_grads, 0)
    for t in m_tasks:
        t.start()
    for k in (1, 2, 3):
        back[k].wait_recv()
    up = dz[...] + own[...] + rs1_r[0].astype(F32) + rs1_r[1].astype(F32) + rs1_r[2].astype(F32)
    grad, dgain, dshift = norm_rows_back(z1[...], vec[2:3, :], up)
    dvec_o[2:3, :] = dgain
    dvec_o[3:4, :] = dshift
    dz1[...] = grad
    low = grad.astype(BF)
    da[f] = low
    dvec_o[1:2, :] = jnp.sum(low.astype(F32), axis=0, keepdims=True)
    came = [None] + [launch(da.at[f], da.at[f], place.plane(k)) for k in (1, 2, 3)]
    for t in a_tasks:
        t.end()
    for t in m_tasks:
        t.middle()
    dkt[...] = jnp.zeros_like(dkt)
    lane = lax.broadcasted_iota(jnp.int32, (ROWS, 128), 1)
    for a in loads:
        a.wait()
    for k in range(4):
        g = place.f_at(-k)
        rows = pl.ds(pl.multiple_of(g * ROWS, ROWS), ROWS)
        if k:
            came[k].wait_recv()
        packed = product_nt(da[g], wo[...])
        ahead, after = packed[:, :128], packed[:, 128:]
        dctx[rows, 0:128] = jnp.where(lane < 64, 0.0, pltpu.roll(ahead, 64, 1)).astype(BF)
        dctx[rows, 128:256] = jnp.where(lane < 64, 0.0, ahead).astype(BF)
        dctx[rows, 256:384] = jnp.where(lane < 64, 0.0, pltpu.roll(after, 64, 1)).astype(BF)

    def attend(i, carry):
        h, b = i // 4, lax.rem(i, 4)
        lanes = pl.ds(pl.multiple_of(h * 128, 128), 128)
        rows = pl.ds(pl.multiple_of(b * ROWS, ROWS), ROWS)
        keys = all_keys(kv, kp, z, b, lanes)
        q, g = qp[rows, lanes], dctx[rows, lanes]
        low = p[h, b]
        pf = low.astype(F32)
        dp = product_nt(g, keys)
        t = pf * dp
        ds = (t - pf * jnp.sum(t, axis=1, keepdims=True)).astype(BF)
        dqf[h, rows, :] = product(ds, keys) * (HEAD_DIM ** (-0.5))
        dkv = product_tn(jnp.concatenate([ds, low], axis=0), jnp.concatenate([q, g], axis=0))
        dkt[:, lanes] += dkv[:1024]
        dself[b, :, lanes] = dkv[1024:1280]
        dpar[b, :, lanes] = dkv[1280:]
        return carry

    lax.fori_loop(0, 12, attend, 0)
    for cc in range(2):
        tgt[cc, 0] = dkt[cc * 512 : (cc + 1) * 512, :].astype(BF)

    def scatter(i, carry):
        zt, ft = 1 + i // 4, lax.rem(i, 4)
        rows = pl.ds(pl.multiple_of(ft * ROWS, ROWS), ROWS)
        here = jnp.where(zt == z, 1.0, 0.0)
        for cc in range(2):
            half = slice(cc * ROWS, (cc + 1) * ROWS)
            total = dself[ft, half, :] * here
            for b in range(4):
                total = total + dpar[b, half, :] * route[b, 4 * zt + ft]
            tgt[cc, zt, rows, :] = total.astype(BF)
        return carry

    lax.fori_loop(0, 12, scatter, 0)
    near = launch(tgt.at[1 - c], tgt_r, place.sibling())
    for g in range(4):
        rows = slice(g * ROWS, (g + 1) * ROWS)
        ahead = jnp.where(lane < 64, dqf[0, rows, :], pltpu.roll(dqf[1, rows, :], 64, 1))
        dqkv[g, :, 0:128] = ahead.astype(BF)
        dqkv[g, :, 128:256] = jnp.where(lane < 64, dqf[2, rows, :], 0.0).astype(BF)
    near.wait_recv()
    for zt in range(4):
        summed[zt] = (tgt[c, zt].astype(F32) + tgt_r[zt].astype(F32)).astype(BF)
    far = [launch(summed.at[place.z_at(k)], summed_r.at[k - 1], place.column(k)) for k in (1, 2, 3)]
    value = product_tn(flat(ctx), flat(da)).astype(BF)
    for cc in range(2):
        po[cc] = value[96 * cc : 96 * (cc + 1), :]
    for a in far:
        a.wait_recv()
    total = summed[z].astype(F32) + summed_r[0].astype(F32) + summed_r[1].astype(F32) + summed_r[2].astype(F32)
    for g in range(4):
        dqkv[g, :, 256:] = total[g * ROWS : (g + 1) * ROWS, :].astype(BF)
    back = [None]
    for k in (1, 2, 3, 0):
        g = place.f_at(-k)
        part = product_nt(dqkv[g], flat(wqkv))
        if k:
            rs2_s[k - 1] = part.astype(BF)
            back.append(launch(rs2_s.at[k - 1], rs2_r.at[k - 1], place.plane(-k)))
        else:
            own[...] = part

    def qkv_grads(i, carry):
        split_rows(pq, xb, dqkv, i)
        return carry

    lax.fori_loop(0, 2, qkv_grads, 0)
    sums = jnp.sum(flat(dqkv).astype(F32), axis=0, keepdims=True)
    dvec_o[0:1, :] = jnp.concatenate([sums, jnp.zeros((1, WIDE - PACKED), F32)], axis=1)
    for t in m_tasks:
        t.end()
    for t in a_tasks:
        t.last()
    for k in (1, 2, 3):
        back[k].wait_recv()
    dx_ref[...] = dz1[...] + own[...] + rs2_r[0].astype(F32) + rs2_r[1].astype(F32) + rs2_r[2].astype(F32)
    for t in m_tasks:
        t.last()
    run.close()


def reduce_kernel(
    pq, po, gsm, dqkv_o, do_o, sm_o, nq, fq, tq, no, fo, to, sm_a, sm_u, sm_b, sm_v, send_sems, recv_sems, local_sems
):
    run = Run(send_sems, recv_sems, local_sems)
    place = run.place
    f = place.f
    launch = run.launch
    run.greet(True)
    tasks = [Collect(run, pq, nq, fq, tq, dqkv_o), CollectOutput(run, po, no, fo, to, do_o)]
    for t in tasks:
        t.start()
    a = launch(gsm, sm_a, place.sibling())
    for t in tasks:
        t.middle()
    a.wait_recv()
    sm_u[...] = gsm[...] + sm_a[...]
    far = [launch(sm_u, sm_b.at[k - 1], place.column(k)) for k in (1, 2, 3)]
    for a in far:
        a.wait_recv()
    sm_v[...] = sm_u[...] + sm_b[0] + sm_b[1] + sm_b[2]
    last = [launch(sm_v, sm_o.at[f], place.plane(k)) for k in (1, 2, 3)]
    sm_o[f] = sm_v[...]
    for t in tasks:
        t.end()
    for a in last:
        a.wait_recv()
    for t in tasks:
        t.last()
    run.close()


ANY = pl.BlockSpec(memory_space=pl.ANY)
VM = pl.BlockSpec(memory_space=pltpu.VMEM)
SM = pl.BlockSpec(memory_space=pltpu.SMEM)
LIMIT = 60 * 1024 * 1024
SEMS = (128, 128, 32)


def shape(*dims, dtype=BF):
    return jax.ShapeDtypeStruct(dims, dtype)


def call(kernel, number, outs, out_specs, in_specs, scratch, args, flops):
    return pl.pallas_call(
        kernel,
        out_shape=tuple(outs),
        in_specs=in_specs,
        out_specs=tuple(out_specs),
        scratch_shapes=[pltpu.VMEM(s.shape, s.dtype) for s in scratch]
        + [pltpu.SemaphoreType.DMA((n,)) for n in SEMS],
        compiler_params=pltpu.CompilerParams(
            collective_id=number, has_side_effects=True, vmem_limit_bytes=LIMIT
        ),
        cost_estimate=pl.CostEstimate(flops=flops, bytes_accessed=20000000, transcendentals=0),
    )(*args)


def column_parts(query, key, value, inner):
    n = query.shape[0] * query.shape[1]
    q = query.reshape(n, 4, 3, 64)
    q = jnp.pad(q, ((0, 0), (0, 0), (0, 1), (0, 0))).reshape(n, 4, 256)
    kv = jnp.stack([key.reshape(n, 4, 3, 64), value.reshape(n, 4, 3, 64)], axis=3).reshape(n, 4, 384)
    up = inner.reshape(n, 4, 4, 192).transpose(0, 2, 1, 3).reshape(n, 4, WIDE)
    return jnp.concatenate([q, kv, up], axis=2).transpose(1, 0, 2)


LOCAL = shape(ROWS, WIDE, dtype=F32)
FULL = shape(4, ROWS, WIDE)
PIECE = shape(3, ROWS, WIDE)
QKV = shape(4, 2, 96, PACKED)
BIG = shape(4, 2, 96, WIDE)
OUTPUT = shape(192, WIDE)
SAVED = (
    FULL, shape(512, SLICE), shape(4, 2, 512, SLICE), shape(4, 2, ROWS, SLICE), shape(3, 4, ROWS, NKEYS),
    shape(4, ROWS, 256), LOCAL, FULL, shape(4, ROWS, WIDE, dtype=F32), FULL, LOCAL,
)


def forward_layer(first, state, qkv, o, in_c, out_c, vec, route, pen, following):
    outs = (LOCAL,) + SAVED + (BIG, BIG) + ((QKV, OUTPUT, QKV, OUTPUT) if first else ())
    got = call(
        lambda *refs: forward_kernel(first, *refs), 1 if first else 2, outs, (VM,) + (ANY,) * (len(outs) - 1),
        [VM] + [ANY] * 4 + [VM] + [SM] * 2 + [ANY] * len(following),
        list(SAVED)
        + [BIG, BIG, QKV, shape(256, WIDE), shape(3, 4, ROWS, 128, dtype=F32), LOCAL]
        + [PIECE] * 4,
        (state, qkv, o, in_c, out_c, vec, route, pen) + tuple(following), 3 * 10**9,
    )
    return got[0], got[1:12], got[12:]


def collect_scratch(columns, rows):
    return [shape(4, 96, columns), shape(3, 96, columns)] + ([shape(96, columns, dtype=F32)] if rows else [])


OUT_SCRATCH = [shape(96, WIDE), shape(4, 96, WIDE), shape(96, WIDE, dtype=F32)]
PARTS = (shape(2, 4, 96, PACKED), shape(2, 96, WIDE))
SHARES = (shape(4, 24, PACKED, dtype=F32), shape(24, WIDE, dtype=F32))


def backward_layer(upstream, weights, vec, route, saved, before):
    wqkv, wo, win, wout = weights
    xb, qp, kv, kp, p, ctx, z1, hb, gp, gl, z2 = saved
    keys = shape(4, 256, SLICE, dtype=F32)
    extra = len(before) > 0
    outs = (LOCAL,) + PARTS + (
        shape(4, 24, WIDE, dtype=F32), shape(96, WIDE, dtype=F32), shape(8, WIDE, dtype=F32)
    ) + (SHARES if extra else ())
    late = [QKV, shape(256, WIDE)] + [SAVED[i] for i in range(6)]
    scratch = late + [
        FULL, FULL, FULL, shape(512, SLICE), shape(3, 512, 128, dtype=F32), shape(4, ROWS, PACKED), LOCAL, LOCAL,
        shape(1024, SLICE, dtype=F32), keys, keys, shape(2, 4, 512, SLICE), shape(4, 512, SLICE),
        shape(4, 512, SLICE), shape(3, 512, SLICE), LOCAL, PIECE, PIECE, PIECE, PIECE,
    ]
    scratch += [shape(2, 4, 96, WIDE)] + collect_scratch(WIDE, True) + [shape(2, 4, 96, WIDE)] + collect_scratch(WIDE, False)
    if extra:
        scratch += collect_scratch(PACKED, True) + OUT_SCRATCH
    return call(
        lambda *refs: backward_kernel(extra, *refs), 4 if extra else 3, outs, (VM,) * len(outs),
        [VM] * 4 + [SM] + [VM] * 5 + [ANY] * 8 + [VM] * len(before), scratch,
        (upstream, win, wout, vec, route, z1, hb, gp, gl, z2, wqkv, wo, xb, qp, kv, kp, p, ctx) + tuple(before),
        6 * 10**9,
    )


def reduce_rest(pq, po, gsm):
    sm = shape(16, WIDE, dtype=F32)
    return call(
        reduce_kernel, 5, SHARES + (shape(4, 16, WIDE, dtype=F32),), (VM,) * 3, [VM] * 3,
        collect_scratch(PACKED, True) + OUT_SCRATCH + [sm, sm, shape(3, 16, WIDE, dtype=F32), sm],
        (pq, po, gsm), 1000,
    )


def slice_body(
    activations, query_weight, query_bias, key_weight, value_weight, value_bias, output_weight, output_bias,
    first_gain, first_shift, inner_weight, inner_bias, outer_weight, outer_bias, second_gain, second_shift,
    cotangent, parents, segments,
):
    place = Place()
    z, f, c = place.z, place.f, place.c
    col = column_parts(query_weight, key_weight, value_weight, inner_weight)
    vectors = (query_bias, value_bias, output_bias, first_gain, first_shift, outer_bias, second_gain, second_shift)
    small = jnp.concatenate([v.reshape(-1) for v in vectors] + [inner_bias.reshape(-1), segments[:1].astype(BF)])
    small = jnp.pad(small, (0, 2048 - small.shape[0])).reshape(16, 128)
    colp, op, smallg = call(
        exchange_kernel, 0, (shape(4, 48, 1408), shape(4, 48, WIDE), shape(4, 2, 4, 16, 128)), (ANY,) * 3, [ANY] * 3,
        [], (col, output_weight.reshape(48, WIDE), small), 1000,
    )
    colp = colp.reshape(4, 2, 24, 1408).transpose(1, 0, 2, 3).reshape(2, 96, 1408)
    op = op.reshape(4, 2, 24, WIDE).transpose(1, 0, 2, 3).reshape(2, 96, WIDE)
    small = smallg.transpose(0, 2, 1, 3, 4).reshape(32, 2048).astype(F32)
    parts = [small[:, i * 48 : (i + 1) * 48].reshape(32, 2, 24).transpose(1, 0, 2).reshape(2, WIDE) for i in range(8)]
    q_all, v_all, o_all, g1, s1, out_all, g2, s2 = parts
    in_all = small[:, 384:576].reshape(4, 4, 2, 2, 96)
    in_mine = lax.dynamic_index_in_dim(in_all, f, 1, keepdims=False).transpose(2, 0, 1, 3).reshape(2, WIDE)
    q_mine = lax.dynamic_slice_in_dim(q_all, 192 * f, 192, 1)
    v_mine = lax.dynamic_slice_in_dim(v_all, 192 * f, 192, 1).reshape(2, 3, 64)
    kv_mine = jnp.pad(v_mine, ((0, 0), (0, 0), (64, 0))).reshape(2, SLICE)
    qkv_mine = jnp.pad(jnp.concatenate([q_mine, jnp.zeros((2, 64), F32), kv_mine], axis=1), ((0, 0), (0, WIDE - PACKED)))
    vecs = jnp.stack([qkv_mine, o_all, g1, s1, in_mine, out_all, g2, s2], axis=1)

    labels = small[:, 576].reshape(16, 2)[:, 0].astype(jnp.int32)
    mine = lax.dynamic_slice_in_dim(labels, 4 * z, 4, 0)
    parent = lookup_rows(mine, parents)
    match = (parent[:, None] == labels[None, :]).astype(jnp.int32)
    branch = parent != labels[0]
    pen = jnp.concatenate(
        [jnp.where(branch, 0.0, MASKED), jnp.where(z > 0, jnp.zeros((4,), F32), MASKED)]
    ).astype(F32)
    route = jnp.where(branch[:, None], match, 0).astype(F32)

    qkv_c = [colp[i, :, :PACKED] for i in range(2)]
    in_c = [colp[i, :, PACKED:] for i in range(2)]
    state, kept0, (win0, wout0, wqkv0, wo0, wqkv1, wo1) = forward_layer(
        True, activations.astype(F32), qkv_c[0], op[0], in_c[0], outer_weight[0], vecs[0], route, pen, (qkv_c[1], op[1])
    )
    state, kept1, (win1, wout1) = forward_layer(
        False, state, wqkv1, wo1, in_c[1], outer_weight[1], vecs[1], route, pen, ()
    )
    outcome = state.astype(BF)
    upstream, pq, po, din1, dout1, dvec1 = backward_layer(
        cotangent.astype(F32), (wqkv1, wo1, win1, wout1), vecs[1], route, kept1, ()
    )
    upstream, pq, po, din0, dout0, dvec0, dqkv1, do1 = backward_layer(
        upstream, (wqkv0, wo0, win0, wout0), vecs[0], route, kept0, (pq, po)
    )
    dqkv0, do0, rsm = reduce_rest(pq, po, jnp.concatenate([dvec0, dvec1]))
    dqkv = jnp.stack([dqkv0, dqkv1]).transpose(0, 2, 1, 3)
    dq = dqkv[..., :192].reshape(2, 24, WIDE)
    dkv = dqkv[..., 256:].reshape(2, 24, 4, 3, 2, 64)
    dk = dkv[..., 0, :].reshape(2, 24, WIDE)
    dv = dkv[..., 1, :].reshape(2, 24, WIDE)
    dinner = jnp.stack([din0, din1]).reshape(2, 4, 24, 4, 192).transpose(0, 2, 3, 1, 4).reshape(2, 24, 3072)
    rsm = rsm.reshape(4, 2, 8, WIDE)
    sums = jnp.sum(rsm, axis=0)
    at = 24 * (8 * z + 2 * f + c)

    def own_part(v):
        return lax.dynamic_slice_in_dim(v, at, 24, 1)

    dqb = rsm[:, :, 0, :192].transpose(1, 0, 2).reshape(2, WIDE)
    dvb = rsm[:, :, 0, 256:640].reshape(4, 2, 3, 2, 64)[:, :, :, 1].transpose(1, 0, 2, 3).reshape(2, WIDE)
    dib = lax.dynamic_index_in_dim(rsm[:, :, 4], f, 0, keepdims=False)
    dib = lax.dynamic_slice_in_dim(dib, 96 * (2 * z + c), 96, 1)
    return (
        outcome, upstream.astype(BF), dq, own_part(dqb), dk, dv, own_part(dvb),
        jnp.stack([do0, do1]), own_part(sums[:, 1]), own_part(sums[:, 2]), own_part(sums[:, 3]),
        dinner, dib, jnp.stack([dout0, dout1]), own_part(sums[:, 5]), own_part(sums[:, 6]), own_part(sums[:, 7]),
    )


def solution(mesh):
    placed = (
        P("fsdp", None),
        P(None, "fsdp", None),
        P(None, "fsdp"),
        P(None, "fsdp", None),
        P(None, "fsdp", None),
        P(None, "fsdp"),
        P(None, "fsdp", None),
        P(None, "fsdp"),
        P(None, "fsdp"),
        P(None, "fsdp"),
        P(None, "fsdp", None),
        P(None, "fsdp"),
        P(None, "fsdp", None),
        P(None, "fsdp"),
        P(None, "fsdp"),
        P(None, "fsdp"),
        P("fsdp", None),
        P(),
        P("fsdp"),
    )
    return jax.shard_map(
        slice_body if mesh.shape["fsdp"] == 32 else body,
        mesh=mesh,
        in_specs=placed,
        out_specs=(
            P("fsdp", None),
            P("fsdp", None),
            P(None, "fsdp", None),
            P(None, "fsdp"),
            P(None, "fsdp", None),
            P(None, "fsdp", None),
            P(None, "fsdp"),
            P(None, "fsdp", None),
            P(None, "fsdp"),
            P(None, "fsdp"),
            P(None, "fsdp"),
            P(None, "fsdp", None),
            P(None, "fsdp"),
            P(None, "fsdp", None),
            P(None, "fsdp"),
            P(None, "fsdp"),
            P(None, "fsdp"),
        ),
        check_vma=False,
    )
```

```python
import jax
import jax.numpy as jnp
from jax import lax
from jax.experimental import pallas as pl
from jax.experimental.pallas import tpu as pltpu
from jax.sharding import PartitionSpec as P

HEADS = 12
HEAD_DIM = 64
LAYERS = 2
TREE_LEN = 4096


EPSILON = 1e-06
MASKED = -1000000000.0


def partner_2(shard, axis, stride):
    return lax.ppermute(shard, axis, [(i, i ^ 1 << stride) for i in range(lax.axis_size(axis))])


def as_sent(shard):
    return jax.tree.map(lambda a: a.astype(jnp.bfloat16) if a.dtype == jnp.float32 else a, shard)


def product(a, b):
    return jnp.dot(a, b, preferred_element_type=jnp.float32)


def product_tn(a, b):
    return lax.dot_general(a, b, (((0,), (0,)), ((), ())), preferred_element_type=jnp.float32)


def product_nt(a, b):
    return lax.dot_general(a, b, (((1,), (1,)), ((), ())), preferred_element_type=jnp.float32)


def exact_gelu(u):
    return jax.nn.gelu(u, approximate=False)


def layer_norm(z, gain_vec, shift_vec):
    centre = z - jnp.mean(z, axis=-1, keepdims=True)
    scaled = centre * lax.rsqrt(jnp.mean(centre * centre, axis=-1, keepdims=True) + EPSILON)
    return scaled * gain_vec.astype(jnp.float32) + shift_vec.astype(jnp.float32)


def norm_backward(z, gain_vec, upstream):
    centre = z - jnp.mean(z, axis=-1, keepdims=True)
    invert = lax.rsqrt(jnp.mean(centre * centre, axis=-1, keepdims=True) + EPSILON)
    scaled = centre * invert
    weighted = upstream * gain_vec.astype(jnp.float32)
    inner = invert * (
        weighted
        - jnp.mean(weighted, axis=-1, keepdims=True)
        - scaled * jnp.mean(weighted * scaled, axis=-1, keepdims=True)
    )
    return (inner, jnp.sum(upstream * scaled, axis=0), jnp.sum(upstream, axis=0))


def lookup_rows(ids, parents):
    table = jnp.arange(parents.shape[0], dtype=jnp.int32)
    return jnp.sum(jnp.where(ids[:, None] == table[None, :], parents[None, :], 0), axis=1)


def join_heads(stacked):
    return stacked.transpose(1, 0, 2).reshape(stacked.shape[1], -1)


def gather_group(key_rows, value_rows, labels, position, bit_count):
    for b in range(bit_count):
        partner = partner_2((key_rows, value_rows, labels), "fsdp", b)
        upper_side = position >> b & 1 == 1
        key_rows = jnp.where(
            upper_side,
            jnp.concatenate([partner[0], key_rows]),
            jnp.concatenate([key_rows, partner[0]]),
        )
        value_rows = jnp.where(
            upper_side,
            jnp.concatenate([partner[1], value_rows]),
            jnp.concatenate([value_rows, partner[1]]),
        )
        labels = jnp.where(
            upper_side, jnp.concatenate([partner[2], labels]), jnp.concatenate([labels, partner[2]])
        )
    return (key_rows, value_rows, labels)


def sum_group(key_grad, value_grad, position, bit_count):
    for b in reversed(range(bit_count)):
        halfway = key_grad.shape[0] // 2
        upper_side = position >> b & 1 == 1
        outgoing = (
            jnp.where(upper_side, key_grad[:halfway], key_grad[halfway:]),
            jnp.where(upper_side, value_grad[:halfway], value_grad[halfway:]),
        )
        partner = partner_2((as_sent(outgoing[0]), as_sent(outgoing[1])), "fsdp", b)
        key_grad = jnp.where(upper_side, key_grad[halfway:], key_grad[:halfway]) + partner[0]
        value_grad = jnp.where(upper_side, value_grad[halfway:], value_grad[:halfway]) + partner[1]
    return (key_grad, value_grad)


def attend_forward(queries, key_rows, value_rows, allowed):
    factor = HEAD_DIM ** (-0.5)

    def one_head(j):
        start = j * HEAD_DIM
        q = lax.dynamic_slice_in_dim(queries, start, HEAD_DIM, 1)
        k = lax.dynamic_slice_in_dim(key_rows, start, HEAD_DIM, 1)
        v = lax.dynamic_slice_in_dim(value_rows, start, HEAD_DIM, 1)
        s = jnp.where(allowed, product_nt(q, k) * factor, MASKED)
        maxima = jnp.max(s, axis=1, keepdims=True)
        e = jnp.exp(s - maxima)
        totals = jnp.sum(e, axis=1, keepdims=True)
        p = (e / totals).astype(jnp.bfloat16)
        return (product(p, v), (maxima + jnp.log(totals))[:, 0])

    stacked, log_total = lax.map(one_head, jnp.arange(HEADS))
    return (join_heads(stacked), log_total)


def attend_backward(queries, key_rows, value_rows, allowed, log_total, grad_context):
    factor = HEAD_DIM ** (-0.5)

    def one_head(j):
        start = j * HEAD_DIM
        q = lax.dynamic_slice_in_dim(queries, start, HEAD_DIM, 1)
        k = lax.dynamic_slice_in_dim(key_rows, start, HEAD_DIM, 1)
        v = lax.dynamic_slice_in_dim(value_rows, start, HEAD_DIM, 1)
        g = lax.dynamic_slice_in_dim(grad_context, start, HEAD_DIM, 1)
        s = jnp.where(allowed, product_nt(q, k) * factor, MASKED)
        p = jnp.where(allowed, jnp.exp(s - log_total[j][:, None]), 0.0)
        grad_p = product_nt(g, v)
        grad_v = product_tn(p.astype(jnp.bfloat16), g)
        grad_s = (p * (grad_p - jnp.sum(p * grad_p, axis=1, keepdims=True))).astype(jnp.bfloat16)
        grad_q = product(grad_s, k) * factor
        grad_k = product_tn(grad_s, q) * factor
        return (grad_q, grad_k, grad_v)

    grad_q, grad_k, grad_v = lax.map(one_head, jnp.arange(HEADS))
    return (join_heads(grad_q), join_heads(grad_k), join_heads(grad_v))


def layer_forward(state, full, segments, parent_one, parent_two, position, bit_count):
    (
        q_weight,
        q_bias,
        k_weight,
        v_weight,
        v_bias,
        o_weight,
        o_bias,
        gain_one,
        shift_one,
        up_weight,
        up_bias,
        down_weight,
        down_bias,
        gain_two,
        shift_two,
    ) = full
    inputs = state.astype(jnp.bfloat16)
    queries = (product(inputs, q_weight) + q_bias).astype(jnp.bfloat16)
    key_local = product(inputs, k_weight).astype(jnp.bfloat16)
    value_local = (product(inputs, v_weight) + v_bias).astype(jnp.bfloat16)
    key_rows, value_rows, labels = gather_group(
        key_local, value_local, segments, position, bit_count
    )
    allowed = (
        (labels[None, :] == segments[:, None])
        | (labels[None, :] == parent_one[:, None])
        | (labels[None, :] == parent_two[:, None])
    )
    context_wide, log_total = attend_forward(queries, key_rows, value_rows, allowed)
    context = context_wide.astype(jnp.bfloat16)
    first_sum = state + product(context, o_weight) + o_bias
    hidden = layer_norm(first_sum, gain_one, shift_one)
    hidden_low = hidden.astype(jnp.bfloat16)
    pre_act = product(hidden_low, up_weight) + up_bias
    gelu_out = exact_gelu(pre_act).astype(jnp.bfloat16)
    second_sum = hidden + product(gelu_out, down_weight) + down_bias
    record = (
        inputs,
        queries,
        key_rows,
        value_rows,
        allowed,
        log_total,
        context,
        first_sum,
        hidden_low,
        pre_act,
        gelu_out,
        second_sum,
    )
    return (record, layer_norm(second_sum, gain_two, shift_two))


def layer_backward(upstream, full, record, position, bit_count):
    (
        q_weight,
        q_bias,
        k_weight,
        v_weight,
        v_bias,
        o_weight,
        o_bias,
        gain_one,
        shift_one,
        up_weight,
        up_bias,
        down_weight,
        down_bias,
        gain_two,
        shift_two,
    ) = full
    (
        inputs,
        queries,
        key_rows,
        value_rows,
        allowed,
        log_total,
        context,
        first_sum,
        hidden_low,
        pre_act,
        gelu_out,
        second_sum,
    ) = record
    grad_z2, grad_gain_two, grad_shift_two = norm_backward(second_sum, gain_two, upstream)
    grad_f = grad_z2.astype(jnp.bfloat16)
    grad_down_bias = jnp.sum(grad_f.astype(jnp.float32), axis=0)
    grad_down = product_tn(gelu_out, grad_f)
    grad_gelu = product_nt(grad_f, down_weight)
    unused_value, gelu_back = jax.vjp(exact_gelu, pre_act)
    grad_u = gelu_back(grad_gelu)[0].astype(jnp.bfloat16)
    grad_up_bias = jnp.sum(grad_u.astype(jnp.float32), axis=0)
    grad_up = product_tn(hidden_low, grad_u)
    grad_h = grad_z2 + product_nt(grad_u, up_weight)
    grad_z1, grad_gain_one, grad_shift_one = norm_backward(first_sum, gain_one, grad_h)
    grad_a = grad_z1.astype(jnp.bfloat16)
    grad_o_bias = jnp.sum(grad_a.astype(jnp.float32), axis=0)
    grad_o = product_tn(context, grad_a)
    grad_context = product_nt(grad_a, o_weight).astype(jnp.bfloat16)
    grad_q, key_grad, value_grad = attend_backward(
        queries, key_rows, value_rows, allowed, log_total, grad_context
    )
    key_grad, value_grad = sum_group(key_grad, value_grad, position, bit_count)
    q_low = grad_q.astype(jnp.bfloat16)
    k_low = key_grad.astype(jnp.bfloat16)
    v_low = value_grad.astype(jnp.bfloat16)
    grad_x = (
        grad_z1
        + product_nt(q_low, q_weight)
        + product_nt(k_low, k_weight)
        + product_nt(v_low, v_weight)
    )
    terms = (
        product_tn(inputs, q_low),
        jnp.sum(q_low.astype(jnp.float32), axis=0),
        product_tn(inputs, k_low),
        product_tn(inputs, v_low),
        jnp.sum(v_low.astype(jnp.float32), axis=0),
        grad_o,
        grad_o_bias,
        grad_gain_one,
        grad_shift_one,
        grad_up,
        grad_up_bias,
        grad_down,
        grad_down_bias,
        grad_gain_two,
        grad_shift_two,
    )
    return (grad_x, terms)


def stack_layers(groups, n):
    return jnp.stack([g[n] for g in groups])


def body(
    activations,
    query_weight,
    query_bias,
    key_weight,
    value_weight,
    value_bias,
    output_weight,
    output_bias,
    first_gain,
    first_shift,
    inner_weight,
    inner_bias,
    outer_weight,
    outer_bias,
    second_gain,
    second_shift,
    cotangent,
    parents,
    segments,
):
    position = lax.axis_index("fsdp")
    bit_count = (TREE_LEN // activations.shape[0]).bit_length() - 1
    parent_one = lookup_rows(segments, parents)
    parent_two = lookup_rows(parent_one, parents)
    state = activations.astype(jnp.float32)
    saved = []
    kept_weights = []
    for i in range(LAYERS):
        full = (
            lax.all_gather(query_weight[i], "fsdp", axis=0, tiled=True),
            lax.all_gather(query_bias[i], "fsdp", axis=0, tiled=True),
            lax.all_gather(key_weight[i], "fsdp", axis=0, tiled=True),
            lax.all_gather(value_weight[i], "fsdp", axis=0, tiled=True),
            lax.all_gather(value_bias[i], "fsdp", axis=0, tiled=True),
            lax.all_gather(output_weight[i], "fsdp", axis=0, tiled=True),
            lax.all_gather(output_bias[i], "fsdp", axis=0, tiled=True),
            lax.all_gather(first_gain[i], "fsdp", axis=0, tiled=True),
            lax.all_gather(first_shift[i], "fsdp", axis=0, tiled=True),
            lax.all_gather(inner_weight[i], "fsdp", axis=0, tiled=True),
            lax.all_gather(inner_bias[i], "fsdp", axis=0, tiled=True),
            lax.all_gather(outer_weight[i], "fsdp", axis=0, tiled=True),
            lax.all_gather(outer_bias[i], "fsdp", axis=0, tiled=True),
            lax.all_gather(second_gain[i], "fsdp", axis=0, tiled=True),
            lax.all_gather(second_shift[i], "fsdp", axis=0, tiled=True),
        )
        kept_weights.append(full)
        record, state = layer_forward(
            state, full, segments, parent_one, parent_two, position, bit_count
        )
        saved.append(record)
    outcome = state.astype(jnp.bfloat16)
    upstream = cotangent.astype(jnp.float32)
    layer_grads = [None] * LAYERS
    for i in reversed(range(LAYERS)):
        full = (
            lax.all_gather(query_weight[i], "fsdp", axis=0, tiled=True),
            lax.all_gather(query_bias[i], "fsdp", axis=0, tiled=True),
            lax.all_gather(key_weight[i], "fsdp", axis=0, tiled=True),
            lax.all_gather(value_weight[i], "fsdp", axis=0, tiled=True),
            lax.all_gather(value_bias[i], "fsdp", axis=0, tiled=True),
            lax.all_gather(output_weight[i], "fsdp", axis=0, tiled=True),
            lax.all_gather(output_bias[i], "fsdp", axis=0, tiled=True),
            lax.all_gather(first_gain[i], "fsdp", axis=0, tiled=True),
            lax.all_gather(first_shift[i], "fsdp", axis=0, tiled=True),
            lax.all_gather(inner_weight[i], "fsdp", axis=0, tiled=True),
            lax.all_gather(inner_bias[i], "fsdp", axis=0, tiled=True),
            lax.all_gather(outer_weight[i], "fsdp", axis=0, tiled=True),
            lax.all_gather(outer_bias[i], "fsdp", axis=0, tiled=True),
            lax.all_gather(second_gain[i], "fsdp", axis=0, tiled=True),
            lax.all_gather(second_shift[i], "fsdp", axis=0, tiled=True),
        )
        upstream, terms = layer_backward(upstream, full, saved[i], position, bit_count)
        layer_grads[i] = (
            lax.psum_scatter(terms[0], "fsdp", scatter_dimension=0, tiled=True),
            lax.psum_scatter(terms[1], "fsdp", scatter_dimension=0, tiled=True),
            lax.psum_scatter(terms[2], "fsdp", scatter_dimension=0, tiled=True),
            lax.psum_scatter(terms[3], "fsdp", scatter_dimension=0, tiled=True),
            lax.psum_scatter(terms[4], "fsdp", scatter_dimension=0, tiled=True),
            lax.psum_scatter(terms[5], "fsdp", scatter_dimension=0, tiled=True),
            lax.psum_scatter(terms[6], "fsdp", scatter_dimension=0, tiled=True),
            lax.psum_scatter(terms[7], "fsdp", scatter_dimension=0, tiled=True),
            lax.psum_scatter(terms[8], "fsdp", scatter_dimension=0, tiled=True),
            lax.psum_scatter(terms[9], "fsdp", scatter_dimension=0, tiled=True),
            lax.psum_scatter(terms[10], "fsdp", scatter_dimension=0, tiled=True),
            lax.psum_scatter(terms[11], "fsdp", scatter_dimension=0, tiled=True),
            lax.psum_scatter(terms[12], "fsdp", scatter_dimension=0, tiled=True),
            lax.psum_scatter(terms[13], "fsdp", scatter_dimension=0, tiled=True),
            lax.psum_scatter(terms[14], "fsdp", scatter_dimension=0, tiled=True),
        )
    shares = tuple((stack_layers(layer_grads, n) for n in range(15)))
    return (outcome, upstream.astype(jnp.bfloat16)) + tuple(shares)


MESH = pl.DeviceIdType.MESH
BF = jnp.bfloat16
F32 = jnp.float32
WIDE = 768
SLICE = 384
PACKED = 640
ROWS = 128
NKEYS = 1536


class Pool:
    def __init__(self, ref):
        self.ref = ref
        self.used = 0

    def take(self):
        self.used += 1
        return self.ref.at[self.used - 1]

    def block(self, n):
        first = self.used
        self.used += n
        return lambda i: self.ref.at[first + i]


class Place:
    def __init__(self):
        me = lax.axis_index("fsdp")
        p = lax.rem(me, 32)
        self.base = me - p
        self.z = p // 8
        self.f = lax.rem(p // 2, 4)
        self.c = lax.rem(p, 2)

    def at(self, z, f, c):
        return self.base + 8 * z + 2 * f + c

    def f_at(self, k):
        return lax.rem(self.f + k + 4, 4)

    def z_at(self, k):
        return lax.rem(self.z + k + 4, 4)

    def plane(self, k):
        return self.at(self.z, self.f_at(k), self.c)

    def across(self, k):
        return self.at(self.z, self.f_at(k), 1 - self.c)

    def column(self, k):
        return self.at(self.z_at(k), self.f, self.c)

    def sibling(self):
        return self.at(self.z, self.f, 1 - self.c)


def remote(src, dst, sems, device):
    return pltpu.make_async_remote_copy(
        src_ref=src, dst_ref=dst, send_sem=sems[0], recv_sem=sems[1], device_id=(device,), device_id_type=MESH
    )


class Run:
    def __init__(self, send_sems, recv_sems, local_sems):
        self.place = Place()
        self.sends, self.recvs, self.locals = Pool(send_sems), Pool(recv_sems), Pool(local_sems)
        self.flying, self.saving = [], []

    def greet(self, wide):
        place = self.place
        there = [place.plane(k) for k in (1, 2, 3)] + [place.column(k) for k in (1, 2, 3)] + [place.sibling()]
        if wide:
            there += [place.across(k) for k in (1, 2, 3)]
        barrier = pltpu.get_barrier_semaphore()
        for dev in there:
            pl.semaphore_signal(barrier, inc=1, device_id=(dev,), device_id_type=MESH)
        pl.semaphore_wait(barrier, len(there))

    def launch(self, src, dst, device):
        a = remote(src, dst, (self.sends.take(), self.recvs.take()), device)
        a.start()
        self.flying.append((None, a))
        return a

    def launch_if(self, cond, src, dst, sems, device):
        a = remote(src, dst, sems, device)

        @pl.when(cond)
        def _():
            a.start()

        self.flying.append((cond, a))
        return a

    def local(self, src, dst):
        a = pltpu.make_async_copy(src, dst, self.locals.take())
        a.start()
        return a

    def save(self, src, dst):
        self.saving.append(self.local(src, dst))

    def close(self):
        for a in self.saving:
            a.wait()
        for cond, a in self.flying:
            if cond is None:
                a.wait_send()
            else:

                @pl.when(cond)
                def _(a=a):
                    a.wait_send()


class Spread:
    def __init__(self, run, chunk, full):
        self.run, self.chunk, self.full = run, chunk, full

    def start(self):
        run, place = self.run, self.run.place
        mine = self.full.at[place.z, place.c]
        self.own = run.local(self.chunk, mine)
        self.far = [run.launch(self.chunk, mine, place.column(k)) for k in (1, 2, 3)]
        self.near = [run.launch(self.chunk, mine, place.sibling())]

    def relay(self):
        run, place = self.run, self.run.place
        for k in (1, 2, 3):
            self.far[k - 1].wait_recv()
            there = self.full.at[place.z_at(-k), place.c]
            self.near.append(run.launch(there, there, place.sibling()))

    def finish(self):
        self.own.wait()
        for a in self.near:
            a.wait_recv()


class SpreadOutput:
    def __init__(self, run, chunk, full):
        self.run, self.chunk = run, chunk
        self.part = full.at[pl.ds(pl.multiple_of(run.place.c * 96, 96), 96)]

    def start(self):
        run, place = self.run, self.run.place
        self.copy = pltpu.make_async_copy(self.chunk, self.part, run.locals.take())

        @pl.when(place.f == place.z)
        def _():
            self.copy.start()

        arrive = run.recvs.take()
        for k in (1, 2, 3):
            self.far = run.launch_if(
                place.f == place.z, self.chunk, self.part, (run.sends.take(), arrive), place.column(k)
            )

    def relay(self):
        run, place = self.run, self.run.place

        @pl.when(place.f == place.z)
        def _():
            self.copy.wait()

        @pl.when(place.f != place.z)
        def _():
            self.far.wait_recv()

        self.near = run.launch(self.part, self.part, place.sibling())

    def finish(self):
        self.near.wait_recv()


class Collect:
    def __init__(self, run, part, near, far, total, out):
        self.run, self.part, self.near, self.far, self.total, self.out = run, part, near, far, total, out

    def start(self):
        place = self.run.place
        self.a = self.run.launch(self.part.at[1 - place.c], self.near, place.sibling())

    def middle(self):
        run, place = self.run, self.run.place
        self.a.wait_recv()

        def add(i, carry):
            self.near[i] = (self.part[place.c, i].astype(F32) + self.near[i].astype(F32)).astype(BF)
            return carry

        lax.fori_loop(0, 4, add, 0)
        self.moves = [
            run.launch(self.near.at[place.z_at(k)], self.far.at[k - 1], place.column(k)) for k in (1, 2, 3)
        ]

    def end(self):
        run, place = self.run, self.run.place
        for a in self.moves:
            a.wait_recv()
        result = self.near[place.z].astype(F32)
        for k in range(3):
            result = result + self.far[k].astype(F32)
        if self.total is None:
            self.out[...] = result
            return
        self.total[...] = result
        scatter_rows(self, self.total, self.out.at[place.f], None)

    def last(self):
        if self.total is None:
            return
        place = self.run.place
        for k in (1, 2, 3):
            g = place.f_at(k)
            remote(
                self.out.at[g], self.out.at[g], (self.send, self.arrive(g)), place.plane(k)
            ).wait_recv()

        @pl.when(place.c != place.f // 2)
        def _():
            remote(
                self.out.at[place.f], self.out.at[place.f], (self.send, self.arrive(place.f)), place.sibling()
            ).wait_recv()


def scatter_rows(task, total, landing, cond):
    run, place = task.run, task.run.place
    arrive = run.recvs.block(4)
    for j in range(4):
        there = place.at(place.z, 2 * place.c + j // 2, j % 2)
        here = jnp.logical_and(place.f == 2 * place.c + j // 2, place.c == j % 2)
        away = jnp.logical_not(here)
        if cond is not None:
            here, away = jnp.logical_and(here, cond), jnp.logical_and(away, cond)
        task.send = run.sends.take()
        slot = arrive(place.f) if cond is None else arrive(0)
        run.launch_if(away, total.at[pl.ds(24 * j, 24)], landing, (task.send, slot), there)

        @pl.when(here)
        def _(j=j):
            landing[...] = total[24 * j : 24 * (j + 1), :]

    task.arrive = arrive


class CollectOutput:
    def __init__(self, run, part, near, far, total, out):
        self.run, self.part, self.near, self.far, self.total, self.out = run, part, near, far, total, out

    def start(self):
        place = self.run.place
        self.a = self.run.launch(self.part.at[1 - place.c], self.near, place.sibling())

    def middle(self):
        run, place = self.run, self.run.place
        self.a.wait_recv()
        self.near[...] = (self.part[place.c].astype(F32) + self.near[...].astype(F32)).astype(BF)
        self.slot = run.recvs.block(4)
        self.one = run.sends.take()
        shift = lax.rem(place.f - place.z + 4, 4)
        run.launch_if(
            place.f != place.z, self.near, self.far.at[shift], (self.one, self.slot(shift)),
            place.at(place.f, place.f, place.c),
        )

    def end(self):
        place = self.run.place

        @pl.when(place.f == place.z)
        def _():
            result = self.near[...].astype(F32)
            for k in (1, 2, 3):
                remote(
                    self.near, self.far.at[k], (self.one, self.slot(k)), place.column(k)
                ).wait_recv()
                result = result + self.far[k].astype(F32)
            self.total[...] = result

        scatter_rows(self, self.total, self.out, place.f == place.z)

    def last(self):
        place = self.run.place
        mine = jnp.logical_and(place.f == place.z, place.c == place.f // 2)

        @pl.when(jnp.logical_not(mine))
        def _():
            remote(self.out, self.out, (self.send, self.arrive(0)), place.sibling()).wait_recv()


def norm_rows(z, gain, shift):
    centre = z - jnp.mean(z, axis=-1, keepdims=True)
    inv = lax.rsqrt(jnp.mean(centre * centre, axis=-1, keepdims=True) + EPSILON)
    return centre * inv * gain + shift


def norm_rows_back(z, gain, upstream):
    centre = z - jnp.mean(z, axis=-1, keepdims=True)
    inv = lax.rsqrt(jnp.mean(centre * centre, axis=-1, keepdims=True) + EPSILON)
    scaled = centre * inv
    weighted = upstream * gain
    inner = inv * (
        weighted
        - jnp.mean(weighted, axis=-1, keepdims=True)
        - scaled * jnp.mean(weighted * scaled, axis=-1, keepdims=True)
    )
    return inner, jnp.sum(upstream * scaled, axis=0, keepdims=True), jnp.sum(upstream, axis=0, keepdims=True)


def exchange_kernel(col, rows_o, small, colp, op, smallg, send_sems, recv_sems, local_sems):
    run = Run(send_sems, recv_sems, local_sems)
    place = run.place
    z, f, c = place.z, place.f, place.c
    mine = c == f // 2
    slot = 2 * lax.rem(f, 2) + c
    own = pltpu.make_async_copy(col.at[f], colp.at[slot], run.locals.take())
    own_o = pltpu.make_async_copy(rows_o, op.at[slot], run.locals.take())
    keep = jnp.logical_and(mine, f == z)

    @pl.when(mine)
    def _():
        own.start()

    @pl.when(keep)
    def _():
        own_o.start()

    own_small = run.local(small, smallg.at[z, c, f])
    run.greet(True)
    first = [run.launch(small, smallg.at[z, c, f], place.plane(k)) for k in (1, 2, 3)]
    arrive, arrive_o = run.recvs.block(4), run.recvs.block(4)
    for k in (1, 2, 3):
        run.launch_if(
            f >= 0, col.at[place.f_at(k)], colp.at[slot], (run.sends.take(), arrive(slot)),
            place.at(z, place.f_at(k), f // 2),
        )
    one = run.sends.take()
    run.launch_if(
        jnp.logical_not(mine), col.at[f], colp.at[slot], (one, arrive(slot)), place.sibling()
    )
    run.launch_if(
        jnp.logical_not(keep), rows_o, op.at[slot], (run.sends.take(), arrive_o(slot)), place.at(z, z, f // 2)
    )
    own_small.wait()
    for a in first:
        a.wait_recv()
    block = smallg.at[z, c]
    far = [run.launch(block, block, place.column(k)) for k in (1, 2, 3)]
    near = [run.launch(block, block, place.sibling())]
    for k in (1, 2, 3):
        far[k - 1].wait_recv()
        there = smallg.at[place.z_at(-k), c]
        near.append(run.launch(there, there, place.sibling()))

    for j in range(4):
        me = jnp.logical_and(f == 2 * c + j // 2, c == j % 2)
        other = jnp.logical_not(me)

        @pl.when(other)
        def _(j=j):
            remote(col.at[0], colp.at[j], (one, arrive(j)), place.sibling()).wait_recv()

        @pl.when(jnp.logical_and(other, f == z))
        def _(j=j):
            remote(rows_o, op.at[j], (one, arrive_o(j)), place.sibling()).wait_recv()

    for a in near:
        a.wait_recv()

    @pl.when(mine)
    def _():
        own.wait()

    @pl.when(keep)
    def _():
        own_o.wait()

    run.close()


class KeyChain:
    def __init__(self, run, trunk, mine, slots, up, down, cs, up_out, down_out, place_in):
        self.run, self.trunk, self.mine, self.slots = run, trunk, mine, slots
        self.up, self.down, self.cs, self.up_out, self.down_out, self.place_in = up, down, cs, up_out, down_out, place_in

    def start(self):
        run, place = self.run, self.run.place
        z, c = place.z, place.c
        self.pairs = [[(run.sends.take(), run.recvs.take()) for _ in range(4)] for _ in range(3)]
        for j in range(4):
            run.launch_if(z == 0, self.mine.at[c, j], self.trunk.at[c, j], self.pairs[0][j], place.column(1))
        self.near = [run.launch(self.mine.at[c], self.mine.at[c], place.sibling())]

        @pl.when(z == 0)
        def _():
            self.trunk[c] = self.mine[c]

        for j in range(4):
            total = self.mine[c, 0] * self.place_in[j, 0].astype(BF)
            for ft in range(1, 4):
                total = total + self.mine[c, ft] * self.place_in[j, ft].astype(BF)
            self.cs[j] = total
            run.launch_if(z == 1, self.cs.at[j], self.up.at[j], self.pairs[1][j], place.column(1))
            run.launch_if(z == 3, self.cs.at[j], self.down.at[j], self.pairs[2][j], place.column(-1))

    def wait(self, which, j):
        dst = (self.trunk.at[self.run.place.c, j], self.up.at[j], self.down.at[j])[which]
        remote(dst, dst, self.pairs[which][j], self.run.place.column(1)).wait_recv()

    def finish(self):
        run, place = self.run, self.run.place
        z, c = place.z, place.c
        trunk = [self.trunk.at[c, j] for j in range(4)]
        for j in range(4):

            @pl.when(z == 1)
            def _(j=j):
                self.wait(0, j)

            run.launch_if(z == 1, trunk[j], trunk[j], self.pairs[0][j], place.column(1))
        for j in range(4):

            @pl.when(z == 2)
            def _(j=j):
                self.wait(1, j)
                self.up_out[j] = self.cs[j] + self.up[j]

            run.launch_if(z == 2, self.up_out.at[j], self.up.at[j], self.pairs[1][j], place.column(1))

            @pl.when(z == 2)
            def _(j=j):
                self.wait(2, j)
                self.down_out[j] = self.cs[j] + self.down[j]

            run.launch_if(z == 2, self.down_out.at[j], self.down.at[j], self.pairs[2][j], place.column(-1))

            @pl.when(z == 2)
            def _(j=j):
                self.slots[c, j] = self.up_out[j] + self.down[j]

        for j in range(4):

            @pl.when(z == 2)
            def _(j=j):
                self.wait(0, j)

            run.launch_if(z == 2, trunk[j], trunk[j], self.pairs[0][j], place.column(1))
        for j in range(4):

            @pl.when(z == 0)
            def _(j=j):
                self.slots[c, j] = self.cs[j]

            @pl.when(z == 1)
            def _(j=j):
                self.wait(2, j)
                self.slots[c, j] = self.cs[j] + self.down[j]

            @pl.when(z == 3)
            def _(j=j):
                self.wait(1, j)
                self.slots[c, j] = self.cs[j] + self.up[j]

        self.near.append(run.launch(self.slots.at[c], self.slots.at[c], place.sibling()))

        @pl.when(z == 3)
        def _():
            for j in range(4):
                self.wait(0, j)

        self.near.append(run.launch(self.trunk.at[c], self.trunk.at[c], place.sibling()))
        for a in self.near:
            a.wait_recv()


class GradChain:
    def __init__(self, run, mine, near, trunk_in, up, down, up_out, down_out, total):
        self.run, self.mine, self.near, self.trunk_in = run, mine, near, trunk_in
        self.up, self.down, self.up_out, self.down_out, self.total = up, down, up_out, down_out, total

    def start(self):
        run, place = self.run, self.run.place
        self.pairs = [[(run.sends.take(), run.recvs.take()) for _ in range(4)] for _ in range(3)]
        self.a = run.launch(self.mine.at[1 - place.c], self.near, place.sibling())

    def wait(self, which, j):
        dst = (self.trunk_in, self.up, self.down)[which].at[j]
        remote(dst, dst, self.pairs[which][j], self.run.place.column(1)).wait_recv()

    def middle(self):
        run, place = self.run, self.run.place
        z, c = place.z, place.c
        self.a.wait_recv()
        near = self.near
        for kind in range(3):
            for j in range(4):
                near[kind, j] = (self.mine[c, kind, j].astype(F32) + near[kind, j].astype(F32)).astype(BF)
                if kind == 0:
                    run.launch_if(z == 3, near.at[0, j], self.trunk_in.at[j], self.pairs[0][j], place.column(-1))
                elif kind == 1:
                    run.launch_if(z == 1, near.at[1, j], self.up.at[j], self.pairs[1][j], place.column(1))
                    run.launch_if(z == 3, near.at[1, j], self.down.at[j], self.pairs[2][j], place.column(-1))

    def pass_on(self):
        run, place = self.run, self.run.place
        z = place.z
        near = self.near
        for j in range(4):
            cond = jnp.logical_or(z == 1, z == 2)

            @pl.when(cond)
            def _(j=j):
                self.wait(0, j)
                near[0, j] = (near[0, j].astype(F32) + self.trunk_in[j].astype(F32)).astype(BF)

            run.launch_if(cond, near.at[0, j], self.trunk_in.at[j], self.pairs[0][j], place.column(-1))

            @pl.when(z == 2)
            def _(j=j):
                self.wait(1, j)
                self.up_out[j] = (near[1, j].astype(F32) + self.up[j].astype(F32)).astype(BF)

            run.launch_if(z == 2, self.up_out.at[j], self.up.at[j], self.pairs[1][j], place.column(1))
        for j in range(4):

            @pl.when(z == 2)
            def _(j=j):
                self.wait(2, j)
                self.down_out[j] = (near[1, j].astype(F32) + self.down[j].astype(F32)).astype(BF)

            run.launch_if(z == 2, self.down_out.at[j], self.down.at[j], self.pairs[2][j], place.column(-1))

    def finish(self, place_in, store):
        place = self.run.place
        z = place.z
        near = self.near

        @pl.when(z == 0)
        def _():
            for j in range(4):
                self.wait(0, j)
                store(j, near[0, j].astype(F32) + self.trunk_in[j].astype(F32))

        @pl.when(z == 1)
        def _():
            for j in range(4):
                self.wait(2, j)
                self.total[j] = (near[1, j].astype(F32) + self.down[j].astype(F32)).astype(BF)

        @pl.when(z == 2)
        def _():
            for j in range(4):
                self.total[j] = (self.up_out[j].astype(F32) + self.down[j].astype(F32)).astype(BF)

        @pl.when(z == 3)
        def _():
            for j in range(4):
                self.wait(1, j)
                self.total[j] = (near[1, j].astype(F32) + self.up[j].astype(F32)).astype(BF)

        @pl.when(z > 0)
        def _():
            for ft in range(4):
                total = near[2, ft].astype(F32)
                for j in range(4):
                    total = total + self.total[j].astype(F32) * place_in[j, ft]
                store(ft, total)


def pick_parents(kp, slots, choose):
    def one(b, carry):
        for cc in range(2):
            total = slots[cc, 0] * choose[b, 0].astype(BF)
            for j in range(1, 4):
                total = total + slots[cc, j] * choose[b, j].astype(BF)
            kp[b, cc] = total
        return carry

    lax.fori_loop(0, 4, one, 0)


def all_keys(trunk, mine, kp, b, lanes):
    return jnp.concatenate(
        [trunk[:, :, :, lanes].reshape(1024, 128), mine[0, b, :, lanes], mine[1, b, :, lanes], kp[b, 0, :, lanes], kp[b, 1, :, lanes]],
        axis=0,
    )


def flat(ref):
    return ref[...].reshape(-1, ref.shape[-1])


def forward_kernel(first, *refs):
    refs = list(refs)

    def take(n):
        out = refs[:n]
        del refs[:n]
        return out

    x_ref, qkv_in, o_in, in_c, out_c, vec, place_in, choose, pen = take(9)
    if first:
        qkv_next, o_next = take(2)
    xn_ref, xb_o, qp_o, trunk_o, mine_o, kp_o, p_o, ctx_o, z1_o, hb_o, gp_o, gl_o, z2_o, win_o, wout_o = take(15)
    if first:
        wqkv_o, wo_o, wqkv_n, wo_n = take(4)
    xb, qp, trunk, mine, kp, p, ctx, z1, hb, gp, gl, z2, win, wout, wqkv, wo, heads, own, rs1_s, rs1_r, rs2_s, rs2_r = take(22)
    chain_refs = take(6)
    run = Run(*refs)
    place = run.place
    z, f, c = place.z, place.f, place.c
    launch = run.launch

    xb[f] = x_ref[...].astype(BF)
    wo[192:256, :] = jnp.zeros((64, WIDE), BF)
    if not first:
        loads = [run.local(qkv_in, wqkv), run.local(o_in, wo.at[pl.ds(0, 192)])]
    run.greet(False)
    came = [None] + [launch(xb.at[f], xb.at[f], place.plane(k)) for k in (1, 2, 3)]
    if first:
        a_tasks = [Spread(run, qkv_in, wqkv), SpreadOutput(run, o_in, wo)]
        for t in a_tasks:
            t.start()
        a_tasks[0].relay()
        a_tasks[0].finish()
    else:
        for a in loads:
            a.wait()
    lane = lax.broadcasted_iota(jnp.int32, (ROWS, 128), 1)
    for k in range(4):
        g = place.f_at(-k)
        if k:
            came[k].wait_recv()
        qkv = product(xb[g], flat(wqkv)) + vec[0:1, :PACKED]
        rows = pl.ds(pl.multiple_of(g * ROWS, ROWS), ROWS)
        mine[c, g] = qkv[:, 256:].astype(BF)
        scaled = qkv[:, :256] * (HEAD_DIM ** (-0.5))
        front = scaled[:, :128]
        qp[rows, 0:128] = jnp.where(lane < 64, front, 0.0).astype(BF)
        qp[rows, 128:256] = jnp.where(lane < 64, pltpu.roll(front, 64, 1), 0.0).astype(BF)
        qp[rows, 256:384] = scaled[:, 128:].astype(BF)
    chain = KeyChain(run, trunk, mine, *chain_refs, place_in)
    chain.start()
    m_tasks = [Spread(run, in_c, win), Spread(run, out_c, wout)]
    run.save(xb, xb_o)
    run.save(qp, qp_o)
    chain.finish()
    for t in m_tasks:
        t.start()
    pick_parents(kp, chain.slots, choose)
    run.save(kp, kp_o)
    run.save(trunk, trunk_o)
    run.save(mine, mine_o)
    if first:
        a_tasks[1].relay()
        n_tasks = [Spread(run, qkv_next, wqkv_n), SpreadOutput(run, o_next, wo_n)]
        for t in n_tasks:
            t.start()

    def attend(i, carry):
        h, b = i // 4, lax.rem(i, 4)
        lanes = pl.ds(pl.multiple_of(h * 128, 128), 128)
        rows = pl.ds(pl.multiple_of(b * ROWS, ROWS), ROWS)
        keys = all_keys(trunk, mine, kp, b, lanes)
        s = product_nt(qp[rows, lanes], keys)
        s = jnp.concatenate(
            [s[:, :1024], s[:, 1024:1280] + pen[4 + b], s[:, 1280:] + pen[b]], axis=1
        )
        e = jnp.exp(s - jnp.max(s, axis=1, keepdims=True))
        pb = (e / jnp.sum(e, axis=1, keepdims=True)).astype(BF)
        p[h, b] = pb
        heads[h, b] = product(pb, keys)
        return carry

    lax.fori_loop(0, 12, attend, 0)
    run.save(p, p_o)
    if first:
        a_tasks[1].finish()
    back = [None]
    for k in (1, 2, 3, 0):
        g = place.f_at(-k)
        ctx[g, :, 0:128] = jnp.where(lane < 64, pltpu.roll(heads[0, g], 64, 1), heads[1, g]).astype(BF)
        ctx[g, :, 128:256] = jnp.where(lane < 64, pltpu.roll(heads[2, g], 64, 1), 0.0).astype(BF)
        part = product(ctx[g], wo[...])
        if k:
            rs1_s[k - 1] = part.astype(BF)
            back.append(launch(rs1_s.at[k - 1], rs1_r.at[k - 1], place.plane(-k)))
        else:
            own[...] = part
    run.save(ctx, ctx_o)
    for t in m_tasks:
        t.relay()
    for k in (1, 2, 3):
        back[k].wait_recv()
    total = own[...] + rs1_r[0].astype(F32) + rs1_r[1].astype(F32) + rs1_r[2].astype(F32)
    zz = x_ref[...] + total + vec[1:2, :]
    z1[...] = zz
    run.save(z1, z1_o)
    hidden = norm_rows(zz, vec[2:3, :], vec[3:4, :])
    hb[f] = hidden.astype(BF)
    came = [None] + [launch(hb.at[f], hb.at[f], place.plane(k)) for k in (1, 2, 3)]
    back = [None]
    for t in m_tasks:
        t.finish()
    for k in range(4):
        g = place.f_at(-k)
        if k:
            came[k].wait_recv()
        u = product(hb[g], flat(win)) + vec[4:5, :]
        cdf = 0.5 * (1.0 + lax.erf(u * (0.5 ** 0.5)))
        gp[g] = cdf + u * jnp.exp(-0.5 * u * u) * 0.3989422804014327
        low = (u * cdf).astype(BF)
        gl[g] = low
        part = product(low, flat(wout))
        if k:
            rs2_s[k - 1] = part.astype(BF)
            back.append(launch(rs2_s.at[k - 1], rs2_r.at[k - 1], place.plane(-k)))
        else:
            own[...] = part
    run.save(hb, hb_o)
    run.save(gp, gp_o)
    run.save(gl, gl_o)
    run.save(win, win_o)
    run.save(wout, wout_o)
    if first:
        run.save(wqkv, wqkv_o)
        run.save(wo.at[pl.ds(0, 192)], wo_o)
        for t in n_tasks:
            t.relay()
    for k in (1, 2, 3):
        back[k].wait_recv()
    total = own[...] + rs2_r[0].astype(F32) + rs2_r[1].astype(F32) + rs2_r[2].astype(F32)
    zz = norm_rows(z1[...], vec[2:3, :], vec[3:4, :]) + total + vec[5:6, :]
    z2[...] = zz
    run.save(z2, z2_o)
    xn_ref[...] = norm_rows(zz, vec[6:7, :], vec[7:8, :])
    if first:
        for t in n_tasks:
            t.finish()
    run.close()


def backward_kernel(extra, *refs):
    refs = list(refs)

    def take(n):
        out = refs[:n]
        del refs[:n]
        return out

    dy_ref, win, wout, vec, place_in, choose, z1, hb, gp, gl, z2 = take(11)
    late_in = take(9)
    if extra:
        pq_in, pk_in, dvec_in = take(3)
    dx_ref, din_o, dout_o, do_o = take(4)
    if extra:
        dq_n, dk_n, dq_o, dk_o, sm_o = take(5)
    else:
        pq, pk, dvec_o = take(3)
    late = take(9)
    wqkv, wo, xb, qp, trunk, mine, kp, p, ctx = late
    (
        df, du, da, dctx, dqf, dqkv, dz, dz1, dkt, dself, dpar, tgt, own, rs1_s, rs1_r, rs2_s, rs2_r,
    ) = take(17)
    chain_refs = take(7)
    pin, nin, fin, tin, pout, nout, fout, po, no, fo, to = take(11)
    if extra:
        pq, pk, dvec_o = take(3)
        nq, fq, tq, nk, fk, tk, nq2, fq2, tq2, nk2, fk2, tk2, sm, sm_a, sm_b, sm_v = take(16)
    run = Run(*refs)
    place = run.place
    z, f, c = place.z, place.f, place.c
    launch = run.launch
    loads = []
    for n, (src, dst) in enumerate(zip(late_in, late)):
        loads.append(run.local(src, dst.at[pl.ds(0, 192)] if n == 1 else dst))
    wo[192:256, :] = jnp.zeros((64, WIDE), BF)

    grad, dgain, dshift = norm_rows_back(z2[...], vec[6:7, :], dy_ref[...])
    dvec_o[6:7, :] = dgain
    dvec_o[7:8, :] = dshift
    dz[...] = grad
    low = grad.astype(BF)
    df[f] = low
    dvec_o[5:6, :] = jnp.sum(low.astype(F32), axis=0, keepdims=True)
    run.greet(True)
    came = [None] + [launch(df.at[f], df.at[f], place.plane(k)) for k in (1, 2, 3)]
    a_tasks = []
    if extra:
        a_tasks = [Collect(run, pq_in, nq, fq, tq, dq_n), Collect(run, pk_in, nk, fk, tk, dk_n)]
    for t in a_tasks:
        t.start()
    back = [None]
    bias = jnp.zeros((1, WIDE), F32)
    for k in range(4):
        g = place.f_at(-k)
        if k:
            came[k].wait_recv()
        low = (product_nt(df[g], flat(wout)) * gp[g]).astype(BF)
        du[g] = low
        bias = bias + jnp.sum(low.astype(F32), axis=0, keepdims=True)
        part = product_nt(low, flat(win))
        if k:
            rs1_s[k - 1] = part.astype(BF)
            back.append(launch(rs1_s.at[k - 1], rs1_r.at[k - 1], place.plane(-k)))
        else:
            own[...] = part
            for t in a_tasks:
                t.middle()
    dvec_o[4:5, :] = bias
    m_tasks = [Collect(run, pin, nin, fin, tin, din_o), Collect(run, pout, nout, fout, None, dout_o)]
    o_task = CollectOutput(run, po, no, fo, to, do_o)

    def split_rows(dst, left, right, i):
        lanes = pl.ds(pl.multiple_of(i * 384, 128), 384)
        value = product_tn(left[:, :, lanes].reshape(512, 384), right).astype(BF)
        for zz in range(2):
            for cc in range(2):
                at = (2 * zz + cc) * 96
                dst[cc, 2 * i + zz] = value[at : at + 96, :]

    def ffn_grads(i, carry):
        split_rows(pout, gl, flat(df), i)
        split_rows(pin, hb, flat(du), i)
        return carry

    lax.fori_loop(0, 2, ffn_grads, 0)
    for t in m_tasks:
        t.start()
    for k in (1, 2, 3):
        back[k].wait_recv()
    up = dz[...] + own[...] + rs1_r[0].astype(F32) + rs1_r[1].astype(F32) + rs1_r[2].astype(F32)
    grad, dgain, dshift = norm_rows_back(z1[...], vec[2:3, :], up)
    dvec_o[2:3, :] = dgain
    dvec_o[3:4, :] = dshift
    dz1[...] = grad
    low = grad.astype(BF)
    da[f] = low
    dvec_o[1:2, :] = jnp.sum(low.astype(F32), axis=0, keepdims=True)
    came = [None] + [launch(da.at[f], da.at[f], place.plane(k)) for k in (1, 2, 3)]
    for t in a_tasks:
        t.end()
    for t in m_tasks:
        t.middle()
    dkt[...] = jnp.zeros_like(dkt)
    lane = lax.broadcasted_iota(jnp.int32, (ROWS, 128), 1)
    for a in loads:
        a.wait()
    for k in range(4):
        g = place.f_at(-k)
        rows = pl.ds(pl.multiple_of(g * ROWS, ROWS), ROWS)
        if k:
            came[k].wait_recv()
        packed = product_nt(da[g], wo[...])
        ahead, after = packed[:, :128], packed[:, 128:]
        dctx[rows, 0:128] = jnp.where(lane < 64, 0.0, pltpu.roll(ahead, 64, 1)).astype(BF)
        dctx[rows, 128:256] = jnp.where(lane < 64, 0.0, ahead).astype(BF)
        dctx[rows, 256:384] = jnp.where(lane < 64, 0.0, pltpu.roll(after, 64, 1)).astype(BF)
    value = product_tn(flat(ctx), flat(da)).astype(BF)
    for cc in range(2):
        po[cc] = value[96 * cc : 96 * (cc + 1), :]
    o_task.start()

    def attend(i, carry):
        h, b = i // 4, lax.rem(i, 4)
        lanes = pl.ds(pl.multiple_of(h * 128, 128), 128)
        rows = pl.ds(pl.multiple_of(b * ROWS, ROWS), ROWS)
        keys = all_keys(trunk, mine, kp, b, lanes)
        q, g = qp[rows, lanes], dctx[rows, lanes]
        low = p[h, b]
        pf = low.astype(F32)
        dp = product_nt(g, keys)
        t = pf * dp
        ds = (t - pf * jnp.sum(t, axis=1, keepdims=True)).astype(BF)
        dqf[h, rows, :] = product(ds, keys) * (HEAD_DIM ** (-0.5))
        dkv = product_tn(jnp.concatenate([ds, low], axis=0), jnp.concatenate([q, g], axis=0))
        dkt[:, lanes] += dkv[:1024]
        dself[b, :, lanes] = dkv[1024:1280]
        dpar[b, :, lanes] = dkv[1280:]
        return carry

    lax.fori_loop(0, 12, attend, 0)
    for cc in range(2):
        for j in range(4):
            at = cc * 512 + j * ROWS
            tgt[cc, 0, j] = dkt[at : at + ROWS, :].astype(BF)

    def scatter(j, carry):
        for cc in range(2):
            half = slice(cc * ROWS, (cc + 1) * ROWS)
            total = dpar[0, half, :] * choose[0, j]
            for b in range(1, 4):
                total = total + dpar[b, half, :] * choose[b, j]
            tgt[cc, 1, j] = total.astype(BF)
            tgt[cc, 2, j] = dself[j, half, :].astype(BF)
        return carry

    lax.fori_loop(0, 4, scatter, 0)
    chain = GradChain(run, tgt, *chain_refs)
    chain.start()
    for g in range(4):
        rows = slice(g * ROWS, (g + 1) * ROWS)
        ahead = jnp.where(lane < 64, dqf[0, rows, :], pltpu.roll(dqf[1, rows, :], 64, 1))
        dqkv[g, :, 0:128] = ahead.astype(BF)
        dqkv[g, :, 128:256] = jnp.where(lane < 64, dqf[2, rows, :], 0.0).astype(BF)
    chain.middle()
    o_task.middle()
    chain.pass_on()

    def q_grads(i, carry):
        split_rows(pq, xb, dqkv[:, :, :256].reshape(512, 256), i)
        return carry

    lax.fori_loop(0, 2, q_grads, 0)

    def store(ft, value):
        dqkv[ft, :, 256:] = value.astype(BF)

    chain.finish(place_in, store)
    back = [None]
    for k in (1, 2, 3, 0):
        g = place.f_at(-k)
        part = product_nt(dqkv[g], flat(wqkv))
        if k:
            rs2_s[k - 1] = part.astype(BF)
            back.append(launch(rs2_s.at[k - 1], rs2_r.at[k - 1], place.plane(-k)))
        else:
            own[...] = part

    def k_grads(i, carry):
        split_rows(pk, xb, dqkv[:, :, 256:].reshape(512, SLICE), i)
        return carry

    lax.fori_loop(0, 2, k_grads, 0)
    sums = jnp.sum(flat(dqkv).astype(F32), axis=0, keepdims=True)
    dvec_o[0:1, :] = jnp.concatenate([sums, jnp.zeros((1, WIDE - PACKED), F32)], axis=1)
    end_tasks = []
    if extra:
        end_tasks = [Collect(run, pk, nk2, fk2, tk2, dk_o), Collect(run, pq, nq2, fq2, tq2, dq_o)]
        for t in end_tasks:
            t.start()
        sm[0:8, :] = dvec_o[...]
        sm[8:16, :] = dvec_in[...]
        sm_near = launch(sm, sm_a, place.sibling())
        for t in end_tasks:
            t.middle()
        sm_near.wait_recv()
        sm_a[...] = sm[...] + sm_a[...]
        sm_far = [launch(sm_a, sm_b.at[k - 1], place.column(k)) for k in (1, 2, 3)]
    for t in m_tasks + [o_task]:
        t.end()
    for t in a_tasks:
        t.last()
    for k in (1, 2, 3):
        back[k].wait_recv()
    dx_ref[...] = dz1[...] + own[...] + rs2_r[0].astype(F32) + rs2_r[1].astype(F32) + rs2_r[2].astype(F32)
    if extra:
        for t in end_tasks:
            t.end()
        for a in sm_far:
            a.wait_recv()
        sm_v[...] = sm_a[...] + sm_b[0] + sm_b[1] + sm_b[2]
        sm_last = [launch(sm_v, sm_o.at[f], place.plane(k)) for k in (1, 2, 3)]
        sm_o[f] = sm_v[...]
        for a in sm_last:
            a.wait_recv()
    for t in m_tasks + [o_task] + end_tasks:
        t.last()
    run.close()


ANY = pl.BlockSpec(memory_space=pl.ANY)
VM = pl.BlockSpec(memory_space=pltpu.VMEM)
SM = pl.BlockSpec(memory_space=pltpu.SMEM)
LIMIT = 60 * 1024 * 1024
SEMS = (160, 160, 32)


def shape(*dims, dtype=BF):
    return jax.ShapeDtypeStruct(dims, dtype)


def call(kernel, number, outs, out_specs, in_specs, scratch, args, flops):
    return pl.pallas_call(
        kernel,
        out_shape=tuple(outs),
        in_specs=in_specs,
        out_specs=tuple(out_specs),
        scratch_shapes=[pltpu.VMEM(s.shape, s.dtype) for s in scratch]
        + [pltpu.SemaphoreType.DMA((n,)) for n in SEMS],
        compiler_params=pltpu.CompilerParams(
            collective_id=number, has_side_effects=True, vmem_limit_bytes=LIMIT
        ),
        cost_estimate=pl.CostEstimate(flops=flops, bytes_accessed=20000000, transcendentals=0),
    )(*args)


def column_parts(query, key, value, inner):
    n = query.shape[0] * query.shape[1]
    q = query.reshape(n, 4, 3, 64)
    q = jnp.pad(q, ((0, 0), (0, 0), (0, 1), (0, 0))).reshape(n, 4, 256)
    kv = jnp.stack([key.reshape(n, 4, 3, 64), value.reshape(n, 4, 3, 64)], axis=3).reshape(n, 4, 384)
    up = inner.reshape(n, 4, 4, 192).transpose(0, 2, 1, 3).reshape(n, 4, WIDE)
    return jnp.concatenate([q, kv, up], axis=2).transpose(1, 0, 2)


LOCAL = shape(ROWS, WIDE, dtype=F32)
FULL = shape(4, ROWS, WIDE)
PIECE = shape(3, ROWS, WIDE)
QKV = shape(4, 2, 96, PACKED)
BIG = shape(4, 2, 96, WIDE)
OUTPUT = shape(192, WIDE)
HALVES = shape(2, 4, ROWS, SLICE)
QUARTERS = shape(4, ROWS, SLICE)
SAVED = (
    FULL, shape(512, SLICE), HALVES, HALVES, shape(4, 2, ROWS, SLICE), shape(3, 4, ROWS, NKEYS),
    shape(4, ROWS, 256), LOCAL, FULL, shape(4, ROWS, WIDE, dtype=F32), FULL, LOCAL,
)


def forward_layer(first, state, qkv, o, in_c, out_c, vec, place_in, choose, pen, following):
    outs = (LOCAL,) + SAVED + (BIG, BIG) + ((QKV, OUTPUT, QKV, OUTPUT) if first else ())
    got = call(
        lambda *refs: forward_kernel(first, *refs), 1 if first else 2, outs, (VM,) + (ANY,) * (len(outs) - 1),
        [VM] + [ANY] * 4 + [VM] + [SM] * 3 + [ANY] * len(following),
        list(SAVED)
        + [BIG, BIG, QKV, shape(256, WIDE), shape(3, 4, ROWS, 128, dtype=F32), LOCAL]
        + [PIECE] * 4 + [HALVES] + [QUARTERS] * 5,
        (state, qkv, o, in_c, out_c, vec, place_in, choose, pen) + tuple(following), 3 * 10**9,
    )
    return got[0], got[1:13], got[13:]


def collect_scratch(columns, rows):
    return [shape(4, 96, columns), shape(3, 96, columns)] + ([shape(96, columns, dtype=F32)] if rows else [])


OUT_SCRATCH = [shape(96, WIDE), shape(4, 96, WIDE), shape(96, WIDE, dtype=F32)]
PARTS = (shape(2, 4, 96, 256), shape(2, 4, 96, SLICE))
SHARES = (shape(4, 24, 256, dtype=F32), shape(4, 24, SLICE, dtype=F32))


def backward_layer(upstream, weights, vec, place_in, choose, saved, before):
    wqkv, wo, win, wout = weights
    xb, qp, trunk, mine, kp, p, ctx, z1, hb, gp, gl, z2 = saved
    keys = shape(4, 256, SLICE, dtype=F32)
    extra = len(before) > 0
    sums, sums2 = shape(8, WIDE, dtype=F32), shape(16, WIDE, dtype=F32)
    outs = (LOCAL, shape(4, 24, WIDE, dtype=F32), shape(96, WIDE, dtype=F32), shape(24, WIDE, dtype=F32))
    outs += SHARES + SHARES + (shape(4, 16, WIDE, dtype=F32),) if extra else PARTS + (sums,)
    scratch = [QKV, shape(256, WIDE)] + list(SAVED[:7]) + [
        FULL, FULL, FULL, shape(512, SLICE), shape(3, 512, 128, dtype=F32), shape(4, ROWS, PACKED), LOCAL, LOCAL,
        shape(1024, SLICE, dtype=F32), keys, keys, shape(2, 3, 4, ROWS, SLICE), LOCAL, PIECE, PIECE, PIECE, PIECE,
        shape(3, 4, ROWS, SLICE),
    ] + [QUARTERS] * 6
    part = shape(2, 4, 96, WIDE)
    scratch += [part] + collect_scratch(WIDE, True) + [part] + collect_scratch(WIDE, False)
    scratch += [shape(2, 96, WIDE)] + OUT_SCRATCH
    if extra:
        scratch += list(PARTS) + [sums]
        scratch += (collect_scratch(256, True) + collect_scratch(SLICE, True)) * 1
        scratch += collect_scratch(256, True) + collect_scratch(SLICE, True)
        scratch += [sums2, sums2, shape(3, 16, WIDE, dtype=F32), sums2]
    return call(
        lambda *refs: backward_kernel(extra, *refs), 4 if extra else 3, outs, (VM,) * len(outs),
        [VM] * 4 + [SM] * 2 + [VM] * 5 + [ANY] * 9 + [VM] * len(before), scratch,
        (upstream, win, wout, vec, place_in, choose, z1, hb, gp, gl, z2, wqkv, wo, xb, qp, trunk, mine, kp, p, ctx)
        + tuple(before),
        6 * 10**9,
    )


def slice_body(
    activations, query_weight, query_bias, key_weight, value_weight, value_bias, output_weight, output_bias,
    first_gain, first_shift, inner_weight, inner_bias, outer_weight, outer_bias, second_gain, second_shift,
    cotangent, parents, segments,
):
    place = Place()
    z, f, c = place.z, place.f, place.c
    col = column_parts(query_weight, key_weight, value_weight, inner_weight)
    vectors = (query_bias, value_bias, output_bias, first_gain, first_shift, outer_bias, second_gain, second_shift)
    label = jnp.broadcast_to(segments[:1].astype(BF)[None], (2, 1))
    small = jnp.concatenate(vectors + (inner_bias, label), axis=1)
    small = jnp.pad(small, ((0, 14), (0, 384 - small.shape[1])))
    colp, op, smallg = call(
        exchange_kernel, 0, (shape(4, 48, 1408), shape(4, 48, WIDE), shape(4, 2, 4, 16, 384)), (ANY,) * 3, [ANY] * 3,
        [], (col, output_weight.reshape(48, WIDE), small), 1000,
    )
    colp = colp.reshape(4, 2, 24, 1408).transpose(1, 0, 2, 3).reshape(2, 96, 1408)
    op = op.reshape(4, 2, 24, WIDE).transpose(1, 0, 2, 3).reshape(2, 96, WIDE)
    small = smallg[:, :, :, :2].transpose(3, 0, 2, 1, 4).astype(F32)
    parts = [small[..., i * 24 : (i + 1) * 24].reshape(2, WIDE) for i in range(8)]
    q_all, v_all, o_all, g1, s1, out_all, g2, s2 = parts
    in_mine = lax.dynamic_index_in_dim(small[..., 192:288], f, 2, keepdims=False).reshape(2, WIDE)
    q_mine = lax.dynamic_slice_in_dim(q_all, 192 * f, 192, 1)
    v_mine = lax.dynamic_slice_in_dim(v_all, 192 * f, 192, 1).reshape(2, 3, 64)
    kv_mine = jnp.pad(v_mine, ((0, 0), (0, 0), (64, 0))).reshape(2, SLICE)
    qkv_mine = jnp.pad(jnp.concatenate([q_mine, jnp.zeros((2, 64), F32), kv_mine], axis=1), ((0, 0), (0, WIDE - PACKED)))
    vecs = jnp.stack([qkv_mine, o_all, g1, s1, in_mine, out_all, g2, s2], axis=1)

    labels = small[0, :, :, 0, 288].reshape(16).astype(jnp.int32)
    above = lookup_rows(labels, parents)
    order = jnp.arange(16, dtype=jnp.int32)
    branch = jnp.logical_and(above == labels[0], order >= 4)
    slot = jnp.where(branch, jnp.sum((branch[:, None] & (order[:, None] < order[None, :])).astype(jnp.int32), axis=0), 4)
    in_slot = slot[None, :] == jnp.arange(4, dtype=jnp.int32)[:, None]
    place_in = lax.dynamic_slice_in_dim(in_slot.astype(F32), 4 * z, 4, 1)
    parent = lax.dynamic_slice_in_dim(above, 4 * z, 4, 0)
    match = parent[:, None, None] == jnp.where(in_slot, labels[None, :], -1)[None]
    choose = jnp.any(match, axis=2).astype(F32)
    pen = jnp.concatenate(
        [jnp.where(jnp.any(match, axis=(1, 2)), 0.0, MASKED), jnp.where(z > 0, jnp.zeros((4,), F32), MASKED)]
    ).astype(F32)

    qkv_c = [colp[i, :, :PACKED] for i in range(2)]
    in_c = [colp[i, :, PACKED:] for i in range(2)]
    state, kept0, (win0, wout0, wqkv0, wo0, wqkv1, wo1) = forward_layer(
        True, activations.astype(F32), qkv_c[0], op[0], in_c[0], outer_weight[0], vecs[0], place_in, choose, pen,
        (qkv_c[1], op[1]),
    )
    state, kept1, (win1, wout1) = forward_layer(
        False, state, wqkv1, wo1, in_c[1], outer_weight[1], vecs[1], place_in, choose, pen, ()
    )
    outcome = state.astype(BF)
    upstream, din1, dout1, do1, pq, pk, dvec1 = backward_layer(
        cotangent.astype(F32), (wqkv1, wo1, win1, wout1), vecs[1], place_in, choose, kept1, ()
    )
    upstream, din0, dout0, do0, dq1, dk1, dq0, dk0, rsm = backward_layer(
        upstream, (wqkv0, wo0, win0, wout0), vecs[0], place_in, choose, kept0, (pq, pk, dvec1)
    )
    dq = jnp.stack([dq0, dq1]).transpose(0, 2, 1, 3)[..., :192].reshape(2, 24, WIDE)
    dkv = jnp.stack([dk0, dk1]).transpose(0, 2, 1, 3).reshape(2, 24, 4, 3, 2, 64)
    dk = dkv[..., 0, :].reshape(2, 24, WIDE)
    dv = dkv[..., 1, :].reshape(2, 24, WIDE)
    dinner = jnp.stack([din0, din1]).reshape(2, 4, 24, 4, 192).transpose(0, 2, 3, 1, 4).reshape(2, 24, 3072)
    rsm = rsm.reshape(4, 2, 8, WIDE)
    sums = jnp.sum(rsm, axis=0)
    dqb = rsm[:, :, 0, :192].transpose(1, 0, 2).reshape(2, WIDE)
    dvb = rsm[:, :, 0, 256:640].reshape(4, 2, 3, 2, 64)[:, :, :, 1].transpose(1, 0, 2, 3).reshape(2, WIDE)
    rows = jnp.stack([dqb, dvb, sums[:, 1], sums[:, 2], sums[:, 3], sums[:, 5], sums[:, 6], sums[:, 7]])
    rows = lax.dynamic_slice_in_dim(rows, 24 * (8 * z + 2 * f + c), 24, 2)
    dib = lax.dynamic_index_in_dim(rsm[:, :, 4], f, 0, keepdims=False)
    dib = lax.dynamic_slice_in_dim(dib, 96 * (2 * z + c), 96, 1)
    return (
        outcome, upstream.astype(BF), dq, rows[0], dk, dv, rows[1], jnp.stack([do0, do1]), rows[2], rows[3], rows[4],
        dinner, dib, jnp.stack([dout0, dout1]), rows[5], rows[6], rows[7],
    )


def solution(mesh):
    placed = (
        P("fsdp", None),
        P(None, "fsdp", None),
        P(None, "fsdp"),
        P(None, "fsdp", None),
        P(None, "fsdp", None),
        P(None, "fsdp"),
        P(None, "fsdp", None),
        P(None, "fsdp"),
        P(None, "fsdp"),
        P(None, "fsdp"),
        P(None, "fsdp", None),
        P(None, "fsdp"),
        P(None, "fsdp", None),
        P(None, "fsdp"),
        P(None, "fsdp"),
        P(None, "fsdp"),
        P("fsdp", None),
        P(),
        P("fsdp"),
    )
    return jax.shard_map(
        slice_body if mesh.shape["fsdp"] == 32 else body,
        mesh=mesh,
        in_specs=placed,
        out_specs=(
            P("fsdp", None),
            P("fsdp", None),
            P(None, "fsdp", None),
            P(None, "fsdp"),
            P(None, "fsdp", None),
            P(None, "fsdp", None),
            P(None, "fsdp"),
            P(None, "fsdp", None),
            P(None, "fsdp"),
            P(None, "fsdp"),
            P(None, "fsdp"),
            P(None, "fsdp", None),
            P(None, "fsdp"),
            P(None, "fsdp", None),
            P(None, "fsdp"),
            P(None, "fsdp"),
            P(None, "fsdp"),
        ),
        check_vma=False,
    )
```

```python
import jax
import jax.numpy as jnp
from jax import lax
from jax.experimental import pallas as pl
from jax.experimental.pallas import tpu as pltpu
from jax.sharding import PartitionSpec as P

HEADS = 12
HEAD_DIM = 64
LAYERS = 2
TREE_LEN = 4096


EPSILON = 1e-06
MASKED = -1000000000.0


def partner_2(shard, axis, stride):
    return lax.ppermute(shard, axis, [(i, i ^ 1 << stride) for i in range(lax.axis_size(axis))])


def as_sent(shard):
    return jax.tree.map(lambda a: a.astype(jnp.bfloat16) if a.dtype == jnp.float32 else a, shard)


def product(a, b):
    return jnp.dot(a, b, preferred_element_type=jnp.float32)


def product_tn(a, b):
    return lax.dot_general(a, b, (((0,), (0,)), ((), ())), preferred_element_type=jnp.float32)


def product_nt(a, b):
    return lax.dot_general(a, b, (((1,), (1,)), ((), ())), preferred_element_type=jnp.float32)


def exact_gelu(u):
    return jax.nn.gelu(u, approximate=False)


def layer_norm(z, gain_vec, shift_vec):
    centre = z - jnp.mean(z, axis=-1, keepdims=True)
    scaled = centre * lax.rsqrt(jnp.mean(centre * centre, axis=-1, keepdims=True) + EPSILON)
    return scaled * gain_vec.astype(jnp.float32) + shift_vec.astype(jnp.float32)


def norm_backward(z, gain_vec, upstream):
    centre = z - jnp.mean(z, axis=-1, keepdims=True)
    invert = lax.rsqrt(jnp.mean(centre * centre, axis=-1, keepdims=True) + EPSILON)
    scaled = centre * invert
    weighted = upstream * gain_vec.astype(jnp.float32)
    inner = invert * (
        weighted
        - jnp.mean(weighted, axis=-1, keepdims=True)
        - scaled * jnp.mean(weighted * scaled, axis=-1, keepdims=True)
    )
    return (inner, jnp.sum(upstream * scaled, axis=0), jnp.sum(upstream, axis=0))


def lookup_rows(ids, parents):
    table = jnp.arange(parents.shape[0], dtype=jnp.int32)
    return jnp.sum(jnp.where(ids[:, None] == table[None, :], parents[None, :], 0), axis=1)


def join_heads(stacked):
    return stacked.transpose(1, 0, 2).reshape(stacked.shape[1], -1)


def gather_group(key_rows, value_rows, labels, position, bit_count):
    for b in range(bit_count):
        partner = partner_2((key_rows, value_rows, labels), "fsdp", b)
        upper_side = position >> b & 1 == 1
        key_rows = jnp.where(
            upper_side,
            jnp.concatenate([partner[0], key_rows]),
            jnp.concatenate([key_rows, partner[0]]),
        )
        value_rows = jnp.where(
            upper_side,
            jnp.concatenate([partner[1], value_rows]),
            jnp.concatenate([value_rows, partner[1]]),
        )
        labels = jnp.where(
            upper_side, jnp.concatenate([partner[2], labels]), jnp.concatenate([labels, partner[2]])
        )
    return (key_rows, value_rows, labels)


def sum_group(key_grad, value_grad, position, bit_count):
    for b in reversed(range(bit_count)):
        halfway = key_grad.shape[0] // 2
        upper_side = position >> b & 1 == 1
        outgoing = (
            jnp.where(upper_side, key_grad[:halfway], key_grad[halfway:]),
            jnp.where(upper_side, value_grad[:halfway], value_grad[halfway:]),
        )
        partner = partner_2((as_sent(outgoing[0]), as_sent(outgoing[1])), "fsdp", b)
        key_grad = jnp.where(upper_side, key_grad[halfway:], key_grad[:halfway]) + partner[0]
        value_grad = jnp.where(upper_side, value_grad[halfway:], value_grad[:halfway]) + partner[1]
    return (key_grad, value_grad)


def attend_forward(queries, key_rows, value_rows, allowed):
    factor = HEAD_DIM ** (-0.5)

    def one_head(j):
        start = j * HEAD_DIM
        q = lax.dynamic_slice_in_dim(queries, start, HEAD_DIM, 1)
        k = lax.dynamic_slice_in_dim(key_rows, start, HEAD_DIM, 1)
        v = lax.dynamic_slice_in_dim(value_rows, start, HEAD_DIM, 1)
        s = jnp.where(allowed, product_nt(q, k) * factor, MASKED)
        maxima = jnp.max(s, axis=1, keepdims=True)
        e = jnp.exp(s - maxima)
        totals = jnp.sum(e, axis=1, keepdims=True)
        p = (e / totals).astype(jnp.bfloat16)
        return (product(p, v), (maxima + jnp.log(totals))[:, 0])

    stacked, log_total = lax.map(one_head, jnp.arange(HEADS))
    return (join_heads(stacked), log_total)


def attend_backward(queries, key_rows, value_rows, allowed, log_total, grad_context):
    factor = HEAD_DIM ** (-0.5)

    def one_head(j):
        start = j * HEAD_DIM
        q = lax.dynamic_slice_in_dim(queries, start, HEAD_DIM, 1)
        k = lax.dynamic_slice_in_dim(key_rows, start, HEAD_DIM, 1)
        v = lax.dynamic_slice_in_dim(value_rows, start, HEAD_DIM, 1)
        g = lax.dynamic_slice_in_dim(grad_context, start, HEAD_DIM, 1)
        s = jnp.where(allowed, product_nt(q, k) * factor, MASKED)
        p = jnp.where(allowed, jnp.exp(s - log_total[j][:, None]), 0.0)
        grad_p = product_nt(g, v)
        grad_v = product_tn(p.astype(jnp.bfloat16), g)
        grad_s = (p * (grad_p - jnp.sum(p * grad_p, axis=1, keepdims=True))).astype(jnp.bfloat16)
        grad_q = product(grad_s, k) * factor
        grad_k = product_tn(grad_s, q) * factor
        return (grad_q, grad_k, grad_v)

    grad_q, grad_k, grad_v = lax.map(one_head, jnp.arange(HEADS))
    return (join_heads(grad_q), join_heads(grad_k), join_heads(grad_v))


def layer_forward(state, full, segments, parent_one, parent_two, position, bit_count):
    (
        q_weight,
        q_bias,
        k_weight,
        v_weight,
        v_bias,
        o_weight,
        o_bias,
        gain_one,
        shift_one,
        up_weight,
        up_bias,
        down_weight,
        down_bias,
        gain_two,
        shift_two,
    ) = full
    inputs = state.astype(jnp.bfloat16)
    queries = (product(inputs, q_weight) + q_bias).astype(jnp.bfloat16)
    key_local = product(inputs, k_weight).astype(jnp.bfloat16)
    value_local = (product(inputs, v_weight) + v_bias).astype(jnp.bfloat16)
    key_rows, value_rows, labels = gather_group(
        key_local, value_local, segments, position, bit_count
    )
    allowed = (
        (labels[None, :] == segments[:, None])
        | (labels[None, :] == parent_one[:, None])
        | (labels[None, :] == parent_two[:, None])
    )
    context_wide, log_total = attend_forward(queries, key_rows, value_rows, allowed)
    context = context_wide.astype(jnp.bfloat16)
    first_sum = state + product(context, o_weight) + o_bias
    hidden = layer_norm(first_sum, gain_one, shift_one)
    hidden_low = hidden.astype(jnp.bfloat16)
    pre_act = product(hidden_low, up_weight) + up_bias
    gelu_out = exact_gelu(pre_act).astype(jnp.bfloat16)
    second_sum = hidden + product(gelu_out, down_weight) + down_bias
    record = (
        inputs,
        queries,
        key_rows,
        value_rows,
        allowed,
        log_total,
        context,
        first_sum,
        hidden_low,
        pre_act,
        gelu_out,
        second_sum,
    )
    return (record, layer_norm(second_sum, gain_two, shift_two))


def layer_backward(upstream, full, record, position, bit_count):
    (
        q_weight,
        q_bias,
        k_weight,
        v_weight,
        v_bias,
        o_weight,
        o_bias,
        gain_one,
        shift_one,
        up_weight,
        up_bias,
        down_weight,
        down_bias,
        gain_two,
        shift_two,
    ) = full
    (
        inputs,
        queries,
        key_rows,
        value_rows,
        allowed,
        log_total,
        context,
        first_sum,
        hidden_low,
        pre_act,
        gelu_out,
        second_sum,
    ) = record
    grad_z2, grad_gain_two, grad_shift_two = norm_backward(second_sum, gain_two, upstream)
    grad_f = grad_z2.astype(jnp.bfloat16)
    grad_down_bias = jnp.sum(grad_f.astype(jnp.float32), axis=0)
    grad_down = product_tn(gelu_out, grad_f)
    grad_gelu = product_nt(grad_f, down_weight)
    unused_value, gelu_back = jax.vjp(exact_gelu, pre_act)
    grad_u = gelu_back(grad_gelu)[0].astype(jnp.bfloat16)
    grad_up_bias = jnp.sum(grad_u.astype(jnp.float32), axis=0)
    grad_up = product_tn(hidden_low, grad_u)
    grad_h = grad_z2 + product_nt(grad_u, up_weight)
    grad_z1, grad_gain_one, grad_shift_one = norm_backward(first_sum, gain_one, grad_h)
    grad_a = grad_z1.astype(jnp.bfloat16)
    grad_o_bias = jnp.sum(grad_a.astype(jnp.float32), axis=0)
    grad_o = product_tn(context, grad_a)
    grad_context = product_nt(grad_a, o_weight).astype(jnp.bfloat16)
    grad_q, key_grad, value_grad = attend_backward(
        queries, key_rows, value_rows, allowed, log_total, grad_context
    )
    key_grad, value_grad = sum_group(key_grad, value_grad, position, bit_count)
    q_low = grad_q.astype(jnp.bfloat16)
    k_low = key_grad.astype(jnp.bfloat16)
    v_low = value_grad.astype(jnp.bfloat16)
    grad_x = (
        grad_z1
        + product_nt(q_low, q_weight)
        + product_nt(k_low, k_weight)
        + product_nt(v_low, v_weight)
    )
    terms = (
        product_tn(inputs, q_low),
        jnp.sum(q_low.astype(jnp.float32), axis=0),
        product_tn(inputs, k_low),
        product_tn(inputs, v_low),
        jnp.sum(v_low.astype(jnp.float32), axis=0),
        grad_o,
        grad_o_bias,
        grad_gain_one,
        grad_shift_one,
        grad_up,
        grad_up_bias,
        grad_down,
        grad_down_bias,
        grad_gain_two,
        grad_shift_two,
    )
    return (grad_x, terms)


def stack_layers(groups, n):
    return jnp.stack([g[n] for g in groups])


def body(
    activations,
    query_weight,
    query_bias,
    key_weight,
    value_weight,
    value_bias,
    output_weight,
    output_bias,
    first_gain,
    first_shift,
    inner_weight,
    inner_bias,
    outer_weight,
    outer_bias,
    second_gain,
    second_shift,
    cotangent,
    parents,
    segments,
):
    position = lax.axis_index("fsdp")
    bit_count = (TREE_LEN // activations.shape[0]).bit_length() - 1
    parent_one = lookup_rows(segments, parents)
    parent_two = lookup_rows(parent_one, parents)
    state = activations.astype(jnp.float32)
    saved = []
    kept_weights = []
    for i in range(LAYERS):
        full = (
            lax.all_gather(query_weight[i], "fsdp", axis=0, tiled=True),
            lax.all_gather(query_bias[i], "fsdp", axis=0, tiled=True),
            lax.all_gather(key_weight[i], "fsdp", axis=0, tiled=True),
            lax.all_gather(value_weight[i], "fsdp", axis=0, tiled=True),
            lax.all_gather(value_bias[i], "fsdp", axis=0, tiled=True),
            lax.all_gather(output_weight[i], "fsdp", axis=0, tiled=True),
            lax.all_gather(output_bias[i], "fsdp", axis=0, tiled=True),
            lax.all_gather(first_gain[i], "fsdp", axis=0, tiled=True),
            lax.all_gather(first_shift[i], "fsdp", axis=0, tiled=True),
            lax.all_gather(inner_weight[i], "fsdp", axis=0, tiled=True),
            lax.all_gather(inner_bias[i], "fsdp", axis=0, tiled=True),
            lax.all_gather(outer_weight[i], "fsdp", axis=0, tiled=True),
            lax.all_gather(outer_bias[i], "fsdp", axis=0, tiled=True),
            lax.all_gather(second_gain[i], "fsdp", axis=0, tiled=True),
            lax.all_gather(second_shift[i], "fsdp", axis=0, tiled=True),
        )
        kept_weights.append(full)
        record, state = layer_forward(
            state, full, segments, parent_one, parent_two, position, bit_count
        )
        saved.append(record)
    outcome = state.astype(jnp.bfloat16)
    upstream = cotangent.astype(jnp.float32)
    layer_grads = [None] * LAYERS
    for i in reversed(range(LAYERS)):
        full = (
            lax.all_gather(query_weight[i], "fsdp", axis=0, tiled=True),
            lax.all_gather(query_bias[i], "fsdp", axis=0, tiled=True),
            lax.all_gather(key_weight[i], "fsdp", axis=0, tiled=True),
            lax.all_gather(value_weight[i], "fsdp", axis=0, tiled=True),
            lax.all_gather(value_bias[i], "fsdp", axis=0, tiled=True),
            lax.all_gather(output_weight[i], "fsdp", axis=0, tiled=True),
            lax.all_gather(output_bias[i], "fsdp", axis=0, tiled=True),
            lax.all_gather(first_gain[i], "fsdp", axis=0, tiled=True),
            lax.all_gather(first_shift[i], "fsdp", axis=0, tiled=True),
            lax.all_gather(inner_weight[i], "fsdp", axis=0, tiled=True),
            lax.all_gather(inner_bias[i], "fsdp", axis=0, tiled=True),
            lax.all_gather(outer_weight[i], "fsdp", axis=0, tiled=True),
            lax.all_gather(outer_bias[i], "fsdp", axis=0, tiled=True),
            lax.all_gather(second_gain[i], "fsdp", axis=0, tiled=True),
            lax.all_gather(second_shift[i], "fsdp", axis=0, tiled=True),
        )
        upstream, terms = layer_backward(upstream, full, saved[i], position, bit_count)
        layer_grads[i] = (
            lax.psum_scatter(terms[0], "fsdp", scatter_dimension=0, tiled=True),
            lax.psum_scatter(terms[1], "fsdp", scatter_dimension=0, tiled=True),
            lax.psum_scatter(terms[2], "fsdp", scatter_dimension=0, tiled=True),
            lax.psum_scatter(terms[3], "fsdp", scatter_dimension=0, tiled=True),
            lax.psum_scatter(terms[4], "fsdp", scatter_dimension=0, tiled=True),
            lax.psum_scatter(terms[5], "fsdp", scatter_dimension=0, tiled=True),
            lax.psum_scatter(terms[6], "fsdp", scatter_dimension=0, tiled=True),
            lax.psum_scatter(terms[7], "fsdp", scatter_dimension=0, tiled=True),
            lax.psum_scatter(terms[8], "fsdp", scatter_dimension=0, tiled=True),
            lax.psum_scatter(terms[9], "fsdp", scatter_dimension=0, tiled=True),
            lax.psum_scatter(terms[10], "fsdp", scatter_dimension=0, tiled=True),
            lax.psum_scatter(terms[11], "fsdp", scatter_dimension=0, tiled=True),
            lax.psum_scatter(terms[12], "fsdp", scatter_dimension=0, tiled=True),
            lax.psum_scatter(terms[13], "fsdp", scatter_dimension=0, tiled=True),
            lax.psum_scatter(terms[14], "fsdp", scatter_dimension=0, tiled=True),
        )
    shares = tuple((stack_layers(layer_grads, n) for n in range(15)))
    return (outcome, upstream.astype(jnp.bfloat16)) + tuple(shares)


MESH = pl.DeviceIdType.MESH
BF = jnp.bfloat16
F32 = jnp.float32
WIDE = 768
SLICE = 384
PACKED = 640
ROWS = 128
NKEYS = 1536


class Pool:
    def __init__(self, ref):
        self.ref = ref
        self.used = 0

    def take(self):
        self.used += 1
        return self.ref.at[self.used - 1]

    def block(self, n):
        first = self.used
        self.used += n
        return lambda i: self.ref.at[first + i]


class Place:
    def __init__(self):
        me = lax.axis_index("fsdp")
        p = lax.rem(me, 32)
        self.base = me - p
        self.z = p // 8
        self.f = lax.rem(p // 2, 4)
        self.c = lax.rem(p, 2)

    def at(self, z, f, c):
        return self.base + 8 * z + 2 * f + c

    def f_at(self, k):
        return lax.rem(self.f + k + 4, 4)

    def z_at(self, k):
        return lax.rem(self.z + k + 4, 4)

    def plane(self, k):
        return self.at(self.z, self.f_at(k), self.c)

    def across(self, k):
        return self.at(self.z, self.f_at(k), 1 - self.c)

    def column(self, k):
        return self.at(self.z_at(k), self.f, self.c)

    def sibling(self):
        return self.at(self.z, self.f, 1 - self.c)


def remote(src, dst, sems, device):
    return pltpu.make_async_remote_copy(
        src_ref=src, dst_ref=dst, send_sem=sems[0], recv_sem=sems[1], device_id=(device,), device_id_type=MESH
    )


class Run:
    def __init__(self, send_sems, recv_sems, local_sems):
        self.place = Place()
        self.sends, self.recvs, self.locals = Pool(send_sems), Pool(recv_sems), Pool(local_sems)
        self.flying, self.saving = [], []

    def greet(self, wide):
        place = self.place
        there = [place.plane(k) for k in (1, 2, 3)] + [place.column(k) for k in (1, 2, 3)] + [place.sibling()]
        if wide:
            there += [place.across(k) for k in (1, 2, 3)]
        barrier = pltpu.get_barrier_semaphore()
        for dev in there:
            pl.semaphore_signal(barrier, inc=1, device_id=(dev,), device_id_type=MESH)
        pl.semaphore_wait(barrier, len(there))

    def launch(self, src, dst, device):
        a = remote(src, dst, (self.sends.take(), self.recvs.take()), device)
        a.start()
        self.flying.append((None, a))
        return a

    def launch_if(self, cond, src, dst, sems, device):
        a = remote(src, dst, sems, device)

        @pl.when(cond)
        def _():
            a.start()

        self.flying.append((cond, a))
        return a

    def local(self, src, dst):
        a = pltpu.make_async_copy(src, dst, self.locals.take())
        a.start()
        return a

    def save(self, src, dst):
        self.saving.append(self.local(src, dst))

    def close(self):
        for a in self.saving:
            a.wait()
        for cond, a in self.flying:
            if cond is None:
                a.wait_send()
            else:

                @pl.when(cond)
                def _(a=a):
                    a.wait_send()


class Spread:
    def __init__(self, run, chunk, full):
        self.run, self.chunk, self.full, self.pairs = run, chunk, full, None

    def start(self, cond=None):
        run, place = self.run, self.run.place
        mine = self.full.at[place.z, place.c]
        if self.pairs is None:
            self.own = pltpu.make_async_copy(self.chunk, mine, run.locals.take())
            self.pairs = [(run.sends.take(), run.recvs.take()) for _ in range(4)]
        cond = place.z >= 0 if cond is None else cond

        @pl.when(cond)
        def _():
            self.own.start()

        there = [place.column(k) for k in (1, 2, 3)] + [place.sibling()]
        copies = [run.launch_if(cond, self.chunk, mine, self.pairs[i], there[i]) for i in range(4)]
        self.far, self.near = copies[:3], copies[3:]

    def relay(self):
        run, place = self.run, self.run.place
        for k in (1, 2, 3):
            self.far[k - 1].wait_recv()
            there = self.full.at[place.z_at(-k), place.c]
            self.near.append(run.launch(there, there, place.sibling()))

    def finish(self):
        self.own.wait()
        for a in self.near:
            a.wait_recv()


class SpreadOutput:
    def __init__(self, run, chunk, full):
        self.run, self.chunk = run, chunk
        self.part = full.at[pl.ds(pl.multiple_of(run.place.c * 96, 96), 96)]

    def start(self):
        run, place = self.run, self.run.place
        self.copy = pltpu.make_async_copy(self.chunk, self.part, run.locals.take())

        @pl.when(place.f == place.z)
        def _():
            self.copy.start()

        arrive = run.recvs.take()
        for k in (1, 2, 3):
            self.far = run.launch_if(
                place.f == place.z, self.chunk, self.part, (run.sends.take(), arrive), place.column(k)
            )

    def relay(self):
        run, place = self.run, self.run.place

        @pl.when(place.f == place.z)
        def _():
            self.copy.wait()

        @pl.when(place.f != place.z)
        def _():
            self.far.wait_recv()

        self.near = run.launch(self.part, self.part, place.sibling())

    def finish(self):
        self.near.wait_recv()


class Collect:
    def __init__(self, run, part, near, far, total, out):
        self.run, self.part, self.near, self.far, self.total, self.out = run, part, near, far, total, out

    def start(self):
        place = self.run.place
        self.a = self.run.launch(self.part.at[1 - place.c], self.near, place.sibling())

    def middle(self):
        run, place = self.run, self.run.place
        self.a.wait_recv()

        def add(i, carry):
            self.near[i] = (self.part[place.c, i].astype(F32) + self.near[i].astype(F32)).astype(BF)
            return carry

        lax.fori_loop(0, 4, add, 0)
        self.moves = [
            run.launch(self.near.at[place.z_at(k)], self.far.at[k - 1], place.column(k)) for k in (1, 2, 3)
        ]

    def end(self):
        run, place = self.run, self.run.place
        for a in self.moves:
            a.wait_recv()
        result = self.near[place.z].astype(F32)
        for k in range(3):
            result = result + self.far[k].astype(F32)
        if self.total is None:
            self.out[...] = result
            return
        self.total[...] = result
        scatter_rows(self, self.total, self.out.at[place.f], None)

    def last(self):
        if self.total is None:
            return
        place = self.run.place
        for k in (1, 2, 3):
            g = place.f_at(k)
            remote(
                self.out.at[g], self.out.at[g], (self.send, self.arrive(g)), place.plane(k)
            ).wait_recv()

        @pl.when(place.c != place.f // 2)
        def _():
            remote(
                self.out.at[place.f], self.out.at[place.f], (self.send, self.arrive(place.f)), place.sibling()
            ).wait_recv()


def scatter_rows(task, total, landing, cond):
    run, place = task.run, task.run.place
    arrive = run.recvs.block(4)
    for j in range(4):
        there = place.at(place.z, 2 * place.c + j // 2, j % 2)
        here = jnp.logical_and(place.f == 2 * place.c + j // 2, place.c == j % 2)
        away = jnp.logical_not(here)
        if cond is not None:
            here, away = jnp.logical_and(here, cond), jnp.logical_and(away, cond)
        task.send = run.sends.take()
        slot = arrive(place.f) if cond is None else arrive(0)
        run.launch_if(away, total.at[pl.ds(24 * j, 24)], landing, (task.send, slot), there)

        @pl.when(here)
        def _(j=j):
            landing[...] = total[24 * j : 24 * (j + 1), :]

    task.arrive = arrive


class CollectOutput:
    def __init__(self, run, part, near, far, total, out):
        self.run, self.part, self.near, self.far, self.total, self.out = run, part, near, far, total, out

    def start(self):
        place = self.run.place
        self.a = self.run.launch(self.part.at[1 - place.c], self.near, place.sibling())

    def middle(self):
        run, place = self.run, self.run.place
        self.a.wait_recv()
        self.near[...] = (self.part[place.c].astype(F32) + self.near[...].astype(F32)).astype(BF)
        self.slot = run.recvs.block(4)
        self.one = run.sends.take()
        shift = lax.rem(place.f - place.z + 4, 4)
        run.launch_if(
            place.f != place.z, self.near, self.far.at[shift], (self.one, self.slot(shift)),
            place.at(place.f, place.f, place.c),
        )

    def end(self):
        place = self.run.place

        @pl.when(place.f == place.z)
        def _():
            result = self.near[...].astype(F32)
            for k in (1, 2, 3):
                remote(
                    self.near, self.far.at[k], (self.one, self.slot(k)), place.column(k)
                ).wait_recv()
                result = result + self.far[k].astype(F32)
            self.total[...] = result

        scatter_rows(self, self.total, self.out, place.f == place.z)

    def last(self):
        place = self.run.place
        mine = jnp.logical_and(place.f == place.z, place.c == place.f // 2)

        @pl.when(jnp.logical_not(mine))
        def _():
            remote(self.out, self.out, (self.send, self.arrive(0)), place.sibling()).wait_recv()


def norm_rows(z, gain, shift):
    centre = z - jnp.mean(z, axis=-1, keepdims=True)
    inv = lax.rsqrt(jnp.mean(centre * centre, axis=-1, keepdims=True) + EPSILON)
    return centre * inv * gain + shift


def norm_rows_back(z, gain, upstream):
    centre = z - jnp.mean(z, axis=-1, keepdims=True)
    inv = lax.rsqrt(jnp.mean(centre * centre, axis=-1, keepdims=True) + EPSILON)
    scaled = centre * inv
    weighted = upstream * gain
    inner = inv * (
        weighted
        - jnp.mean(weighted, axis=-1, keepdims=True)
        - scaled * jnp.mean(weighted * scaled, axis=-1, keepdims=True)
    )
    return inner, jnp.sum(upstream * scaled, axis=0, keepdims=True), jnp.sum(upstream, axis=0, keepdims=True)


def exchange_kernel(col, rows_o, small, colp, op, smallg, send_sems, recv_sems, local_sems):
    run = Run(send_sems, recv_sems, local_sems)
    place = run.place
    z, f, c = place.z, place.f, place.c
    mine = c == f // 2
    slot = 2 * lax.rem(f, 2) + c
    own = pltpu.make_async_copy(col.at[f], colp.at[slot], run.locals.take())
    own_o = pltpu.make_async_copy(rows_o, op.at[slot], run.locals.take())
    keep = jnp.logical_and(mine, f == z)

    @pl.when(mine)
    def _():
        own.start()

    @pl.when(keep)
    def _():
        own_o.start()

    own_small = run.local(small, smallg.at[z, c, f])
    run.greet(True)
    first = [run.launch(small, smallg.at[z, c, f], place.plane(k)) for k in (1, 2, 3)]
    arrive, arrive_o = run.recvs.block(4), run.recvs.block(4)
    for k in (1, 2, 3):
        run.launch_if(
            f >= 0, col.at[place.f_at(k)], colp.at[slot], (run.sends.take(), arrive(slot)),
            place.at(z, place.f_at(k), f // 2),
        )
    one = run.sends.take()
    run.launch_if(
        jnp.logical_not(mine), col.at[f], colp.at[slot], (one, arrive(slot)), place.sibling()
    )
    run.launch_if(
        jnp.logical_not(keep), rows_o, op.at[slot], (run.sends.take(), arrive_o(slot)), place.at(z, z, f // 2)
    )
    own_small.wait()
    for a in first:
        a.wait_recv()
    block = smallg.at[z, c]
    far = [run.launch(block, block, place.column(k)) for k in (1, 2, 3)]
    near = [run.launch(block, block, place.sibling())]
    for k in (1, 2, 3):
        far[k - 1].wait_recv()
        there = smallg.at[place.z_at(-k), c]
        near.append(run.launch(there, there, place.sibling()))

    for j in range(4):
        me = jnp.logical_and(f == 2 * c + j // 2, c == j % 2)
        other = jnp.logical_not(me)

        @pl.when(other)
        def _(j=j):
            remote(col.at[0], colp.at[j], (one, arrive(j)), place.sibling()).wait_recv()

        @pl.when(jnp.logical_and(other, f == z))
        def _(j=j):
            remote(rows_o, op.at[j], (one, arrive_o(j)), place.sibling()).wait_recv()

    for a in near:
        a.wait_recv()

    @pl.when(mine)
    def _():
        own.wait()

    @pl.when(keep)
    def _():
        own_o.wait()

    run.close()


class KeyChain:
    def __init__(self, run, trunk, mine, slots, up, down, cs, up_out, down_out, place_in):
        self.run, self.trunk, self.mine, self.slots = run, trunk, mine, slots
        self.up, self.down, self.cs, self.up_out, self.down_out, self.place_in = up, down, cs, up_out, down_out, place_in

    def start(self):
        run, place = self.run, self.run.place
        z, c = place.z, place.c
        self.pairs = [[(run.sends.take(), run.recvs.take()) for _ in range(4)] for _ in range(3)]
        for j in range(4):
            run.launch_if(z == 0, self.mine.at[c, j], self.trunk.at[c, j], self.pairs[0][j], place.column(1))
        self.near = [run.launch(self.mine.at[c], self.mine.at[c], place.sibling())]

        @pl.when(z == 0)
        def _():
            self.trunk[c] = self.mine[c]

        for j in range(4):
            total = self.mine[c, 0] * self.place_in[j, 0].astype(BF)
            for ft in range(1, 4):
                total = total + self.mine[c, ft] * self.place_in[j, ft].astype(BF)
            self.cs[j] = total
            run.launch_if(z == 1, self.cs.at[j], self.up.at[j], self.pairs[1][j], place.column(1))
            run.launch_if(z == 3, self.cs.at[j], self.down.at[j], self.pairs[2][j], place.column(-1))

    def wait(self, which, j):
        dst = (self.trunk.at[self.run.place.c, j], self.up.at[j], self.down.at[j])[which]
        remote(dst, dst, self.pairs[which][j], self.run.place.column(1)).wait_recv()

    def finish(self):
        run, place = self.run, self.run.place
        z, c = place.z, place.c
        trunk = [self.trunk.at[c, j] for j in range(4)]
        for j in range(4):

            @pl.when(z == 1)
            def _(j=j):
                self.wait(0, j)

            run.launch_if(z == 1, trunk[j], trunk[j], self.pairs[0][j], place.column(1))
        for j in range(4):

            @pl.when(z == 2)
            def _(j=j):
                self.wait(1, j)
                self.up_out[j] = self.cs[j] + self.up[j]

            run.launch_if(z == 2, self.up_out.at[j], self.up.at[j], self.pairs[1][j], place.column(1))

            @pl.when(z == 2)
            def _(j=j):
                self.wait(2, j)
                self.down_out[j] = self.cs[j] + self.down[j]

            run.launch_if(z == 2, self.down_out.at[j], self.down.at[j], self.pairs[2][j], place.column(-1))

            @pl.when(z == 2)
            def _(j=j):
                self.slots[c, j] = self.up_out[j] + self.down[j]

        for j in range(4):

            @pl.when(z == 2)
            def _(j=j):
                self.wait(0, j)

            run.launch_if(z == 2, trunk[j], trunk[j], self.pairs[0][j], place.column(1))
        for j in range(4):

            @pl.when(z == 0)
            def _(j=j):
                self.slots[c, j] = self.cs[j]

            @pl.when(z == 1)
            def _(j=j):
                self.wait(2, j)
                self.slots[c, j] = self.cs[j] + self.down[j]

            @pl.when(z == 3)
            def _(j=j):
                self.wait(1, j)
                self.slots[c, j] = self.cs[j] + self.up[j]

        self.near.append(run.launch(self.slots.at[c], self.slots.at[c], place.sibling()))

        @pl.when(z == 3)
        def _():
            for j in range(4):
                self.wait(0, j)

        self.near.append(run.launch(self.trunk.at[c], self.trunk.at[c], place.sibling()))
        for a in self.near:
            a.wait_recv()


class GradChain:
    def __init__(self, run, mine, near, trunk_in, up, down, up_out, down_out, total):
        self.run, self.mine, self.near, self.trunk_in = run, mine, near, trunk_in
        self.up, self.down, self.up_out, self.down_out, self.total = up, down, up_out, down_out, total

    def start(self):
        run, place = self.run, self.run.place
        self.pairs = [[(run.sends.take(), run.recvs.take()) for _ in range(4)] for _ in range(3)]
        self.a = run.launch(self.mine.at[1 - place.c], self.near, place.sibling())

    def wait(self, which, j):
        dst = (self.trunk_in, self.up, self.down)[which].at[j]
        remote(dst, dst, self.pairs[which][j], self.run.place.column(1)).wait_recv()

    def middle(self):
        run, place = self.run, self.run.place
        z, c = place.z, place.c
        self.a.wait_recv()
        near = self.near
        for kind in range(3):
            for j in range(4):
                near[kind, j] = (self.mine[c, kind, j].astype(F32) + near[kind, j].astype(F32)).astype(BF)
                if kind == 0:
                    run.launch_if(z == 3, near.at[0, j], self.trunk_in.at[j], self.pairs[0][j], place.column(-1))
                elif kind == 1:
                    run.launch_if(z == 1, near.at[1, j], self.up.at[j], self.pairs[1][j], place.column(1))
                    run.launch_if(z == 3, near.at[1, j], self.down.at[j], self.pairs[2][j], place.column(-1))

    def pass_on(self):
        run, place = self.run, self.run.place
        z = place.z
        near = self.near
        for j in range(4):
            cond = jnp.logical_or(z == 1, z == 2)

            @pl.when(cond)
            def _(j=j):
                self.wait(0, j)
                near[0, j] = (near[0, j].astype(F32) + self.trunk_in[j].astype(F32)).astype(BF)

            run.launch_if(cond, near.at[0, j], self.trunk_in.at[j], self.pairs[0][j], place.column(-1))

            @pl.when(z == 2)
            def _(j=j):
                self.wait(1, j)
                self.up_out[j] = (near[1, j].astype(F32) + self.up[j].astype(F32)).astype(BF)

            run.launch_if(z == 2, self.up_out.at[j], self.up.at[j], self.pairs[1][j], place.column(1))
        for j in range(4):

            @pl.when(z == 2)
            def _(j=j):
                self.wait(2, j)
                self.down_out[j] = (near[1, j].astype(F32) + self.down[j].astype(F32)).astype(BF)

            run.launch_if(z == 2, self.down_out.at[j], self.down.at[j], self.pairs[2][j], place.column(-1))

    def finish(self, place_in, store):
        place = self.run.place
        z = place.z
        near = self.near

        @pl.when(z == 0)
        def _():
            for j in range(4):
                self.wait(0, j)
                store(j, near[0, j].astype(F32) + self.trunk_in[j].astype(F32))

        @pl.when(z == 1)
        def _():
            for j in range(4):
                self.wait(2, j)
                self.total[j] = (near[1, j].astype(F32) + self.down[j].astype(F32)).astype(BF)

        @pl.when(z == 2)
        def _():
            for j in range(4):
                self.total[j] = (self.up_out[j].astype(F32) + self.down[j].astype(F32)).astype(BF)

        @pl.when(z == 3)
        def _():
            for j in range(4):
                self.wait(1, j)
                self.total[j] = (near[1, j].astype(F32) + self.up[j].astype(F32)).astype(BF)

        @pl.when(z > 0)
        def _():
            for ft in range(4):
                total = near[2, ft].astype(F32)
                for j in range(4):
                    total = total + self.total[j].astype(F32) * place_in[j, ft]
                store(ft, total)


def pick_parents(kp, slots, choose):
    def one(b, carry):
        for cc in range(2):
            total = slots[cc, 0] * choose[b, 0].astype(BF)
            for j in range(1, 4):
                total = total + slots[cc, j] * choose[b, j].astype(BF)
            kp[b, cc] = total
        return carry

    lax.fori_loop(0, 4, one, 0)


def all_keys(trunk, mine, kp, b, lanes):
    return jnp.concatenate(
        [trunk[:, :, :, lanes].reshape(1024, 128), mine[0, b, :, lanes], mine[1, b, :, lanes], kp[b, 0, :, lanes], kp[b, 1, :, lanes]],
        axis=0,
    )


def flat(ref):
    return ref[...].reshape(-1, ref.shape[-1])


def forward_kernel(first, *refs):
    refs = list(refs)

    def take(n):
        out = refs[:n]
        del refs[:n]
        return out

    x_ref, qkv_in, o_in, in_c, out_c, vec, place_in, choose, pen = take(9)
    if first:
        qkv_next, o_next = take(2)
    xn_ref, xb_o, qp_o, trunk_o, mine_o, kp_o, p_o, ctx_o, z1_o, hb_o, gp_o, gl_o, z2_o, win_o, wout_o = take(15)
    if first:
        wqkv_o, wo_o, wqkv_n, wo_n = take(4)
    xb, qp, trunk, mine, kp, p, ctx, z1, hb, gp, gl, z2, win, wout, wqkv, wo, heads, own, rs1_s, rs1_r, rs2_s, rs2_r = take(22)
    chain_refs = take(6)
    run = Run(*refs)
    place = run.place
    z, f, c = place.z, place.f, place.c
    launch = run.launch

    xb[f] = x_ref[...].astype(BF)
    wo[192:256, :] = jnp.zeros((64, WIDE), BF)
    if not first:
        loads = [run.local(qkv_in, wqkv), run.local(o_in, wo.at[pl.ds(0, 192)])]
    run.greet(False)
    came = [None] + [launch(xb.at[f], xb.at[f], place.plane(k)) for k in (1, 2, 3)]
    m_tasks = [Spread(run, in_c, win), Spread(run, out_c, wout)]
    if not first:
        m_tasks[0].start()
    if first:
        a_tasks = [Spread(run, qkv_in, wqkv), SpreadOutput(run, o_in, wo)]
        for t in a_tasks:
            t.start()
        a_tasks[0].relay()
        a_tasks[0].finish()
    else:
        for a in loads:
            a.wait()
    lane = lax.broadcasted_iota(jnp.int32, (ROWS, 128), 1)
    for k in range(4):
        g = place.f_at(-k)
        if k:
            came[k].wait_recv()
        qkv = product(xb[g], flat(wqkv)) + vec[0:1, :PACKED]
        rows = pl.ds(pl.multiple_of(g * ROWS, ROWS), ROWS)
        mine[c, g] = qkv[:, 256:].astype(BF)
        scaled = qkv[:, :256] * (HEAD_DIM ** (-0.5))
        front = scaled[:, :128]
        qp[rows, 0:128] = jnp.where(lane < 64, front, 0.0).astype(BF)
        qp[rows, 128:256] = jnp.where(lane < 64, pltpu.roll(front, 64, 1), 0.0).astype(BF)
        qp[rows, 256:384] = scaled[:, 128:].astype(BF)
    chain = KeyChain(run, trunk, mine, *chain_refs, place_in)
    chain.start()
    run.save(xb, xb_o)
    run.save(qp, qp_o)
    chain.finish()
    late_tasks = m_tasks if first else m_tasks[1:]
    for t in late_tasks:
        t.start(z > 0)
    pick_parents(kp, chain.slots, choose)
    run.save(kp, kp_o)
    run.save(trunk, trunk_o)
    run.save(mine, mine_o)
    if first:
        a_tasks[1].relay()

    def attend(i, carry):
        h, b = i // 4, lax.rem(i, 4)
        lanes = pl.ds(pl.multiple_of(h * 128, 128), 128)
        rows = pl.ds(pl.multiple_of(b * ROWS, ROWS), ROWS)
        keys = all_keys(trunk, mine, kp, b, lanes)
        s = product_nt(qp[rows, lanes], keys)
        s = jnp.concatenate(
            [s[:, :1024], s[:, 1024:1280] + pen[4 + b], s[:, 1280:] + pen[b]], axis=1
        )
        e = jnp.exp(s - jnp.max(s, axis=1, keepdims=True))
        pb = (e * (1.0 / jnp.sum(e, axis=1, keepdims=True))).astype(BF)
        p[h, b] = pb
        heads[h, b] = product(pb, keys)
        return carry

    lax.fori_loop(0, 12, attend, 0)
    run.save(p, p_o)
    if first:
        a_tasks[1].finish()
    back = [None]
    for k in (1, 2, 3, 0):
        g = place.f_at(-k)
        ctx[g, :, 0:128] = jnp.where(lane < 64, pltpu.roll(heads[0, g], 64, 1), heads[1, g]).astype(BF)
        ctx[g, :, 128:256] = jnp.where(lane < 64, pltpu.roll(heads[2, g], 64, 1), 0.0).astype(BF)
        part = product(ctx[g], wo[...])
        if k:
            rs1_s[k - 1] = part.astype(BF)
            back.append(launch(rs1_s.at[k - 1], rs1_r.at[k - 1], place.plane(-k)))
        else:
            own[...] = part
    run.save(ctx, ctx_o)
    for k in (1, 2, 3):
        back[k].wait_recv()
    for t in late_tasks:
        t.start(z == 0)
    total = own[...] + rs1_r[0].astype(F32) + rs1_r[1].astype(F32) + rs1_r[2].astype(F32)
    zz = x_ref[...] + total + vec[1:2, :]
    z1[...] = zz
    run.save(z1, z1_o)
    hidden = norm_rows(zz, vec[2:3, :], vec[3:4, :])
    hb[f] = hidden.astype(BF)
    came = [None] + [launch(hb.at[f], hb.at[f], place.plane(k)) for k in (1, 2, 3)]
    back = [None]
    for t in m_tasks:
        t.relay()
    if first:
        n_tasks = [Spread(run, qkv_next, wqkv_n), SpreadOutput(run, o_next, wo_n)]
        for t in n_tasks:
            t.start()
    for t in m_tasks:
        t.finish()
    for k in range(4):
        g = place.f_at(-k)
        if k:
            came[k].wait_recv()
        u = product(hb[g], flat(win)) + vec[4:5, :]
        cdf = 0.5 * (1.0 + lax.erf(u * (0.5 ** 0.5)))
        gp[g] = cdf + u * jnp.exp(-0.5 * u * u) * 0.3989422804014327
        low = (u * cdf).astype(BF)
        gl[g] = low
        part = product(low, flat(wout))
        if k:
            rs2_s[k - 1] = part.astype(BF)
            back.append(launch(rs2_s.at[k - 1], rs2_r.at[k - 1], place.plane(-k)))
        else:
            own[...] = part
    run.save(hb, hb_o)
    run.save(gp, gp_o)
    run.save(gl, gl_o)
    run.save(win, win_o)
    run.save(wout, wout_o)
    if first:
        run.save(wqkv, wqkv_o)
        run.save(wo.at[pl.ds(0, 192)], wo_o)
    for k in (1, 2, 3):
        back[k].wait_recv()
    total = own[...] + rs2_r[0].astype(F32) + rs2_r[1].astype(F32) + rs2_r[2].astype(F32)
    zz = norm_rows(z1[...], vec[2:3, :], vec[3:4, :]) + total + vec[5:6, :]
    z2[...] = zz
    run.save(z2, z2_o)
    xn_ref[...] = norm_rows(zz, vec[6:7, :], vec[7:8, :])
    if first:
        for t in n_tasks:
            t.relay()
        for t in n_tasks:
            t.finish()
    run.close()


def backward_kernel(extra, *refs):
    refs = list(refs)

    def take(n):
        out = refs[:n]
        del refs[:n]
        return out

    dy_ref, vec, place_in, choose, z2 = take(5)
    late_in = take(15)
    if extra:
        pq_in, pk_in, dvec_in = take(3)
    dx_ref, din_o, dout_o, do_o = take(4)
    if extra:
        dq_n, dk_n, dq_o, dk_o, sm_o = take(5)
    else:
        pq, pk, dvec_o = take(3)
    late = take(15)
    wout, gp, win, gl, hb, z1, wo, ctx, trunk, mine, kp, qp, p, xb, wqkv = late
    (
        df, du, da, dctx, dqf, dqkv, dz, dz1, dkt, dself, dpar, tgt, own, rs1_s, rs1_r, rs2_s, rs2_r,
    ) = take(17)
    chain_refs = take(7)
    pin, nin, fin, tin, pout, nout, fout, po, no, fo, to = take(11)
    if extra:
        pq, pk, dvec_o = take(3)
        nq, fq, tq, nk, fk, tk, nq2, fq2, tq2, nk2, fk2, tk2, sm, sm_a, sm_b, sm_v = take(16)
    run = Run(*refs)
    place = run.place
    z, f, c = place.z, place.f, place.c
    launch = run.launch
    loads = []
    for n, (src, dst) in enumerate(zip(late_in, late)):
        loads.append(run.local(src, dst.at[pl.ds(0, 192)] if n == 6 else dst))
    wo[192:256, :] = jnp.zeros((64, WIDE), BF)

    grad, dgain, dshift = norm_rows_back(z2[...], vec[6:7, :], dy_ref[...])
    dvec_o[6:7, :] = dgain
    dvec_o[7:8, :] = dshift
    dz[...] = grad
    low = grad.astype(BF)
    df[f] = low
    dvec_o[5:6, :] = jnp.sum(low.astype(F32), axis=0, keepdims=True)
    run.greet(True)
    came = [None] + [launch(df.at[f], df.at[f], place.plane(k)) for k in (1, 2, 3)]
    a_tasks = []
    if extra:
        a_tasks = [Collect(run, pq_in, nq, fq, tq, dq_n), Collect(run, pk_in, nk, fk, tk, dk_n)]
    for t in a_tasks:
        t.start()
    back = [None]
    bias = jnp.zeros((1, WIDE), F32)
    for n in range(3):
        loads[n].wait()
    for k in range(4):
        g = place.f_at(-k)
        if k:
            came[k].wait_recv()
        low = (product_nt(df[g], flat(wout)) * gp[g]).astype(BF)
        du[g] = low
        bias = bias + jnp.sum(low.astype(F32), axis=0, keepdims=True)
        part = product_nt(low, flat(win))
        if k:
            rs1_s[k - 1] = part.astype(BF)
            back.append(launch(rs1_s.at[k - 1], rs1_r.at[k - 1], place.plane(-k)))
        else:
            own[...] = part
            for t in a_tasks:
                t.middle()
    dvec_o[4:5, :] = bias
    m_tasks = [Collect(run, pin, nin, fin, tin, din_o), Collect(run, pout, nout, fout, None, dout_o)]
    o_task = CollectOutput(run, po, no, fo, to, do_o)

    def split_rows(dst, left, right, i):
        lanes = pl.ds(pl.multiple_of(i * 384, 128), 384)
        value = product_tn(left[:, :, lanes].reshape(512, 384), right).astype(BF)
        for zz in range(2):
            for cc in range(2):
                at = (2 * zz + cc) * 96
                dst[cc, 2 * i + zz] = value[at : at + 96, :]

    def ffn_grads(i, carry):
        split_rows(pout, gl, flat(df), i)
        split_rows(pin, hb, flat(du), i)
        return carry

    for n in range(3, 5):
        loads[n].wait()
    lax.fori_loop(0, 2, ffn_grads, 0)
    for t in m_tasks:
        t.start()
    for k in (1, 2, 3):
        back[k].wait_recv()
    up = dz[...] + own[...] + rs1_r[0].astype(F32) + rs1_r[1].astype(F32) + rs1_r[2].astype(F32)
    loads[5].wait()
    grad, dgain, dshift = norm_rows_back(z1[...], vec[2:3, :], up)
    dvec_o[2:3, :] = dgain
    dvec_o[3:4, :] = dshift
    dz1[...] = grad
    low = grad.astype(BF)
    da[f] = low
    dvec_o[1:2, :] = jnp.sum(low.astype(F32), axis=0, keepdims=True)
    came = [None] + [launch(da.at[f], da.at[f], place.plane(k)) for k in (1, 2, 3)]
    for t in a_tasks:
        t.end()
    for t in m_tasks:
        t.middle()
    dkt[...] = jnp.zeros_like(dkt)
    lane = lax.broadcasted_iota(jnp.int32, (ROWS, 128), 1)
    for a in loads[6:]:
        a.wait()
    for k in range(4):
        g = place.f_at(-k)
        rows = pl.ds(pl.multiple_of(g * ROWS, ROWS), ROWS)
        if k:
            came[k].wait_recv()
        packed = product_nt(da[g], wo[...])
        ahead, after = packed[:, :128], packed[:, 128:]
        dctx[rows, 0:128] = jnp.where(lane < 64, 0.0, pltpu.roll(ahead, 64, 1)).astype(BF)
        dctx[rows, 128:256] = jnp.where(lane < 64, 0.0, ahead).astype(BF)
        dctx[rows, 256:384] = jnp.where(lane < 64, 0.0, pltpu.roll(after, 64, 1)).astype(BF)
    value = product_tn(flat(ctx), flat(da)).astype(BF)
    for cc in range(2):
        po[cc] = value[96 * cc : 96 * (cc + 1), :]
    o_task.start()
    o_task.middle()

    def attend(i, carry):
        h, b = i // 4, lax.rem(i, 4)
        lanes = pl.ds(pl.multiple_of(h * 128, 128), 128)
        rows = pl.ds(pl.multiple_of(b * ROWS, ROWS), ROWS)
        keys = all_keys(trunk, mine, kp, b, lanes)
        q, g = qp[rows, lanes], dctx[rows, lanes]
        low = p[h, b]
        pf = low.astype(F32)
        dp = product_nt(g, keys)
        t = pf * dp
        ds = (t - pf * jnp.sum(t, axis=1, keepdims=True)).astype(BF)
        dqf[h, rows, :] = product(ds, keys) * (HEAD_DIM ** (-0.5))
        dkv = product_tn(jnp.concatenate([ds, low], axis=0), jnp.concatenate([q, g], axis=0))
        dkt[:, lanes] += dkv[:1024]
        dself[b, :, lanes] = dkv[1024:1280]
        dpar[b, :, lanes] = dkv[1280:]
        return carry

    lax.fori_loop(0, 12, attend, 0)
    for cc in range(2):
        for j in range(4):
            at = cc * 512 + j * ROWS
            tgt[cc, 0, j] = dkt[at : at + ROWS, :].astype(BF)

    def scatter(j, carry):
        for cc in range(2):
            half = slice(cc * ROWS, (cc + 1) * ROWS)
            total = dpar[0, half, :] * choose[0, j]
            for b in range(1, 4):
                total = total + dpar[b, half, :] * choose[b, j]
            tgt[cc, 1, j] = total.astype(BF)
            tgt[cc, 2, j] = dself[j, half, :].astype(BF)
        return carry

    lax.fori_loop(0, 4, scatter, 0)
    chain = GradChain(run, tgt, *chain_refs)
    chain.start()
    for g in range(4):
        rows = slice(g * ROWS, (g + 1) * ROWS)
        ahead = jnp.where(lane < 64, dqf[0, rows, :], pltpu.roll(dqf[1, rows, :], 64, 1))
        dqkv[g, :, 0:128] = ahead.astype(BF)
        dqkv[g, :, 128:256] = jnp.where(lane < 64, dqf[2, rows, :], 0.0).astype(BF)
    chain.middle()
    for t in m_tasks:
        t.end()
    chain.pass_on()

    def q_grads(i, carry):
        split_rows(pq, xb, dqkv[:, :, :256].reshape(512, 256), i)
        return carry

    lax.fori_loop(0, 2, q_grads, 0)
    end_tasks = []
    if extra:
        end_tasks = [Collect(run, pk, nk2, fk2, tk2, dk_o), Collect(run, pq, nq2, fq2, tq2, dq_o)]
        end_tasks[1].start()

    def store(ft, value):
        dqkv[ft, :, 256:] = value.astype(BF)

    chain.finish(place_in, store)

    def k_grads(i, carry):
        split_rows(pk, xb, dqkv[:, :, 256:].reshape(512, SLICE), i)
        return carry

    lax.fori_loop(0, 2, k_grads, 0)
    if extra:
        end_tasks[0].start()
        end_tasks[1].middle()
        end_tasks[0].middle()
    back = [None]
    for k in (1, 2, 3, 0):
        g = place.f_at(-k)
        part = product_nt(dqkv[g], flat(wqkv))
        if k:
            rs2_s[k - 1] = part.astype(BF)
            back.append(launch(rs2_s.at[k - 1], rs2_r.at[k - 1], place.plane(-k)))
        else:
            own[...] = part

    sums = jnp.sum(flat(dqkv).astype(F32), axis=0, keepdims=True)
    dvec_o[0:1, :] = jnp.concatenate([sums, jnp.zeros((1, WIDE - PACKED), F32)], axis=1)
    if extra:
        sm[0:8, :] = dvec_o[...]
        sm[8:16, :] = dvec_in[...]
        sm_near = launch(sm, sm_a, place.sibling())
        sm_near.wait_recv()
        sm_a[...] = sm[...] + sm_a[...]
        sm_far = [launch(sm_a, sm_b.at[k - 1], place.column(k)) for k in (1, 2, 3)]
    o_task.end()
    for t in a_tasks:
        t.last()
    for k in (1, 2, 3):
        back[k].wait_recv()
    dx_ref[...] = dz1[...] + own[...] + rs2_r[0].astype(F32) + rs2_r[1].astype(F32) + rs2_r[2].astype(F32)
    if extra:
        for t in end_tasks:
            t.end()
        for a in sm_far:
            a.wait_recv()
        sm_v[...] = sm_a[...] + sm_b[0] + sm_b[1] + sm_b[2]
        sm_last = [launch(sm_v, sm_o.at[f], place.plane(k)) for k in (1, 2, 3)]
        sm_o[f] = sm_v[...]
        for a in sm_last:
            a.wait_recv()
    for t in m_tasks + [o_task] + end_tasks:
        t.last()
    run.close()


ANY = pl.BlockSpec(memory_space=pl.ANY)
VM = pl.BlockSpec(memory_space=pltpu.VMEM)
SM = pl.BlockSpec(memory_space=pltpu.SMEM)
LIMIT = 60 * 1024 * 1024
SEMS = (160, 160, 32)


def shape(*dims, dtype=BF):
    return jax.ShapeDtypeStruct(dims, dtype)


def call(kernel, number, outs, out_specs, in_specs, scratch, args, flops):
    return pl.pallas_call(
        kernel,
        out_shape=tuple(outs),
        in_specs=in_specs,
        out_specs=tuple(out_specs),
        scratch_shapes=[pltpu.VMEM(s.shape, s.dtype) for s in scratch]
        + [pltpu.SemaphoreType.DMA((n,)) for n in SEMS],
        compiler_params=pltpu.CompilerParams(
            collective_id=number, has_side_effects=True, vmem_limit_bytes=LIMIT
        ),
        cost_estimate=pl.CostEstimate(flops=flops, bytes_accessed=20000000, transcendentals=0),
    )(*args)


def column_parts(query, key, value, inner):
    n = query.shape[0] * query.shape[1]
    q = query.reshape(n, 4, 3, 64)
    q = jnp.pad(q, ((0, 0), (0, 0), (0, 1), (0, 0))).reshape(n, 4, 256)
    kv = jnp.stack([key.reshape(n, 4, 3, 64), value.reshape(n, 4, 3, 64)], axis=3).reshape(n, 4, 384)
    up = inner.reshape(n, 4, 4, 192).transpose(0, 2, 1, 3).reshape(n, 4, WIDE)
    return jnp.concatenate([q, kv, up], axis=2).transpose(1, 0, 2)


LOCAL = shape(ROWS, WIDE, dtype=F32)
FULL = shape(4, ROWS, WIDE)
PIECE = shape(3, ROWS, WIDE)
QKV = shape(4, 2, 96, PACKED)
BIG = shape(4, 2, 96, WIDE)
OUTPUT = shape(192, WIDE)
HALVES = shape(2, 4, ROWS, SLICE)
QUARTERS = shape(4, ROWS, SLICE)
SAVED = (
    FULL, shape(512, SLICE), HALVES, HALVES, shape(4, 2, ROWS, SLICE), shape(3, 4, ROWS, NKEYS),
    shape(4, ROWS, 256), LOCAL, FULL, shape(4, ROWS, WIDE, dtype=F32), FULL, LOCAL,
)


def forward_layer(first, state, qkv, o, in_c, out_c, vec, place_in, choose, pen, following):
    outs = (LOCAL,) + SAVED + (BIG, BIG) + ((QKV, OUTPUT, QKV, OUTPUT) if first else ())
    got = call(
        lambda *refs: forward_kernel(first, *refs), 1 if first else 2, outs, (VM,) + (ANY,) * (len(outs) - 1),
        [VM] + [ANY] * 4 + [VM] + [SM] * 3 + [ANY] * len(following),
        list(SAVED)
        + [BIG, BIG, QKV, shape(256, WIDE), shape(3, 4, ROWS, 128, dtype=F32), LOCAL]
        + [PIECE] * 4 + [HALVES] + [QUARTERS] * 5,
        (state, qkv, o, in_c, out_c, vec, place_in, choose, pen) + tuple(following), 3 * 10**9,
    )
    return got[0], got[1:13], got[13:]


def collect_scratch(columns, rows):
    return [shape(4, 96, columns), shape(3, 96, columns)] + ([shape(96, columns, dtype=F32)] if rows else [])


OUT_SCRATCH = [shape(96, WIDE), shape(4, 96, WIDE), shape(96, WIDE, dtype=F32)]
PARTS = (shape(2, 4, 96, 256), shape(2, 4, 96, SLICE))
SHARES = (shape(4, 24, 256, dtype=F32), shape(4, 24, SLICE, dtype=F32))


def backward_layer(upstream, weights, vec, place_in, choose, saved, before):
    wqkv, wo, win, wout = weights
    xb, qp, trunk, mine, kp, p, ctx, z1, hb, gp, gl, z2 = saved
    keys = shape(4, 256, SLICE, dtype=F32)
    extra = len(before) > 0
    sums, sums2 = shape(8, WIDE, dtype=F32), shape(16, WIDE, dtype=F32)
    outs = (LOCAL, shape(4, 24, WIDE, dtype=F32), shape(96, WIDE, dtype=F32), shape(24, WIDE, dtype=F32))
    outs += SHARES + SHARES + (shape(4, 16, WIDE, dtype=F32),) if extra else PARTS + (sums,)
    scratch = [BIG, SAVED[9], BIG, FULL, FULL, LOCAL, shape(256, WIDE), SAVED[6], HALVES, HALVES, SAVED[4], SAVED[1], SAVED[5], FULL, QKV] + [
        FULL, FULL, FULL, shape(512, SLICE), shape(3, 512, 128, dtype=F32), shape(4, ROWS, PACKED), LOCAL, LOCAL,
        shape(1024, SLICE, dtype=F32), keys, keys, shape(2, 3, 4, ROWS, SLICE), LOCAL, PIECE, PIECE, PIECE, PIECE,
        shape(3, 4, ROWS, SLICE),
    ] + [QUARTERS] * 6
    part = shape(2, 4, 96, WIDE)
    scratch += [part] + collect_scratch(WIDE, True) + [part] + collect_scratch(WIDE, False)
    scratch += [shape(2, 96, WIDE)] + OUT_SCRATCH
    if extra:
        scratch += list(PARTS) + [sums]
        scratch += (collect_scratch(256, True) + collect_scratch(SLICE, True)) * 1
        scratch += collect_scratch(256, True) + collect_scratch(SLICE, True)
        scratch += [sums2, sums2, shape(3, 16, WIDE, dtype=F32), sums2]
    return call(
        lambda *refs: backward_kernel(extra, *refs), 4 if extra else 3, outs, (VM,) * len(outs),
        [VM] * 2 + [SM] * 2 + [VM] + [ANY] * 15 + [VM] * len(before), scratch,
        (upstream, vec, place_in, choose, z2, wout, gp, win, gl, hb, z1, wo, ctx, trunk, mine, kp, qp, p, xb, wqkv)
        + tuple(before),
        6 * 10**9,
    )


def slice_body(
    activations, query_weight, query_bias, key_weight, value_weight, value_bias, output_weight, output_bias,
    first_gain, first_shift, inner_weight, inner_bias, outer_weight, outer_bias, second_gain, second_shift,
    cotangent, parents, segments,
):
    place = Place()
    z, f, c = place.z, place.f, place.c
    col = column_parts(query_weight, key_weight, value_weight, inner_weight)
    vectors = (query_bias, value_bias, output_bias, first_gain, first_shift, outer_bias, second_gain, second_shift)
    label = jnp.broadcast_to(segments[:1].astype(BF)[None], (2, 1))
    small = jnp.concatenate(vectors + (inner_bias, label), axis=1)
    small = jnp.pad(small, ((0, 14), (0, 384 - small.shape[1])))
    colp, op, smallg = call(
        exchange_kernel, 0, (shape(4, 48, 1408), shape(4, 48, WIDE), shape(4, 2, 4, 16, 384)), (ANY,) * 3, [ANY] * 3,
        [], (col, output_weight.reshape(48, WIDE), small), 1000,
    )
    colp = colp.reshape(4, 2, 24, 1408).transpose(1, 0, 2, 3).reshape(2, 96, 1408)
    op = op.reshape(4, 2, 24, WIDE).transpose(1, 0, 2, 3).reshape(2, 96, WIDE)
    small = smallg[:, :, :, :2].transpose(3, 0, 2, 1, 4).astype(F32)
    parts = [small[..., i * 24 : (i + 1) * 24].reshape(2, WIDE) for i in range(8)]
    q_all, v_all, o_all, g1, s1, out_all, g2, s2 = parts
    in_mine = lax.dynamic_index_in_dim(small[..., 192:288], f, 2, keepdims=False).reshape(2, WIDE)
    q_mine = lax.dynamic_slice_in_dim(q_all, 192 * f, 192, 1)
    v_mine = lax.dynamic_slice_in_dim(v_all, 192 * f, 192, 1).reshape(2, 3, 64)
    kv_mine = jnp.pad(v_mine, ((0, 0), (0, 0), (64, 0))).reshape(2, SLICE)
    qkv_mine = jnp.pad(jnp.concatenate([q_mine, jnp.zeros((2, 64), F32), kv_mine], axis=1), ((0, 0), (0, WIDE - PACKED)))
    vecs = jnp.stack([qkv_mine, o_all, g1, s1, in_mine, out_all, g2, s2], axis=1)

    labels = small[0, :, :, 0, 288].reshape(16).astype(jnp.int32)
    above = lookup_rows(labels, parents)
    order = jnp.arange(16, dtype=jnp.int32)
    branch = jnp.logical_and(above == labels[0], order >= 4)
    slot = jnp.where(branch, jnp.sum((branch[:, None] & (order[:, None] < order[None, :])).astype(jnp.int32), axis=0), 4)
    in_slot = slot[None, :] == jnp.arange(4, dtype=jnp.int32)[:, None]
    place_in = lax.dynamic_slice_in_dim(in_slot.astype(F32), 4 * z, 4, 1)
    parent = lax.dynamic_slice_in_dim(above, 4 * z, 4, 0)
    match = parent[:, None, None] == jnp.where(in_slot, labels[None, :], -1)[None]
    choose = jnp.any(match, axis=2).astype(F32)
    pen = jnp.concatenate(
        [jnp.where(jnp.any(match, axis=(1, 2)), 0.0, MASKED), jnp.where(z > 0, jnp.zeros((4,), F32), MASKED)]
    ).astype(F32)

    qkv_c = [colp[i, :, :PACKED] for i in range(2)]
    in_c = [colp[i, :, PACKED:] for i in range(2)]
    state, kept0, (win0, wout0, wqkv0, wo0, wqkv1, wo1) = forward_layer(
        True, activations.astype(F32), qkv_c[0], op[0], in_c[0], outer_weight[0], vecs[0], place_in, choose, pen,
        (qkv_c[1], op[1]),
    )
    state, kept1, (win1, wout1) = forward_layer(
        False, state, wqkv1, wo1, in_c[1], outer_weight[1], vecs[1], place_in, choose, pen, ()
    )
    outcome = state.astype(BF)
    upstream, din1, dout1, do1, pq, pk, dvec1 = backward_layer(
        cotangent.astype(F32), (wqkv1, wo1, win1, wout1), vecs[1], place_in, choose, kept1, ()
    )
    upstream, din0, dout0, do0, dq1, dk1, dq0, dk0, rsm = backward_layer(
        upstream, (wqkv0, wo0, win0, wout0), vecs[0], place_in, choose, kept0, (pq, pk, dvec1)
    )
    dq = jnp.stack([dq0, dq1]).transpose(0, 2, 1, 3)[..., :192].reshape(2, 24, WIDE)
    dkv = jnp.stack([dk0, dk1]).transpose(0, 2, 1, 3).reshape(2, 24, 4, 3, 2, 64)
    dk = dkv[..., 0, :].reshape(2, 24, WIDE)
    dv = dkv[..., 1, :].reshape(2, 24, WIDE)
    dinner = jnp.stack([din0, din1]).reshape(2, 4, 24, 4, 192).transpose(0, 2, 3, 1, 4).reshape(2, 24, 3072)
    rsm = rsm.reshape(4, 2, 8, WIDE)
    sums = jnp.sum(rsm, axis=0)
    dqb = rsm[:, :, 0, :192].transpose(1, 0, 2).reshape(2, WIDE)
    dvb = rsm[:, :, 0, 256:640].reshape(4, 2, 3, 2, 64)[:, :, :, 1].transpose(1, 0, 2, 3).reshape(2, WIDE)
    rows = jnp.stack([dqb, dvb, sums[:, 1], sums[:, 2], sums[:, 3], sums[:, 5], sums[:, 6], sums[:, 7]])
    rows = lax.dynamic_slice_in_dim(rows, 24 * (8 * z + 2 * f + c), 24, 2)
    dib = lax.dynamic_index_in_dim(rsm[:, :, 4], f, 0, keepdims=False)
    dib = lax.dynamic_slice_in_dim(dib, 96 * (2 * z + c), 96, 1)
    return (
        outcome, upstream.astype(BF), dq, rows[0], dk, dv, rows[1], jnp.stack([do0, do1]), rows[2], rows[3], rows[4],
        dinner, dib, jnp.stack([dout0, dout1]), rows[5], rows[6], rows[7],
    )


def solution(mesh):
    placed = (
        P("fsdp", None),
        P(None, "fsdp", None),
        P(None, "fsdp"),
        P(None, "fsdp", None),
        P(None, "fsdp", None),
        P(None, "fsdp"),
        P(None, "fsdp", None),
        P(None, "fsdp"),
        P(None, "fsdp"),
        P(None, "fsdp"),
        P(None, "fsdp", None),
        P(None, "fsdp"),
        P(None, "fsdp", None),
        P(None, "fsdp"),
        P(None, "fsdp"),
        P(None, "fsdp"),
        P("fsdp", None),
        P(),
        P("fsdp"),
    )
    return jax.shard_map(
        slice_body if mesh.shape["fsdp"] == 32 else body,
        mesh=mesh,
        in_specs=placed,
        out_specs=(
            P("fsdp", None),
            P("fsdp", None),
            P(None, "fsdp", None),
            P(None, "fsdp"),
            P(None, "fsdp", None),
            P(None, "fsdp", None),
            P(None, "fsdp"),
            P(None, "fsdp", None),
            P(None, "fsdp"),
            P(None, "fsdp"),
            P(None, "fsdp"),
            P(None, "fsdp", None),
            P(None, "fsdp"),
            P(None, "fsdp", None),
            P(None, "fsdp"),
            P(None, "fsdp"),
            P(None, "fsdp"),
        ),
        check_vma=False,
    )
```

```python
import jax
import jax.numpy as jnp
from jax import lax
from jax.experimental import pallas as pl
from jax.experimental.pallas import tpu as pltpu
from jax.sharding import PartitionSpec as P

HEADS = 12
HEAD_DIM = 64
LAYERS = 2
TREE_LEN = 4096


EPSILON = 1e-06
MASKED = -1000000000.0


def partner_2(shard, axis, stride):
    return lax.ppermute(shard, axis, [(i, i ^ 1 << stride) for i in range(lax.axis_size(axis))])


def as_sent(shard):
    return jax.tree.map(lambda a: a.astype(jnp.bfloat16) if a.dtype == jnp.float32 else a, shard)


def product(a, b):
    return jnp.dot(a, b, preferred_element_type=jnp.float32)


def product_tn(a, b):
    return lax.dot_general(a, b, (((0,), (0,)), ((), ())), preferred_element_type=jnp.float32)


def product_nt(a, b):
    return lax.dot_general(a, b, (((1,), (1,)), ((), ())), preferred_element_type=jnp.float32)


def exact_gelu(u):
    return jax.nn.gelu(u, approximate=False)


def layer_norm(z, gain_vec, shift_vec):
    centre = z - jnp.mean(z, axis=-1, keepdims=True)
    scaled = centre * lax.rsqrt(jnp.mean(centre * centre, axis=-1, keepdims=True) + EPSILON)
    return scaled * gain_vec.astype(jnp.float32) + shift_vec.astype(jnp.float32)


def norm_backward(z, gain_vec, upstream):
    centre = z - jnp.mean(z, axis=-1, keepdims=True)
    invert = lax.rsqrt(jnp.mean(centre * centre, axis=-1, keepdims=True) + EPSILON)
    scaled = centre * invert
    weighted = upstream * gain_vec.astype(jnp.float32)
    inner = invert * (
        weighted
        - jnp.mean(weighted, axis=-1, keepdims=True)
        - scaled * jnp.mean(weighted * scaled, axis=-1, keepdims=True)
    )
    return (inner, jnp.sum(upstream * scaled, axis=0), jnp.sum(upstream, axis=0))


def lookup_rows(ids, parents):
    table = jnp.arange(parents.shape[0], dtype=jnp.int32)
    return jnp.sum(jnp.where(ids[:, None] == table[None, :], parents[None, :], 0), axis=1)


def join_heads(stacked):
    return stacked.transpose(1, 0, 2).reshape(stacked.shape[1], -1)


def gather_group(key_rows, value_rows, labels, position, bit_count):
    for b in range(bit_count):
        partner = partner_2((key_rows, value_rows, labels), "fsdp", b)
        upper_side = position >> b & 1 == 1
        key_rows = jnp.where(
            upper_side,
            jnp.concatenate([partner[0], key_rows]),
            jnp.concatenate([key_rows, partner[0]]),
        )
        value_rows = jnp.where(
            upper_side,
            jnp.concatenate([partner[1], value_rows]),
            jnp.concatenate([value_rows, partner[1]]),
        )
        labels = jnp.where(
            upper_side, jnp.concatenate([partner[2], labels]), jnp.concatenate([labels, partner[2]])
        )
    return (key_rows, value_rows, labels)


def sum_group(key_grad, value_grad, position, bit_count):
    for b in reversed(range(bit_count)):
        halfway = key_grad.shape[0] // 2
        upper_side = position >> b & 1 == 1
        outgoing = (
            jnp.where(upper_side, key_grad[:halfway], key_grad[halfway:]),
            jnp.where(upper_side, value_grad[:halfway], value_grad[halfway:]),
        )
        partner = partner_2((as_sent(outgoing[0]), as_sent(outgoing[1])), "fsdp", b)
        key_grad = jnp.where(upper_side, key_grad[halfway:], key_grad[:halfway]) + partner[0]
        value_grad = jnp.where(upper_side, value_grad[halfway:], value_grad[:halfway]) + partner[1]
    return (key_grad, value_grad)


def attend_forward(queries, key_rows, value_rows, allowed):
    factor = HEAD_DIM ** (-0.5)

    def one_head(j):
        start = j * HEAD_DIM
        q = lax.dynamic_slice_in_dim(queries, start, HEAD_DIM, 1)
        k = lax.dynamic_slice_in_dim(key_rows, start, HEAD_DIM, 1)
        v = lax.dynamic_slice_in_dim(value_rows, start, HEAD_DIM, 1)
        s = jnp.where(allowed, product_nt(q, k) * factor, MASKED)
        maxima = jnp.max(s, axis=1, keepdims=True)
        e = jnp.exp(s - maxima)
        totals = jnp.sum(e, axis=1, keepdims=True)
        p = (e / totals).astype(jnp.bfloat16)
        return (product(p, v), (maxima + jnp.log(totals))[:, 0])

    stacked, log_total = lax.map(one_head, jnp.arange(HEADS))
    return (join_heads(stacked), log_total)


def attend_backward(queries, key_rows, value_rows, allowed, log_total, grad_context):
    factor = HEAD_DIM ** (-0.5)

    def one_head(j):
        start = j * HEAD_DIM
        q = lax.dynamic_slice_in_dim(queries, start, HEAD_DIM, 1)
        k = lax.dynamic_slice_in_dim(key_rows, start, HEAD_DIM, 1)
        v = lax.dynamic_slice_in_dim(value_rows, start, HEAD_DIM, 1)
        g = lax.dynamic_slice_in_dim(grad_context, start, HEAD_DIM, 1)
        s = jnp.where(allowed, product_nt(q, k) * factor, MASKED)
        p = jnp.where(allowed, jnp.exp(s - log_total[j][:, None]), 0.0)
        grad_p = product_nt(g, v)
        grad_v = product_tn(p.astype(jnp.bfloat16), g)
        grad_s = (p * (grad_p - jnp.sum(p * grad_p, axis=1, keepdims=True))).astype(jnp.bfloat16)
        grad_q = product(grad_s, k) * factor
        grad_k = product_tn(grad_s, q) * factor
        return (grad_q, grad_k, grad_v)

    grad_q, grad_k, grad_v = lax.map(one_head, jnp.arange(HEADS))
    return (join_heads(grad_q), join_heads(grad_k), join_heads(grad_v))


def layer_forward(state, full, segments, parent_one, parent_two, position, bit_count):
    (
        q_weight,
        q_bias,
        k_weight,
        v_weight,
        v_bias,
        o_weight,
        o_bias,
        gain_one,
        shift_one,
        up_weight,
        up_bias,
        down_weight,
        down_bias,
        gain_two,
        shift_two,
    ) = full
    inputs = state.astype(jnp.bfloat16)
    queries = (product(inputs, q_weight) + q_bias).astype(jnp.bfloat16)
    key_local = product(inputs, k_weight).astype(jnp.bfloat16)
    value_local = (product(inputs, v_weight) + v_bias).astype(jnp.bfloat16)
    key_rows, value_rows, labels = gather_group(
        key_local, value_local, segments, position, bit_count
    )
    allowed = (
        (labels[None, :] == segments[:, None])
        | (labels[None, :] == parent_one[:, None])
        | (labels[None, :] == parent_two[:, None])
    )
    context_wide, log_total = attend_forward(queries, key_rows, value_rows, allowed)
    context = context_wide.astype(jnp.bfloat16)
    first_sum = state + product(context, o_weight) + o_bias
    hidden = layer_norm(first_sum, gain_one, shift_one)
    hidden_low = hidden.astype(jnp.bfloat16)
    pre_act = product(hidden_low, up_weight) + up_bias
    gelu_out = exact_gelu(pre_act).astype(jnp.bfloat16)
    second_sum = hidden + product(gelu_out, down_weight) + down_bias
    record = (
        inputs,
        queries,
        key_rows,
        value_rows,
        allowed,
        log_total,
        context,
        first_sum,
        hidden_low,
        pre_act,
        gelu_out,
        second_sum,
    )
    return (record, layer_norm(second_sum, gain_two, shift_two))


def layer_backward(upstream, full, record, position, bit_count):
    (
        q_weight,
        q_bias,
        k_weight,
        v_weight,
        v_bias,
        o_weight,
        o_bias,
        gain_one,
        shift_one,
        up_weight,
        up_bias,
        down_weight,
        down_bias,
        gain_two,
        shift_two,
    ) = full
    (
        inputs,
        queries,
        key_rows,
        value_rows,
        allowed,
        log_total,
        context,
        first_sum,
        hidden_low,
        pre_act,
        gelu_out,
        second_sum,
    ) = record
    grad_z2, grad_gain_two, grad_shift_two = norm_backward(second_sum, gain_two, upstream)
    grad_f = grad_z2.astype(jnp.bfloat16)
    grad_down_bias = jnp.sum(grad_f.astype(jnp.float32), axis=0)
    grad_down = product_tn(gelu_out, grad_f)
    grad_gelu = product_nt(grad_f, down_weight)
    unused_value, gelu_back = jax.vjp(exact_gelu, pre_act)
    grad_u = gelu_back(grad_gelu)[0].astype(jnp.bfloat16)
    grad_up_bias = jnp.sum(grad_u.astype(jnp.float32), axis=0)
    grad_up = product_tn(hidden_low, grad_u)
    grad_h = grad_z2 + product_nt(grad_u, up_weight)
    grad_z1, grad_gain_one, grad_shift_one = norm_backward(first_sum, gain_one, grad_h)
    grad_a = grad_z1.astype(jnp.bfloat16)
    grad_o_bias = jnp.sum(grad_a.astype(jnp.float32), axis=0)
    grad_o = product_tn(context, grad_a)
    grad_context = product_nt(grad_a, o_weight).astype(jnp.bfloat16)
    grad_q, key_grad, value_grad = attend_backward(
        queries, key_rows, value_rows, allowed, log_total, grad_context
    )
    key_grad, value_grad = sum_group(key_grad, value_grad, position, bit_count)
    q_low = grad_q.astype(jnp.bfloat16)
    k_low = key_grad.astype(jnp.bfloat16)
    v_low = value_grad.astype(jnp.bfloat16)
    grad_x = (
        grad_z1
        + product_nt(q_low, q_weight)
        + product_nt(k_low, k_weight)
        + product_nt(v_low, v_weight)
    )
    terms = (
        product_tn(inputs, q_low),
        jnp.sum(q_low.astype(jnp.float32), axis=0),
        product_tn(inputs, k_low),
        product_tn(inputs, v_low),
        jnp.sum(v_low.astype(jnp.float32), axis=0),
        grad_o,
        grad_o_bias,
        grad_gain_one,
        grad_shift_one,
        grad_up,
        grad_up_bias,
        grad_down,
        grad_down_bias,
        grad_gain_two,
        grad_shift_two,
    )
    return (grad_x, terms)


def stack_layers(groups, n):
    return jnp.stack([g[n] for g in groups])


def body(
    activations,
    query_weight,
    query_bias,
    key_weight,
    value_weight,
    value_bias,
    output_weight,
    output_bias,
    first_gain,
    first_shift,
    inner_weight,
    inner_bias,
    outer_weight,
    outer_bias,
    second_gain,
    second_shift,
    cotangent,
    parents,
    segments,
):
    position = lax.axis_index("fsdp")
    bit_count = (TREE_LEN // activations.shape[0]).bit_length() - 1
    parent_one = lookup_rows(segments, parents)
    parent_two = lookup_rows(parent_one, parents)
    state = activations.astype(jnp.float32)
    saved = []
    kept_weights = []
    for i in range(LAYERS):
        full = (
            lax.all_gather(query_weight[i], "fsdp", axis=0, tiled=True),
            lax.all_gather(query_bias[i], "fsdp", axis=0, tiled=True),
            lax.all_gather(key_weight[i], "fsdp", axis=0, tiled=True),
            lax.all_gather(value_weight[i], "fsdp", axis=0, tiled=True),
            lax.all_gather(value_bias[i], "fsdp", axis=0, tiled=True),
            lax.all_gather(output_weight[i], "fsdp", axis=0, tiled=True),
            lax.all_gather(output_bias[i], "fsdp", axis=0, tiled=True),
            lax.all_gather(first_gain[i], "fsdp", axis=0, tiled=True),
            lax.all_gather(first_shift[i], "fsdp", axis=0, tiled=True),
            lax.all_gather(inner_weight[i], "fsdp", axis=0, tiled=True),
            lax.all_gather(inner_bias[i], "fsdp", axis=0, tiled=True),
            lax.all_gather(outer_weight[i], "fsdp", axis=0, tiled=True),
            lax.all_gather(outer_bias[i], "fsdp", axis=0, tiled=True),
            lax.all_gather(second_gain[i], "fsdp", axis=0, tiled=True),
            lax.all_gather(second_shift[i], "fsdp", axis=0, tiled=True),
        )
        kept_weights.append(full)
        record, state = layer_forward(
            state, full, segments, parent_one, parent_two, position, bit_count
        )
        saved.append(record)
    outcome = state.astype(jnp.bfloat16)
    upstream = cotangent.astype(jnp.float32)
    layer_grads = [None] * LAYERS
    for i in reversed(range(LAYERS)):
        full = (
            lax.all_gather(query_weight[i], "fsdp", axis=0, tiled=True),
            lax.all_gather(query_bias[i], "fsdp", axis=0, tiled=True),
            lax.all_gather(key_weight[i], "fsdp", axis=0, tiled=True),
            lax.all_gather(value_weight[i], "fsdp", axis=0, tiled=True),
            lax.all_gather(value_bias[i], "fsdp", axis=0, tiled=True),
            lax.all_gather(output_weight[i], "fsdp", axis=0, tiled=True),
            lax.all_gather(output_bias[i], "fsdp", axis=0, tiled=True),
            lax.all_gather(first_gain[i], "fsdp", axis=0, tiled=True),
            lax.all_gather(first_shift[i], "fsdp", axis=0, tiled=True),
            lax.all_gather(inner_weight[i], "fsdp", axis=0, tiled=True),
            lax.all_gather(inner_bias[i], "fsdp", axis=0, tiled=True),
            lax.all_gather(outer_weight[i], "fsdp", axis=0, tiled=True),
            lax.all_gather(outer_bias[i], "fsdp", axis=0, tiled=True),
            lax.all_gather(second_gain[i], "fsdp", axis=0, tiled=True),
            lax.all_gather(second_shift[i], "fsdp", axis=0, tiled=True),
        )
        upstream, terms = layer_backward(upstream, full, saved[i], position, bit_count)
        layer_grads[i] = (
            lax.psum_scatter(terms[0], "fsdp", scatter_dimension=0, tiled=True),
            lax.psum_scatter(terms[1], "fsdp", scatter_dimension=0, tiled=True),
            lax.psum_scatter(terms[2], "fsdp", scatter_dimension=0, tiled=True),
            lax.psum_scatter(terms[3], "fsdp", scatter_dimension=0, tiled=True),
            lax.psum_scatter(terms[4], "fsdp", scatter_dimension=0, tiled=True),
            lax.psum_scatter(terms[5], "fsdp", scatter_dimension=0, tiled=True),
            lax.psum_scatter(terms[6], "fsdp", scatter_dimension=0, tiled=True),
            lax.psum_scatter(terms[7], "fsdp", scatter_dimension=0, tiled=True),
            lax.psum_scatter(terms[8], "fsdp", scatter_dimension=0, tiled=True),
            lax.psum_scatter(terms[9], "fsdp", scatter_dimension=0, tiled=True),
            lax.psum_scatter(terms[10], "fsdp", scatter_dimension=0, tiled=True),
            lax.psum_scatter(terms[11], "fsdp", scatter_dimension=0, tiled=True),
            lax.psum_scatter(terms[12], "fsdp", scatter_dimension=0, tiled=True),
            lax.psum_scatter(terms[13], "fsdp", scatter_dimension=0, tiled=True),
            lax.psum_scatter(terms[14], "fsdp", scatter_dimension=0, tiled=True),
        )
    shares = tuple((stack_layers(layer_grads, n) for n in range(15)))
    return (outcome, upstream.astype(jnp.bfloat16)) + tuple(shares)


MESH = pl.DeviceIdType.MESH
BF = jnp.bfloat16
F32 = jnp.float32
WIDE = 768
SLICE = 384
PACKED = 640
ROWS = 128
NKEYS = 1536


class Pool:
    def __init__(self, ref):
        self.ref = ref
        self.used = 0

    def take(self):
        self.used += 1
        return self.ref.at[self.used - 1]

    def block(self, n):
        first = self.used
        self.used += n
        return lambda i: self.ref.at[first + i]


class Place:
    def __init__(self):
        me = lax.axis_index("fsdp")
        p = lax.rem(me, 32)
        self.base = me - p
        self.z = p // 8
        self.f = lax.rem(p // 2, 4)
        self.c = lax.rem(p, 2)

    def at(self, z, f, c):
        return self.base + 8 * z + 2 * f + c

    def f_at(self, k):
        return lax.rem(self.f + k + 4, 4)

    def z_at(self, k):
        return lax.rem(self.z + k + 4, 4)

    def plane(self, k):
        return self.at(self.z, self.f_at(k), self.c)

    def across(self, k):
        return self.at(self.z, self.f_at(k), 1 - self.c)

    def column(self, k):
        return self.at(self.z_at(k), self.f, self.c)

    def sibling(self):
        return self.at(self.z, self.f, 1 - self.c)


def remote(src, dst, sems, device):
    return pltpu.make_async_remote_copy(
        src_ref=src, dst_ref=dst, send_sem=sems[0], recv_sem=sems[1], device_id=(device,), device_id_type=MESH
    )


class Run:
    def __init__(self, send_sems, recv_sems, local_sems):
        self.place = Place()
        self.sends, self.recvs, self.locals = Pool(send_sems), Pool(recv_sems), Pool(local_sems)
        self.flying, self.saving = [], []

    def greet(self, wide):
        place = self.place
        there = [place.plane(k) for k in (1, 2, 3)] + [place.column(k) for k in (1, 2, 3)] + [place.sibling()]
        if wide:
            there += [place.across(k) for k in (1, 2, 3)]
        barrier = pltpu.get_barrier_semaphore()
        for dev in there:
            pl.semaphore_signal(barrier, inc=1, device_id=(dev,), device_id_type=MESH)
        pl.semaphore_wait(barrier, len(there))

    def launch(self, src, dst, device):
        a = remote(src, dst, (self.sends.take(), self.recvs.take()), device)
        a.start()
        self.flying.append((None, a))
        return a

    def launch_if(self, cond, src, dst, sems, device):
        a = remote(src, dst, sems, device)

        @pl.when(cond)
        def _():
            a.start()

        self.flying.append((cond, a))
        return a

    def local(self, src, dst):
        a = pltpu.make_async_copy(src, dst, self.locals.take())
        a.start()
        return a

    def save(self, src, dst):
        self.saving.append(self.local(src, dst))

    def close(self):
        for a in self.saving:
            a.wait()
        for cond, a in self.flying:
            if cond is None:
                a.wait_send()
            else:

                @pl.when(cond)
                def _(a=a):
                    a.wait_send()


class Spread:
    def __init__(self, run, chunk, full):
        self.run, self.chunk, self.full, self.pairs = run, chunk, full, None

    def start(self, cond=None):
        run, place = self.run, self.run.place
        mine = self.full.at[place.z, place.c]
        if self.pairs is None:
            self.own = pltpu.make_async_copy(self.chunk, mine, run.locals.take())
            self.pairs = [(run.sends.take(), run.recvs.take()) for _ in range(4)]
        cond = place.z >= 0 if cond is None else cond

        @pl.when(cond)
        def _():
            self.own.start()

        there = [place.column(k) for k in (1, 2, 3)] + [place.sibling()]
        copies = [run.launch_if(cond, self.chunk, mine, self.pairs[i], there[i]) for i in range(4)]
        self.far, self.near = copies[:3], copies[3:]

    def relay(self):
        run, place = self.run, self.run.place
        for k in (1, 2, 3):
            self.far[k - 1].wait_recv()
            there = self.full.at[place.z_at(-k), place.c]
            self.near.append(run.launch(there, there, place.sibling()))

    def finish(self):
        self.own.wait()
        for a in self.near:
            a.wait_recv()


class SpreadOutput:
    def __init__(self, run, chunk, full):
        self.run, self.chunk = run, chunk
        self.part = full.at[pl.ds(pl.multiple_of(run.place.c * 96, 96), 96)]

    def start(self):
        run, place = self.run, self.run.place
        self.copy = pltpu.make_async_copy(self.chunk, self.part, run.locals.take())

        @pl.when(place.f == place.z)
        def _():
            self.copy.start()

        arrive = run.recvs.take()
        for k in (1, 2, 3):
            self.far = run.launch_if(
                place.f == place.z, self.chunk, self.part, (run.sends.take(), arrive), place.column(k)
            )

    def relay(self):
        run, place = self.run, self.run.place

        @pl.when(place.f == place.z)
        def _():
            self.copy.wait()

        @pl.when(place.f != place.z)
        def _():
            self.far.wait_recv()

        self.near = run.launch(self.part, self.part, place.sibling())

    def finish(self):
        self.near.wait_recv()


class Collect:
    def __init__(self, run, part, near, far, total, out):
        self.run, self.part, self.near, self.far, self.total, self.out = run, part, near, far, total, out

    def start(self):
        place = self.run.place
        self.a = self.run.launch(self.part.at[1 - place.c], self.near, place.sibling())

    def middle(self):
        run, place = self.run, self.run.place
        self.a.wait_recv()

        def add(i, carry):
            self.near[i] = (self.part[place.c, i].astype(F32) + self.near[i].astype(F32)).astype(BF)
            return carry

        lax.fori_loop(0, 4, add, 0)
        self.moves = [
            run.launch(self.near.at[place.z_at(k)], self.far.at[k - 1], place.column(k)) for k in (1, 2, 3)
        ]

    def end(self):
        run, place = self.run, self.run.place
        for a in self.moves:
            a.wait_recv()
        result = self.near[place.z].astype(F32)
        for k in range(3):
            result = result + self.far[k].astype(F32)
        if self.total is None:
            self.out[...] = result
            return
        self.total[...] = result
        scatter_rows(self, self.total, self.out.at[place.f], None)

    def last(self):
        if self.total is None:
            return
        place = self.run.place
        for k in (1, 2, 3):
            g = place.f_at(k)
            remote(
                self.out.at[g], self.out.at[g], (self.send, self.arrive(g)), place.plane(k)
            ).wait_recv()

        @pl.when(place.c != place.f // 2)
        def _():
            remote(
                self.out.at[place.f], self.out.at[place.f], (self.send, self.arrive(place.f)), place.sibling()
            ).wait_recv()


def scatter_rows(task, total, landing, cond):
    run, place = task.run, task.run.place
    arrive = run.recvs.block(4)
    for j in range(4):
        there = place.at(place.z, 2 * place.c + j // 2, j % 2)
        here = jnp.logical_and(place.f == 2 * place.c + j // 2, place.c == j % 2)
        away = jnp.logical_not(here)
        if cond is not None:
            here, away = jnp.logical_and(here, cond), jnp.logical_and(away, cond)
        task.send = run.sends.take()
        slot = arrive(place.f) if cond is None else arrive(0)
        run.launch_if(away, total.at[pl.ds(24 * j, 24)], landing, (task.send, slot), there)

        @pl.when(here)
        def _(j=j):
            landing[...] = total[24 * j : 24 * (j + 1), :]

    task.arrive = arrive


class CollectOutput:
    def __init__(self, run, part, near, far, total, out):
        self.run, self.part, self.near, self.far, self.total, self.out = run, part, near, far, total, out

    def start(self):
        place = self.run.place
        self.a = self.run.launch(self.part.at[1 - place.c], self.near, place.sibling())

    def middle(self):
        run, place = self.run, self.run.place
        self.a.wait_recv()
        self.near[...] = (self.part[place.c].astype(F32) + self.near[...].astype(F32)).astype(BF)
        self.slot = run.recvs.block(4)
        self.one = run.sends.take()
        shift = lax.rem(place.f - place.z + 4, 4)
        run.launch_if(
            place.f != place.z, self.near, self.far.at[shift], (self.one, self.slot(shift)),
            place.at(place.f, place.f, place.c),
        )

    def end(self):
        place = self.run.place

        @pl.when(place.f == place.z)
        def _():
            result = self.near[...].astype(F32)
            for k in (1, 2, 3):
                remote(
                    self.near, self.far.at[k], (self.one, self.slot(k)), place.column(k)
                ).wait_recv()
                result = result + self.far[k].astype(F32)
            self.total[...] = result

        scatter_rows(self, self.total, self.out, place.f == place.z)

    def last(self):
        place = self.run.place
        mine = jnp.logical_and(place.f == place.z, place.c == place.f // 2)

        @pl.when(jnp.logical_not(mine))
        def _():
            remote(self.out, self.out, (self.send, self.arrive(0)), place.sibling()).wait_recv()


def norm_rows(z, gain, shift):
    centre = z - jnp.mean(z, axis=-1, keepdims=True)
    inv = lax.rsqrt(jnp.mean(centre * centre, axis=-1, keepdims=True) + EPSILON)
    return centre * inv * gain + shift


def norm_rows_back(z, gain, upstream):
    centre = z - jnp.mean(z, axis=-1, keepdims=True)
    inv = lax.rsqrt(jnp.mean(centre * centre, axis=-1, keepdims=True) + EPSILON)
    scaled = centre * inv
    weighted = upstream * gain
    inner = inv * (
        weighted
        - jnp.mean(weighted, axis=-1, keepdims=True)
        - scaled * jnp.mean(weighted * scaled, axis=-1, keepdims=True)
    )
    return inner, jnp.sum(upstream * scaled, axis=0, keepdims=True), jnp.sum(upstream, axis=0, keepdims=True)


def exchange_kernel(col, rows_o, small, colp, op, smallg, send_sems, recv_sems, local_sems):
    run = Run(send_sems, recv_sems, local_sems)
    place = run.place
    z, f, c = place.z, place.f, place.c
    mine = c == f // 2
    slot = 2 * lax.rem(f, 2) + c
    own = pltpu.make_async_copy(col.at[f], colp.at[slot], run.locals.take())
    own_o = pltpu.make_async_copy(rows_o, op.at[slot], run.locals.take())
    keep = jnp.logical_and(mine, f == z)

    @pl.when(mine)
    def _():
        own.start()

    @pl.when(keep)
    def _():
        own_o.start()

    own_small = run.local(small, smallg.at[z, c, f])
    run.greet(True)
    first = [run.launch(small, smallg.at[z, c, f], place.plane(k)) for k in (1, 2, 3)]
    arrive, arrive_o = run.recvs.block(4), run.recvs.block(4)
    for k in (1, 2, 3):
        run.launch_if(
            f >= 0, col.at[place.f_at(k)], colp.at[slot], (run.sends.take(), arrive(slot)),
            place.at(z, place.f_at(k), f // 2),
        )
    one = run.sends.take()
    run.launch_if(
        jnp.logical_not(mine), col.at[f], colp.at[slot], (one, arrive(slot)), place.sibling()
    )
    run.launch_if(
        jnp.logical_not(keep), rows_o, op.at[slot], (run.sends.take(), arrive_o(slot)), place.at(z, z, f // 2)
    )
    own_small.wait()
    for a in first:
        a.wait_recv()
    block = smallg.at[z, c]
    far = [run.launch(block, block, place.column(k)) for k in (1, 2, 3)]
    near = [run.launch(block, block, place.sibling())]
    for k in (1, 2, 3):
        far[k - 1].wait_recv()
        there = smallg.at[place.z_at(-k), c]
        near.append(run.launch(there, there, place.sibling()))

    for j in range(4):
        me = jnp.logical_and(f == 2 * c + j // 2, c == j % 2)
        other = jnp.logical_not(me)

        @pl.when(other)
        def _(j=j):
            remote(col.at[0], colp.at[j], (one, arrive(j)), place.sibling()).wait_recv()

        @pl.when(jnp.logical_and(other, f == z))
        def _(j=j):
            remote(rows_o, op.at[j], (one, arrive_o(j)), place.sibling()).wait_recv()

    for a in near:
        a.wait_recv()

    @pl.when(mine)
    def _():
        own.wait()

    @pl.when(keep)
    def _():
        own_o.wait()

    run.close()


class TrunkRows:
    def __init__(self, run, xb, tx):
        self.run, self.xb, self.tx = run, xb, tx

    def start(self):
        run, place = self.run, self.run.place
        self.parts = [pl.ds(0, 64), pl.ds(64, 64)]
        self.pairs = [(run.sends.take(), run.recvs.take()) for _ in range(2)]
        for q in range(2):
            run.launch_if(
                place.z == 0, self.xb.at[place.f, self.parts[q]], self.tx.at[place.f, self.parts[q]],
                self.pairs[q], place.column(1),
            )

    def pass_on(self):
        run, place = self.run, self.run.place
        self.round = []
        for q in range(2):
            block = self.tx.at[place.f, self.parts[q]]

            @pl.when(place.z > 0)
            def _():
                remote(block, block, self.pairs[q], place.column(1)).wait_recv()

            between = jnp.logical_and(place.z > 0, place.z < 3)
            run.launch_if(between, block, block, self.pairs[q], place.column(1))
            for k in (1, 2, 3):
                pair = (run.sends.take(), run.recvs.take())
                self.round.append((k, run.launch_if(place.z > 0, block, block, pair, place.plane(k))))

    def wait(self, k):
        for kk, a in self.round:
            if kk == k:
                a.wait_recv()


class KeyChain:
    def __init__(self, run, mine, slots, up, down, cs, up_out, down_out, place_in):
        self.run, self.mine, self.slots = run, mine, slots
        self.up, self.down, self.cs, self.up_out, self.down_out, self.place_in = up, down, cs, up_out, down_out, place_in

    def start(self):
        run, place = self.run, self.run.place
        z, c = place.z, place.c
        self.pairs = [[(run.sends.take(), run.recvs.take()) for _ in range(4)] for _ in range(2)]
        for j in range(4):
            total = self.mine[c, 0] * self.place_in[j, 0].astype(BF)
            for ft in range(1, 4):
                total = total + self.mine[c, ft] * self.place_in[j, ft].astype(BF)
            self.cs[j] = total
            run.launch_if(z == 1, self.cs.at[j], self.up.at[j], self.pairs[0][j], place.column(1))
            run.launch_if(z == 3, self.cs.at[j], self.down.at[j], self.pairs[1][j], place.column(-1))
        self.near = [run.launch(self.mine.at[c], self.mine.at[c], place.sibling())]

    def wait(self, which, j):
        dst = (self.up.at[j], self.down.at[j])[which]
        remote(dst, dst, self.pairs[which][j], self.run.place.column(1)).wait_recv()

    def finish(self):
        run, place = self.run, self.run.place
        z, c = place.z, place.c
        for j in range(4):

            @pl.when(z == 2)
            def _(j=j):
                self.wait(0, j)
                self.up_out[j] = self.cs[j] + self.up[j]

            run.launch_if(z == 2, self.up_out.at[j], self.up.at[j], self.pairs[0][j], place.column(1))

            @pl.when(z == 2)
            def _(j=j):
                self.wait(1, j)
                self.down_out[j] = self.cs[j] + self.down[j]

            run.launch_if(z == 2, self.down_out.at[j], self.down.at[j], self.pairs[1][j], place.column(-1))

            @pl.when(z == 2)
            def _(j=j):
                self.slots[c, j] = self.up_out[j] + self.down[j]

        for j in range(4):

            @pl.when(z == 0)
            def _(j=j):
                self.slots[c, j] = self.cs[j]

            @pl.when(z == 1)
            def _(j=j):
                self.wait(1, j)
                self.slots[c, j] = self.cs[j] + self.down[j]

            @pl.when(z == 3)
            def _(j=j):
                self.wait(0, j)
                self.slots[c, j] = self.cs[j] + self.up[j]

        self.near.append(run.launch(self.slots.at[c], self.slots.at[c], place.sibling()))
        for a in self.near:
            a.wait_recv()


class GradChain:
    def __init__(self, run, mine, near, trunk_in, up, down, up_out, down_out, total):
        self.run, self.mine, self.near, self.trunk_in = run, mine, near, trunk_in
        self.up, self.down, self.up_out, self.down_out, self.total = up, down, up_out, down_out, total

    def start(self):
        run, place = self.run, self.run.place
        self.pairs = [[(run.sends.take(), run.recvs.take()) for _ in range(4)] for _ in range(3)]
        self.a = run.launch(self.mine.at[1 - place.c], self.near, place.sibling())

    def wait(self, which, j):
        dst = (self.trunk_in, self.up, self.down)[which].at[j]
        remote(dst, dst, self.pairs[which][j], self.run.place.column(1)).wait_recv()

    def middle(self):
        run, place = self.run, self.run.place
        z, c = place.z, place.c
        self.a.wait_recv()
        near = self.near
        for kind in range(3):
            for j in range(4):
                near[kind, j] = (self.mine[c, kind, j].astype(F32) + near[kind, j].astype(F32)).astype(BF)
                if kind == 0:
                    run.launch_if(z == 3, near.at[0, j], self.trunk_in.at[j], self.pairs[0][j], place.column(-1))
                elif kind == 1:
                    run.launch_if(z == 1, near.at[1, j], self.up.at[j], self.pairs[1][j], place.column(1))
                    run.launch_if(z == 3, near.at[1, j], self.down.at[j], self.pairs[2][j], place.column(-1))

    def pass_on(self):
        run, place = self.run, self.run.place
        z = place.z
        near = self.near
        for j in range(4):
            cond = jnp.logical_or(z == 1, z == 2)

            @pl.when(cond)
            def _(j=j):
                self.wait(0, j)
                near[0, j] = (near[0, j].astype(F32) + self.trunk_in[j].astype(F32)).astype(BF)

            run.launch_if(cond, near.at[0, j], self.trunk_in.at[j], self.pairs[0][j], place.column(-1))

            @pl.when(z == 2)
            def _(j=j):
                self.wait(1, j)
                self.up_out[j] = (near[1, j].astype(F32) + self.up[j].astype(F32)).astype(BF)

            run.launch_if(z == 2, self.up_out.at[j], self.up.at[j], self.pairs[1][j], place.column(1))
        for j in range(4):

            @pl.when(z == 2)
            def _(j=j):
                self.wait(2, j)
                self.down_out[j] = (near[1, j].astype(F32) + self.down[j].astype(F32)).astype(BF)

            run.launch_if(z == 2, self.down_out.at[j], self.down.at[j], self.pairs[2][j], place.column(-1))

    def finish(self, place_in, store):
        place = self.run.place
        z = place.z
        near = self.near

        @pl.when(z == 0)
        def _():
            for j in range(4):
                self.wait(0, j)
                store(j, near[0, j].astype(F32) + self.trunk_in[j].astype(F32))

        @pl.when(z == 1)
        def _():
            for j in range(4):
                self.wait(2, j)
                self.total[j] = (near[1, j].astype(F32) + self.down[j].astype(F32)).astype(BF)

        @pl.when(z == 2)
        def _():
            for j in range(4):
                self.total[j] = (self.up_out[j].astype(F32) + self.down[j].astype(F32)).astype(BF)

        @pl.when(z == 3)
        def _():
            for j in range(4):
                self.wait(1, j)
                self.total[j] = (near[1, j].astype(F32) + self.up[j].astype(F32)).astype(BF)

        @pl.when(z > 0)
        def _():
            for ft in range(4):
                total = near[2, ft].astype(F32)
                for j in range(4):
                    total = total + self.total[j].astype(F32) * place_in[j, ft]
                store(ft, total)


def pick_parents(kp, slots, choose):
    def one(b, carry):
        for cc in range(2):
            total = slots[cc, 0] * choose[b, 0].astype(BF)
            for j in range(1, 4):
                total = total + slots[cc, j] * choose[b, j].astype(BF)
            kp[b, cc] = total
        return carry

    lax.fori_loop(0, 4, one, 0)


def all_keys(trunk, mine, kp, b, lanes):
    return jnp.concatenate(
        [trunk[:, :, :, lanes].reshape(1024, 128), mine[0, b, :, lanes], mine[1, b, :, lanes], kp[b, 0, :, lanes], kp[b, 1, :, lanes]],
        axis=0,
    )


def flat(ref):
    return ref[...].reshape(-1, ref.shape[-1])


def forward_kernel(first, *refs):
    refs = list(refs)

    def take(n):
        out = refs[:n]
        del refs[:n]
        return out

    x_ref, chunks, rows_o, rows_out, vecs, place_in, choose, pen = take(8)
    if not first:
        qkv_in, o_in = take(2)
    layer = 0 if first else 1
    vec = vecs.at[layer]
    in_c, out_c = chunks.at[layer, :, pl.ds(PACKED, WIDE)], rows_out.at[layer]
    if first:
        qkv_in, o_in = chunks.at[0, :, pl.ds(0, PACKED)], rows_o.at[0]
        qkv_next, o_next = chunks.at[1, :, pl.ds(0, PACKED)], rows_o.at[1]
    xn_ref, xb_o, qp_o, trunk_o, mine_o, kp_o, p_o, ctx_o, z1_o, hb_o, gp_o, gl_o, z2_o, win_o, wout_o = take(15)
    if first:
        wqkv_o, wo_o, wqkv_n, wo_n = take(4)
    xb, qp, trunk, mine, kp, p, ctx, z1, hb, gp, gl, z2, win, wout, wqkv, wo, heads, own, rs1_s, rs1_r, rs2_s, rs2_r = take(22)
    tx, *chain_refs = take(7)
    run = Run(*refs)
    place = run.place
    z, f, c = place.z, place.f, place.c
    launch = run.launch

    xb[f] = x_ref[...].astype(BF)
    wo[192:256, :] = jnp.zeros((64, WIDE), BF)
    if not first:
        loads = [run.local(qkv_in, wqkv), run.local(o_in, wo.at[pl.ds(0, 192)])]
    run.greet(False)
    came = [None] + [launch(xb.at[f], xb.at[f], place.plane(k)) for k in (1, 2, 3)]
    trunk_rows = TrunkRows(run, xb, tx)
    trunk_rows.start()
    m_tasks = [Spread(run, in_c, win), Spread(run, out_c, wout)]
    if first:
        a_tasks = [Spread(run, qkv_in, wqkv), SpreadOutput(run, o_in, wo)]
        for t in a_tasks:
            t.start()
        trunk_rows.pass_on()
        a_tasks[0].relay()
        a_tasks[0].finish()
    else:
        trunk_rows.pass_on()
        for a in loads:
            a.wait()
    lane = lax.broadcasted_iota(jnp.int32, (ROWS, 128), 1)
    for k in range(4):
        g = place.f_at(-k)
        if k:
            came[k].wait_recv()
        qkv = product(xb[g], flat(wqkv)) + vec[0:1, :PACKED]
        rows = pl.ds(pl.multiple_of(g * ROWS, ROWS), ROWS)
        mine[c, g] = qkv[:, 256:].astype(BF)
        scaled = qkv[:, :256] * (HEAD_DIM ** (-0.5))
        front = scaled[:, :128]
        qp[rows, 0:128] = jnp.where(lane < 64, front, 0.0).astype(BF)
        qp[rows, 128:256] = jnp.where(lane < 64, pltpu.roll(front, 64, 1), 0.0).astype(BF)
        qp[rows, 256:384] = scaled[:, 128:].astype(BF)
    chain = KeyChain(run, mine, *chain_refs, place_in)
    chain.start()

    @pl.when(z == 0)
    def _():
        trunk[c] = mine[c]

    @pl.when(z > 0)
    def _():
        for k in range(4):
            g = place.f_at(-k)
            if k:
                trunk_rows.wait(k)
            keys = product(tx[g], flat(wqkv)[:, 256:]) + vec[0:1, 256:PACKED]
            trunk[c, g] = keys.astype(BF)

    trunk_near = launch(trunk.at[c], trunk.at[c], place.sibling())
    run.save(xb, xb_o)
    run.save(qp, qp_o)
    chain.finish()
    trunk_near.wait_recv()
    late_tasks = m_tasks
    for t in late_tasks:
        t.start(z > 0)
    pick_parents(kp, chain.slots, choose)
    run.save(kp, kp_o)
    run.save(trunk, trunk_o)
    run.save(mine, mine_o)
    if first:
        a_tasks[1].relay()

    def attend(i, carry):
        h, b = i // 4, lax.rem(i, 4)
        lanes = pl.ds(pl.multiple_of(h * 128, 128), 128)
        rows = pl.ds(pl.multiple_of(b * ROWS, ROWS), ROWS)
        keys = all_keys(trunk, mine, kp, b, lanes)
        s = product_nt(qp[rows, lanes], keys)
        s = jnp.concatenate(
            [s[:, :1024], s[:, 1024:1280] + pen[4 + b], s[:, 1280:] + pen[b]], axis=1
        )
        e = jnp.exp(s - jnp.max(s, axis=1, keepdims=True))
        pb = (e * (1.0 / jnp.sum(e, axis=1, keepdims=True))).astype(BF)
        p[h, b] = pb
        heads[h, b] = product(pb, keys)
        return carry

    lax.fori_loop(0, 12, attend, 0)
    run.save(p, p_o)
    if first:
        a_tasks[1].finish()
    back = [None]
    for k in (1, 2, 3, 0):
        g = place.f_at(-k)
        ctx[g, :, 0:128] = jnp.where(lane < 64, pltpu.roll(heads[0, g], 64, 1), heads[1, g]).astype(BF)
        ctx[g, :, 128:256] = jnp.where(lane < 64, pltpu.roll(heads[2, g], 64, 1), 0.0).astype(BF)
        part = product(ctx[g], wo[...])
        if k:
            rs1_s[k - 1] = part.astype(BF)
            back.append(launch(rs1_s.at[k - 1], rs1_r.at[k - 1], place.plane(-k)))
        else:
            own[...] = part
    run.save(ctx, ctx_o)
    for k in (1, 2, 3):
        back[k].wait_recv()
    for t in late_tasks:
        t.start(z == 0)
    total = own[...] + rs1_r[0].astype(F32) + rs1_r[1].astype(F32) + rs1_r[2].astype(F32)
    zz = x_ref[...].astype(F32) + total + vec[1:2, :]
    z1[...] = zz
    run.save(z1, z1_o)
    hidden = norm_rows(zz, vec[2:3, :], vec[3:4, :])
    hb[f] = hidden.astype(BF)
    came = [None] + [launch(hb.at[f], hb.at[f], place.plane(k)) for k in (1, 2, 3)]
    back = [None]
    for t in m_tasks:
        t.relay()
    if first:
        n_tasks = [Spread(run, qkv_next, wqkv_n), SpreadOutput(run, o_next, wo_n)]
        for t in n_tasks:
            t.start()
    for t in m_tasks:
        t.finish()
    for k in range(4):
        g = place.f_at(-k)
        if k:
            came[k].wait_recv()
        u = product(hb[g], flat(win)) + vec[4:5, :]
        cdf = 0.5 * (1.0 + lax.erf(u * (0.5 ** 0.5)))
        gp[g] = cdf + u * jnp.exp(-0.5 * u * u) * 0.3989422804014327
        low = (u * cdf).astype(BF)
        gl[g] = low
        part = product(low, flat(wout))
        if k:
            rs2_s[k - 1] = part.astype(BF)
            back.append(launch(rs2_s.at[k - 1], rs2_r.at[k - 1], place.plane(-k)))
        else:
            own[...] = part
    run.save(hb, hb_o)
    run.save(gp, gp_o)
    run.save(gl, gl_o)
    run.save(win, win_o)
    run.save(wout, wout_o)
    if first:
        run.save(wqkv, wqkv_o)
        run.save(wo.at[pl.ds(0, 192)], wo_o)
    for k in (1, 2, 3):
        back[k].wait_recv()
    total = own[...] + rs2_r[0].astype(F32) + rs2_r[1].astype(F32) + rs2_r[2].astype(F32)
    zz = norm_rows(z1[...], vec[2:3, :], vec[3:4, :]) + total + vec[5:6, :]
    z2[...] = zz
    run.save(z2, z2_o)
    xn_ref[...] = norm_rows(zz, vec[6:7, :], vec[7:8, :]).astype(xn_ref.dtype)
    if first:
        for t in n_tasks:
            t.relay()
        for t in n_tasks:
            t.finish()
    run.close()


def backward_kernel(extra, *refs):
    refs = list(refs)

    def take(n):
        out = refs[:n]
        del refs[:n]
        return out

    dy_ref, vecs, place_in, choose, z2 = take(5)
    vec = vecs.at[0 if extra else 1]
    late_in = take(15)
    if extra:
        pq_in, pk_in, dvec_in = take(3)
    dx_ref, din_o, dout_o, do_o = take(4)
    if extra:
        dq_n, dk_n, dq_o, dk_o, sm_o = take(5)
    else:
        pq, pk, dvec_o = take(3)
    late = take(15)
    wout, gp, win, gl, hb, z1, wo, ctx, trunk, mine, kp, qp, p, xb, wqkv = late
    (
        df, du, da, dctx, dqf, dqkv, dz, dz1, dkt, dself, dpar, tgt, own, rs1_s, rs1_r, rs2_s, rs2_r,
    ) = take(17)
    chain_refs = take(7)
    pin, nin, fin, tin, pout, nout, fout, po, no, fo, to = take(11)
    if extra:
        pq, pk, dvec_o = take(3)
        nq, fq, tq, nk, fk, tk, nq2, fq2, tq2, nk2, fk2, tk2, sm, sm_a, sm_b, sm_v = take(16)
    run = Run(*refs)
    place = run.place
    z, f, c = place.z, place.f, place.c
    launch = run.launch
    loads = []
    for n, (src, dst) in enumerate(zip(late_in, late)):
        loads.append(run.local(src, dst.at[pl.ds(0, 192)] if n == 6 else dst))
    wo[192:256, :] = jnp.zeros((64, WIDE), BF)

    grad, dgain, dshift = norm_rows_back(z2[...], vec[6:7, :], dy_ref[...].astype(F32))
    dvec_o[6:7, :] = dgain
    dvec_o[7:8, :] = dshift
    dz[...] = grad
    low = grad.astype(BF)
    df[f] = low
    dvec_o[5:6, :] = jnp.sum(low.astype(F32), axis=0, keepdims=True)
    run.greet(True)
    came = [None] + [launch(df.at[f], df.at[f], place.plane(k)) for k in (1, 2, 3)]
    a_tasks = []
    if extra:
        a_tasks = [Collect(run, pq_in, nq, fq, tq, dq_n), Collect(run, pk_in, nk, fk, tk, dk_n)]
    for t in a_tasks:
        t.start()
    back = [None]
    bias = jnp.zeros((1, WIDE), F32)
    for n in range(3):
        loads[n].wait()
    for k in range(4):
        g = place.f_at(-k)
        if k:
            came[k].wait_recv()
        low = (product_nt(df[g], flat(wout)) * gp[g]).astype(BF)
        du[g] = low
        bias = bias + jnp.sum(low.astype(F32), axis=0, keepdims=True)
        part = product_nt(low, flat(win))
        if k:
            rs1_s[k - 1] = part.astype(BF)
            back.append(launch(rs1_s.at[k - 1], rs1_r.at[k - 1], place.plane(-k)))
        else:
            own[...] = part
            for t in a_tasks:
                t.middle()
    dvec_o[4:5, :] = bias
    m_tasks = [Collect(run, pin, nin, fin, tin, din_o), Collect(run, pout, nout, fout, None, dout_o)]
    o_task = CollectOutput(run, po, no, fo, to, do_o)

    def split_rows(dst, left, right, i):
        lanes = pl.ds(pl.multiple_of(i * 384, 128), 384)
        value = product_tn(left[:, :, lanes].reshape(512, 384), right).astype(BF)
        for zz in range(2):
            for cc in range(2):
                at = (2 * zz + cc) * 96
                dst[cc, 2 * i + zz] = value[at : at + 96, :]

    def ffn_grads(i, carry):
        split_rows(pout, gl, flat(df), i)
        split_rows(pin, hb, flat(du), i)
        return carry

    for n in range(3, 5):
        loads[n].wait()
    lax.fori_loop(0, 2, ffn_grads, 0)
    for t in m_tasks:
        t.start()
    for k in (1, 2, 3):
        back[k].wait_recv()
    up = dz[...] + own[...] + rs1_r[0].astype(F32) + rs1_r[1].astype(F32) + rs1_r[2].astype(F32)
    loads[5].wait()
    grad, dgain, dshift = norm_rows_back(z1[...], vec[2:3, :], up)
    dvec_o[2:3, :] = dgain
    dvec_o[3:4, :] = dshift
    dz1[...] = grad
    low = grad.astype(BF)
    da[f] = low
    dvec_o[1:2, :] = jnp.sum(low.astype(F32), axis=0, keepdims=True)
    came = [None] + [launch(da.at[f], da.at[f], place.plane(k)) for k in (1, 2, 3)]
    for t in a_tasks:
        t.end()
    for t in m_tasks:
        t.middle()
    dkt[...] = jnp.zeros_like(dkt)
    lane = lax.broadcasted_iota(jnp.int32, (ROWS, 128), 1)
    for a in loads[6:]:
        a.wait()
    for k in range(4):
        g = place.f_at(-k)
        rows = pl.ds(pl.multiple_of(g * ROWS, ROWS), ROWS)
        if k:
            came[k].wait_recv()
        packed = product_nt(da[g], wo[...])
        ahead, after = packed[:, :128], packed[:, 128:]
        dctx[rows, 0:128] = jnp.where(lane < 64, 0.0, pltpu.roll(ahead, 64, 1)).astype(BF)
        dctx[rows, 128:256] = jnp.where(lane < 64, 0.0, ahead).astype(BF)
        dctx[rows, 256:384] = jnp.where(lane < 64, 0.0, pltpu.roll(after, 64, 1)).astype(BF)
    value = product_tn(flat(ctx), flat(da)).astype(BF)
    for cc in range(2):
        po[cc] = value[96 * cc : 96 * (cc + 1), :]
    o_task.start()
    o_task.middle()

    def attend(i, carry):
        h, b = i // 4, lax.rem(i, 4)
        lanes = pl.ds(pl.multiple_of(h * 128, 128), 128)
        rows = pl.ds(pl.multiple_of(b * ROWS, ROWS), ROWS)
        keys = all_keys(trunk, mine, kp, b, lanes)
        q, g = qp[rows, lanes], dctx[rows, lanes]
        low = p[h, b]
        pf = low.astype(F32)
        dp = product_nt(g, keys)
        t = pf * dp
        ds = (t - pf * jnp.sum(t, axis=1, keepdims=True)).astype(BF)
        dqf[h, rows, :] = product(ds, keys) * (HEAD_DIM ** (-0.5))
        dkv = product_tn(jnp.concatenate([ds, low], axis=0), jnp.concatenate([q, g], axis=0))
        dkt[:, lanes] += dkv[:1024]
        dself[b, :, lanes] = dkv[1024:1280]
        dpar[b, :, lanes] = dkv[1280:]
        return carry

    lax.fori_loop(0, 12, attend, 0)
    for cc in range(2):
        for j in range(4):
            at = cc * 512 + j * ROWS
            tgt[cc, 0, j] = dkt[at : at + ROWS, :].astype(BF)

    def scatter(j, carry):
        for cc in range(2):
            half = slice(cc * ROWS, (cc + 1) * ROWS)
            total = dpar[0, half, :] * choose[0, j]
            for b in range(1, 4):
                total = total + dpar[b, half, :] * choose[b, j]
            tgt[cc, 1, j] = total.astype(BF)
            tgt[cc, 2, j] = dself[j, half, :].astype(BF)
        return carry

    lax.fori_loop(0, 4, scatter, 0)
    chain = GradChain(run, tgt, *chain_refs)
    chain.start()
    for g in range(4):
        rows = slice(g * ROWS, (g + 1) * ROWS)
        ahead = jnp.where(lane < 64, dqf[0, rows, :], pltpu.roll(dqf[1, rows, :], 64, 1))
        dqkv[g, :, 0:128] = ahead.astype(BF)
        dqkv[g, :, 128:256] = jnp.where(lane < 64, dqf[2, rows, :], 0.0).astype(BF)
    chain.middle()
    for t in m_tasks:
        t.end()
    chain.pass_on()

    def q_grads(i, carry):
        split_rows(pq, xb, dqkv[:, :, :256].reshape(512, 256), i)
        return carry

    lax.fori_loop(0, 2, q_grads, 0)
    end_tasks = []
    if extra:
        end_tasks = [Collect(run, pk, nk2, fk2, tk2, dk_o), Collect(run, pq, nq2, fq2, tq2, dq_o)]
        end_tasks[1].start()

    def store(ft, value):
        dqkv[ft, :, 256:] = value.astype(BF)

    chain.finish(place_in, store)

    def k_grads(i, carry):
        split_rows(pk, xb, dqkv[:, :, 256:].reshape(512, SLICE), i)
        return carry

    lax.fori_loop(0, 2, k_grads, 0)
    if extra:
        end_tasks[0].start()
        end_tasks[1].middle()
        end_tasks[0].middle()
    back = [None]
    for k in (1, 2, 3, 0):
        g = place.f_at(-k)
        part = product_nt(dqkv[g], flat(wqkv))
        if k:
            rs2_s[k - 1] = part.astype(BF)
            back.append(launch(rs2_s.at[k - 1], rs2_r.at[k - 1], place.plane(-k)))
        else:
            own[...] = part

    sums = jnp.sum(flat(dqkv).astype(F32), axis=0, keepdims=True)
    dvec_o[0:1, :] = jnp.concatenate([sums, jnp.zeros((1, WIDE - PACKED), F32)], axis=1)
    if extra:
        sm[0:8, :] = dvec_o[...]
        sm[8:16, :] = dvec_in[...]
        sm_near = launch(sm, sm_a, place.sibling())
        sm_near.wait_recv()
        sm_a[...] = sm[...] + sm_a[...]
        sm_far = [launch(sm_a, sm_b.at[k - 1], place.column(k)) for k in (1, 2, 3)]
    o_task.end()
    for t in a_tasks:
        t.last()
    for k in (1, 2, 3):
        back[k].wait_recv()
    total = dz1[...] + own[...] + rs2_r[0].astype(F32) + rs2_r[1].astype(F32) + rs2_r[2].astype(F32)
    dx_ref[...] = total.astype(dx_ref.dtype)
    if extra:
        for t in end_tasks:
            t.end()
        for a in sm_far:
            a.wait_recv()
        sm_v[...] = sm_a[...] + sm_b[0] + sm_b[1] + sm_b[2]
        sm_last = [launch(sm_v, sm_o.at[f], place.plane(k)) for k in (1, 2, 3)]
        sm_o[f] = sm_v[...]
        for a in sm_last:
            a.wait_recv()
    for t in m_tasks + [o_task] + end_tasks:
        t.last()
    run.close()


ANY = pl.BlockSpec(memory_space=pl.ANY)
VM = pl.BlockSpec(memory_space=pltpu.VMEM)
SM = pl.BlockSpec(memory_space=pltpu.SMEM)
LIMIT = 60 * 1024 * 1024
SEMS = (160, 160, 32)


def shape(*dims, dtype=BF):
    return jax.ShapeDtypeStruct(dims, dtype)


def call(kernel, number, outs, out_specs, in_specs, scratch, args, flops):
    return pl.pallas_call(
        kernel,
        out_shape=tuple(outs),
        in_specs=in_specs,
        out_specs=tuple(out_specs),
        scratch_shapes=[pltpu.VMEM(s.shape, s.dtype) for s in scratch]
        + [pltpu.SemaphoreType.DMA((n,)) for n in SEMS],
        compiler_params=pltpu.CompilerParams(
            collective_id=number, has_side_effects=True, vmem_limit_bytes=LIMIT
        ),
        cost_estimate=pl.CostEstimate(flops=flops, bytes_accessed=20000000, transcendentals=0),
    )(*args)


def column_parts(query, key, value, inner):
    n = query.shape[0] * query.shape[1]
    q = query.reshape(n, 4, 3, 64)
    q = jnp.pad(q, ((0, 0), (0, 0), (0, 1), (0, 0))).reshape(n, 4, 256)
    kv = jnp.stack([key.reshape(n, 4, 3, 64), value.reshape(n, 4, 3, 64)], axis=3).reshape(n, 4, 384)
    up = inner.reshape(n, 4, 4, 192).transpose(0, 2, 1, 3).reshape(n, 4, WIDE)
    return jnp.concatenate([q, kv, up], axis=2).transpose(1, 0, 2)


LOCAL = shape(ROWS, WIDE, dtype=F32)
FULL = shape(4, ROWS, WIDE)
PIECE = shape(3, ROWS, WIDE)
QKV = shape(4, 2, 96, PACKED)
BIG = shape(4, 2, 96, WIDE)
OUTPUT = shape(192, WIDE)
HALVES = shape(2, 4, ROWS, SLICE)
QUARTERS = shape(4, ROWS, SLICE)
SAVED = (
    FULL, shape(512, SLICE), HALVES, HALVES, shape(4, 2, ROWS, SLICE), shape(3, 4, ROWS, NKEYS),
    shape(4, ROWS, 256), LOCAL, FULL, shape(4, ROWS, WIDE, dtype=F32), FULL, LOCAL,
)


def forward_layer(first, state, chunks, rows_o, rows_out, vecs, place_in, choose, pen, here):
    outs = (LOCAL if first else shape(ROWS, WIDE),) + SAVED + (BIG, BIG) + ((QKV, OUTPUT, QKV, OUTPUT) if first else ())
    got = call(
        lambda *refs: forward_kernel(first, *refs), 1 if first else 2, outs, (VM,) + (ANY,) * (len(outs) - 1),
        [VM] + [ANY] * 3 + [VM] + [SM] * 3 + [ANY] * len(here),
        list(SAVED)
        + [BIG, BIG, QKV, shape(256, WIDE), shape(3, 4, ROWS, 128, dtype=F32), LOCAL]
        + [PIECE] * 4 + [FULL, HALVES] + [QUARTERS] * 5,
        (state, chunks, rows_o, rows_out, vecs, place_in, choose, pen) + tuple(here), 3 * 10**9,
    )
    return got[0], got[1:13], got[13:]


def collect_scratch(columns, rows):
    return [shape(4, 96, columns), shape(3, 96, columns)] + ([shape(96, columns, dtype=F32)] if rows else [])


OUT_SCRATCH = [shape(96, WIDE), shape(4, 96, WIDE), shape(96, WIDE, dtype=F32)]
PARTS = (shape(2, 4, 96, 256), shape(2, 4, 96, SLICE))
SHARES = (shape(4, 24, 256, dtype=F32), shape(4, 24, SLICE, dtype=F32))


def backward_layer(upstream, weights, vec, place_in, choose, saved, before):
    wqkv, wo, win, wout = weights
    xb, qp, trunk, mine, kp, p, ctx, z1, hb, gp, gl, z2 = saved
    keys = shape(4, 256, SLICE, dtype=F32)
    extra = len(before) > 0
    sums, sums2 = shape(8, WIDE, dtype=F32), shape(16, WIDE, dtype=F32)
    outs = (shape(ROWS, WIDE) if extra else LOCAL,)
    outs += (shape(4, 24, WIDE, dtype=F32), shape(96, WIDE, dtype=F32), shape(24, WIDE, dtype=F32))
    outs += SHARES + SHARES + (shape(4, 16, WIDE, dtype=F32),) if extra else PARTS + (sums,)
    scratch = [BIG, SAVED[9], BIG, FULL, FULL, LOCAL, shape(256, WIDE), SAVED[6], HALVES, HALVES, SAVED[4], SAVED[1], SAVED[5], FULL, QKV] + [
        FULL, FULL, FULL, shape(512, SLICE), shape(3, 512, 128, dtype=F32), shape(4, ROWS, PACKED), LOCAL, LOCAL,
        shape(1024, SLICE, dtype=F32), keys, keys, shape(2, 3, 4, ROWS, SLICE), LOCAL, PIECE, PIECE, PIECE, PIECE,
        shape(3, 4, ROWS, SLICE),
    ] + [QUARTERS] * 6
    part = shape(2, 4, 96, WIDE)
    scratch += [part] + collect_scratch(WIDE, True) + [part] + collect_scratch(WIDE, False)
    scratch += [shape(2, 96, WIDE)] + OUT_SCRATCH
    if extra:
        scratch += list(PARTS) + [sums]
        scratch += (collect_scratch(256, True) + collect_scratch(SLICE, True)) * 1
        scratch += collect_scratch(256, True) + collect_scratch(SLICE, True)
        scratch += [sums2, sums2, shape(3, 16, WIDE, dtype=F32), sums2]
    return call(
        lambda *refs: backward_kernel(extra, *refs), 4 if extra else 3, outs, (VM,) * len(outs),
        [VM] * 2 + [SM] * 2 + [VM] + [ANY] * 15 + [VM] * len(before), scratch,
        (upstream, vec, place_in, choose, z2, wout, gp, win, gl, hb, z1, wo, ctx, trunk, mine, kp, qp, p, xb, wqkv)
        + tuple(before),
        6 * 10**9,
    )


def slice_body(
    activations, query_weight, query_bias, key_weight, value_weight, value_bias, output_weight, output_bias,
    first_gain, first_shift, inner_weight, inner_bias, outer_weight, outer_bias, second_gain, second_shift,
    cotangent, parents, segments,
):
    place = Place()
    z, f, c = place.z, place.f, place.c
    col = column_parts(query_weight, key_weight, value_weight, inner_weight)
    vectors = (query_bias, value_bias, output_bias, first_gain, first_shift, outer_bias, second_gain, second_shift)
    label = jnp.broadcast_to(segments[:1].astype(BF)[None], (2, 1))
    small = jnp.concatenate(vectors + (inner_bias, label), axis=1)
    small = jnp.pad(small, ((0, 14), (0, 384 - small.shape[1])))
    colp, op, smallg = call(
        exchange_kernel, 0, (shape(4, 48, 1408), shape(4, 48, WIDE), shape(4, 2, 4, 16, 384)), (ANY,) * 3, [ANY] * 3,
        [], (col, output_weight.reshape(48, WIDE), small), 1000,
    )
    colp = colp.reshape(4, 2, 24, 1408).transpose(1, 0, 2, 3).reshape(2, 96, 1408)
    op = op.reshape(4, 2, 24, WIDE).transpose(1, 0, 2, 3).reshape(2, 96, WIDE)
    small = smallg[:, :, :, :2].transpose(3, 0, 2, 1, 4).astype(F32)
    parts = [small[..., i * 24 : (i + 1) * 24].reshape(2, WIDE) for i in range(8)]
    q_all, v_all, o_all, g1, s1, out_all, g2, s2 = parts
    in_mine = lax.dynamic_index_in_dim(small[..., 192:288], f, 2, keepdims=False).reshape(2, WIDE)
    q_mine = lax.dynamic_slice_in_dim(q_all, 192 * f, 192, 1)
    v_mine = lax.dynamic_slice_in_dim(v_all, 192 * f, 192, 1).reshape(2, 3, 64)
    kv_mine = jnp.pad(v_mine, ((0, 0), (0, 0), (64, 0))).reshape(2, SLICE)
    qkv_mine = jnp.pad(jnp.concatenate([q_mine, jnp.zeros((2, 64), F32), kv_mine], axis=1), ((0, 0), (0, WIDE - PACKED)))
    vecs = jnp.stack([qkv_mine, o_all, g1, s1, in_mine, out_all, g2, s2], axis=1)

    labels = small[0, :, :, 0, 288].reshape(16).astype(jnp.int32)
    above = lookup_rows(labels, parents)
    order = jnp.arange(16, dtype=jnp.int32)
    branch = jnp.logical_and(above == labels[0], order >= 4)
    slot = jnp.where(branch, jnp.sum((branch[:, None] & (order[:, None] < order[None, :])).astype(jnp.int32), axis=0), 4)
    in_slot = slot[None, :] == jnp.arange(4, dtype=jnp.int32)[:, None]
    place_in = lax.dynamic_slice_in_dim(in_slot.astype(F32), 4 * z, 4, 1)
    parent = lax.dynamic_slice_in_dim(above, 4 * z, 4, 0)
    match = parent[:, None, None] == jnp.where(in_slot, labels[None, :], -1)[None]
    choose = jnp.any(match, axis=2).astype(F32)
    pen = jnp.concatenate(
        [jnp.where(jnp.any(match, axis=(1, 2)), 0.0, MASKED), jnp.where(z > 0, jnp.zeros((4,), F32), MASKED)]
    ).astype(F32)

    shared = (colp, op, outer_weight, vecs, place_in, choose, pen)
    state, kept0, (win0, wout0, wqkv0, wo0, wqkv1, wo1) = forward_layer(True, activations, *shared, ())
    outcome, kept1, (win1, wout1) = forward_layer(False, state, *shared, (wqkv1, wo1))
    upstream, din1, dout1, do1, pq, pk, dvec1 = backward_layer(
        cotangent, (wqkv1, wo1, win1, wout1), vecs, place_in, choose, kept1, ()
    )
    upstream, din0, dout0, do0, dq1, dk1, dq0, dk0, rsm = backward_layer(
        upstream, (wqkv0, wo0, win0, wout0), vecs, place_in, choose, kept0, (pq, pk, dvec1)
    )
    dq = jnp.stack([dq0, dq1]).transpose(0, 2, 1, 3)[..., :192].reshape(2, 24, WIDE)
    dkv = jnp.stack([dk0, dk1]).transpose(0, 2, 1, 3).reshape(2, 24, 4, 3, 2, 64)
    dk = dkv[..., 0, :].reshape(2, 24, WIDE)
    dv = dkv[..., 1, :].reshape(2, 24, WIDE)
    dinner = jnp.stack([din0, din1]).reshape(2, 4, 24, 4, 192).transpose(0, 2, 3, 1, 4).reshape(2, 24, 3072)
    rsm = rsm.reshape(4, 2, 8, WIDE)
    sums = jnp.sum(rsm, axis=0)
    dqb = rsm[:, :, 0, :192].transpose(1, 0, 2).reshape(2, WIDE)
    dvb = rsm[:, :, 0, 256:640].reshape(4, 2, 3, 2, 64)[:, :, :, 1].transpose(1, 0, 2, 3).reshape(2, WIDE)
    rows = jnp.stack([dqb, dvb, sums[:, 1], sums[:, 2], sums[:, 3], sums[:, 5], sums[:, 6], sums[:, 7]])
    rows = lax.dynamic_slice_in_dim(rows, 24 * (8 * z + 2 * f + c), 24, 2)
    dib = lax.dynamic_index_in_dim(rsm[:, :, 4], f, 0, keepdims=False)
    dib = lax.dynamic_slice_in_dim(dib, 96 * (2 * z + c), 96, 1)
    return (
        outcome, upstream, dq, rows[0], dk, dv, rows[1], jnp.stack([do0, do1]), rows[2], rows[3], rows[4],
        dinner, dib, jnp.stack([dout0, dout1]), rows[5], rows[6], rows[7],
    )


def solution(mesh):
    placed = (
        P("fsdp", None),
        P(None, "fsdp", None),
        P(None, "fsdp"),
        P(None, "fsdp", None),
        P(None, "fsdp", None),
        P(None, "fsdp"),
        P(None, "fsdp", None),
        P(None, "fsdp"),
        P(None, "fsdp"),
        P(None, "fsdp"),
        P(None, "fsdp", None),
        P(None, "fsdp"),
        P(None, "fsdp", None),
        P(None, "fsdp"),
        P(None, "fsdp"),
        P(None, "fsdp"),
        P("fsdp", None),
        P(),
        P("fsdp"),
    )
    return jax.shard_map(
        slice_body if mesh.shape["fsdp"] == 32 else body,
        mesh=mesh,
        in_specs=placed,
        out_specs=(
            P("fsdp", None),
            P("fsdp", None),
            P(None, "fsdp", None),
            P(None, "fsdp"),
            P(None, "fsdp", None),
            P(None, "fsdp", None),
            P(None, "fsdp"),
            P(None, "fsdp", None),
            P(None, "fsdp"),
            P(None, "fsdp"),
            P(None, "fsdp"),
            P(None, "fsdp", None),
            P(None, "fsdp"),
            P(None, "fsdp", None),
            P(None, "fsdp"),
            P(None, "fsdp"),
            P(None, "fsdp"),
        ),
        check_vma=False,
    )
```

```python
import jax
import jax.numpy as jnp
from jax import lax
from jax.experimental import pallas as pl
from jax.experimental.pallas import tpu as pltpu
from jax.sharding import PartitionSpec as P

HEADS = 12
HEAD_DIM = 64
LAYERS = 2
TREE_LEN = 4096


EPSILON = 1e-06
MASKED = -1000000000.0


def partner_2(shard, axis, stride):
    return lax.ppermute(shard, axis, [(i, i ^ 1 << stride) for i in range(lax.axis_size(axis))])


def as_sent(shard):
    return jax.tree.map(lambda a: a.astype(jnp.bfloat16) if a.dtype == jnp.float32 else a, shard)


def product(a, b):
    return jnp.dot(a, b, preferred_element_type=jnp.float32)


def product_tn(a, b):
    return lax.dot_general(a, b, (((0,), (0,)), ((), ())), preferred_element_type=jnp.float32)


def product_nt(a, b):
    return lax.dot_general(a, b, (((1,), (1,)), ((), ())), preferred_element_type=jnp.float32)


def exact_gelu(u):
    return jax.nn.gelu(u, approximate=False)


def layer_norm(z, gain_vec, shift_vec):
    centre = z - jnp.mean(z, axis=-1, keepdims=True)
    scaled = centre * lax.rsqrt(jnp.mean(centre * centre, axis=-1, keepdims=True) + EPSILON)
    return scaled * gain_vec.astype(jnp.float32) + shift_vec.astype(jnp.float32)


def norm_backward(z, gain_vec, upstream):
    centre = z - jnp.mean(z, axis=-1, keepdims=True)
    invert = lax.rsqrt(jnp.mean(centre * centre, axis=-1, keepdims=True) + EPSILON)
    scaled = centre * invert
    weighted = upstream * gain_vec.astype(jnp.float32)
    inner = invert * (
        weighted
        - jnp.mean(weighted, axis=-1, keepdims=True)
        - scaled * jnp.mean(weighted * scaled, axis=-1, keepdims=True)
    )
    return (inner, jnp.sum(upstream * scaled, axis=0), jnp.sum(upstream, axis=0))


def lookup_rows(ids, parents):
    table = jnp.arange(parents.shape[0], dtype=jnp.int32)
    return jnp.sum(jnp.where(ids[:, None] == table[None, :], parents[None, :], 0), axis=1)


def join_heads(stacked):
    return stacked.transpose(1, 0, 2).reshape(stacked.shape[1], -1)


def gather_group(key_rows, value_rows, labels, position, bit_count):
    for b in range(bit_count):
        partner = partner_2((key_rows, value_rows, labels), "fsdp", b)
        upper_side = position >> b & 1 == 1
        key_rows = jnp.where(
            upper_side,
            jnp.concatenate([partner[0], key_rows]),
            jnp.concatenate([key_rows, partner[0]]),
        )
        value_rows = jnp.where(
            upper_side,
            jnp.concatenate([partner[1], value_rows]),
            jnp.concatenate([value_rows, partner[1]]),
        )
        labels = jnp.where(
            upper_side, jnp.concatenate([partner[2], labels]), jnp.concatenate([labels, partner[2]])
        )
    return (key_rows, value_rows, labels)


def sum_group(key_grad, value_grad, position, bit_count):
    for b in reversed(range(bit_count)):
        halfway = key_grad.shape[0] // 2
        upper_side = position >> b & 1 == 1
        outgoing = (
            jnp.where(upper_side, key_grad[:halfway], key_grad[halfway:]),
            jnp.where(upper_side, value_grad[:halfway], value_grad[halfway:]),
        )
        partner = partner_2((as_sent(outgoing[0]), as_sent(outgoing[1])), "fsdp", b)
        key_grad = jnp.where(upper_side, key_grad[halfway:], key_grad[:halfway]) + partner[0]
        value_grad = jnp.where(upper_side, value_grad[halfway:], value_grad[:halfway]) + partner[1]
    return (key_grad, value_grad)


def attend_forward(queries, key_rows, value_rows, allowed):
    factor = HEAD_DIM ** (-0.5)

    def one_head(j):
        start = j * HEAD_DIM
        q = lax.dynamic_slice_in_dim(queries, start, HEAD_DIM, 1)
        k = lax.dynamic_slice_in_dim(key_rows, start, HEAD_DIM, 1)
        v = lax.dynamic_slice_in_dim(value_rows, start, HEAD_DIM, 1)
        s = jnp.where(allowed, product_nt(q, k) * factor, MASKED)
        maxima = jnp.max(s, axis=1, keepdims=True)
        e = jnp.exp(s - maxima)
        totals = jnp.sum(e, axis=1, keepdims=True)
        p = (e / totals).astype(jnp.bfloat16)
        return (product(p, v), (maxima + jnp.log(totals))[:, 0])

    stacked, log_total = lax.map(one_head, jnp.arange(HEADS))
    return (join_heads(stacked), log_total)


def attend_backward(queries, key_rows, value_rows, allowed, log_total, grad_context):
    factor = HEAD_DIM ** (-0.5)

    def one_head(j):
        start = j * HEAD_DIM
        q = lax.dynamic_slice_in_dim(queries, start, HEAD_DIM, 1)
        k = lax.dynamic_slice_in_dim(key_rows, start, HEAD_DIM, 1)
        v = lax.dynamic_slice_in_dim(value_rows, start, HEAD_DIM, 1)
        g = lax.dynamic_slice_in_dim(grad_context, start, HEAD_DIM, 1)
        s = jnp.where(allowed, product_nt(q, k) * factor, MASKED)
        p = jnp.where(allowed, jnp.exp(s - log_total[j][:, None]), 0.0)
        grad_p = product_nt(g, v)
        grad_v = product_tn(p.astype(jnp.bfloat16), g)
        grad_s = (p * (grad_p - jnp.sum(p * grad_p, axis=1, keepdims=True))).astype(jnp.bfloat16)
        grad_q = product(grad_s, k) * factor
        grad_k = product_tn(grad_s, q) * factor
        return (grad_q, grad_k, grad_v)

    grad_q, grad_k, grad_v = lax.map(one_head, jnp.arange(HEADS))
    return (join_heads(grad_q), join_heads(grad_k), join_heads(grad_v))


def layer_forward(state, full, segments, parent_one, parent_two, position, bit_count):
    (
        q_weight,
        q_bias,
        k_weight,
        v_weight,
        v_bias,
        o_weight,
        o_bias,
        gain_one,
        shift_one,
        up_weight,
        up_bias,
        down_weight,
        down_bias,
        gain_two,
        shift_two,
    ) = full
    inputs = state.astype(jnp.bfloat16)
    queries = (product(inputs, q_weight) + q_bias).astype(jnp.bfloat16)
    key_local = product(inputs, k_weight).astype(jnp.bfloat16)
    value_local = (product(inputs, v_weight) + v_bias).astype(jnp.bfloat16)
    key_rows, value_rows, labels = gather_group(
        key_local, value_local, segments, position, bit_count
    )
    allowed = (
        (labels[None, :] == segments[:, None])
        | (labels[None, :] == parent_one[:, None])
        | (labels[None, :] == parent_two[:, None])
    )
    context_wide, log_total = attend_forward(queries, key_rows, value_rows, allowed)
    context = context_wide.astype(jnp.bfloat16)
    first_sum = state + product(context, o_weight) + o_bias
    hidden = layer_norm(first_sum, gain_one, shift_one)
    hidden_low = hidden.astype(jnp.bfloat16)
    pre_act = product(hidden_low, up_weight) + up_bias
    gelu_out = exact_gelu(pre_act).astype(jnp.bfloat16)
    second_sum = hidden + product(gelu_out, down_weight) + down_bias
    record = (
        inputs,
        queries,
        key_rows,
        value_rows,
        allowed,
        log_total,
        context,
        first_sum,
        hidden_low,
        pre_act,
        gelu_out,
        second_sum,
    )
    return (record, layer_norm(second_sum, gain_two, shift_two))


def layer_backward(upstream, full, record, position, bit_count):
    (
        q_weight,
        q_bias,
        k_weight,
        v_weight,
        v_bias,
        o_weight,
        o_bias,
        gain_one,
        shift_one,
        up_weight,
        up_bias,
        down_weight,
        down_bias,
        gain_two,
        shift_two,
    ) = full
    (
        inputs,
        queries,
        key_rows,
        value_rows,
        allowed,
        log_total,
        context,
        first_sum,
        hidden_low,
        pre_act,
        gelu_out,
        second_sum,
    ) = record
    grad_z2, grad_gain_two, grad_shift_two = norm_backward(second_sum, gain_two, upstream)
    grad_f = grad_z2.astype(jnp.bfloat16)
    grad_down_bias = jnp.sum(grad_f.astype(jnp.float32), axis=0)
    grad_down = product_tn(gelu_out, grad_f)
    grad_gelu = product_nt(grad_f, down_weight)
    unused_value, gelu_back = jax.vjp(exact_gelu, pre_act)
    grad_u = gelu_back(grad_gelu)[0].astype(jnp.bfloat16)
    grad_up_bias = jnp.sum(grad_u.astype(jnp.float32), axis=0)
    grad_up = product_tn(hidden_low, grad_u)
    grad_h = grad_z2 + product_nt(grad_u, up_weight)
    grad_z1, grad_gain_one, grad_shift_one = norm_backward(first_sum, gain_one, grad_h)
    grad_a = grad_z1.astype(jnp.bfloat16)
    grad_o_bias = jnp.sum(grad_a.astype(jnp.float32), axis=0)
    grad_o = product_tn(context, grad_a)
    grad_context = product_nt(grad_a, o_weight).astype(jnp.bfloat16)
    grad_q, key_grad, value_grad = attend_backward(
        queries, key_rows, value_rows, allowed, log_total, grad_context
    )
    key_grad, value_grad = sum_group(key_grad, value_grad, position, bit_count)
    q_low = grad_q.astype(jnp.bfloat16)
    k_low = key_grad.astype(jnp.bfloat16)
    v_low = value_grad.astype(jnp.bfloat16)
    grad_x = (
        grad_z1
        + product_nt(q_low, q_weight)
        + product_nt(k_low, k_weight)
        + product_nt(v_low, v_weight)
    )
    terms = (
        product_tn(inputs, q_low),
        jnp.sum(q_low.astype(jnp.float32), axis=0),
        product_tn(inputs, k_low),
        product_tn(inputs, v_low),
        jnp.sum(v_low.astype(jnp.float32), axis=0),
        grad_o,
        grad_o_bias,
        grad_gain_one,
        grad_shift_one,
        grad_up,
        grad_up_bias,
        grad_down,
        grad_down_bias,
        grad_gain_two,
        grad_shift_two,
    )
    return (grad_x, terms)


def stack_layers(groups, n):
    return jnp.stack([g[n] for g in groups])


def body(
    activations,
    query_weight,
    query_bias,
    key_weight,
    value_weight,
    value_bias,
    output_weight,
    output_bias,
    first_gain,
    first_shift,
    inner_weight,
    inner_bias,
    outer_weight,
    outer_bias,
    second_gain,
    second_shift,
    cotangent,
    parents,
    segments,
):
    position = lax.axis_index("fsdp")
    bit_count = (TREE_LEN // activations.shape[0]).bit_length() - 1
    parent_one = lookup_rows(segments, parents)
    parent_two = lookup_rows(parent_one, parents)
    state = activations.astype(jnp.float32)
    saved = []
    kept_weights = []
    for i in range(LAYERS):
        full = (
            lax.all_gather(query_weight[i], "fsdp", axis=0, tiled=True),
            lax.all_gather(query_bias[i], "fsdp", axis=0, tiled=True),
            lax.all_gather(key_weight[i], "fsdp", axis=0, tiled=True),
            lax.all_gather(value_weight[i], "fsdp", axis=0, tiled=True),
            lax.all_gather(value_bias[i], "fsdp", axis=0, tiled=True),
            lax.all_gather(output_weight[i], "fsdp", axis=0, tiled=True),
            lax.all_gather(output_bias[i], "fsdp", axis=0, tiled=True),
            lax.all_gather(first_gain[i], "fsdp", axis=0, tiled=True),
            lax.all_gather(first_shift[i], "fsdp", axis=0, tiled=True),
            lax.all_gather(inner_weight[i], "fsdp", axis=0, tiled=True),
            lax.all_gather(inner_bias[i], "fsdp", axis=0, tiled=True),
            lax.all_gather(outer_weight[i], "fsdp", axis=0, tiled=True),
            lax.all_gather(outer_bias[i], "fsdp", axis=0, tiled=True),
            lax.all_gather(second_gain[i], "fsdp", axis=0, tiled=True),
            lax.all_gather(second_shift[i], "fsdp", axis=0, tiled=True),
        )
        kept_weights.append(full)
        record, state = layer_forward(
            state, full, segments, parent_one, parent_two, position, bit_count
        )
        saved.append(record)
    outcome = state.astype(jnp.bfloat16)
    upstream = cotangent.astype(jnp.float32)
    layer_grads = [None] * LAYERS
    for i in reversed(range(LAYERS)):
        full = (
            lax.all_gather(query_weight[i], "fsdp", axis=0, tiled=True),
            lax.all_gather(query_bias[i], "fsdp", axis=0, tiled=True),
            lax.all_gather(key_weight[i], "fsdp", axis=0, tiled=True),
            lax.all_gather(value_weight[i], "fsdp", axis=0, tiled=True),
            lax.all_gather(value_bias[i], "fsdp", axis=0, tiled=True),
            lax.all_gather(output_weight[i], "fsdp", axis=0, tiled=True),
            lax.all_gather(output_bias[i], "fsdp", axis=0, tiled=True),
            lax.all_gather(first_gain[i], "fsdp", axis=0, tiled=True),
            lax.all_gather(first_shift[i], "fsdp", axis=0, tiled=True),
            lax.all_gather(inner_weight[i], "fsdp", axis=0, tiled=True),
            lax.all_gather(inner_bias[i], "fsdp", axis=0, tiled=True),
            lax.all_gather(outer_weight[i], "fsdp", axis=0, tiled=True),
            lax.all_gather(outer_bias[i], "fsdp", axis=0, tiled=True),
            lax.all_gather(second_gain[i], "fsdp", axis=0, tiled=True),
            lax.all_gather(second_shift[i], "fsdp", axis=0, tiled=True),
        )
        upstream, terms = layer_backward(upstream, full, saved[i], position, bit_count)
        layer_grads[i] = (
            lax.psum_scatter(terms[0], "fsdp", scatter_dimension=0, tiled=True),
            lax.psum_scatter(terms[1], "fsdp", scatter_dimension=0, tiled=True),
            lax.psum_scatter(terms[2], "fsdp", scatter_dimension=0, tiled=True),
            lax.psum_scatter(terms[3], "fsdp", scatter_dimension=0, tiled=True),
            lax.psum_scatter(terms[4], "fsdp", scatter_dimension=0, tiled=True),
            lax.psum_scatter(terms[5], "fsdp", scatter_dimension=0, tiled=True),
            lax.psum_scatter(terms[6], "fsdp", scatter_dimension=0, tiled=True),
            lax.psum_scatter(terms[7], "fsdp", scatter_dimension=0, tiled=True),
            lax.psum_scatter(terms[8], "fsdp", scatter_dimension=0, tiled=True),
            lax.psum_scatter(terms[9], "fsdp", scatter_dimension=0, tiled=True),
            lax.psum_scatter(terms[10], "fsdp", scatter_dimension=0, tiled=True),
            lax.psum_scatter(terms[11], "fsdp", scatter_dimension=0, tiled=True),
            lax.psum_scatter(terms[12], "fsdp", scatter_dimension=0, tiled=True),
            lax.psum_scatter(terms[13], "fsdp", scatter_dimension=0, tiled=True),
            lax.psum_scatter(terms[14], "fsdp", scatter_dimension=0, tiled=True),
        )
    shares = tuple((stack_layers(layer_grads, n) for n in range(15)))
    return (outcome, upstream.astype(jnp.bfloat16)) + tuple(shares)


MESH = pl.DeviceIdType.MESH
BF = jnp.bfloat16
F32 = jnp.float32
WIDE = 768
SLICE = 384
PACKED = 640
ROWS = 128
NKEYS = 1536


class Pool:
    def __init__(self, ref):
        self.ref = ref
        self.used = 0

    def take(self):
        self.used += 1
        return self.ref.at[self.used - 1]

    def block(self, n):
        first = self.used
        self.used += n
        return lambda i: self.ref.at[first + i]


class Place:
    def __init__(self):
        me = lax.axis_index("fsdp")
        p = lax.rem(me, 32)
        self.base = me - p
        self.z = p // 8
        self.f = lax.rem(p // 2, 4)
        self.c = lax.rem(p, 2)

    def at(self, z, f, c):
        return self.base + 8 * z + 2 * f + c

    def f_at(self, k):
        return lax.rem(self.f + k + 4, 4)

    def z_at(self, k):
        return lax.rem(self.z + k + 4, 4)

    def plane(self, k):
        return self.at(self.z, self.f_at(k), self.c)

    def across(self, k):
        return self.at(self.z, self.f_at(k), 1 - self.c)

    def column(self, k):
        return self.at(self.z_at(k), self.f, self.c)

    def sibling(self):
        return self.at(self.z, self.f, 1 - self.c)


def remote(src, dst, sems, device):
    return pltpu.make_async_remote_copy(
        src_ref=src, dst_ref=dst, send_sem=sems[0], recv_sem=sems[1], device_id=(device,), device_id_type=MESH
    )


class Run:
    def __init__(self, send_sems, recv_sems, local_sems):
        self.place = Place()
        self.sends, self.recvs, self.locals = Pool(send_sems), Pool(recv_sems), Pool(local_sems)
        self.flying, self.saving = [], []

    def greet(self, wide):
        place = self.place
        there = [place.plane(k) for k in (1, 2, 3)] + [place.column(k) for k in (1, 2, 3)] + [place.sibling()]
        if wide:
            there += [place.across(k) for k in (1, 2, 3)]
        barrier = pltpu.get_barrier_semaphore()
        for dev in there:
            pl.semaphore_signal(barrier, inc=1, device_id=(dev,), device_id_type=MESH)
        pl.semaphore_wait(barrier, len(there))

    def launch(self, src, dst, device):
        a = remote(src, dst, (self.sends.take(), self.recvs.take()), device)
        a.start()
        self.flying.append((None, a))
        return a

    def launch_if(self, cond, src, dst, sems, device):
        a = remote(src, dst, sems, device)

        @pl.when(cond)
        def _():
            a.start()

        self.flying.append((cond, a))
        return a

    def local(self, src, dst):
        a = pltpu.make_async_copy(src, dst, self.locals.take())
        a.start()
        return a

    def save(self, src, dst):
        self.saving.append(self.local(src, dst))

    def close(self):
        for a in self.saving:
            a.wait()
        for cond, a in self.flying:
            if cond is None:
                a.wait_send()
            else:

                @pl.when(cond)
                def _(a=a):
                    a.wait_send()


class Spread:
    def __init__(self, run, chunk, full):
        self.run, self.chunk, self.full, self.pairs = run, chunk, full, None

    def start(self, cond=None):
        run, place = self.run, self.run.place
        mine = self.full.at[place.z, place.c]
        if self.pairs is None:
            self.own = pltpu.make_async_copy(self.chunk, mine, run.locals.take())
            self.pairs = [(run.sends.take(), run.recvs.take()) for _ in range(4)]
        cond = place.z >= 0 if cond is None else cond

        @pl.when(cond)
        def _():
            self.own.start()

        there = [place.column(k) for k in (1, 2, 3)] + [place.sibling()]
        copies = [run.launch_if(cond, self.chunk, mine, self.pairs[i], there[i]) for i in range(4)]
        self.far, self.near = copies[:3], copies[3:]

    def relay(self):
        run, place = self.run, self.run.place
        for k in (1, 2, 3):
            self.far[k - 1].wait_recv()
            there = self.full.at[place.z_at(-k), place.c]
            self.near.append(run.launch(there, there, place.sibling()))

    def finish(self):
        self.own.wait()
        for a in self.near:
            a.wait_recv()


class SpreadOutput:
    def __init__(self, run, chunk, full):
        self.run, self.chunk = run, chunk
        self.part = full.at[pl.ds(pl.multiple_of(run.place.c * 96, 96), 96)]

    def start(self):
        run, place = self.run, self.run.place
        self.copy = pltpu.make_async_copy(self.chunk, self.part, run.locals.take())

        @pl.when(place.f == place.z)
        def _():
            self.copy.start()

        arrive = run.recvs.take()
        for k in (1, 2, 3):
            self.far = run.launch_if(
                place.f == place.z, self.chunk, self.part, (run.sends.take(), arrive), place.column(k)
            )

    def relay(self):
        run, place = self.run, self.run.place

        @pl.when(place.f == place.z)
        def _():
            self.copy.wait()

        @pl.when(place.f != place.z)
        def _():
            self.far.wait_recv()

        self.near = run.launch(self.part, self.part, place.sibling())

    def finish(self):
        self.near.wait_recv()


class Collect:
    def __init__(self, run, part, near, far, total, out):
        self.run, self.part, self.near, self.far, self.total, self.out = run, part, near, far, total, out

    def start(self):
        place = self.run.place
        self.a = self.run.launch(self.part.at[1 - place.c], self.near, place.sibling())

    def middle(self):
        run, place = self.run, self.run.place
        self.a.wait_recv()

        def add(i, carry):
            self.near[i] = (self.part[place.c, i].astype(F32) + self.near[i].astype(F32)).astype(BF)
            return carry

        lax.fori_loop(0, 4, add, 0)
        self.moves = [
            run.launch(self.near.at[place.z_at(k)], self.far.at[k - 1], place.column(k)) for k in (1, 2, 3)
        ]

    def end(self):
        run, place = self.run, self.run.place
        for a in self.moves:
            a.wait_recv()
        result = self.near[place.z].astype(F32)
        for k in range(3):
            result = result + self.far[k].astype(F32)
        if self.total is None:
            self.out[...] = result
            return
        self.total[...] = result
        scatter_rows(self, self.total, self.out.at[place.f], None)

    def last(self):
        if self.total is None:
            return
        place = self.run.place
        for k in (1, 2, 3):
            g = place.f_at(k)
            remote(
                self.out.at[g], self.out.at[g], (self.send, self.arrive(g)), place.plane(k)
            ).wait_recv()

        @pl.when(place.c != place.f // 2)
        def _():
            remote(
                self.out.at[place.f], self.out.at[place.f], (self.send, self.arrive(place.f)), place.sibling()
            ).wait_recv()


def scatter_rows(task, total, landing, cond):
    run, place = task.run, task.run.place
    arrive = run.recvs.block(4)
    for j in range(4):
        there = place.at(place.z, 2 * place.c + j // 2, j % 2)
        here = jnp.logical_and(place.f == 2 * place.c + j // 2, place.c == j % 2)
        away = jnp.logical_not(here)
        if cond is not None:
            here, away = jnp.logical_and(here, cond), jnp.logical_and(away, cond)
        task.send = run.sends.take()
        slot = arrive(place.f) if cond is None else arrive(0)
        run.launch_if(away, total.at[pl.ds(24 * j, 24)], landing, (task.send, slot), there)

        @pl.when(here)
        def _(j=j):
            landing[...] = total[24 * j : 24 * (j + 1), :]

    task.arrive = arrive


class CollectOutput:
    def __init__(self, run, part, near, far, total, out):
        self.run, self.part, self.near, self.far, self.total, self.out = run, part, near, far, total, out

    def start(self):
        place = self.run.place
        self.a = self.run.launch(self.part.at[1 - place.c], self.near, place.sibling())

    def middle(self):
        run, place = self.run, self.run.place
        self.a.wait_recv()
        self.near[...] = (self.part[place.c].astype(F32) + self.near[...].astype(F32)).astype(BF)
        self.slot = run.recvs.block(4)
        self.one = run.sends.take()
        shift = lax.rem(place.f - place.z + 4, 4)
        run.launch_if(
            place.f != place.z, self.near, self.far.at[shift], (self.one, self.slot(shift)),
            place.at(place.f, place.f, place.c),
        )

    def end(self):
        place = self.run.place

        @pl.when(place.f == place.z)
        def _():
            result = self.near[...].astype(F32)
            for k in (1, 2, 3):
                remote(
                    self.near, self.far.at[k], (self.one, self.slot(k)), place.column(k)
                ).wait_recv()
                result = result + self.far[k].astype(F32)
            self.total[...] = result

        scatter_rows(self, self.total, self.out, place.f == place.z)

    def last(self):
        place = self.run.place
        mine = jnp.logical_and(place.f == place.z, place.c == place.f // 2)

        @pl.when(jnp.logical_not(mine))
        def _():
            remote(self.out, self.out, (self.send, self.arrive(0)), place.sibling()).wait_recv()


def norm_rows(z, gain, shift):
    centre = z - jnp.mean(z, axis=-1, keepdims=True)
    inv = lax.rsqrt(jnp.mean(centre * centre, axis=-1, keepdims=True) + EPSILON)
    return centre * inv * gain + shift


def norm_rows_back(z, gain, upstream):
    centre = z - jnp.mean(z, axis=-1, keepdims=True)
    inv = lax.rsqrt(jnp.mean(centre * centre, axis=-1, keepdims=True) + EPSILON)
    scaled = centre * inv
    weighted = upstream * gain
    inner = inv * (
        weighted
        - jnp.mean(weighted, axis=-1, keepdims=True)
        - scaled * jnp.mean(weighted * scaled, axis=-1, keepdims=True)
    )
    return inner, jnp.sum(upstream * scaled, axis=0, keepdims=True), jnp.sum(upstream, axis=0, keepdims=True)


def exchange_kernel(col, rows_o, small, colp, op, smallg, send_sems, recv_sems, local_sems):
    run = Run(send_sems, recv_sems, local_sems)
    place = run.place
    z, f, c = place.z, place.f, place.c
    mine = c == f // 2
    slot = 2 * lax.rem(f, 2) + c
    own = pltpu.make_async_copy(col.at[f], colp.at[slot], run.locals.take())
    own_o = pltpu.make_async_copy(rows_o, op.at[slot], run.locals.take())
    keep = jnp.logical_and(mine, f == z)

    @pl.when(mine)
    def _():
        own.start()

    @pl.when(keep)
    def _():
        own_o.start()

    own_small = run.local(small, smallg.at[z, c, f])
    run.greet(True)
    first = [run.launch(small, smallg.at[z, c, f], place.plane(k)) for k in (1, 2, 3)]
    arrive, arrive_o = run.recvs.block(4), run.recvs.block(4)
    for k in (1, 2, 3):
        run.launch_if(
            f >= 0, col.at[place.f_at(k)], colp.at[slot], (run.sends.take(), arrive(slot)),
            place.at(z, place.f_at(k), f // 2),
        )
    one = run.sends.take()
    run.launch_if(
        jnp.logical_not(mine), col.at[f], colp.at[slot], (one, arrive(slot)), place.sibling()
    )
    run.launch_if(
        jnp.logical_not(keep), rows_o, op.at[slot], (run.sends.take(), arrive_o(slot)), place.at(z, z, f // 2)
    )
    own_small.wait()
    for a in first:
        a.wait_recv()
    block = smallg.at[z, c]
    far = [run.launch(block, block, place.column(k)) for k in (1, 2, 3)]
    near = [run.launch(block, block, place.sibling())]
    for k in (1, 2, 3):
        far[k - 1].wait_recv()
        there = smallg.at[place.z_at(-k), c]
        near.append(run.launch(there, there, place.sibling()))

    for j in range(4):
        me = jnp.logical_and(f == 2 * c + j // 2, c == j % 2)
        other = jnp.logical_not(me)

        @pl.when(other)
        def _(j=j):
            remote(col.at[0], colp.at[j], (one, arrive(j)), place.sibling()).wait_recv()

        @pl.when(jnp.logical_and(other, f == z))
        def _(j=j):
            remote(rows_o, op.at[j], (one, arrive_o(j)), place.sibling()).wait_recv()

    for a in near:
        a.wait_recv()

    @pl.when(mine)
    def _():
        own.wait()

    @pl.when(keep)
    def _():
        own_o.wait()

    run.close()


class TrunkRows:
    def __init__(self, run, xb, tx):
        self.run, self.xb, self.tx = run, xb, tx

    def start(self):
        run, place = self.run, self.run.place
        self.parts = [pl.ds(0, 64), pl.ds(64, 64)]
        self.pairs = [(run.sends.take(), run.recvs.take()) for _ in range(2)]
        for q in range(2):
            run.launch_if(
                place.z == 0, self.xb.at[place.f, self.parts[q]], self.tx.at[place.f, self.parts[q]],
                self.pairs[q], place.column(1),
            )

    def pass_on(self):
        run, place = self.run, self.run.place
        self.round = []
        for q in range(2):
            block = self.tx.at[place.f, self.parts[q]]

            @pl.when(place.z > 0)
            def _():
                remote(block, block, self.pairs[q], place.column(1)).wait_recv()

            between = jnp.logical_and(place.z > 0, place.z < 3)
            run.launch_if(between, block, block, self.pairs[q], place.column(1))
            for k in (1, 2, 3):
                pair = (run.sends.take(), run.recvs.take())
                self.round.append((k, run.launch_if(place.z > 0, block, block, pair, place.plane(k))))

    def wait(self, k):
        for kk, a in self.round:
            if kk == k:
                a.wait_recv()


class KeyChain:
    def __init__(self, run, mine, slots, up, down, cs, up_out, down_out, place_in):
        self.run, self.mine, self.slots = run, mine, slots
        self.up, self.down, self.cs, self.up_out, self.down_out, self.place_in = up, down, cs, up_out, down_out, place_in

    def start(self):
        run, place = self.run, self.run.place
        z, c = place.z, place.c
        self.pairs = [[(run.sends.take(), run.recvs.take()) for _ in range(4)] for _ in range(2)]
        for j in range(4):
            total = self.mine[c, 0] * self.place_in[j, 0].astype(BF)
            for ft in range(1, 4):
                total = total + self.mine[c, ft] * self.place_in[j, ft].astype(BF)
            self.cs[j] = total
            run.launch_if(z == 1, self.cs.at[j], self.up.at[j], self.pairs[0][j], place.column(1))
            run.launch_if(z == 3, self.cs.at[j], self.down.at[j], self.pairs[1][j], place.column(-1))
        self.near = [run.launch(self.mine.at[c], self.mine.at[c], place.sibling())]

    def wait(self, which, j):
        dst = (self.up.at[j], self.down.at[j])[which]
        remote(dst, dst, self.pairs[which][j], self.run.place.column(1)).wait_recv()

    def finish(self):
        run, place = self.run, self.run.place
        z, c = place.z, place.c
        for j in range(4):

            @pl.when(z == 2)
            def _(j=j):
                self.wait(0, j)
                self.up_out[j] = self.cs[j] + self.up[j]

            run.launch_if(z == 2, self.up_out.at[j], self.up.at[j], self.pairs[0][j], place.column(1))

            @pl.when(z == 2)
            def _(j=j):
                self.wait(1, j)
                self.down_out[j] = self.cs[j] + self.down[j]

            run.launch_if(z == 2, self.down_out.at[j], self.down.at[j], self.pairs[1][j], place.column(-1))

            @pl.when(z == 2)
            def _(j=j):
                self.slots[c, j] = self.up_out[j] + self.down[j]

        for j in range(4):

            @pl.when(z == 0)
            def _(j=j):
                self.slots[c, j] = self.cs[j]

            @pl.when(z == 1)
            def _(j=j):
                self.wait(1, j)
                self.slots[c, j] = self.cs[j] + self.down[j]

            @pl.when(z == 3)
            def _(j=j):
                self.wait(0, j)
                self.slots[c, j] = self.cs[j] + self.up[j]

        self.near.append(run.launch(self.slots.at[c], self.slots.at[c], place.sibling()))
        for a in self.near:
            a.wait_recv()


class GradChain:
    def __init__(self, run, mine, near, trunk_in, up, down, up_out, down_out, total):
        self.run, self.mine, self.near, self.trunk_in = run, mine, near, trunk_in
        self.up, self.down, self.up_out, self.down_out, self.total = up, down, up_out, down_out, total

    def start(self):
        run, place = self.run, self.run.place
        self.pairs = [[(run.sends.take(), run.recvs.take()) for _ in range(4)] for _ in range(3)]
        self.a = run.launch(self.mine.at[1 - place.c], self.near, place.sibling())

    def wait(self, which, j):
        dst = (self.trunk_in, self.up, self.down)[which].at[j]
        remote(dst, dst, self.pairs[which][j], self.run.place.column(1)).wait_recv()

    def middle(self):
        run, place = self.run, self.run.place
        z, c = place.z, place.c
        self.a.wait_recv()
        near = self.near
        for kind in range(3):
            for j in range(4):
                near[kind, j] = (self.mine[c, kind, j].astype(F32) + near[kind, j].astype(F32)).astype(BF)
                if kind == 0:
                    run.launch_if(z == 3, near.at[0, j], self.trunk_in.at[j], self.pairs[0][j], place.column(-1))
                elif kind == 1:
                    run.launch_if(z == 1, near.at[1, j], self.up.at[j], self.pairs[1][j], place.column(1))
                    run.launch_if(z == 3, near.at[1, j], self.down.at[j], self.pairs[2][j], place.column(-1))

    def pass_on(self):
        run, place = self.run, self.run.place
        z = place.z
        near = self.near
        for j in range(4):
            cond = jnp.logical_or(z == 1, z == 2)

            @pl.when(cond)
            def _(j=j):
                self.wait(0, j)
                near[0, j] = (near[0, j].astype(F32) + self.trunk_in[j].astype(F32)).astype(BF)

            run.launch_if(cond, near.at[0, j], self.trunk_in.at[j], self.pairs[0][j], place.column(-1))

            @pl.when(z == 2)
            def _(j=j):
                self.wait(1, j)
                self.up_out[j] = (near[1, j].astype(F32) + self.up[j].astype(F32)).astype(BF)

            run.launch_if(z == 2, self.up_out.at[j], self.up.at[j], self.pairs[1][j], place.column(1))
        for j in range(4):

            @pl.when(z == 2)
            def _(j=j):
                self.wait(2, j)
                self.down_out[j] = (near[1, j].astype(F32) + self.down[j].astype(F32)).astype(BF)

            run.launch_if(z == 2, self.down_out.at[j], self.down.at[j], self.pairs[2][j], place.column(-1))

    def finish(self, place_in, store):
        place = self.run.place
        z = place.z
        near = self.near

        @pl.when(z == 0)
        def _():
            for j in range(4):
                self.wait(0, j)
                store(j, near[0, j].astype(F32) + self.trunk_in[j].astype(F32))

        @pl.when(z == 1)
        def _():
            for j in range(4):
                self.wait(2, j)
                self.total[j] = (near[1, j].astype(F32) + self.down[j].astype(F32)).astype(BF)

        @pl.when(z == 2)
        def _():
            for j in range(4):
                self.total[j] = (self.up_out[j].astype(F32) + self.down[j].astype(F32)).astype(BF)

        @pl.when(z == 3)
        def _():
            for j in range(4):
                self.wait(1, j)
                self.total[j] = (near[1, j].astype(F32) + self.up[j].astype(F32)).astype(BF)

        @pl.when(z > 0)
        def _():
            for ft in range(4):
                total = near[2, ft].astype(F32)
                for j in range(4):
                    total = total + self.total[j].astype(F32) * place_in[j, ft]
                store(ft, total)


def pick_parents(kp, slots, choose):
    def one(b, carry):
        for cc in range(2):
            total = slots[cc, 0] * choose[b, 0].astype(BF)
            for j in range(1, 4):
                total = total + slots[cc, j] * choose[b, j].astype(BF)
            kp[b, cc] = total
        return carry

    lax.fori_loop(0, 4, one, 0)


def all_keys(trunk, mine, kp, b, lanes):
    return jnp.concatenate(
        [trunk[:, :, :, lanes].reshape(1024, 128), mine[0, b, :, lanes], mine[1, b, :, lanes], kp[b, 0, :, lanes], kp[b, 1, :, lanes]],
        axis=0,
    )


def flat(ref):
    return ref[...].reshape(-1, ref.shape[-1])


def forward_kernel(*refs):
    run = Run(*refs[-3:])
    run.prepare = lambda: run.greet(False)
    forward_body(True, run, list(refs[:-3]))
    run.close()


def forward_body(first, run, refs):

    def take(n):
        out = refs[:n]
        del refs[:n]
        return out

    x_ref, chunks, rows_o, rows_out, vecs, place_in, choose, pen = take(8)
    if not first:
        qkv_in, o_in = take(2)
    layer = 0 if first else 1
    vec = vecs.at[layer]
    in_c, out_c = chunks.at[layer, :, pl.ds(PACKED, WIDE)], rows_out.at[layer]
    if first:
        qkv_in, o_in = chunks.at[0, :, pl.ds(0, PACKED)], rows_o.at[0]
        qkv_next, o_next = chunks.at[1, :, pl.ds(0, PACKED)], rows_o.at[1]
    xn_ref = take(1)[0]
    if first:
        xb_o, qp_o, trunk_o, mine_o, kp_o, p_o, ctx_o, z1_o, hb_o, gp_o, gl_o, z2_o, win_o, wout_o = take(14)
        wqkv_o, wo_o, wqkv_n, wo_n = take(4)
    xb, qp, trunk, mine, kp, p, ctx, z1, hb, gp, gl, z2, win, wout, wqkv, wo, heads, own, rs1_s, rs1_r, rs2_s, rs2_r = take(22)
    tx, *chain_refs = take(7)
    place = run.place
    z, f, c = place.z, place.f, place.c
    launch = run.launch

    xb[f] = x_ref[...].astype(BF)
    wo[192:256, :] = jnp.zeros((64, WIDE), BF)
    if not first:
        loads = [run.local(qkv_in, wqkv), run.local(o_in, wo.at[pl.ds(0, 192)])]
    run.prepare()
    came = [None] + [launch(xb.at[f], xb.at[f], place.plane(k)) for k in (1, 2, 3)]
    trunk_rows = TrunkRows(run, xb, tx)
    trunk_rows.start()
    m_tasks = [Spread(run, in_c, win), Spread(run, out_c, wout)]
    if first:
        a_tasks = [Spread(run, qkv_in, wqkv), SpreadOutput(run, o_in, wo)]
        for t in a_tasks:
            t.start()
        trunk_rows.pass_on()
        a_tasks[0].relay()
        a_tasks[0].finish()
    else:
        trunk_rows.pass_on()
        for a in loads:
            a.wait()
    lane = lax.broadcasted_iota(jnp.int32, (ROWS, 128), 1)
    for k in range(4):
        g = place.f_at(-k)
        if k:
            came[k].wait_recv()
        qkv = product(xb[g], flat(wqkv)) + vec[0:1, :PACKED]
        rows = pl.ds(pl.multiple_of(g * ROWS, ROWS), ROWS)
        mine[c, g] = qkv[:, 256:].astype(BF)
        scaled = qkv[:, :256] * (HEAD_DIM ** (-0.5))
        front = scaled[:, :128]
        qp[rows, 0:128] = jnp.where(lane < 64, front, 0.0).astype(BF)
        qp[rows, 128:256] = jnp.where(lane < 64, pltpu.roll(front, 64, 1), 0.0).astype(BF)
        qp[rows, 256:384] = scaled[:, 128:].astype(BF)
    chain = KeyChain(run, mine, *chain_refs, place_in)
    chain.start()

    @pl.when(z == 0)
    def _():
        trunk[c] = mine[c]

    @pl.when(z > 0)
    def _():
        for k in range(4):
            g = place.f_at(-k)
            if k:
                trunk_rows.wait(k)
            keys = product(tx[g], flat(wqkv)[:, 256:]) + vec[0:1, 256:PACKED]
            trunk[c, g] = keys.astype(BF)

    trunk_near = launch(trunk.at[c], trunk.at[c], place.sibling())
    if first:
        run.save(xb, xb_o)
    if first:
        run.save(qp, qp_o)
    chain.finish()
    trunk_near.wait_recv()
    late_tasks = m_tasks
    for t in late_tasks:
        t.start(z > 0)
    pick_parents(kp, chain.slots, choose)
    if first:
        run.save(kp, kp_o)
    if first:
        run.save(trunk, trunk_o)
    if first:
        run.save(mine, mine_o)
    if first:
        a_tasks[1].relay()

    def attend(i, carry):
        h, b = i // 4, lax.rem(i, 4)
        lanes = pl.ds(pl.multiple_of(h * 128, 128), 128)
        rows = pl.ds(pl.multiple_of(b * ROWS, ROWS), ROWS)
        keys = all_keys(trunk, mine, kp, b, lanes)
        s = product_nt(qp[rows, lanes], keys)
        s = jnp.concatenate(
            [s[:, :1024], s[:, 1024:1280] + pen[4 + b], s[:, 1280:] + pen[b]], axis=1
        )
        e = jnp.exp(s - jnp.max(s, axis=1, keepdims=True))
        pb = (e * (1.0 / jnp.sum(e, axis=1, keepdims=True))).astype(BF)
        p[h, b] = pb
        heads[h, b] = product(pb, keys)
        return carry

    lax.fori_loop(0, 12, attend, 0)
    if first:
        run.save(p, p_o)
    if first:
        a_tasks[1].finish()
    back = [None]
    for k in (1, 2, 3, 0):
        g = place.f_at(-k)
        ctx[g, :, 0:128] = jnp.where(lane < 64, pltpu.roll(heads[0, g], 64, 1), heads[1, g]).astype(BF)
        ctx[g, :, 128:256] = jnp.where(lane < 64, pltpu.roll(heads[2, g], 64, 1), 0.0).astype(BF)
        part = product(ctx[g], wo[...])
        if k:
            rs1_s[k - 1] = part.astype(BF)
            back.append(launch(rs1_s.at[k - 1], rs1_r.at[k - 1], place.plane(-k)))
        else:
            own[...] = part
    if first:
        run.save(ctx, ctx_o)
    for k in (1, 2, 3):
        back[k].wait_recv()
    for t in late_tasks:
        t.start(z == 0)
    total = own[...] + rs1_r[0].astype(F32) + rs1_r[1].astype(F32) + rs1_r[2].astype(F32)
    zz = x_ref[...].astype(F32) + total + vec[1:2, :]
    z1[...] = zz
    if first:
        run.save(z1, z1_o)
    hidden = norm_rows(zz, vec[2:3, :], vec[3:4, :])
    hb[f] = hidden.astype(BF)
    came = [None] + [launch(hb.at[f], hb.at[f], place.plane(k)) for k in (1, 2, 3)]
    back = [None]
    for t in m_tasks:
        t.relay()
    if first:
        n_tasks = [Spread(run, qkv_next, wqkv_n), SpreadOutput(run, o_next, wo_n)]
        for t in n_tasks:
            t.start()
    for t in m_tasks:
        t.finish()
    for k in range(4):
        g = place.f_at(-k)
        if k:
            came[k].wait_recv()
        u = product(hb[g], flat(win)) + vec[4:5, :]
        cdf = 0.5 * (1.0 + lax.erf(u * (0.5 ** 0.5)))
        gp[g] = cdf + u * jnp.exp(-0.5 * u * u) * 0.3989422804014327
        low = (u * cdf).astype(BF)
        gl[g] = low
        part = product(low, flat(wout))
        if k:
            rs2_s[k - 1] = part.astype(BF)
            back.append(launch(rs2_s.at[k - 1], rs2_r.at[k - 1], place.plane(-k)))
        else:
            own[...] = part
    if first:
        run.save(hb, hb_o)
    if first:
        run.save(gp, gp_o)
    if first:
        run.save(gl, gl_o)
    if first:
        run.save(win, win_o)
    if first:
        run.save(wout, wout_o)
    if first:
        run.save(wqkv, wqkv_o)
        run.save(wo.at[pl.ds(0, 192)], wo_o)
    for k in (1, 2, 3):
        back[k].wait_recv()
    total = own[...] + rs2_r[0].astype(F32) + rs2_r[1].astype(F32) + rs2_r[2].astype(F32)
    zz = norm_rows(z1[...], vec[2:3, :], vec[3:4, :]) + total + vec[5:6, :]
    z2[...] = zz
    if first:
        run.save(z2, z2_o)
    xn_ref[...] = norm_rows(zz, vec[6:7, :], vec[7:8, :]).astype(xn_ref.dtype)
    if first:
        for t in n_tasks:
            t.relay()
        for t in n_tasks:
            t.finish()
    return z2, (wout, gp, win, gl, hb, z1, wo, ctx, trunk, mine, kp, qp, p, xb, wqkv)


def turn_kernel(*refs):
    run = Run(*refs[-3:])
    run.prepare = lambda: run.greet(True)
    refs = list(refs[:-3])
    ahead, dy_ref, xn_ref, outs, kept, rest = refs[:10], refs[10], refs[11], refs[12:19], refs[19:48], refs[48:]
    held = forward_body(False, run, ahead + [xn_ref] + kept)
    backward_body(False, run, [dy_ref] + ahead[4:7] + outs + rest, held)
    run.close()


def backward_kernel(*refs):
    run = Run(*refs[-3:])
    backward_body(True, run, list(refs[:-3]), None)
    run.close()


def backward_body(extra, run, refs, held):

    def take(n):
        out = refs[:n]
        del refs[:n]
        return out

    dy_ref, vecs, place_in, choose = take(4)
    vec = vecs.at[0 if extra else 1]
    if extra:
        z2 = take(1)[0]
        late_in = take(15)
        pq_in, pk_in, dvec_in = take(3)
    dx_ref, din_o, dout_o, do_o = take(4)
    if extra:
        dq_n, dk_n, dq_o, dk_o, sm_o = take(5)
    else:
        pq, pk, dvec_o = take(3)
    if extra:
        late = take(15)
    else:
        z2, late = held
    wout, gp, win, gl, hb, z1, wo, ctx, trunk, mine, kp, qp, p, xb, wqkv = late
    (
        df, du, da, dctx, dqf, dqkv, dz, dz1, dkt, dself, dpar, tgt, own, rs1_s, rs1_r, rs2_s, rs2_r,
    ) = take(17)
    chain_refs = take(7)
    pin, nin, fin, tin, pout, nout, fout, po, no, fo, to = take(11)
    if extra:
        pq, pk, dvec_o = take(3)
        nq, fq, tq, nk, fk, tk, nq2, fq2, tq2, nk2, fk2, tk2, sm, sm_a, sm_b, sm_v = take(16)
    place = run.place
    z, f, c = place.z, place.f, place.c
    launch = run.launch
    loads = []
    if extra:
        for n, (src, dst) in enumerate(zip(late_in, late)):
            loads.append(run.local(src, dst.at[pl.ds(0, 192)] if n == 6 else dst))
        wo[192:256, :] = jnp.zeros((64, WIDE), BF)

    grad, dgain, dshift = norm_rows_back(z2[...], vec[6:7, :], dy_ref[...].astype(F32))
    dvec_o[6:7, :] = dgain
    dvec_o[7:8, :] = dshift
    dz[...] = grad
    low = grad.astype(BF)
    df[f] = low
    dvec_o[5:6, :] = jnp.sum(low.astype(F32), axis=0, keepdims=True)
    if extra:
        run.greet(True)
    came = [None] + [launch(df.at[f], df.at[f], place.plane(k)) for k in (1, 2, 3)]
    a_tasks = []
    if extra:
        a_tasks = [Collect(run, pq_in, nq, fq, tq, dq_n), Collect(run, pk_in, nk, fk, tk, dk_n)]
    for t in a_tasks:
        t.start()
    back = [None]
    bias = jnp.zeros((1, WIDE), F32)
    for a in loads[:3]:
        a.wait()
    for k in range(4):
        g = place.f_at(-k)
        if k:
            came[k].wait_recv()
        low = (product_nt(df[g], flat(wout)) * gp[g]).astype(BF)
        du[g] = low
        bias = bias + jnp.sum(low.astype(F32), axis=0, keepdims=True)
        part = product_nt(low, flat(win))
        if k:
            rs1_s[k - 1] = part.astype(BF)
            back.append(launch(rs1_s.at[k - 1], rs1_r.at[k - 1], place.plane(-k)))
        else:
            own[...] = part
            for t in a_tasks:
                t.middle()
    dvec_o[4:5, :] = bias
    m_tasks = [Collect(run, pin, nin, fin, tin, din_o), Collect(run, pout, nout, fout, None, dout_o)]
    o_task = CollectOutput(run, po, no, fo, to, do_o)

    def split_rows(dst, left, right, i):
        lanes = pl.ds(pl.multiple_of(i * 384, 128), 384)
        value = product_tn(left[:, :, lanes].reshape(512, 384), right).astype(BF)
        for zz in range(2):
            for cc in range(2):
                at = (2 * zz + cc) * 96
                dst[cc, 2 * i + zz] = value[at : at + 96, :]

    def ffn_grads(i, carry):
        split_rows(pout, gl, flat(df), i)
        split_rows(pin, hb, flat(du), i)
        return carry

    for a in loads[3:5]:
        a.wait()
    lax.fori_loop(0, 2, ffn_grads, 0)
    for t in m_tasks:
        t.start()
    for k in (1, 2, 3):
        back[k].wait_recv()
    up = dz[...] + own[...] + rs1_r[0].astype(F32) + rs1_r[1].astype(F32) + rs1_r[2].astype(F32)
    for a in loads[5:6]:
        a.wait()
    grad, dgain, dshift = norm_rows_back(z1[...], vec[2:3, :], up)
    dvec_o[2:3, :] = dgain
    dvec_o[3:4, :] = dshift
    dz1[...] = grad
    low = grad.astype(BF)
    da[f] = low
    dvec_o[1:2, :] = jnp.sum(low.astype(F32), axis=0, keepdims=True)
    came = [None] + [launch(da.at[f], da.at[f], place.plane(k)) for k in (1, 2, 3)]
    for t in a_tasks:
        t.end()
    for t in m_tasks:
        t.middle()
    dkt[...] = jnp.zeros_like(dkt)
    lane = lax.broadcasted_iota(jnp.int32, (ROWS, 128), 1)
    for a in loads[6:]:
        a.wait()
    for k in range(4):
        g = place.f_at(-k)
        rows = pl.ds(pl.multiple_of(g * ROWS, ROWS), ROWS)
        if k:
            came[k].wait_recv()
        packed = product_nt(da[g], wo[...])
        ahead, after = packed[:, :128], packed[:, 128:]
        dctx[rows, 0:128] = jnp.where(lane < 64, 0.0, pltpu.roll(ahead, 64, 1)).astype(BF)
        dctx[rows, 128:256] = jnp.where(lane < 64, 0.0, ahead).astype(BF)
        dctx[rows, 256:384] = jnp.where(lane < 64, 0.0, pltpu.roll(after, 64, 1)).astype(BF)
    value = product_tn(flat(ctx), flat(da)).astype(BF)
    for cc in range(2):
        po[cc] = value[96 * cc : 96 * (cc + 1), :]
    o_task.start()
    o_task.middle()

    def attend(i, carry):
        h, b = i // 4, lax.rem(i, 4)
        lanes = pl.ds(pl.multiple_of(h * 128, 128), 128)
        rows = pl.ds(pl.multiple_of(b * ROWS, ROWS), ROWS)
        keys = all_keys(trunk, mine, kp, b, lanes)
        q, g = qp[rows, lanes], dctx[rows, lanes]
        low = p[h, b]
        pf = low.astype(F32)
        dp = product_nt(g, keys)
        t = pf * dp
        ds = (t - pf * jnp.sum(t, axis=1, keepdims=True)).astype(BF)
        dqf[h, rows, :] = product(ds, keys) * (HEAD_DIM ** (-0.5))
        dkv = product_tn(jnp.concatenate([ds, low], axis=0), jnp.concatenate([q, g], axis=0))
        dkt[:, lanes] += dkv[:1024]
        dself[b, :, lanes] = dkv[1024:1280]
        dpar[b, :, lanes] = dkv[1280:]
        return carry

    lax.fori_loop(0, 12, attend, 0)
    for cc in range(2):
        for j in range(4):
            at = cc * 512 + j * ROWS
            tgt[cc, 0, j] = dkt[at : at + ROWS, :].astype(BF)

    def scatter(j, carry):
        for cc in range(2):
            half = slice(cc * ROWS, (cc + 1) * ROWS)
            total = dpar[0, half, :] * choose[0, j]
            for b in range(1, 4):
                total = total + dpar[b, half, :] * choose[b, j]
            tgt[cc, 1, j] = total.astype(BF)
            tgt[cc, 2, j] = dself[j, half, :].astype(BF)
        return carry

    lax.fori_loop(0, 4, scatter, 0)
    chain = GradChain(run, tgt, *chain_refs)
    chain.start()
    for g in range(4):
        rows = slice(g * ROWS, (g + 1) * ROWS)
        ahead = jnp.where(lane < 64, dqf[0, rows, :], pltpu.roll(dqf[1, rows, :], 64, 1))
        dqkv[g, :, 0:128] = ahead.astype(BF)
        dqkv[g, :, 128:256] = jnp.where(lane < 64, dqf[2, rows, :], 0.0).astype(BF)
    chain.middle()
    for t in m_tasks:
        t.end()
    chain.pass_on()

    def q_grads(i, carry):
        split_rows(pq, xb, dqkv[:, :, :256].reshape(512, 256), i)
        return carry

    lax.fori_loop(0, 2, q_grads, 0)
    end_tasks = []
    if extra:
        end_tasks = [Collect(run, pk, nk2, fk2, tk2, dk_o), Collect(run, pq, nq2, fq2, tq2, dq_o)]
        end_tasks[1].start()

    def store(ft, value):
        dqkv[ft, :, 256:] = value.astype(BF)

    chain.finish(place_in, store)

    def k_grads(i, carry):
        split_rows(pk, xb, dqkv[:, :, 256:].reshape(512, SLICE), i)
        return carry

    lax.fori_loop(0, 2, k_grads, 0)
    if extra:
        end_tasks[0].start()
        end_tasks[1].middle()
        end_tasks[0].middle()
    back = [None]
    for k in (1, 2, 3, 0):
        g = place.f_at(-k)
        part = product_nt(dqkv[g], flat(wqkv))
        if k:
            rs2_s[k - 1] = part.astype(BF)
            back.append(launch(rs2_s.at[k - 1], rs2_r.at[k - 1], place.plane(-k)))
        else:
            own[...] = part

    sums = jnp.sum(flat(dqkv).astype(F32), axis=0, keepdims=True)
    dvec_o[0:1, :] = jnp.concatenate([sums, jnp.zeros((1, WIDE - PACKED), F32)], axis=1)
    if extra:
        sm[0:8, :] = dvec_o[...]
        sm[8:16, :] = dvec_in[...]
        sm_near = launch(sm, sm_a, place.sibling())
        sm_near.wait_recv()
        sm_a[...] = sm[...] + sm_a[...]
        sm_far = [launch(sm_a, sm_b.at[k - 1], place.column(k)) for k in (1, 2, 3)]
    o_task.end()
    for t in a_tasks:
        t.last()
    for k in (1, 2, 3):
        back[k].wait_recv()
    total = dz1[...] + own[...] + rs2_r[0].astype(F32) + rs2_r[1].astype(F32) + rs2_r[2].astype(F32)
    dx_ref[...] = total.astype(dx_ref.dtype)
    if extra:
        for t in end_tasks:
            t.end()
        for a in sm_far:
            a.wait_recv()
        sm_v[...] = sm_a[...] + sm_b[0] + sm_b[1] + sm_b[2]
        sm_last = [launch(sm_v, sm_o.at[f], place.plane(k)) for k in (1, 2, 3)]
        sm_o[f] = sm_v[...]
        for a in sm_last:
            a.wait_recv()
    for t in m_tasks + [o_task] + end_tasks:
        t.last()


ANY = pl.BlockSpec(memory_space=pl.ANY)
VM = pl.BlockSpec(memory_space=pltpu.VMEM)
SM = pl.BlockSpec(memory_space=pltpu.SMEM)
LIMIT = 60 * 1024 * 1024
SEMS = (256, 256, 32)


def shape(*dims, dtype=BF):
    return jax.ShapeDtypeStruct(dims, dtype)


def call(kernel, number, outs, out_specs, in_specs, scratch, args, flops):
    return pl.pallas_call(
        kernel,
        out_shape=tuple(outs),
        in_specs=in_specs,
        out_specs=tuple(out_specs),
        scratch_shapes=[pltpu.VMEM(s.shape, s.dtype) for s in scratch]
        + [pltpu.SemaphoreType.DMA((n,)) for n in SEMS],
        compiler_params=pltpu.CompilerParams(
            collective_id=number, has_side_effects=True, vmem_limit_bytes=LIMIT
        ),
        cost_estimate=pl.CostEstimate(flops=flops, bytes_accessed=20000000, transcendentals=0),
    )(*args)


def column_parts(query, key, value, inner):
    n = query.shape[0] * query.shape[1]
    q = query.reshape(n, 4, 3, 64)
    q = jnp.pad(q, ((0, 0), (0, 0), (0, 1), (0, 0))).reshape(n, 4, 256)
    kv = jnp.stack([key.reshape(n, 4, 3, 64), value.reshape(n, 4, 3, 64)], axis=3).reshape(n, 4, 384)
    up = inner.reshape(n, 4, 4, 192).transpose(0, 2, 1, 3).reshape(n, 4, WIDE)
    return jnp.concatenate([q, kv, up], axis=2).transpose(1, 0, 2)


LOCAL = shape(ROWS, WIDE, dtype=F32)
FULL = shape(4, ROWS, WIDE)
PIECE = shape(3, ROWS, WIDE)
QKV = shape(4, 2, 96, PACKED)
BIG = shape(4, 2, 96, WIDE)
OUTPUT = shape(192, WIDE)
HALVES = shape(2, 4, ROWS, SLICE)
QUARTERS = shape(4, ROWS, SLICE)
SAVED = (
    FULL, shape(512, SLICE), HALVES, HALVES, shape(4, 2, ROWS, SLICE), shape(3, 4, ROWS, NKEYS),
    shape(4, ROWS, 256), LOCAL, FULL, shape(4, ROWS, WIDE, dtype=F32), FULL, LOCAL,
)


FORWARD_SCRATCH = (
    list(SAVED)
    + [BIG, BIG, QKV, shape(256, WIDE), shape(3, 4, ROWS, 128, dtype=F32), LOCAL]
    + [PIECE] * 4 + [FULL, HALVES] + [QUARTERS] * 5
)


def forward_layer(state, chunks, rows_o, rows_out, vecs, place_in, choose, pen):
    outs = (LOCAL,) + SAVED + (BIG, BIG, QKV, OUTPUT, QKV, OUTPUT)
    got = call(
        forward_kernel, 1, outs, (VM,) + (ANY,) * (len(outs) - 1), [VM] + [ANY] * 3 + [VM] + [SM] * 3,
        FORWARD_SCRATCH, (state, chunks, rows_o, rows_out, vecs, place_in, choose, pen), 3 * 10**9,
    )
    return got[0], got[1:13], got[13:]


def collect_scratch(columns, rows):
    return [shape(4, 96, columns), shape(3, 96, columns)] + ([shape(96, columns, dtype=F32)] if rows else [])


OUT_SCRATCH = [shape(96, WIDE), shape(4, 96, WIDE), shape(96, WIDE, dtype=F32)]
PARTS = (shape(2, 4, 96, 256), shape(2, 4, 96, SLICE))
SHARES = (shape(4, 24, 256, dtype=F32), shape(4, 24, SLICE, dtype=F32))


def backward_scratch():
    keys = shape(4, 256, SLICE, dtype=F32)
    part = shape(2, 4, 96, WIDE)
    scratch = [
        FULL, FULL, FULL, shape(512, SLICE), shape(3, 512, 128, dtype=F32), shape(4, ROWS, PACKED), LOCAL, LOCAL,
        shape(1024, SLICE, dtype=F32), keys, keys, shape(2, 3, 4, ROWS, SLICE), LOCAL, PIECE, PIECE, PIECE, PIECE,
        shape(3, 4, ROWS, SLICE),
    ] + [QUARTERS] * 6
    scratch += [part] + collect_scratch(WIDE, True) + [part] + collect_scratch(WIDE, False)
    return scratch + [shape(2, 96, WIDE)] + OUT_SCRATCH


SUMS, SUMS2 = shape(8, WIDE, dtype=F32), shape(16, WIDE, dtype=F32)
GRADS = (shape(4, 24, WIDE, dtype=F32), shape(96, WIDE, dtype=F32), shape(24, WIDE, dtype=F32))


def turn_layer(state, chunks, rows_o, rows_out, vecs, place_in, choose, pen, wqkv, wo, upstream):
    outs = (shape(ROWS, WIDE), LOCAL) + GRADS + PARTS + (SUMS,)
    return call(
        turn_kernel, 2, outs, (VM,) * len(outs), [VM] + [ANY] * 3 + [VM] + [SM] * 3 + [ANY] * 2 + [VM],
        FORWARD_SCRATCH + backward_scratch(),
        (state, chunks, rows_o, rows_out, vecs, place_in, choose, pen, wqkv, wo, upstream), 9 * 10**9,
    )


def backward_layer(upstream, weights, vecs, place_in, choose, saved, before):
    wqkv, wo, win, wout = weights
    xb, qp, trunk, mine, kp, p, ctx, z1, hb, gp, gl, z2 = saved
    outs = (shape(ROWS, WIDE),) + GRADS + SHARES + SHARES + (shape(4, 16, WIDE, dtype=F32),)
    scratch = [
        BIG, SAVED[9], BIG, FULL, FULL, LOCAL, shape(256, WIDE), SAVED[6], HALVES, HALVES, SAVED[4], SAVED[1], SAVED[5],
        FULL, QKV,
    ] + backward_scratch()
    scratch += list(PARTS) + [SUMS]
    scratch += (collect_scratch(256, True) + collect_scratch(SLICE, True)) * 2
    scratch += [SUMS2, SUMS2, shape(3, 16, WIDE, dtype=F32), SUMS2]
    return call(
        backward_kernel, 4, outs, (VM,) * len(outs), [VM] * 2 + [SM] * 2 + [VM] + [ANY] * 15 + [VM] * 3, scratch,
        (upstream, vecs, place_in, choose, z2, wout, gp, win, gl, hb, z1, wo, ctx, trunk, mine, kp, qp, p, xb, wqkv)
        + tuple(before),
        6 * 10**9,
    )


def slice_body(
    activations, query_weight, query_bias, key_weight, value_weight, value_bias, output_weight, output_bias,
    first_gain, first_shift, inner_weight, inner_bias, outer_weight, outer_bias, second_gain, second_shift,
    cotangent, parents, segments,
):
    place = Place()
    z, f, c = place.z, place.f, place.c
    col = column_parts(query_weight, key_weight, value_weight, inner_weight)
    vectors = (query_bias, value_bias, output_bias, first_gain, first_shift, outer_bias, second_gain, second_shift)
    label = jnp.broadcast_to(segments[:1].astype(BF)[None], (2, 1))
    small = jnp.concatenate(vectors + (inner_bias, label), axis=1)
    small = jnp.pad(small, ((0, 14), (0, 384 - small.shape[1])))
    colp, op, smallg = call(
        exchange_kernel, 0, (shape(4, 48, 1408), shape(4, 48, WIDE), shape(4, 2, 4, 16, 384)), (ANY,) * 3, [ANY] * 3,
        [], (col, output_weight.reshape(48, WIDE), small), 1000,
    )
    colp = colp.reshape(4, 2, 24, 1408).transpose(1, 0, 2, 3).reshape(2, 96, 1408)
    op = op.reshape(4, 2, 24, WIDE).transpose(1, 0, 2, 3).reshape(2, 96, WIDE)
    small = smallg[:, :, :, :2].transpose(3, 0, 2, 1, 4).astype(F32)
    parts = [small[..., i * 24 : (i + 1) * 24].reshape(2, WIDE) for i in range(8)]
    q_all, v_all, o_all, g1, s1, out_all, g2, s2 = parts
    in_mine = lax.dynamic_index_in_dim(small[..., 192:288], f, 2, keepdims=False).reshape(2, WIDE)
    q_mine = lax.dynamic_slice_in_dim(q_all, 192 * f, 192, 1)
    v_mine = lax.dynamic_slice_in_dim(v_all, 192 * f, 192, 1).reshape(2, 3, 64)
    kv_mine = jnp.pad(v_mine, ((0, 0), (0, 0), (64, 0))).reshape(2, SLICE)
    qkv_mine = jnp.pad(jnp.concatenate([q_mine, jnp.zeros((2, 64), F32), kv_mine], axis=1), ((0, 0), (0, WIDE - PACKED)))
    vecs = jnp.stack([qkv_mine, o_all, g1, s1, in_mine, out_all, g2, s2], axis=1)

    labels = small[0, :, :, 0, 288].reshape(16).astype(jnp.int32)
    above = lookup_rows(labels, parents)
    order = jnp.arange(16, dtype=jnp.int32)
    branch = jnp.logical_and(above == labels[0], order >= 4)
    slot = jnp.where(branch, jnp.sum((branch[:, None] & (order[:, None] < order[None, :])).astype(jnp.int32), axis=0), 4)
    in_slot = slot[None, :] == jnp.arange(4, dtype=jnp.int32)[:, None]
    place_in = lax.dynamic_slice_in_dim(in_slot.astype(F32), 4 * z, 4, 1)
    parent = lax.dynamic_slice_in_dim(above, 4 * z, 4, 0)
    match = parent[:, None, None] == jnp.where(in_slot, labels[None, :], -1)[None]
    choose = jnp.any(match, axis=2).astype(F32)
    pen = jnp.concatenate(
        [jnp.where(jnp.any(match, axis=(1, 2)), 0.0, MASKED), jnp.where(z > 0, jnp.zeros((4,), F32), MASKED)]
    ).astype(F32)

    shared = (colp, op, outer_weight, vecs, place_in, choose, pen)
    state, kept0, (win0, wout0, wqkv0, wo0, wqkv1, wo1) = forward_layer(activations, *shared)
    outcome, upstream, din1, dout1, do1, pq, pk, dvec1 = turn_layer(state, *shared, wqkv1, wo1, cotangent)
    upstream, din0, dout0, do0, dq1, dk1, dq0, dk0, rsm = backward_layer(
        upstream, (wqkv0, wo0, win0, wout0), vecs, place_in, choose, kept0, (pq, pk, dvec1)
    )
    dq = jnp.stack([dq0, dq1]).transpose(0, 2, 1, 3)[..., :192].reshape(2, 24, WIDE)
    dkv = jnp.stack([dk0, dk1]).transpose(0, 2, 1, 3).reshape(2, 24, 4, 3, 2, 64)
    dk = dkv[..., 0, :].reshape(2, 24, WIDE)
    dv = dkv[..., 1, :].reshape(2, 24, WIDE)
    dinner = jnp.stack([din0, din1]).reshape(2, 4, 24, 4, 192).transpose(0, 2, 3, 1, 4).reshape(2, 24, 3072)
    rsm = rsm.reshape(4, 2, 8, WIDE)
    sums = jnp.sum(rsm, axis=0)
    dqb = rsm[:, :, 0, :192].transpose(1, 0, 2).reshape(2, WIDE)
    dvb = rsm[:, :, 0, 256:640].reshape(4, 2, 3, 2, 64)[:, :, :, 1].transpose(1, 0, 2, 3).reshape(2, WIDE)
    rows = jnp.stack([dqb, dvb, sums[:, 1], sums[:, 2], sums[:, 3], sums[:, 5], sums[:, 6], sums[:, 7]])
    rows = lax.dynamic_slice_in_dim(rows, 24 * (8 * z + 2 * f + c), 24, 2)
    dib = lax.dynamic_index_in_dim(rsm[:, :, 4], f, 0, keepdims=False)
    dib = lax.dynamic_slice_in_dim(dib, 96 * (2 * z + c), 96, 1)
    return (
        outcome, upstream, dq, rows[0], dk, dv, rows[1], jnp.stack([do0, do1]), rows[2], rows[3], rows[4],
        dinner, dib, jnp.stack([dout0, dout1]), rows[5], rows[6], rows[7],
    )


def solution(mesh):
    placed = (
        P("fsdp", None),
        P(None, "fsdp", None),
        P(None, "fsdp"),
        P(None, "fsdp", None),
        P(None, "fsdp", None),
        P(None, "fsdp"),
        P(None, "fsdp", None),
        P(None, "fsdp"),
        P(None, "fsdp"),
        P(None, "fsdp"),
        P(None, "fsdp", None),
        P(None, "fsdp"),
        P(None, "fsdp", None),
        P(None, "fsdp"),
        P(None, "fsdp"),
        P(None, "fsdp"),
        P("fsdp", None),
        P(),
        P("fsdp"),
    )
    return jax.shard_map(
        slice_body if mesh.shape["fsdp"] == 32 else body,
        mesh=mesh,
        in_specs=placed,
        out_specs=(
            P("fsdp", None),
            P("fsdp", None),
            P(None, "fsdp", None),
            P(None, "fsdp"),
            P(None, "fsdp", None),
            P(None, "fsdp", None),
            P(None, "fsdp"),
            P(None, "fsdp", None),
            P(None, "fsdp"),
            P(None, "fsdp"),
            P(None, "fsdp"),
            P(None, "fsdp", None),
            P(None, "fsdp"),
            P(None, "fsdp", None),
            P(None, "fsdp"),
            P(None, "fsdp"),
            P(None, "fsdp"),
        ),
        check_vma=False,
    )
```

```python
import jax
import jax.numpy as jnp
from jax import lax
from jax.experimental import pallas as pl
from jax.experimental.pallas import tpu as pltpu
from jax.sharding import PartitionSpec as P

HEADS = 12
HEAD_DIM = 64
LAYERS = 2
TREE_LEN = 4096


EPSILON = 1e-06
MASKED = -1000000000.0


def partner_2(shard, axis, stride):
    return lax.ppermute(shard, axis, [(i, i ^ 1 << stride) for i in range(lax.axis_size(axis))])


def as_sent(shard):
    return jax.tree.map(lambda a: a.astype(jnp.bfloat16) if a.dtype == jnp.float32 else a, shard)


def product(a, b):
    return jnp.dot(a, b, preferred_element_type=jnp.float32)


def product_tn(a, b):
    return lax.dot_general(a, b, (((0,), (0,)), ((), ())), preferred_element_type=jnp.float32)


def product_nt(a, b):
    return lax.dot_general(a, b, (((1,), (1,)), ((), ())), preferred_element_type=jnp.float32)


def exact_gelu(u):
    return jax.nn.gelu(u, approximate=False)


def layer_norm(z, gain_vec, shift_vec):
    centre = z - jnp.mean(z, axis=-1, keepdims=True)
    scaled = centre * lax.rsqrt(jnp.mean(centre * centre, axis=-1, keepdims=True) + EPSILON)
    return scaled * gain_vec.astype(jnp.float32) + shift_vec.astype(jnp.float32)


def norm_backward(z, gain_vec, upstream):
    centre = z - jnp.mean(z, axis=-1, keepdims=True)
    invert = lax.rsqrt(jnp.mean(centre * centre, axis=-1, keepdims=True) + EPSILON)
    scaled = centre * invert
    weighted = upstream * gain_vec.astype(jnp.float32)
    inner = invert * (
        weighted
        - jnp.mean(weighted, axis=-1, keepdims=True)
        - scaled * jnp.mean(weighted * scaled, axis=-1, keepdims=True)
    )
    return (inner, jnp.sum(upstream * scaled, axis=0), jnp.sum(upstream, axis=0))


def lookup_rows(ids, parents):
    table = jnp.arange(parents.shape[0], dtype=jnp.int32)
    return jnp.sum(jnp.where(ids[:, None] == table[None, :], parents[None, :], 0), axis=1)


def join_heads(stacked):
    return stacked.transpose(1, 0, 2).reshape(stacked.shape[1], -1)


def gather_group(key_rows, value_rows, labels, position, bit_count):
    for b in range(bit_count):
        partner = partner_2((key_rows, value_rows, labels), "fsdp", b)
        upper_side = position >> b & 1 == 1
        key_rows = jnp.where(
            upper_side,
            jnp.concatenate([partner[0], key_rows]),
            jnp.concatenate([key_rows, partner[0]]),
        )
        value_rows = jnp.where(
            upper_side,
            jnp.concatenate([partner[1], value_rows]),
            jnp.concatenate([value_rows, partner[1]]),
        )
        labels = jnp.where(
            upper_side, jnp.concatenate([partner[2], labels]), jnp.concatenate([labels, partner[2]])
        )
    return (key_rows, value_rows, labels)


def sum_group(key_grad, value_grad, position, bit_count):
    for b in reversed(range(bit_count)):
        halfway = key_grad.shape[0] // 2
        upper_side = position >> b & 1 == 1
        outgoing = (
            jnp.where(upper_side, key_grad[:halfway], key_grad[halfway:]),
            jnp.where(upper_side, value_grad[:halfway], value_grad[halfway:]),
        )
        partner = partner_2((as_sent(outgoing[0]), as_sent(outgoing[1])), "fsdp", b)
        key_grad = jnp.where(upper_side, key_grad[halfway:], key_grad[:halfway]) + partner[0]
        value_grad = jnp.where(upper_side, value_grad[halfway:], value_grad[:halfway]) + partner[1]
    return (key_grad, value_grad)


def attend_forward(queries, key_rows, value_rows, allowed):
    factor = HEAD_DIM ** (-0.5)

    def one_head(j):
        start = j * HEAD_DIM
        q = lax.dynamic_slice_in_dim(queries, start, HEAD_DIM, 1)
        k = lax.dynamic_slice_in_dim(key_rows, start, HEAD_DIM, 1)
        v = lax.dynamic_slice_in_dim(value_rows, start, HEAD_DIM, 1)
        s = jnp.where(allowed, product_nt(q, k) * factor, MASKED)
        maxima = jnp.max(s, axis=1, keepdims=True)
        e = jnp.exp(s - maxima)
        totals = jnp.sum(e, axis=1, keepdims=True)
        p = (e / totals).astype(jnp.bfloat16)
        return (product(p, v), (maxima + jnp.log(totals))[:, 0])

    stacked, log_total = lax.map(one_head, jnp.arange(HEADS))
    return (join_heads(stacked), log_total)


def attend_backward(queries, key_rows, value_rows, allowed, log_total, grad_context):
    factor = HEAD_DIM ** (-0.5)

    def one_head(j):
        start = j * HEAD_DIM
        q = lax.dynamic_slice_in_dim(queries, start, HEAD_DIM, 1)
        k = lax.dynamic_slice_in_dim(key_rows, start, HEAD_DIM, 1)
        v = lax.dynamic_slice_in_dim(value_rows, start, HEAD_DIM, 1)
        g = lax.dynamic_slice_in_dim(grad_context, start, HEAD_DIM, 1)
        s = jnp.where(allowed, product_nt(q, k) * factor, MASKED)
        p = jnp.where(allowed, jnp.exp(s - log_total[j][:, None]), 0.0)
        grad_p = product_nt(g, v)
        grad_v = product_tn(p.astype(jnp.bfloat16), g)
        grad_s = (p * (grad_p - jnp.sum(p * grad_p, axis=1, keepdims=True))).astype(jnp.bfloat16)
        grad_q = product(grad_s, k) * factor
        grad_k = product_tn(grad_s, q) * factor
        return (grad_q, grad_k, grad_v)

    grad_q, grad_k, grad_v = lax.map(one_head, jnp.arange(HEADS))
    return (join_heads(grad_q), join_heads(grad_k), join_heads(grad_v))


def layer_forward(state, full, segments, parent_one, parent_two, position, bit_count):
    (
        q_weight,
        q_bias,
        k_weight,
        v_weight,
        v_bias,
        o_weight,
        o_bias,
        gain_one,
        shift_one,
        up_weight,
        up_bias,
        down_weight,
        down_bias,
        gain_two,
        shift_two,
    ) = full
    inputs = state.astype(jnp.bfloat16)
    queries = (product(inputs, q_weight) + q_bias).astype(jnp.bfloat16)
    key_local = product(inputs, k_weight).astype(jnp.bfloat16)
    value_local = (product(inputs, v_weight) + v_bias).astype(jnp.bfloat16)
    key_rows, value_rows, labels = gather_group(
        key_local, value_local, segments, position, bit_count
    )
    allowed = (
        (labels[None, :] == segments[:, None])
        | (labels[None, :] == parent_one[:, None])
        | (labels[None, :] == parent_two[:, None])
    )
    context_wide, log_total = attend_forward(queries, key_rows, value_rows, allowed)
    context = context_wide.astype(jnp.bfloat16)
    first_sum = state + product(context, o_weight) + o_bias
    hidden = layer_norm(first_sum, gain_one, shift_one)
    hidden_low = hidden.astype(jnp.bfloat16)
    pre_act = product(hidden_low, up_weight) + up_bias
    gelu_out = exact_gelu(pre_act).astype(jnp.bfloat16)
    second_sum = hidden + product(gelu_out, down_weight) + down_bias
    record = (
        inputs,
        queries,
        key_rows,
        value_rows,
        allowed,
        log_total,
        context,
        first_sum,
        hidden_low,
        pre_act,
        gelu_out,
        second_sum,
    )
    return (record, layer_norm(second_sum, gain_two, shift_two))


def layer_backward(upstream, full, record, position, bit_count):
    (
        q_weight,
        q_bias,
        k_weight,
        v_weight,
        v_bias,
        o_weight,
        o_bias,
        gain_one,
        shift_one,
        up_weight,
        up_bias,
        down_weight,
        down_bias,
        gain_two,
        shift_two,
    ) = full
    (
        inputs,
        queries,
        key_rows,
        value_rows,
        allowed,
        log_total,
        context,
        first_sum,
        hidden_low,
        pre_act,
        gelu_out,
        second_sum,
    ) = record
    grad_z2, grad_gain_two, grad_shift_two = norm_backward(second_sum, gain_two, upstream)
    grad_f = grad_z2.astype(jnp.bfloat16)
    grad_down_bias = jnp.sum(grad_f.astype(jnp.float32), axis=0)
    grad_down = product_tn(gelu_out, grad_f)
    grad_gelu = product_nt(grad_f, down_weight)
    unused_value, gelu_back = jax.vjp(exact_gelu, pre_act)
    grad_u = gelu_back(grad_gelu)[0].astype(jnp.bfloat16)
    grad_up_bias = jnp.sum(grad_u.astype(jnp.float32), axis=0)
    grad_up = product_tn(hidden_low, grad_u)
    grad_h = grad_z2 + product_nt(grad_u, up_weight)
    grad_z1, grad_gain_one, grad_shift_one = norm_backward(first_sum, gain_one, grad_h)
    grad_a = grad_z1.astype(jnp.bfloat16)
    grad_o_bias = jnp.sum(grad_a.astype(jnp.float32), axis=0)
    grad_o = product_tn(context, grad_a)
    grad_context = product_nt(grad_a, o_weight).astype(jnp.bfloat16)
    grad_q, key_grad, value_grad = attend_backward(
        queries, key_rows, value_rows, allowed, log_total, grad_context
    )
    key_grad, value_grad = sum_group(key_grad, value_grad, position, bit_count)
    q_low = grad_q.astype(jnp.bfloat16)
    k_low = key_grad.astype(jnp.bfloat16)
    v_low = value_grad.astype(jnp.bfloat16)
    grad_x = (
        grad_z1
        + product_nt(q_low, q_weight)
        + product_nt(k_low, k_weight)
        + product_nt(v_low, v_weight)
    )
    terms = (
        product_tn(inputs, q_low),
        jnp.sum(q_low.astype(jnp.float32), axis=0),
        product_tn(inputs, k_low),
        product_tn(inputs, v_low),
        jnp.sum(v_low.astype(jnp.float32), axis=0),
        grad_o,
        grad_o_bias,
        grad_gain_one,
        grad_shift_one,
        grad_up,
        grad_up_bias,
        grad_down,
        grad_down_bias,
        grad_gain_two,
        grad_shift_two,
    )
    return (grad_x, terms)


def stack_layers(groups, n):
    return jnp.stack([g[n] for g in groups])


def body(
    activations,
    query_weight,
    query_bias,
    key_weight,
    value_weight,
    value_bias,
    output_weight,
    output_bias,
    first_gain,
    first_shift,
    inner_weight,
    inner_bias,
    outer_weight,
    outer_bias,
    second_gain,
    second_shift,
    cotangent,
    parents,
    segments,
):
    position = lax.axis_index("fsdp")
    bit_count = (TREE_LEN // activations.shape[0]).bit_length() - 1
    parent_one = lookup_rows(segments, parents)
    parent_two = lookup_rows(parent_one, parents)
    state = activations.astype(jnp.float32)
    saved = []
    kept_weights = []
    for i in range(LAYERS):
        full = (
            lax.all_gather(query_weight[i], "fsdp", axis=0, tiled=True),
            lax.all_gather(query_bias[i], "fsdp", axis=0, tiled=True),
            lax.all_gather(key_weight[i], "fsdp", axis=0, tiled=True),
            lax.all_gather(value_weight[i], "fsdp", axis=0, tiled=True),
            lax.all_gather(value_bias[i], "fsdp", axis=0, tiled=True),
            lax.all_gather(output_weight[i], "fsdp", axis=0, tiled=True),
            lax.all_gather(output_bias[i], "fsdp", axis=0, tiled=True),
            lax.all_gather(first_gain[i], "fsdp", axis=0, tiled=True),
            lax.all_gather(first_shift[i], "fsdp", axis=0, tiled=True),
            lax.all_gather(inner_weight[i], "fsdp", axis=0, tiled=True),
            lax.all_gather(inner_bias[i], "fsdp", axis=0, tiled=True),
            lax.all_gather(outer_weight[i], "fsdp", axis=0, tiled=True),
            lax.all_gather(outer_bias[i], "fsdp", axis=0, tiled=True),
            lax.all_gather(second_gain[i], "fsdp", axis=0, tiled=True),
            lax.all_gather(second_shift[i], "fsdp", axis=0, tiled=True),
        )
        kept_weights.append(full)
        record, state = layer_forward(
            state, full, segments, parent_one, parent_two, position, bit_count
        )
        saved.append(record)
    outcome = state.astype(jnp.bfloat16)
    upstream = cotangent.astype(jnp.float32)
    layer_grads = [None] * LAYERS
    for i in reversed(range(LAYERS)):
        full = (
            lax.all_gather(query_weight[i], "fsdp", axis=0, tiled=True),
            lax.all_gather(query_bias[i], "fsdp", axis=0, tiled=True),
            lax.all_gather(key_weight[i], "fsdp", axis=0, tiled=True),
            lax.all_gather(value_weight[i], "fsdp", axis=0, tiled=True),
            lax.all_gather(value_bias[i], "fsdp", axis=0, tiled=True),
            lax.all_gather(output_weight[i], "fsdp", axis=0, tiled=True),
            lax.all_gather(output_bias[i], "fsdp", axis=0, tiled=True),
            lax.all_gather(first_gain[i], "fsdp", axis=0, tiled=True),
            lax.all_gather(first_shift[i], "fsdp", axis=0, tiled=True),
            lax.all_gather(inner_weight[i], "fsdp", axis=0, tiled=True),
            lax.all_gather(inner_bias[i], "fsdp", axis=0, tiled=True),
            lax.all_gather(outer_weight[i], "fsdp", axis=0, tiled=True),
            lax.all_gather(outer_bias[i], "fsdp", axis=0, tiled=True),
            lax.all_gather(second_gain[i], "fsdp", axis=0, tiled=True),
            lax.all_gather(second_shift[i], "fsdp", axis=0, tiled=True),
        )
        upstream, terms = layer_backward(upstream, full, saved[i], position, bit_count)
        layer_grads[i] = (
            lax.psum_scatter(terms[0], "fsdp", scatter_dimension=0, tiled=True),
            lax.psum_scatter(terms[1], "fsdp", scatter_dimension=0, tiled=True),
            lax.psum_scatter(terms[2], "fsdp", scatter_dimension=0, tiled=True),
            lax.psum_scatter(terms[3], "fsdp", scatter_dimension=0, tiled=True),
            lax.psum_scatter(terms[4], "fsdp", scatter_dimension=0, tiled=True),
            lax.psum_scatter(terms[5], "fsdp", scatter_dimension=0, tiled=True),
            lax.psum_scatter(terms[6], "fsdp", scatter_dimension=0, tiled=True),
            lax.psum_scatter(terms[7], "fsdp", scatter_dimension=0, tiled=True),
            lax.psum_scatter(terms[8], "fsdp", scatter_dimension=0, tiled=True),
            lax.psum_scatter(terms[9], "fsdp", scatter_dimension=0, tiled=True),
            lax.psum_scatter(terms[10], "fsdp", scatter_dimension=0, tiled=True),
            lax.psum_scatter(terms[11], "fsdp", scatter_dimension=0, tiled=True),
            lax.psum_scatter(terms[12], "fsdp", scatter_dimension=0, tiled=True),
            lax.psum_scatter(terms[13], "fsdp", scatter_dimension=0, tiled=True),
            lax.psum_scatter(terms[14], "fsdp", scatter_dimension=0, tiled=True),
        )
    shares = tuple((stack_layers(layer_grads, n) for n in range(15)))
    return (outcome, upstream.astype(jnp.bfloat16)) + tuple(shares)


MESH = pl.DeviceIdType.MESH
BF = jnp.bfloat16
F32 = jnp.float32
WIDE = 768
SLICE = 384
PACKED = 640
ROWS = 128
NKEYS = 1536


class Pool:
    def __init__(self, ref):
        self.ref = ref
        self.used = 0

    def take(self):
        self.used += 1
        return self.ref.at[self.used - 1]

    def block(self, n):
        first = self.used
        self.used += n
        return lambda i: self.ref.at[first + i]


class Place:
    def __init__(self):
        me = lax.axis_index("fsdp")
        p = lax.rem(me, 32)
        self.base = me - p
        self.z = p // 8
        self.f = lax.rem(p // 2, 4)
        self.c = lax.rem(p, 2)

    def at(self, z, f, c):
        return self.base + 8 * z + 2 * f + c

    def f_at(self, k):
        return lax.rem(self.f + k + 4, 4)

    def z_at(self, k):
        return lax.rem(self.z + k + 4, 4)

    def plane(self, k):
        return self.at(self.z, self.f_at(k), self.c)

    def across(self, k):
        return self.at(self.z, self.f_at(k), 1 - self.c)

    def column(self, k):
        return self.at(self.z_at(k), self.f, self.c)

    def sibling(self):
        return self.at(self.z, self.f, 1 - self.c)


def remote(src, dst, sems, device):
    return pltpu.make_async_remote_copy(
        src_ref=src, dst_ref=dst, send_sem=sems[0], recv_sem=sems[1], device_id=(device,), device_id_type=MESH
    )


class Run:
    def __init__(self, send_sems, recv_sems, local_sems):
        self.place = Place()
        self.sends, self.recvs, self.locals = Pool(send_sems), Pool(recv_sems), Pool(local_sems)
        self.flying, self.saving = [], []

    def greet(self, wide):
        place = self.place
        there = [place.plane(k) for k in (1, 2, 3)] + [place.column(k) for k in (1, 2, 3)] + [place.sibling()]
        if wide:
            there += [place.across(k) for k in (1, 2, 3)]
        barrier = pltpu.get_barrier_semaphore()
        for dev in there:
            pl.semaphore_signal(barrier, inc=1, device_id=(dev,), device_id_type=MESH)
        pl.semaphore_wait(barrier, len(there))

    def launch(self, src, dst, device):
        a = remote(src, dst, (self.sends.take(), self.recvs.take()), device)
        a.start()
        self.flying.append((None, a))
        return a

    def launch_if(self, cond, src, dst, sems, device):
        a = remote(src, dst, sems, device)

        @pl.when(cond)
        def _():
            a.start()

        self.flying.append((cond, a))
        return a

    def local(self, src, dst):
        a = pltpu.make_async_copy(src, dst, self.locals.take())
        a.start()
        return a

    def save(self, src, dst):
        self.saving.append(self.local(src, dst))

    def close(self):
        for a in self.saving:
            a.wait()
        for cond, a in self.flying:
            if cond is None:
                a.wait_send()
            else:

                @pl.when(cond)
                def _(a=a):
                    a.wait_send()


class Spread:
    def __init__(self, run, chunk, full):
        self.run, self.chunk, self.full, self.pairs = run, chunk, full, None

    def start(self, cond=None):
        run, place = self.run, self.run.place
        mine = self.full.at[place.z, place.c]
        if self.pairs is None:
            self.own = pltpu.make_async_copy(self.chunk, mine, run.locals.take())
            self.pairs = [(run.sends.take(), run.recvs.take()) for _ in range(4)]
        cond = place.z >= 0 if cond is None else cond

        @pl.when(cond)
        def _():
            self.own.start()

        there = [place.column(k) for k in (1, 2, 3)] + [place.sibling()]
        copies = [run.launch_if(cond, self.chunk, mine, self.pairs[i], there[i]) for i in range(4)]
        self.far, self.near = copies[:3], copies[3:]

    def relay(self):
        run, place = self.run, self.run.place
        for k in (1, 2, 3):
            self.far[k - 1].wait_recv()
            there = self.full.at[place.z_at(-k), place.c]
            self.near.append(run.launch(there, there, place.sibling()))

    def finish(self):
        self.own.wait()
        for a in self.near:
            a.wait_recv()


class SpreadOutput:
    def __init__(self, run, chunk, full):
        self.run, self.chunk = run, chunk
        self.part = full.at[pl.ds(pl.multiple_of(run.place.c * 96, 96), 96)]

    def start(self):
        run, place = self.run, self.run.place
        self.copy = pltpu.make_async_copy(self.chunk, self.part, run.locals.take())

        @pl.when(place.f == place.z)
        def _():
            self.copy.start()

        arrive = run.recvs.take()
        for k in (1, 2, 3):
            self.far = run.launch_if(
                place.f == place.z, self.chunk, self.part, (run.sends.take(), arrive), place.column(k)
            )

    def relay(self):
        run, place = self.run, self.run.place

        @pl.when(place.f == place.z)
        def _():
            self.copy.wait()

        @pl.when(place.f != place.z)
        def _():
            self.far.wait_recv()

        self.near = run.launch(self.part, self.part, place.sibling())

    def finish(self):
        self.near.wait_recv()


class Collect:
    def __init__(self, run, part, near, far, total, out):
        self.run, self.part, self.near, self.far, self.total, self.out = run, part, near, far, total, out

    def start(self):
        place = self.run.place
        self.a = self.run.launch(self.part.at[1 - place.c], self.near, place.sibling())

    def middle(self):
        run, place = self.run, self.run.place
        self.a.wait_recv()

        def add(i, carry):
            self.near[i] = (self.part[place.c, i].astype(F32) + self.near[i].astype(F32)).astype(BF)
            return carry

        lax.fori_loop(0, 4, add, 0)
        self.moves = [
            run.launch(self.near.at[place.z_at(k)], self.far.at[k - 1], place.column(k)) for k in (1, 2, 3)
        ]

    def end(self):
        run, place = self.run, self.run.place
        for a in self.moves:
            a.wait_recv()
        result = self.near[place.z].astype(F32)
        for k in range(3):
            result = result + self.far[k].astype(F32)
        if self.total is None:
            self.out[...] = result
            return
        self.total[...] = result
        scatter_rows(self, self.total, self.out.at[place.f], None)

    def last(self):
        if self.total is None:
            return
        place = self.run.place
        for k in (1, 2, 3):
            g = place.f_at(k)
            remote(
                self.out.at[g], self.out.at[g], (self.send, self.arrive(g)), place.plane(k)
            ).wait_recv()

        @pl.when(place.c != place.f // 2)
        def _():
            remote(
                self.out.at[place.f], self.out.at[place.f], (self.send, self.arrive(place.f)), place.sibling()
            ).wait_recv()


def scatter_rows(task, total, landing, cond):
    run, place = task.run, task.run.place
    arrive = run.recvs.block(4)
    for j in range(4):
        there = place.at(place.z, 2 * place.c + j // 2, j % 2)
        here = jnp.logical_and(place.f == 2 * place.c + j // 2, place.c == j % 2)
        away = jnp.logical_not(here)
        if cond is not None:
            here, away = jnp.logical_and(here, cond), jnp.logical_and(away, cond)
        task.send = run.sends.take()
        slot = arrive(place.f) if cond is None else arrive(0)
        run.launch_if(away, total.at[pl.ds(24 * j, 24)], landing, (task.send, slot), there)

        @pl.when(here)
        def _(j=j):
            landing[...] = total[24 * j : 24 * (j + 1), :]

    task.arrive = arrive


class CollectOutput:
    def __init__(self, run, part, near, far, total, out):
        self.run, self.part, self.near, self.far, self.total, self.out = run, part, near, far, total, out

    def start(self):
        place = self.run.place
        self.a = self.run.launch(self.part.at[1 - place.c], self.near, place.sibling())

    def middle(self):
        run, place = self.run, self.run.place
        self.a.wait_recv()
        self.near[...] = (self.part[place.c].astype(F32) + self.near[...].astype(F32)).astype(BF)
        self.slot = run.recvs.block(4)
        self.one = run.sends.take()
        shift = lax.rem(place.f - place.z + 4, 4)
        run.launch_if(
            place.f != place.z, self.near, self.far.at[shift], (self.one, self.slot(shift)),
            place.at(place.f, place.f, place.c),
        )

    def end(self):
        place = self.run.place

        @pl.when(place.f == place.z)
        def _():
            result = self.near[...].astype(F32)
            for k in (1, 2, 3):
                remote(
                    self.near, self.far.at[k], (self.one, self.slot(k)), place.column(k)
                ).wait_recv()
                result = result + self.far[k].astype(F32)
            self.total[...] = result

        scatter_rows(self, self.total, self.out, place.f == place.z)

    def last(self):
        place = self.run.place
        mine = jnp.logical_and(place.f == place.z, place.c == place.f // 2)

        @pl.when(jnp.logical_not(mine))
        def _():
            remote(self.out, self.out, (self.send, self.arrive(0)), place.sibling()).wait_recv()


def norm_rows(z, gain, shift):
    centre = z - jnp.mean(z, axis=-1, keepdims=True)
    inv = lax.rsqrt(jnp.mean(centre * centre, axis=-1, keepdims=True) + EPSILON)
    return centre * inv * gain + shift


def norm_rows_back(z, gain, upstream):
    centre = z - jnp.mean(z, axis=-1, keepdims=True)
    inv = lax.rsqrt(jnp.mean(centre * centre, axis=-1, keepdims=True) + EPSILON)
    scaled = centre * inv
    weighted = upstream * gain
    inner = inv * (
        weighted
        - jnp.mean(weighted, axis=-1, keepdims=True)
        - scaled * jnp.mean(weighted * scaled, axis=-1, keepdims=True)
    )
    return inner, jnp.sum(upstream * scaled, axis=0, keepdims=True), jnp.sum(upstream, axis=0, keepdims=True)


def exchange_kernel(col, rows_o, small, colp, op, smallg, send_sems, recv_sems, local_sems):
    run = Run(send_sems, recv_sems, local_sems)
    place = run.place
    z, f, c = place.z, place.f, place.c
    mine = c == f // 2
    slot = 2 * lax.rem(f, 2) + c
    own = pltpu.make_async_copy(col.at[f], colp.at[slot], run.locals.take())
    own_o = pltpu.make_async_copy(rows_o, op.at[slot], run.locals.take())
    keep = jnp.logical_and(mine, f == z)

    @pl.when(mine)
    def _():
        own.start()

    @pl.when(keep)
    def _():
        own_o.start()

    own_small = run.local(small, smallg.at[z, c, f])
    run.greet(True)
    first = [run.launch(small, smallg.at[z, c, f], place.plane(k)) for k in (1, 2, 3)]
    arrive, arrive_o = run.recvs.block(4), run.recvs.block(4)
    for k in (1, 2, 3):
        run.launch_if(
            f >= 0, col.at[place.f_at(k)], colp.at[slot], (run.sends.take(), arrive(slot)),
            place.at(z, place.f_at(k), f // 2),
        )
    one = run.sends.take()
    run.launch_if(
        jnp.logical_not(mine), col.at[f], colp.at[slot], (one, arrive(slot)), place.sibling()
    )
    run.launch_if(
        jnp.logical_not(keep), rows_o, op.at[slot], (run.sends.take(), arrive_o(slot)), place.at(z, z, f // 2)
    )
    own_small.wait()
    for a in first:
        a.wait_recv()
    block = smallg.at[z, c]
    far = [run.launch(block, block, place.column(k)) for k in (1, 2, 3)]
    near = [run.launch(block, block, place.sibling())]
    for k in (1, 2, 3):
        far[k - 1].wait_recv()
        there = smallg.at[place.z_at(-k), c]
        near.append(run.launch(there, there, place.sibling()))

    for j in range(4):
        me = jnp.logical_and(f == 2 * c + j // 2, c == j % 2)
        other = jnp.logical_not(me)

        @pl.when(other)
        def _(j=j):
            remote(col.at[0], colp.at[j], (one, arrive(j)), place.sibling()).wait_recv()

        @pl.when(jnp.logical_and(other, f == z))
        def _(j=j):
            remote(rows_o, op.at[j], (one, arrive_o(j)), place.sibling()).wait_recv()

    for a in near:
        a.wait_recv()

    @pl.when(mine)
    def _():
        own.wait()

    @pl.when(keep)
    def _():
        own_o.wait()

    run.close()


class TrunkRows:
    def __init__(self, run, xb, tx):
        self.run, self.xb, self.tx = run, xb, tx

    def start(self):
        run, place = self.run, self.run.place
        self.parts = [pl.ds(0, 64), pl.ds(64, 64)]
        self.pairs = [(run.sends.take(), run.recvs.take()) for _ in range(2)]
        for q in range(2):
            run.launch_if(
                place.z == 0, self.xb.at[place.f, self.parts[q]], self.tx.at[place.f, self.parts[q]],
                self.pairs[q], place.column(1),
            )

    def pass_on(self):
        run, place = self.run, self.run.place
        self.round = []
        for q in range(2):
            block = self.tx.at[place.f, self.parts[q]]

            @pl.when(place.z > 0)
            def _():
                remote(block, block, self.pairs[q], place.column(1)).wait_recv()

            between = jnp.logical_and(place.z > 0, place.z < 3)
            run.launch_if(between, block, block, self.pairs[q], place.column(1))
            for k in (1, 2, 3):
                pair = (run.sends.take(), run.recvs.take())
                self.round.append((k, run.launch_if(place.z > 0, block, block, pair, place.plane(k))))

    def wait(self, k):
        for kk, a in self.round:
            if kk == k:
                a.wait_recv()


class KeyChain:
    def __init__(self, run, mine, slots, up, down, cs, up_out, down_out, place_in):
        self.run, self.mine, self.slots = run, mine, slots
        self.up, self.down, self.cs, self.up_out, self.down_out, self.place_in = up, down, cs, up_out, down_out, place_in

    def start(self):
        run, place = self.run, self.run.place
        z, c = place.z, place.c
        self.pairs = [[(run.sends.take(), run.recvs.take()) for _ in range(4)] for _ in range(2)]
        for j in range(4):
            total = self.mine[c, 0] * self.place_in[j, 0].astype(BF)
            for ft in range(1, 4):
                total = total + self.mine[c, ft] * self.place_in[j, ft].astype(BF)
            self.cs[j] = total
            run.launch_if(z == 1, self.cs.at[j], self.up.at[j], self.pairs[0][j], place.column(1))
            run.launch_if(z == 3, self.cs.at[j], self.down.at[j], self.pairs[1][j], place.column(-1))
        self.near = [run.launch(self.mine.at[c], self.mine.at[c], place.sibling())]

    def wait(self, which, j):
        dst = (self.up.at[j], self.down.at[j])[which]
        remote(dst, dst, self.pairs[which][j], self.run.place.column(1)).wait_recv()

    def finish(self):
        run, place = self.run, self.run.place
        z, c = place.z, place.c
        for j in range(4):

            @pl.when(z == 2)
            def _(j=j):
                self.wait(0, j)
                self.up_out[j] = self.cs[j] + self.up[j]

            run.launch_if(z == 2, self.up_out.at[j], self.up.at[j], self.pairs[0][j], place.column(1))

            @pl.when(z == 2)
            def _(j=j):
                self.wait(1, j)
                self.down_out[j] = self.cs[j] + self.down[j]

            run.launch_if(z == 2, self.down_out.at[j], self.down.at[j], self.pairs[1][j], place.column(-1))

            @pl.when(z == 2)
            def _(j=j):
                self.slots[c, j] = self.up_out[j] + self.down[j]

        for j in range(4):

            @pl.when(z == 0)
            def _(j=j):
                self.slots[c, j] = self.cs[j]

            @pl.when(z == 1)
            def _(j=j):
                self.wait(1, j)
                self.slots[c, j] = self.cs[j] + self.down[j]

            @pl.when(z == 3)
            def _(j=j):
                self.wait(0, j)
                self.slots[c, j] = self.cs[j] + self.up[j]

        self.near.append(run.launch(self.slots.at[c], self.slots.at[c], place.sibling()))
        for a in self.near:
            a.wait_recv()


class GradChain:
    def __init__(self, run, mine, near, trunk_in, up, down, up_out, down_out, total):
        self.run, self.mine, self.near, self.trunk_in = run, mine, near, trunk_in
        self.up, self.down, self.up_out, self.down_out, self.total = up, down, up_out, down_out, total

    def start(self):
        run, place = self.run, self.run.place
        self.pairs = [[(run.sends.take(), run.recvs.take()) for _ in range(4)] for _ in range(3)]
        self.arrive = []
        self.hand_over(0)

    def hand_over(self, kind):
        run, place = self.run, self.run.place
        self.arrive.append(run.launch(self.mine.at[1 - place.c, kind], self.near.at[kind], place.sibling()))

    def wait(self, which, j):
        dst = (self.trunk_in, self.up, self.down)[which].at[j]
        remote(dst, dst, self.pairs[which][j], self.run.place.column(1)).wait_recv()

    def middle(self):
        run, place = self.run, self.run.place
        z, c = place.z, place.c
        near = self.near
        for kind in range(3):
            self.arrive[kind].wait_recv()
            for j in range(4):
                near[kind, j] = (self.mine[c, kind, j].astype(F32) + near[kind, j].astype(F32)).astype(BF)
                if kind == 0:
                    run.launch_if(z == 3, near.at[0, j], self.trunk_in.at[j], self.pairs[0][j], place.column(-1))
                elif kind == 1:
                    run.launch_if(z == 1, near.at[1, j], self.up.at[j], self.pairs[1][j], place.column(1))
                    run.launch_if(z == 3, near.at[1, j], self.down.at[j], self.pairs[2][j], place.column(-1))

    def pass_on(self):
        run, place = self.run, self.run.place
        z = place.z
        near = self.near
        for j in range(4):
            cond = jnp.logical_or(z == 1, z == 2)

            @pl.when(cond)
            def _(j=j):
                self.wait(0, j)
                near[0, j] = (near[0, j].astype(F32) + self.trunk_in[j].astype(F32)).astype(BF)

            run.launch_if(cond, near.at[0, j], self.trunk_in.at[j], self.pairs[0][j], place.column(-1))

            @pl.when(z == 2)
            def _(j=j):
                self.wait(1, j)
                self.up_out[j] = (near[1, j].astype(F32) + self.up[j].astype(F32)).astype(BF)

            run.launch_if(z == 2, self.up_out.at[j], self.up.at[j], self.pairs[1][j], place.column(1))
        for j in range(4):

            @pl.when(z == 2)
            def _(j=j):
                self.wait(2, j)
                self.down_out[j] = (near[1, j].astype(F32) + self.down[j].astype(F32)).astype(BF)

            run.launch_if(z == 2, self.down_out.at[j], self.down.at[j], self.pairs[2][j], place.column(-1))

    def finish(self, place_in, store):
        place = self.run.place
        z = place.z
        near = self.near

        @pl.when(z == 0)
        def _():
            for j in range(4):
                self.wait(0, j)
                store(j, near[0, j].astype(F32) + self.trunk_in[j].astype(F32))

        @pl.when(z == 1)
        def _():
            for j in range(4):
                self.wait(2, j)
                self.total[j] = (near[1, j].astype(F32) + self.down[j].astype(F32)).astype(BF)

        @pl.when(z == 2)
        def _():
            for j in range(4):
                self.total[j] = (self.up_out[j].astype(F32) + self.down[j].astype(F32)).astype(BF)

        @pl.when(z == 3)
        def _():
            for j in range(4):
                self.wait(1, j)
                self.total[j] = (near[1, j].astype(F32) + self.up[j].astype(F32)).astype(BF)

        @pl.when(z > 0)
        def _():
            for ft in range(4):
                total = near[2, ft].astype(F32)
                for j in range(4):
                    total = total + self.total[j].astype(F32) * place_in[j, ft]
                store(ft, total)


def pick_parents(kp, slots, choose):
    def one(b, carry):
        for cc in range(2):
            total = slots[cc, 0] * choose[b, 0].astype(BF)
            for j in range(1, 4):
                total = total + slots[cc, j] * choose[b, j].astype(BF)
            kp[b, cc] = total
        return carry

    lax.fori_loop(0, 4, one, 0)


def all_keys(trunk, mine, kp, b, lanes):
    return jnp.concatenate(
        [trunk[:, :, :, lanes].reshape(1024, 128), mine[0, b, :, lanes], mine[1, b, :, lanes], kp[b, 0, :, lanes], kp[b, 1, :, lanes]],
        axis=0,
    )


def flat(ref):
    return ref[...].reshape(-1, ref.shape[-1])


def forward_kernel(*refs):
    run = Run(*refs[-3:])
    run.prepare = lambda: run.greet(False)
    forward_body(True, run, list(refs[:-3]))
    run.close()


def forward_body(first, run, refs):

    def take(n):
        out = refs[:n]
        del refs[:n]
        return out

    x_ref, chunks, rows_o, rows_out, vecs, place_in, choose, pen = take(8)
    if not first:
        qkv_in, o_in = take(2)
    layer = 0 if first else 1
    vec = vecs.at[layer]
    in_c, out_c = chunks.at[layer, :, pl.ds(PACKED, WIDE)], rows_out.at[layer]
    if first:
        qkv_in, o_in = chunks.at[0, :, pl.ds(0, PACKED)], rows_o.at[0]
        qkv_next, o_next = chunks.at[1, :, pl.ds(0, PACKED)], rows_o.at[1]
    xn_ref = take(1)[0]
    if first:
        xb_o, qp_o, trunk_o, mine_o, kp_o, p_o, ctx_o, z1_o, hb_o, gp_o, gl_o, z2_o, win_o, wout_o = take(14)
        wqkv_o, wo_o, wqkv_n, wo_n = take(4)
    xb, qp, trunk, mine, kp, p, ctx, z1, hb, gp, gl, z2, win, wout, wqkv, wo, heads, own, rs1_s, rs1_r, rs2_s, rs2_r = take(22)
    tx, *chain_refs = take(7)
    place = run.place
    z, f, c = place.z, place.f, place.c
    launch = run.launch

    xb[f] = x_ref[...].astype(BF)
    wo[192:256, :] = jnp.zeros((64, WIDE), BF)
    if not first:
        loads = [run.local(qkv_in, wqkv), run.local(o_in, wo.at[pl.ds(0, 192)])]
    run.prepare()
    came = [None] + [launch(xb.at[f], xb.at[f], place.plane(k)) for k in (1, 2, 3)]
    trunk_rows = TrunkRows(run, xb, tx)
    trunk_rows.start()
    m_tasks = [Spread(run, in_c, win), Spread(run, out_c, wout)]
    if first:
        a_tasks = [Spread(run, qkv_in, wqkv), SpreadOutput(run, o_in, wo)]
        for t in a_tasks:
            t.start()
        trunk_rows.pass_on()
        a_tasks[0].relay()
        a_tasks[0].finish()
    else:
        trunk_rows.pass_on()
        for a in loads:
            a.wait()
    lane = lax.broadcasted_iota(jnp.int32, (ROWS, 128), 1)
    for k in range(4):
        g = place.f_at(-k)
        if k:
            came[k].wait_recv()
        qkv = product(xb[g], flat(wqkv)) + vec[0:1, :PACKED]
        rows = pl.ds(pl.multiple_of(g * ROWS, ROWS), ROWS)
        mine[c, g] = qkv[:, 256:].astype(BF)
        scaled = qkv[:, :256] * (HEAD_DIM ** (-0.5))
        front = scaled[:, :128]
        qp[rows, 0:128] = jnp.where(lane < 64, front, 0.0).astype(BF)
        qp[rows, 128:256] = jnp.where(lane < 64, pltpu.roll(front, 64, 1), 0.0).astype(BF)
        qp[rows, 256:384] = scaled[:, 128:].astype(BF)
    chain = KeyChain(run, mine, *chain_refs, place_in)
    chain.start()

    @pl.when(z == 0)
    def _():
        trunk[c] = mine[c]

    @pl.when(z > 0)
    def _():
        for k in range(4):
            g = place.f_at(-k)
            if k:
                trunk_rows.wait(k)
            keys = product(tx[g], flat(wqkv)[:, 256:]) + vec[0:1, 256:PACKED]
            trunk[c, g] = keys.astype(BF)

    trunk_near = launch(trunk.at[c], trunk.at[c], place.sibling())
    if first:
        run.save(xb, xb_o)
    if first:
        run.save(qp, qp_o)
    chain.finish()
    trunk_near.wait_recv()
    late_tasks = m_tasks
    for t in late_tasks:
        t.start(z > 0)
    pick_parents(kp, chain.slots, choose)
    if first:
        run.save(kp, kp_o)
    if first:
        run.save(trunk, trunk_o)
    if first:
        run.save(mine, mine_o)
    if first:
        a_tasks[1].relay()

    def attend(i, carry):
        h, b = i // 4, lax.rem(i, 4)
        lanes = pl.ds(pl.multiple_of(h * 128, 128), 128)
        rows = pl.ds(pl.multiple_of(b * ROWS, ROWS), ROWS)
        keys = all_keys(trunk, mine, kp, b, lanes)
        s = product_nt(qp[rows, lanes], keys)
        s = jnp.concatenate(
            [s[:, :1024], s[:, 1024:1280] + pen[4 + b], s[:, 1280:] + pen[b]], axis=1
        )
        e = jnp.exp(s - jnp.max(s, axis=1, keepdims=True))
        pb = (e * (1.0 / jnp.sum(e, axis=1, keepdims=True))).astype(BF)
        p[h, b] = pb
        heads[h, b] = product(pb, keys)
        return carry

    lax.fori_loop(0, 12, attend, 0, unroll=2)
    if first:
        run.save(p, p_o)
    if first:
        a_tasks[1].finish()
    back = [None]
    for k in (1, 2, 3, 0):
        g = place.f_at(-k)
        ctx[g, :, 0:128] = jnp.where(lane < 64, pltpu.roll(heads[0, g], 64, 1), heads[1, g]).astype(BF)
        ctx[g, :, 128:256] = jnp.where(lane < 64, pltpu.roll(heads[2, g], 64, 1), 0.0).astype(BF)
        part = product(ctx[g], wo[...])
        if k:
            rs1_s[k - 1] = part.astype(BF)
            back.append(launch(rs1_s.at[k - 1], rs1_r.at[k - 1], place.plane(-k)))
        else:
            own[...] = part
    if first:
        run.save(ctx, ctx_o)
    for k in (1, 2, 3):
        back[k].wait_recv()
    for t in late_tasks:
        t.start(z == 0)
    total = own[...] + rs1_r[0].astype(F32) + rs1_r[1].astype(F32) + rs1_r[2].astype(F32)
    zz = x_ref[...].astype(F32) + total + vec[1:2, :]
    z1[...] = zz
    if first:
        run.save(z1, z1_o)
    hidden = norm_rows(zz, vec[2:3, :], vec[3:4, :])
    hb[f] = hidden.astype(BF)
    came = [None] + [launch(hb.at[f], hb.at[f], place.plane(k)) for k in (1, 2, 3)]
    back = [None]
    for t in m_tasks:
        t.relay()
    if first:
        n_tasks = [Spread(run, qkv_next, wqkv_n), SpreadOutput(run, o_next, wo_n)]
        for t in n_tasks:
            t.start()
    for t in m_tasks:
        t.finish()
    for k in range(4):
        g = place.f_at(-k)
        if k:
            came[k].wait_recv()
        u = product(hb[g], flat(win)) + vec[4:5, :]
        cdf = 0.5 * (1.0 + lax.erf(u * (0.5 ** 0.5)))
        gp[g] = cdf + u * jnp.exp(-0.5 * u * u) * 0.3989422804014327
        low = (u * cdf).astype(BF)
        gl[g] = low
        part = product(low, flat(wout))
        if k:
            rs2_s[k - 1] = part.astype(BF)
            back.append(launch(rs2_s.at[k - 1], rs2_r.at[k - 1], place.plane(-k)))
        else:
            own[...] = part
    if first:
        run.save(hb, hb_o)
    if first:
        run.save(gp, gp_o)
    if first:
        run.save(gl, gl_o)
    if first:
        run.save(win, win_o)
    if first:
        run.save(wout, wout_o)
    if first:
        run.save(wqkv, wqkv_o)
        run.save(wo.at[pl.ds(0, 192)], wo_o)
    for k in (1, 2, 3):
        back[k].wait_recv()
    total = own[...] + rs2_r[0].astype(F32) + rs2_r[1].astype(F32) + rs2_r[2].astype(F32)
    zz = norm_rows(z1[...], vec[2:3, :], vec[3:4, :]) + total + vec[5:6, :]
    z2[...] = zz
    if first:
        run.save(z2, z2_o)
    xn_ref[...] = norm_rows(zz, vec[6:7, :], vec[7:8, :]).astype(xn_ref.dtype)
    if first:
        for t in n_tasks:
            t.relay()
        for t in n_tasks:
            t.finish()
    return z2, (wout, gp, win, gl, hb, z1, wo, ctx, trunk, mine, kp, qp, p, xb, wqkv)


def turn_kernel(*refs):
    run = Run(*refs[-3:])
    run.prepare = lambda: run.greet(True)
    refs = list(refs[:-3])
    ahead, dy_ref, xn_ref, outs, kept, rest = refs[:10], refs[10], refs[11], refs[12:19], refs[19:48], refs[48:]
    held = forward_body(False, run, ahead + [xn_ref] + kept)
    backward_body(False, run, [dy_ref] + ahead[4:7] + outs + rest, held)
    run.close()


def backward_kernel(*refs):
    run = Run(*refs[-3:])
    backward_body(True, run, list(refs[:-3]), None)
    run.close()


def backward_body(extra, run, refs, held):

    def take(n):
        out = refs[:n]
        del refs[:n]
        return out

    dy_ref, vecs, place_in, choose = take(4)
    vec = vecs.at[0 if extra else 1]
    if extra:
        z2 = take(1)[0]
        late_in = take(15)
        pq_in, pk_in, dvec_in = take(3)
    dx_ref, din_o, dout_o, do_o = take(4)
    if extra:
        dq_n, dk_n, dq_o, dk_o, sm_o = take(5)
    else:
        pq, pk, dvec_o = take(3)
    if extra:
        late = take(15)
    else:
        z2, late = held
    wout, gp, win, gl, hb, z1, wo, ctx, trunk, mine, kp, qp, p, xb, wqkv = late
    (
        df, du, da, dctx, dqf, dqkv, dz, dz1, dkt, dself, dpar, tgt, own, rs1_s, rs1_r, rs2_s, rs2_r,
    ) = take(17)
    chain_refs = take(7)
    pin, nin, fin, tin, pout, nout, fout, po, no, fo, to = take(11)
    if extra:
        pq, pk, dvec_o = take(3)
        nq, fq, tq, nk, fk, tk, nq2, fq2, tq2, nk2, fk2, tk2, sm, sm_a, sm_b, sm_v = take(16)
    place = run.place
    z, f, c = place.z, place.f, place.c
    launch = run.launch
    loads = []
    if extra:
        for n, (src, dst) in enumerate(zip(late_in, late)):
            loads.append(run.local(src, dst.at[pl.ds(0, 192)] if n == 6 else dst))
        wo[192:256, :] = jnp.zeros((64, WIDE), BF)

    grad, dgain, dshift = norm_rows_back(z2[...], vec[6:7, :], dy_ref[...].astype(F32))
    dvec_o[6:7, :] = dgain
    dvec_o[7:8, :] = dshift
    dz[...] = grad
    low = grad.astype(BF)
    df[f] = low
    dvec_o[5:6, :] = jnp.sum(low.astype(F32), axis=0, keepdims=True)
    if extra:
        run.greet(True)
    came = [None] + [launch(df.at[f], df.at[f], place.plane(k)) for k in (1, 2, 3)]
    a_tasks = []
    if extra:
        a_tasks = [Collect(run, pq_in, nq, fq, tq, dq_n), Collect(run, pk_in, nk, fk, tk, dk_n)]
    for t in a_tasks:
        t.start()
    back = [None]
    bias = jnp.zeros((1, WIDE), F32)
    for a in loads[:3]:
        a.wait()
    for k in range(4):
        g = place.f_at(-k)
        if k:
            came[k].wait_recv()
        low = (product_nt(df[g], flat(wout)) * gp[g]).astype(BF)
        du[g] = low
        bias = bias + jnp.sum(low.astype(F32), axis=0, keepdims=True)
        part = product_nt(low, flat(win))
        if k:
            rs1_s[k - 1] = part.astype(BF)
            back.append(launch(rs1_s.at[k - 1], rs1_r.at[k - 1], place.plane(-k)))
        else:
            own[...] = part
            for t in a_tasks:
                t.middle()
    dvec_o[4:5, :] = bias
    m_tasks = [Collect(run, pin, nin, fin, tin, din_o), Collect(run, pout, nout, fout, None, dout_o)]
    o_task = CollectOutput(run, po, no, fo, to, do_o)

    def split_rows(dst, left, right, i):
        lanes = pl.ds(pl.multiple_of(i * 384, 128), 384)
        value = product_tn(left[:, :, lanes].reshape(512, 384), right).astype(BF)
        for zz in range(2):
            for cc in range(2):
                at = (2 * zz + cc) * 96
                dst[cc, 2 * i + zz] = value[at : at + 96, :]

    def ffn_grads(i, carry):
        split_rows(pout, gl, flat(df), i)
        split_rows(pin, hb, flat(du), i)
        return carry

    for a in loads[3:5]:
        a.wait()
    lax.fori_loop(0, 2, ffn_grads, 0)
    for t in m_tasks:
        t.start()
    for t in m_tasks:
        t.middle()
    for k in (1, 2, 3):
        back[k].wait_recv()
    up = dz[...] + own[...] + rs1_r[0].astype(F32) + rs1_r[1].astype(F32) + rs1_r[2].astype(F32)
    for a in loads[5:6]:
        a.wait()
    grad, dgain, dshift = norm_rows_back(z1[...], vec[2:3, :], up)
    dvec_o[2:3, :] = dgain
    dvec_o[3:4, :] = dshift
    dz1[...] = grad
    low = grad.astype(BF)
    da[f] = low
    dvec_o[1:2, :] = jnp.sum(low.astype(F32), axis=0, keepdims=True)
    came = [None] + [launch(da.at[f], da.at[f], place.plane(k)) for k in (1, 2, 3)]
    for t in a_tasks:
        t.end()
    dkt[...] = jnp.zeros_like(dkt)
    lane = lax.broadcasted_iota(jnp.int32, (ROWS, 128), 1)
    for a in loads[6:]:
        a.wait()
    for k in range(4):
        g = place.f_at(-k)
        rows = pl.ds(pl.multiple_of(g * ROWS, ROWS), ROWS)
        if k:
            came[k].wait_recv()
        packed = product_nt(da[g], wo[...])
        ahead, after = packed[:, :128], packed[:, 128:]
        dctx[rows, 0:128] = jnp.where(lane < 64, 0.0, pltpu.roll(ahead, 64, 1)).astype(BF)
        dctx[rows, 128:256] = jnp.where(lane < 64, 0.0, ahead).astype(BF)
        dctx[rows, 256:384] = jnp.where(lane < 64, 0.0, pltpu.roll(after, 64, 1)).astype(BF)
    value = product_tn(flat(ctx), flat(da)).astype(BF)
    for cc in range(2):
        po[cc] = value[96 * cc : 96 * (cc + 1), :]
    o_task.start()
    o_task.middle()

    def attend(i, carry):
        h, b = i // 4, lax.rem(i, 4)
        lanes = pl.ds(pl.multiple_of(h * 128, 128), 128)
        rows = pl.ds(pl.multiple_of(b * ROWS, ROWS), ROWS)
        keys = all_keys(trunk, mine, kp, b, lanes)
        q, g = qp[rows, lanes], dctx[rows, lanes]
        low = p[h, b]
        pf = low.astype(F32)
        dp = product_nt(g, keys)
        t = pf * dp
        ds = (t - pf * jnp.sum(t, axis=1, keepdims=True)).astype(BF)
        dqf[h, rows, :] = product(ds, keys) * (HEAD_DIM ** (-0.5))
        dkv = product_tn(jnp.concatenate([ds, low], axis=0), jnp.concatenate([q, g], axis=0))
        dkt[:, lanes] += dkv[:1024]
        dself[b, :, lanes] = dkv[1024:1280]
        dpar[b, :, lanes] = dkv[1280:]
        return carry

    lax.fori_loop(0, 12, attend, 0)
    for cc in range(2):
        for j in range(4):
            at = cc * 512 + j * ROWS
            tgt[cc, 0, j] = dkt[at : at + ROWS, :].astype(BF)

    chain = GradChain(run, tgt, *chain_refs)
    chain.start()

    def scatter(j, carry):
        for cc in range(2):
            half = slice(cc * ROWS, (cc + 1) * ROWS)
            total = dpar[0, half, :] * choose[0, j]
            for b in range(1, 4):
                total = total + dpar[b, half, :] * choose[b, j]
            tgt[cc, 1, j] = total.astype(BF)
            tgt[cc, 2, j] = dself[j, half, :].astype(BF)
        return carry

    lax.fori_loop(0, 4, scatter, 0)
    chain.hand_over(1)
    chain.hand_over(2)
    for g in range(4):
        rows = slice(g * ROWS, (g + 1) * ROWS)
        ahead = jnp.where(lane < 64, dqf[0, rows, :], pltpu.roll(dqf[1, rows, :], 64, 1))
        dqkv[g, :, 0:128] = ahead.astype(BF)
        dqkv[g, :, 128:256] = jnp.where(lane < 64, dqf[2, rows, :], 0.0).astype(BF)
    chain.middle()
    for t in m_tasks:
        t.end()
    chain.pass_on()

    def q_grads(i, carry):
        split_rows(pq, xb, dqkv[:, :, :256].reshape(512, 256), i)
        return carry

    lax.fori_loop(0, 2, q_grads, 0)
    end_tasks = []
    if extra:
        end_tasks = [Collect(run, pk, nk2, fk2, tk2, dk_o), Collect(run, pq, nq2, fq2, tq2, dq_o)]
        end_tasks[1].start()

    def store(ft, value):
        dqkv[ft, :, 256:] = value.astype(BF)

    chain.finish(place_in, store)

    def k_grads(i, carry):
        split_rows(pk, xb, dqkv[:, :, 256:].reshape(512, SLICE), i)
        return carry

    lax.fori_loop(0, 2, k_grads, 0)
    if extra:
        end_tasks[0].start()
        end_tasks[1].middle()
        end_tasks[0].middle()
    back = [None]
    for k in (1, 2, 3, 0):
        g = place.f_at(-k)
        part = product_nt(dqkv[g], flat(wqkv))
        if k:
            rs2_s[k - 1] = part.astype(BF)
            back.append(launch(rs2_s.at[k - 1], rs2_r.at[k - 1], place.plane(-k)))
        else:
            own[...] = part

    sums = jnp.sum(flat(dqkv).astype(F32), axis=0, keepdims=True)
    dvec_o[0:1, :] = jnp.concatenate([sums, jnp.zeros((1, WIDE - PACKED), F32)], axis=1)
    if extra:
        sm[0:8, :] = dvec_o[...]
        sm[8:16, :] = dvec_in[...]
        sm_near = launch(sm, sm_a, place.sibling())
        sm_near.wait_recv()
        sm_a[...] = sm[...] + sm_a[...]
        sm_far = [launch(sm_a, sm_b.at[k - 1], place.column(k)) for k in (1, 2, 3)]
    o_task.end()
    for t in a_tasks:
        t.last()
    for k in (1, 2, 3):
        back[k].wait_recv()
    total = dz1[...] + own[...] + rs2_r[0].astype(F32) + rs2_r[1].astype(F32) + rs2_r[2].astype(F32)
    dx_ref[...] = total.astype(dx_ref.dtype)
    if extra:
        for t in end_tasks:
            t.end()
        for a in sm_far:
            a.wait_recv()
        sm_v[...] = sm_a[...] + sm_b[0] + sm_b[1] + sm_b[2]
        sm_last = [launch(sm_v, sm_o.at[f], place.plane(k)) for k in (1, 2, 3)]
        sm_o[f] = sm_v[...]
        for a in sm_last:
            a.wait_recv()
    for t in m_tasks + [o_task] + end_tasks:
        t.last()


ANY = pl.BlockSpec(memory_space=pl.ANY)
VM = pl.BlockSpec(memory_space=pltpu.VMEM)
SM = pl.BlockSpec(memory_space=pltpu.SMEM)
LIMIT = 60 * 1024 * 1024
SEMS = (256, 256, 32)


def shape(*dims, dtype=BF):
    return jax.ShapeDtypeStruct(dims, dtype)


def call(kernel, number, outs, out_specs, in_specs, scratch, args, flops):
    return pl.pallas_call(
        kernel,
        out_shape=tuple(outs),
        in_specs=in_specs,
        out_specs=tuple(out_specs),
        scratch_shapes=[pltpu.VMEM(s.shape, s.dtype) for s in scratch]
        + [pltpu.SemaphoreType.DMA((n,)) for n in SEMS],
        compiler_params=pltpu.CompilerParams(
            collective_id=number, has_side_effects=True, vmem_limit_bytes=LIMIT
        ),
        cost_estimate=pl.CostEstimate(flops=flops, bytes_accessed=20000000, transcendentals=0),
    )(*args)


def column_parts(query, key, value, inner):
    n = query.shape[0] * query.shape[1]
    q = query.reshape(n, 4, 3, 64)
    q = jnp.pad(q, ((0, 0), (0, 0), (0, 1), (0, 0))).reshape(n, 4, 256)
    kv = jnp.stack([key.reshape(n, 4, 3, 64), value.reshape(n, 4, 3, 64)], axis=3).reshape(n, 4, 384)
    up = inner.reshape(n, 4, 4, 192).transpose(0, 2, 1, 3).reshape(n, 4, WIDE)
    return jnp.concatenate([q, kv, up], axis=2).transpose(1, 0, 2)


LOCAL = shape(ROWS, WIDE, dtype=F32)
FULL = shape(4, ROWS, WIDE)
PIECE = shape(3, ROWS, WIDE)
QKV = shape(4, 2, 96, PACKED)
BIG = shape(4, 2, 96, WIDE)
OUTPUT = shape(192, WIDE)
HALVES = shape(2, 4, ROWS, SLICE)
QUARTERS = shape(4, ROWS, SLICE)
SAVED = (
    FULL, shape(512, SLICE), HALVES, HALVES, shape(4, 2, ROWS, SLICE), shape(3, 4, ROWS, NKEYS),
    shape(4, ROWS, 256), LOCAL, FULL, shape(4, ROWS, WIDE, dtype=F32), FULL, LOCAL,
)


FORWARD_SCRATCH = (
    list(SAVED)
    + [BIG, BIG, QKV, shape(256, WIDE), shape(3, 4, ROWS, 128, dtype=F32), LOCAL]
    + [PIECE] * 4 + [FULL, HALVES] + [QUARTERS] * 5
)


def forward_layer(state, chunks, rows_o, rows_out, vecs, place_in, choose, pen):
    outs = (LOCAL,) + SAVED + (BIG, BIG, QKV, OUTPUT, QKV, OUTPUT)
    got = call(
        forward_kernel, 1, outs, (VM,) + (ANY,) * (len(outs) - 1), [VM] + [ANY] * 3 + [VM] + [SM] * 3,
        FORWARD_SCRATCH, (state, chunks, rows_o, rows_out, vecs, place_in, choose, pen), 3 * 10**9,
    )
    return got[0], got[1:13], got[13:]


def collect_scratch(columns, rows):
    return [shape(4, 96, columns), shape(3, 96, columns)] + ([shape(96, columns, dtype=F32)] if rows else [])


OUT_SCRATCH = [shape(96, WIDE), shape(4, 96, WIDE), shape(96, WIDE, dtype=F32)]
PARTS = (shape(2, 4, 96, 256), shape(2, 4, 96, SLICE))
SHARES = (shape(4, 24, 256, dtype=F32), shape(4, 24, SLICE, dtype=F32))


def backward_scratch():
    keys = shape(4, 256, SLICE, dtype=F32)
    part = shape(2, 4, 96, WIDE)
    scratch = [
        FULL, FULL, FULL, shape(512, SLICE), shape(3, 512, 128, dtype=F32), shape(4, ROWS, PACKED), LOCAL, LOCAL,
        shape(1024, SLICE, dtype=F32), keys, keys, shape(2, 3, 4, ROWS, SLICE), LOCAL, PIECE, PIECE, PIECE, PIECE,
        shape(3, 4, ROWS, SLICE),
    ] + [QUARTERS] * 6
    scratch += [part] + collect_scratch(WIDE, True) + [part] + collect_scratch(WIDE, False)
    return scratch + [shape(2, 96, WIDE)] + OUT_SCRATCH


SUMS, SUMS2 = shape(8, WIDE, dtype=F32), shape(16, WIDE, dtype=F32)
GRADS = (shape(4, 24, WIDE, dtype=F32), shape(96, WIDE, dtype=F32), shape(24, WIDE, dtype=F32))


def turn_layer(state, chunks, rows_o, rows_out, vecs, place_in, choose, pen, wqkv, wo, upstream):
    outs = (shape(ROWS, WIDE), LOCAL) + GRADS + PARTS + (SUMS,)
    return call(
        turn_kernel, 2, outs, (VM,) * len(outs), [VM] + [ANY] * 3 + [VM] + [SM] * 3 + [ANY] * 2 + [VM],
        FORWARD_SCRATCH + backward_scratch(),
        (state, chunks, rows_o, rows_out, vecs, place_in, choose, pen, wqkv, wo, upstream), 9 * 10**9,
    )


def backward_layer(upstream, weights, vecs, place_in, choose, saved, before):
    wqkv, wo, win, wout = weights
    xb, qp, trunk, mine, kp, p, ctx, z1, hb, gp, gl, z2 = saved
    outs = (shape(ROWS, WIDE),) + GRADS + SHARES + SHARES + (shape(4, 16, WIDE, dtype=F32),)
    scratch = [
        BIG, SAVED[9], BIG, FULL, FULL, LOCAL, shape(256, WIDE), SAVED[6], HALVES, HALVES, SAVED[4], SAVED[1], SAVED[5],
        FULL, QKV,
    ] + backward_scratch()
    scratch += list(PARTS) + [SUMS]
    scratch += (collect_scratch(256, True) + collect_scratch(SLICE, True)) * 2
    scratch += [SUMS2, SUMS2, shape(3, 16, WIDE, dtype=F32), SUMS2]
    return call(
        backward_kernel, 4, outs, (VM,) * len(outs), [VM] * 2 + [SM] * 2 + [VM] + [ANY] * 15 + [VM] * 3, scratch,
        (upstream, vecs, place_in, choose, z2, wout, gp, win, gl, hb, z1, wo, ctx, trunk, mine, kp, qp, p, xb, wqkv)
        + tuple(before),
        6 * 10**9,
    )


def slice_body(
    activations, query_weight, query_bias, key_weight, value_weight, value_bias, output_weight, output_bias,
    first_gain, first_shift, inner_weight, inner_bias, outer_weight, outer_bias, second_gain, second_shift,
    cotangent, parents, segments,
):
    place = Place()
    z, f, c = place.z, place.f, place.c
    col = column_parts(query_weight, key_weight, value_weight, inner_weight)
    vectors = (query_bias, value_bias, output_bias, first_gain, first_shift, outer_bias, second_gain, second_shift)
    label = jnp.broadcast_to(segments[:1].astype(BF)[None], (2, 1))
    small = jnp.concatenate(vectors + (inner_bias, label), axis=1)
    small = jnp.pad(small, ((0, 14), (0, 384 - small.shape[1])))
    colp, op, smallg = call(
        exchange_kernel, 0, (shape(4, 48, 1408), shape(4, 48, WIDE), shape(4, 2, 4, 16, 384)), (ANY,) * 3, [ANY] * 3,
        [], (col, output_weight.reshape(48, WIDE), small), 1000,
    )
    colp = colp.reshape(4, 2, 24, 1408).transpose(1, 0, 2, 3).reshape(2, 96, 1408)
    op = op.reshape(4, 2, 24, WIDE).transpose(1, 0, 2, 3).reshape(2, 96, WIDE)
    small = smallg[:, :, :, :2].transpose(3, 0, 2, 1, 4).astype(F32)
    parts = [small[..., i * 24 : (i + 1) * 24].reshape(2, WIDE) for i in range(8)]
    q_all, v_all, o_all, g1, s1, out_all, g2, s2 = parts
    in_mine = lax.dynamic_index_in_dim(small[..., 192:288], f, 2, keepdims=False).reshape(2, WIDE)
    q_mine = lax.dynamic_slice_in_dim(q_all, 192 * f, 192, 1)
    v_mine = lax.dynamic_slice_in_dim(v_all, 192 * f, 192, 1).reshape(2, 3, 64)
    kv_mine = jnp.pad(v_mine, ((0, 0), (0, 0), (64, 0))).reshape(2, SLICE)
    qkv_mine = jnp.pad(jnp.concatenate([q_mine, jnp.zeros((2, 64), F32), kv_mine], axis=1), ((0, 0), (0, WIDE - PACKED)))
    vecs = jnp.stack([qkv_mine, o_all, g1, s1, in_mine, out_all, g2, s2], axis=1)

    labels = small[0, :, :, 0, 288].reshape(16).astype(jnp.int32)
    above = lookup_rows(labels, parents)
    order = jnp.arange(16, dtype=jnp.int32)
    branch = jnp.logical_and(above == labels[0], order >= 4)
    slot = jnp.where(branch, jnp.sum((branch[:, None] & (order[:, None] < order[None, :])).astype(jnp.int32), axis=0), 4)
    in_slot = slot[None, :] == jnp.arange(4, dtype=jnp.int32)[:, None]
    place_in = lax.dynamic_slice_in_dim(in_slot.astype(F32), 4 * z, 4, 1)
    parent = lax.dynamic_slice_in_dim(above, 4 * z, 4, 0)
    match = parent[:, None, None] == jnp.where(in_slot, labels[None, :], -1)[None]
    choose = jnp.any(match, axis=2).astype(F32)
    pen = jnp.concatenate(
        [jnp.where(jnp.any(match, axis=(1, 2)), 0.0, MASKED), jnp.where(z > 0, jnp.zeros((4,), F32), MASKED)]
    ).astype(F32)

    shared = (colp, op, outer_weight, vecs, place_in, choose, pen)
    state, kept0, (win0, wout0, wqkv0, wo0, wqkv1, wo1) = forward_layer(activations, *shared)
    outcome, upstream, din1, dout1, do1, pq, pk, dvec1 = turn_layer(state, *shared, wqkv1, wo1, cotangent)
    upstream, din0, dout0, do0, dq1, dk1, dq0, dk0, rsm = backward_layer(
        upstream, (wqkv0, wo0, win0, wout0), vecs, place_in, choose, kept0, (pq, pk, dvec1)
    )
    dq = jnp.stack([dq0, dq1]).transpose(0, 2, 1, 3)[..., :192].reshape(2, 24, WIDE)
    dkv = jnp.stack([dk0, dk1]).transpose(0, 2, 1, 3).reshape(2, 24, 4, 3, 2, 64)
    dk = dkv[..., 0, :].reshape(2, 24, WIDE)
    dv = dkv[..., 1, :].reshape(2, 24, WIDE)
    dinner = jnp.stack([din0, din1]).reshape(2, 4, 24, 4, 192).transpose(0, 2, 3, 1, 4).reshape(2, 24, 3072)
    rsm = rsm.reshape(4, 2, 8, WIDE)
    sums = jnp.sum(rsm, axis=0)
    dqb = rsm[:, :, 0, :192].transpose(1, 0, 2).reshape(2, WIDE)
    dvb = rsm[:, :, 0, 256:640].reshape(4, 2, 3, 2, 64)[:, :, :, 1].transpose(1, 0, 2, 3).reshape(2, WIDE)
    rows = jnp.stack([dqb, dvb, sums[:, 1], sums[:, 2], sums[:, 3], sums[:, 5], sums[:, 6], sums[:, 7]])
    rows = lax.dynamic_slice_in_dim(rows, 24 * (8 * z + 2 * f + c), 24, 2)
    dib = lax.dynamic_index_in_dim(rsm[:, :, 4], f, 0, keepdims=False)
    dib = lax.dynamic_slice_in_dim(dib, 96 * (2 * z + c), 96, 1)
    return (
        outcome, upstream, dq, rows[0], dk, dv, rows[1], jnp.stack([do0, do1]), rows[2], rows[3], rows[4],
        dinner, dib, jnp.stack([dout0, dout1]), rows[5], rows[6], rows[7],
    )


def solution(mesh):
    placed = (
        P("fsdp", None),
        P(None, "fsdp", None),
        P(None, "fsdp"),
        P(None, "fsdp", None),
        P(None, "fsdp", None),
        P(None, "fsdp"),
        P(None, "fsdp", None),
        P(None, "fsdp"),
        P(None, "fsdp"),
        P(None, "fsdp"),
        P(None, "fsdp", None),
        P(None, "fsdp"),
        P(None, "fsdp", None),
        P(None, "fsdp"),
        P(None, "fsdp"),
        P(None, "fsdp"),
        P("fsdp", None),
        P(),
        P("fsdp"),
    )
    return jax.shard_map(
        slice_body if mesh.shape["fsdp"] == 32 else body,
        mesh=mesh,
        in_specs=placed,
        out_specs=(
            P("fsdp", None),
            P("fsdp", None),
            P(None, "fsdp", None),
            P(None, "fsdp"),
            P(None, "fsdp", None),
            P(None, "fsdp", None),
            P(None, "fsdp"),
            P(None, "fsdp", None),
            P(None, "fsdp"),
            P(None, "fsdp"),
            P(None, "fsdp"),
            P(None, "fsdp", None),
            P(None, "fsdp"),
            P(None, "fsdp", None),
            P(None, "fsdp"),
            P(None, "fsdp"),
            P(None, "fsdp"),
        ),
        check_vma=False,
    )
```

```python
import jax
import jax.numpy as jnp
from jax import lax
from jax.experimental import pallas as pl
from jax.experimental.pallas import tpu as pltpu
from jax.sharding import PartitionSpec as P

HEADS = 12
HEAD_DIM = 64
LAYERS = 2
TREE_LEN = 4096


EPSILON = 1e-06
MASKED = -1000000000.0


def partner_2(shard, axis, stride):
    return lax.ppermute(shard, axis, [(i, i ^ 1 << stride) for i in range(lax.axis_size(axis))])


def as_sent(shard):
    return jax.tree.map(lambda a: a.astype(jnp.bfloat16) if a.dtype == jnp.float32 else a, shard)


def product(a, b):
    return jnp.dot(a, b, preferred_element_type=jnp.float32)


def product_tn(a, b):
    return lax.dot_general(a, b, (((0,), (0,)), ((), ())), preferred_element_type=jnp.float32)


def product_nt(a, b):
    return lax.dot_general(a, b, (((1,), (1,)), ((), ())), preferred_element_type=jnp.float32)


def exact_gelu(u):
    return jax.nn.gelu(u, approximate=False)


def layer_norm(z, gain_vec, shift_vec):
    centre = z - jnp.mean(z, axis=-1, keepdims=True)
    scaled = centre * lax.rsqrt(jnp.mean(centre * centre, axis=-1, keepdims=True) + EPSILON)
    return scaled * gain_vec.astype(jnp.float32) + shift_vec.astype(jnp.float32)


def norm_backward(z, gain_vec, upstream):
    centre = z - jnp.mean(z, axis=-1, keepdims=True)
    invert = lax.rsqrt(jnp.mean(centre * centre, axis=-1, keepdims=True) + EPSILON)
    scaled = centre * invert
    weighted = upstream * gain_vec.astype(jnp.float32)
    inner = invert * (
        weighted
        - jnp.mean(weighted, axis=-1, keepdims=True)
        - scaled * jnp.mean(weighted * scaled, axis=-1, keepdims=True)
    )
    return (inner, jnp.sum(upstream * scaled, axis=0), jnp.sum(upstream, axis=0))


def lookup_rows(ids, parents):
    table = jnp.arange(parents.shape[0], dtype=jnp.int32)
    return jnp.sum(jnp.where(ids[:, None] == table[None, :], parents[None, :], 0), axis=1)


def join_heads(stacked):
    return stacked.transpose(1, 0, 2).reshape(stacked.shape[1], -1)


def gather_group(key_rows, value_rows, labels, position, bit_count):
    for b in range(bit_count):
        partner = partner_2((key_rows, value_rows, labels), "fsdp", b)
        upper_side = position >> b & 1 == 1
        key_rows = jnp.where(
            upper_side,
            jnp.concatenate([partner[0], key_rows]),
            jnp.concatenate([key_rows, partner[0]]),
        )
        value_rows = jnp.where(
            upper_side,
            jnp.concatenate([partner[1], value_rows]),
            jnp.concatenate([value_rows, partner[1]]),
        )
        labels = jnp.where(
            upper_side, jnp.concatenate([partner[2], labels]), jnp.concatenate([labels, partner[2]])
        )
    return (key_rows, value_rows, labels)


def sum_group(key_grad, value_grad, position, bit_count):
    for b in reversed(range(bit_count)):
        halfway = key_grad.shape[0] // 2
        upper_side = position >> b & 1 == 1
        outgoing = (
            jnp.where(upper_side, key_grad[:halfway], key_grad[halfway:]),
            jnp.where(upper_side, value_grad[:halfway], value_grad[halfway:]),
        )
        partner = partner_2((as_sent(outgoing[0]), as_sent(outgoing[1])), "fsdp", b)
        key_grad = jnp.where(upper_side, key_grad[halfway:], key_grad[:halfway]) + partner[0]
        value_grad = jnp.where(upper_side, value_grad[halfway:], value_grad[:halfway]) + partner[1]
    return (key_grad, value_grad)


def attend_forward(queries, key_rows, value_rows, allowed):
    factor = HEAD_DIM ** (-0.5)

    def one_head(j):
        start = j * HEAD_DIM
        q = lax.dynamic_slice_in_dim(queries, start, HEAD_DIM, 1)
        k = lax.dynamic_slice_in_dim(key_rows, start, HEAD_DIM, 1)
        v = lax.dynamic_slice_in_dim(value_rows, start, HEAD_DIM, 1)
        s = jnp.where(allowed, product_nt(q, k) * factor, MASKED)
        maxima = jnp.max(s, axis=1, keepdims=True)
        e = jnp.exp(s - maxima)
        totals = jnp.sum(e, axis=1, keepdims=True)
        p = (e / totals).astype(jnp.bfloat16)
        return (product(p, v), (maxima + jnp.log(totals))[:, 0])

    stacked, log_total = lax.map(one_head, jnp.arange(HEADS))
    return (join_heads(stacked), log_total)


def attend_backward(queries, key_rows, value_rows, allowed, log_total, grad_context):
    factor = HEAD_DIM ** (-0.5)

    def one_head(j):
        start = j * HEAD_DIM
        q = lax.dynamic_slice_in_dim(queries, start, HEAD_DIM, 1)
        k = lax.dynamic_slice_in_dim(key_rows, start, HEAD_DIM, 1)
        v = lax.dynamic_slice_in_dim(value_rows, start, HEAD_DIM, 1)
        g = lax.dynamic_slice_in_dim(grad_context, start, HEAD_DIM, 1)
        s = jnp.where(allowed, product_nt(q, k) * factor, MASKED)
        p = jnp.where(allowed, jnp.exp(s - log_total[j][:, None]), 0.0)
        grad_p = product_nt(g, v)
        grad_v = product_tn(p.astype(jnp.bfloat16), g)
        grad_s = (p * (grad_p - jnp.sum(p * grad_p, axis=1, keepdims=True))).astype(jnp.bfloat16)
        grad_q = product(grad_s, k) * factor
        grad_k = product_tn(grad_s, q) * factor
        return (grad_q, grad_k, grad_v)

    grad_q, grad_k, grad_v = lax.map(one_head, jnp.arange(HEADS))
    return (join_heads(grad_q), join_heads(grad_k), join_heads(grad_v))


def layer_forward(state, full, segments, parent_one, parent_two, position, bit_count):
    (
        q_weight,
        q_bias,
        k_weight,
        v_weight,
        v_bias,
        o_weight,
        o_bias,
        gain_one,
        shift_one,
        up_weight,
        up_bias,
        down_weight,
        down_bias,
        gain_two,
        shift_two,
    ) = full
    inputs = state.astype(jnp.bfloat16)
    queries = (product(inputs, q_weight) + q_bias).astype(jnp.bfloat16)
    key_local = product(inputs, k_weight).astype(jnp.bfloat16)
    value_local = (product(inputs, v_weight) + v_bias).astype(jnp.bfloat16)
    key_rows, value_rows, labels = gather_group(
        key_local, value_local, segments, position, bit_count
    )
    allowed = (
        (labels[None, :] == segments[:, None])
        | (labels[None, :] == parent_one[:, None])
        | (labels[None, :] == parent_two[:, None])
    )
    context_wide, log_total = attend_forward(queries, key_rows, value_rows, allowed)
    context = context_wide.astype(jnp.bfloat16)
    first_sum = state + product(context, o_weight) + o_bias
    hidden = layer_norm(first_sum, gain_one, shift_one)
    hidden_low = hidden.astype(jnp.bfloat16)
    pre_act = product(hidden_low, up_weight) + up_bias
    gelu_out = exact_gelu(pre_act).astype(jnp.bfloat16)
    second_sum = hidden + product(gelu_out, down_weight) + down_bias
    record = (
        inputs,
        queries,
        key_rows,
        value_rows,
        allowed,
        log_total,
        context,
        first_sum,
        hidden_low,
        pre_act,
        gelu_out,
        second_sum,
    )
    return (record, layer_norm(second_sum, gain_two, shift_two))


def layer_backward(upstream, full, record, position, bit_count):
    (
        q_weight,
        q_bias,
        k_weight,
        v_weight,
        v_bias,
        o_weight,
        o_bias,
        gain_one,
        shift_one,
        up_weight,
        up_bias,
        down_weight,
        down_bias,
        gain_two,
        shift_two,
    ) = full
    (
        inputs,
        queries,
        key_rows,
        value_rows,
        allowed,
        log_total,
        context,
        first_sum,
        hidden_low,
        pre_act,
        gelu_out,
        second_sum,
    ) = record
    grad_z2, grad_gain_two, grad_shift_two = norm_backward(second_sum, gain_two, upstream)
    grad_f = grad_z2.astype(jnp.bfloat16)
    grad_down_bias = jnp.sum(grad_f.astype(jnp.float32), axis=0)
    grad_down = product_tn(gelu_out, grad_f)
    grad_gelu = product_nt(grad_f, down_weight)
    unused_value, gelu_back = jax.vjp(exact_gelu, pre_act)
    grad_u = gelu_back(grad_gelu)[0].astype(jnp.bfloat16)
    grad_up_bias = jnp.sum(grad_u.astype(jnp.float32), axis=0)
    grad_up = product_tn(hidden_low, grad_u)
    grad_h = grad_z2 + product_nt(grad_u, up_weight)
    grad_z1, grad_gain_one, grad_shift_one = norm_backward(first_sum, gain_one, grad_h)
    grad_a = grad_z1.astype(jnp.bfloat16)
    grad_o_bias = jnp.sum(grad_a.astype(jnp.float32), axis=0)
    grad_o = product_tn(context, grad_a)
    grad_context = product_nt(grad_a, o_weight).astype(jnp.bfloat16)
    grad_q, key_grad, value_grad = attend_backward(
        queries, key_rows, value_rows, allowed, log_total, grad_context
    )
    key_grad, value_grad = sum_group(key_grad, value_grad, position, bit_count)
    q_low = grad_q.astype(jnp.bfloat16)
    k_low = key_grad.astype(jnp.bfloat16)
    v_low = value_grad.astype(jnp.bfloat16)
    grad_x = (
        grad_z1
        + product_nt(q_low, q_weight)
        + product_nt(k_low, k_weight)
        + product_nt(v_low, v_weight)
    )
    terms = (
        product_tn(inputs, q_low),
        jnp.sum(q_low.astype(jnp.float32), axis=0),
        product_tn(inputs, k_low),
        product_tn(inputs, v_low),
        jnp.sum(v_low.astype(jnp.float32), axis=0),
        grad_o,
        grad_o_bias,
        grad_gain_one,
        grad_shift_one,
        grad_up,
        grad_up_bias,
        grad_down,
        grad_down_bias,
        grad_gain_two,
        grad_shift_two,
    )
    return (grad_x, terms)


def stack_layers(groups, n):
    return jnp.stack([g[n] for g in groups])


def body(
    activations,
    query_weight,
    query_bias,
    key_weight,
    value_weight,
    value_bias,
    output_weight,
    output_bias,
    first_gain,
    first_shift,
    inner_weight,
    inner_bias,
    outer_weight,
    outer_bias,
    second_gain,
    second_shift,
    cotangent,
    parents,
    segments,
):
    position = lax.axis_index("fsdp")
    bit_count = (TREE_LEN // activations.shape[0]).bit_length() - 1
    parent_one = lookup_rows(segments, parents)
    parent_two = lookup_rows(parent_one, parents)
    state = activations.astype(jnp.float32)
    saved = []
    kept_weights = []
    for i in range(LAYERS):
        full = (
            lax.all_gather(query_weight[i], "fsdp", axis=0, tiled=True),
            lax.all_gather(query_bias[i], "fsdp", axis=0, tiled=True),
            lax.all_gather(key_weight[i], "fsdp", axis=0, tiled=True),
            lax.all_gather(value_weight[i], "fsdp", axis=0, tiled=True),
            lax.all_gather(value_bias[i], "fsdp", axis=0, tiled=True),
            lax.all_gather(output_weight[i], "fsdp", axis=0, tiled=True),
            lax.all_gather(output_bias[i], "fsdp", axis=0, tiled=True),
            lax.all_gather(first_gain[i], "fsdp", axis=0, tiled=True),
            lax.all_gather(first_shift[i], "fsdp", axis=0, tiled=True),
            lax.all_gather(inner_weight[i], "fsdp", axis=0, tiled=True),
            lax.all_gather(inner_bias[i], "fsdp", axis=0, tiled=True),
            lax.all_gather(outer_weight[i], "fsdp", axis=0, tiled=True),
            lax.all_gather(outer_bias[i], "fsdp", axis=0, tiled=True),
            lax.all_gather(second_gain[i], "fsdp", axis=0, tiled=True),
            lax.all_gather(second_shift[i], "fsdp", axis=0, tiled=True),
        )
        kept_weights.append(full)
        record, state = layer_forward(
            state, full, segments, parent_one, parent_two, position, bit_count
        )
        saved.append(record)
    outcome = state.astype(jnp.bfloat16)
    upstream = cotangent.astype(jnp.float32)
    layer_grads = [None] * LAYERS
    for i in reversed(range(LAYERS)):
        full = (
            lax.all_gather(query_weight[i], "fsdp", axis=0, tiled=True),
            lax.all_gather(query_bias[i], "fsdp", axis=0, tiled=True),
            lax.all_gather(key_weight[i], "fsdp", axis=0, tiled=True),
            lax.all_gather(value_weight[i], "fsdp", axis=0, tiled=True),
            lax.all_gather(value_bias[i], "fsdp", axis=0, tiled=True),
            lax.all_gather(output_weight[i], "fsdp", axis=0, tiled=True),
            lax.all_gather(output_bias[i], "fsdp", axis=0, tiled=True),
            lax.all_gather(first_gain[i], "fsdp", axis=0, tiled=True),
            lax.all_gather(first_shift[i], "fsdp", axis=0, tiled=True),
            lax.all_gather(inner_weight[i], "fsdp", axis=0, tiled=True),
            lax.all_gather(inner_bias[i], "fsdp", axis=0, tiled=True),
            lax.all_gather(outer_weight[i], "fsdp", axis=0, tiled=True),
            lax.all_gather(outer_bias[i], "fsdp", axis=0, tiled=True),
            lax.all_gather(second_gain[i], "fsdp", axis=0, tiled=True),
            lax.all_gather(second_shift[i], "fsdp", axis=0, tiled=True),
        )
        upstream, terms = layer_backward(upstream, full, saved[i], position, bit_count)
        layer_grads[i] = (
            lax.psum_scatter(terms[0], "fsdp", scatter_dimension=0, tiled=True),
            lax.psum_scatter(terms[1], "fsdp", scatter_dimension=0, tiled=True),
            lax.psum_scatter(terms[2], "fsdp", scatter_dimension=0, tiled=True),
            lax.psum_scatter(terms[3], "fsdp", scatter_dimension=0, tiled=True),
            lax.psum_scatter(terms[4], "fsdp", scatter_dimension=0, tiled=True),
            lax.psum_scatter(terms[5], "fsdp", scatter_dimension=0, tiled=True),
            lax.psum_scatter(terms[6], "fsdp", scatter_dimension=0, tiled=True),
            lax.psum_scatter(terms[7], "fsdp", scatter_dimension=0, tiled=True),
            lax.psum_scatter(terms[8], "fsdp", scatter_dimension=0, tiled=True),
            lax.psum_scatter(terms[9], "fsdp", scatter_dimension=0, tiled=True),
            lax.psum_scatter(terms[10], "fsdp", scatter_dimension=0, tiled=True),
            lax.psum_scatter(terms[11], "fsdp", scatter_dimension=0, tiled=True),
            lax.psum_scatter(terms[12], "fsdp", scatter_dimension=0, tiled=True),
            lax.psum_scatter(terms[13], "fsdp", scatter_dimension=0, tiled=True),
            lax.psum_scatter(terms[14], "fsdp", scatter_dimension=0, tiled=True),
        )
    shares = tuple((stack_layers(layer_grads, n) for n in range(15)))
    return (outcome, upstream.astype(jnp.bfloat16)) + tuple(shares)


MESH = pl.DeviceIdType.MESH
BF = jnp.bfloat16
F32 = jnp.float32
WIDE = 768
SLICE = 384
PACKED = 640
ROWS = 128
NKEYS = 1536


class Pool:
    def __init__(self, ref):
        self.ref = ref
        self.used = 0

    def take(self):
        self.used += 1
        return self.ref.at[self.used - 1]

    def block(self, n):
        first = self.used
        self.used += n
        return lambda i: self.ref.at[first + i]


class Place:
    def __init__(self):
        me = lax.axis_index("fsdp")
        p = lax.rem(me, 32)
        self.base = me - p
        self.z = p // 8
        self.f = lax.rem(p // 2, 4)
        self.c = lax.rem(p, 2)

    def at(self, z, f, c):
        return self.base + 8 * z + 2 * f + c

    def f_at(self, k):
        return lax.rem(self.f + k + 4, 4)

    def z_at(self, k):
        return lax.rem(self.z + k + 4, 4)

    def plane(self, k):
        return self.at(self.z, self.f_at(k), self.c)

    def across(self, k):
        return self.at(self.z, self.f_at(k), 1 - self.c)

    def column(self, k):
        return self.at(self.z_at(k), self.f, self.c)

    def sibling(self):
        return self.at(self.z, self.f, 1 - self.c)


def remote(src, dst, sems, device):
    return pltpu.make_async_remote_copy(
        src_ref=src, dst_ref=dst, send_sem=sems[0], recv_sem=sems[1], device_id=(device,), device_id_type=MESH
    )


class Run:
    def __init__(self, send_sems, recv_sems, local_sems):
        self.place = Place()
        self.sends, self.recvs, self.locals = Pool(send_sems), Pool(recv_sems), Pool(local_sems)
        self.flying, self.saving = [], []

    def greet(self, wide):
        place = self.place
        there = [place.plane(k) for k in (1, 2, 3)] + [place.column(k) for k in (1, 2, 3)] + [place.sibling()]
        if wide:
            there += [place.across(k) for k in (1, 2, 3)]
        barrier = pltpu.get_barrier_semaphore()
        for dev in there:
            pl.semaphore_signal(barrier, inc=1, device_id=(dev,), device_id_type=MESH)
        pl.semaphore_wait(barrier, len(there))

    def launch(self, src, dst, device):
        a = remote(src, dst, (self.sends.take(), self.recvs.take()), device)
        a.start()
        self.flying.append((None, a))
        return a

    def launch_if(self, cond, src, dst, sems, device):
        a = remote(src, dst, sems, device)

        @pl.when(cond)
        def _():
            a.start()

        self.flying.append((cond, a))
        return a

    def local(self, src, dst):
        a = pltpu.make_async_copy(src, dst, self.locals.take())
        a.start()
        return a

    def save(self, src, dst):
        self.saving.append(self.local(src, dst))

    def close(self):
        for a in self.saving:
            a.wait()
        for cond, a in self.flying:
            if cond is None:
                a.wait_send()
            else:

                @pl.when(cond)
                def _(a=a):
                    a.wait_send()


class Spread:
    def __init__(self, run, chunk, full):
        self.run, self.chunk, self.full, self.pairs = run, chunk, full, None

    def start(self, cond=None):
        run, place = self.run, self.run.place
        mine = self.full.at[place.z, place.c]
        if self.pairs is None:
            self.own = pltpu.make_async_copy(self.chunk, mine, run.locals.take())
            self.pairs = [(run.sends.take(), run.recvs.take()) for _ in range(4)]
        cond = place.z >= 0 if cond is None else cond

        @pl.when(cond)
        def _():
            self.own.start()

        there = [place.column(k) for k in (1, 2, 3)] + [place.sibling()]
        copies = [run.launch_if(cond, self.chunk, mine, self.pairs[i], there[i]) for i in range(4)]
        self.far, self.near = copies[:3], copies[3:]

    def relay(self):
        run, place = self.run, self.run.place
        for k in (1, 2, 3):
            self.far[k - 1].wait_recv()
            there = self.full.at[place.z_at(-k), place.c]
            self.near.append(run.launch(there, there, place.sibling()))

    def finish(self):
        self.own.wait()
        for a in self.near:
            a.wait_recv()


class SpreadOutput:
    def __init__(self, run, chunk, full):
        self.run, self.chunk = run, chunk
        self.part = full.at[pl.ds(pl.multiple_of(run.place.c * 96, 96), 96)]

    def start(self):
        run, place = self.run, self.run.place
        self.copy = pltpu.make_async_copy(self.chunk, self.part, run.locals.take())

        @pl.when(place.f == place.z)
        def _():
            self.copy.start()

        arrive = run.recvs.take()
        for k in (1, 2, 3):
            self.far = run.launch_if(
                place.f == place.z, self.chunk, self.part, (run.sends.take(), arrive), place.column(k)
            )

    def relay(self):
        run, place = self.run, self.run.place

        @pl.when(place.f == place.z)
        def _():
            self.copy.wait()

        @pl.when(place.f != place.z)
        def _():
            self.far.wait_recv()

        self.near = run.launch(self.part, self.part, place.sibling())

    def finish(self):
        self.near.wait_recv()


class Collect:
    def __init__(self, run, part, near, far, total, out):
        self.run, self.part, self.near, self.far, self.total, self.out = run, part, near, far, total, out

    def start(self):
        place = self.run.place
        self.a = self.run.launch(self.part.at[1 - place.c], self.near, place.sibling())

    def middle(self):
        run, place = self.run, self.run.place
        self.a.wait_recv()

        def add(i, carry):
            self.near[i] = (self.part[place.c, i].astype(F32) + self.near[i].astype(F32)).astype(BF)
            return carry

        lax.fori_loop(0, 4, add, 0)
        self.moves = [
            run.launch(self.near.at[place.z_at(k)], self.far.at[k - 1], place.column(k)) for k in (1, 2, 3)
        ]

    def end(self):
        run, place = self.run, self.run.place
        for a in self.moves:
            a.wait_recv()
        result = self.near[place.z].astype(F32)
        for k in range(3):
            result = result + self.far[k].astype(F32)
        if self.total is None:
            self.out[...] = result
            return
        self.total[...] = result
        scatter_rows(self, self.total, self.out.at[place.f], None)

    def last(self):
        if self.total is None:
            return
        place = self.run.place
        for k in (1, 2, 3):
            g = place.f_at(k)
            remote(
                self.out.at[g], self.out.at[g], (self.send, self.arrive(g)), place.plane(k)
            ).wait_recv()

        @pl.when(place.c != place.f // 2)
        def _():
            remote(
                self.out.at[place.f], self.out.at[place.f], (self.send, self.arrive(place.f)), place.sibling()
            ).wait_recv()


def scatter_rows(task, total, landing, cond):
    run, place = task.run, task.run.place
    arrive = run.recvs.block(4)
    for j in range(4):
        there = place.at(place.z, 2 * place.c + j // 2, j % 2)
        here = jnp.logical_and(place.f == 2 * place.c + j // 2, place.c == j % 2)
        away = jnp.logical_not(here)
        if cond is not None:
            here, away = jnp.logical_and(here, cond), jnp.logical_and(away, cond)
        task.send = run.sends.take()
        slot = arrive(place.f) if cond is None else arrive(0)
        run.launch_if(away, total.at[pl.ds(24 * j, 24)], landing, (task.send, slot), there)

        @pl.when(here)
        def _(j=j):
            landing[...] = total[24 * j : 24 * (j + 1), :]

    task.arrive = arrive


class CollectOutput:
    def __init__(self, run, part, near, far, total, out):
        self.run, self.part, self.near, self.far, self.total, self.out = run, part, near, far, total, out

    def start(self):
        place = self.run.place
        self.a = self.run.launch(self.part.at[1 - place.c], self.near, place.sibling())

    def middle(self):
        run, place = self.run, self.run.place
        self.a.wait_recv()
        self.near[...] = (self.part[place.c].astype(F32) + self.near[...].astype(F32)).astype(BF)
        self.slot = run.recvs.block(4)
        self.one = run.sends.take()
        shift = lax.rem(place.f - place.z + 4, 4)
        run.launch_if(
            place.f != place.z, self.near, self.far.at[shift], (self.one, self.slot(shift)),
            place.at(place.f, place.f, place.c),
        )

    def end(self):
        place = self.run.place

        @pl.when(place.f == place.z)
        def _():
            result = self.near[...].astype(F32)
            for k in (1, 2, 3):
                remote(
                    self.near, self.far.at[k], (self.one, self.slot(k)), place.column(k)
                ).wait_recv()
                result = result + self.far[k].astype(F32)
            self.total[...] = result

        scatter_rows(self, self.total, self.out, place.f == place.z)

    def last(self):
        place = self.run.place
        mine = jnp.logical_and(place.f == place.z, place.c == place.f // 2)

        @pl.when(jnp.logical_not(mine))
        def _():
            remote(self.out, self.out, (self.send, self.arrive(0)), place.sibling()).wait_recv()


def norm_rows(z, gain, shift):
    centre = z - jnp.mean(z, axis=-1, keepdims=True)
    inv = lax.rsqrt(jnp.mean(centre * centre, axis=-1, keepdims=True) + EPSILON)
    return centre * inv * gain + shift


def norm_rows_back(z, gain, upstream):
    centre = z - jnp.mean(z, axis=-1, keepdims=True)
    inv = lax.rsqrt(jnp.mean(centre * centre, axis=-1, keepdims=True) + EPSILON)
    scaled = centre * inv
    weighted = upstream * gain
    inner = inv * (
        weighted
        - jnp.mean(weighted, axis=-1, keepdims=True)
        - scaled * jnp.mean(weighted * scaled, axis=-1, keepdims=True)
    )
    return inner, jnp.sum(upstream * scaled, axis=0, keepdims=True), jnp.sum(upstream, axis=0, keepdims=True)


def exchange_kernel(col, rows_o, small, colp, op, smallg, send_sems, recv_sems, local_sems):
    run = Run(send_sems, recv_sems, local_sems)
    place = run.place
    z, f, c = place.z, place.f, place.c
    mine = c == f // 2
    slot = 2 * lax.rem(f, 2) + c
    own = pltpu.make_async_copy(col.at[f], colp.at[slot], run.locals.take())
    own_o = pltpu.make_async_copy(rows_o, op.at[slot], run.locals.take())
    keep = jnp.logical_and(mine, f == z)

    @pl.when(mine)
    def _():
        own.start()

    @pl.when(keep)
    def _():
        own_o.start()

    own_small = run.local(small, smallg.at[z, c, f])
    run.greet(True)
    first = [run.launch(small, smallg.at[z, c, f], place.plane(k)) for k in (1, 2, 3)]
    arrive, arrive_o = run.recvs.block(4), run.recvs.block(4)
    for k in (1, 2, 3):
        run.launch_if(
            f >= 0, col.at[place.f_at(k)], colp.at[slot], (run.sends.take(), arrive(slot)),
            place.at(z, place.f_at(k), f // 2),
        )
    one = run.sends.take()
    run.launch_if(
        jnp.logical_not(mine), col.at[f], colp.at[slot], (one, arrive(slot)), place.sibling()
    )
    run.launch_if(
        jnp.logical_not(keep), rows_o, op.at[slot], (run.sends.take(), arrive_o(slot)), place.at(z, z, f // 2)
    )
    own_small.wait()
    for a in first:
        a.wait_recv()
    block = smallg.at[z, c]
    far = [run.launch(block, block, place.column(k)) for k in (1, 2, 3)]
    near = [run.launch(block, block, place.sibling())]
    for k in (1, 2, 3):
        far[k - 1].wait_recv()
        there = smallg.at[place.z_at(-k), c]
        near.append(run.launch(there, there, place.sibling()))

    for j in range(4):
        me = jnp.logical_and(f == 2 * c + j // 2, c == j % 2)
        other = jnp.logical_not(me)

        @pl.when(other)
        def _(j=j):
            remote(col.at[0], colp.at[j], (one, arrive(j)), place.sibling()).wait_recv()

        @pl.when(jnp.logical_and(other, f == z))
        def _(j=j):
            remote(rows_o, op.at[j], (one, arrive_o(j)), place.sibling()).wait_recv()

    for a in near:
        a.wait_recv()

    @pl.when(mine)
    def _():
        own.wait()

    @pl.when(keep)
    def _():
        own_o.wait()

    run.close()


class TrunkRows:
    def __init__(self, run, xb, tx):
        self.run, self.xb, self.tx = run, xb, tx

    def start(self):
        run, place = self.run, self.run.place
        self.parts = [pl.ds(0, 64), pl.ds(64, 64)]
        self.pairs = [(run.sends.take(), run.recvs.take()) for _ in range(2)]
        for q in range(2):
            run.launch_if(
                place.z == 0, self.xb.at[place.f, self.parts[q]], self.tx.at[place.f, self.parts[q]],
                self.pairs[q], place.column(1),
            )

    def pass_on(self):
        run, place = self.run, self.run.place
        self.round = []
        for q in range(2):
            block = self.tx.at[place.f, self.parts[q]]

            @pl.when(place.z > 0)
            def _():
                remote(block, block, self.pairs[q], place.column(1)).wait_recv()

            between = jnp.logical_and(place.z > 0, place.z < 3)
            run.launch_if(between, block, block, self.pairs[q], place.column(1))
            for k in (1, 2, 3):
                pair = (run.sends.take(), run.recvs.take())
                self.round.append((k, run.launch_if(place.z > 0, block, block, pair, place.plane(k))))

    def wait(self, k):
        for kk, a in self.round:
            if kk == k:
                a.wait_recv()


class KeyChain:
    def __init__(self, run, mine, slots, up, down, cs, up_out, down_out, place_in):
        self.run, self.mine, self.slots = run, mine, slots
        self.up, self.down, self.cs, self.up_out, self.down_out, self.place_in = up, down, cs, up_out, down_out, place_in

    def start(self):
        run, place = self.run, self.run.place
        z, c = place.z, place.c
        self.pairs = [[(run.sends.take(), run.recvs.take()) for _ in range(4)] for _ in range(2)]
        for j in range(4):
            total = self.mine[c, 0] * self.place_in[j, 0].astype(BF)
            for ft in range(1, 4):
                total = total + self.mine[c, ft] * self.place_in[j, ft].astype(BF)
            self.cs[j] = total
            run.launch_if(z == 1, self.cs.at[j], self.up.at[j], self.pairs[0][j], place.column(1))
            run.launch_if(z == 3, self.cs.at[j], self.down.at[j], self.pairs[1][j], place.column(-1))
        self.near = [run.launch(self.mine.at[c], self.mine.at[c], place.sibling())]

    def wait(self, which, j):
        dst = (self.up.at[j], self.down.at[j])[which]
        remote(dst, dst, self.pairs[which][j], self.run.place.column(1)).wait_recv()

    def finish(self):
        run, place = self.run, self.run.place
        z, c = place.z, place.c
        for j in range(4):

            @pl.when(z == 2)
            def _(j=j):
                self.wait(0, j)
                self.up_out[j] = self.cs[j] + self.up[j]

            run.launch_if(z == 2, self.up_out.at[j], self.up.at[j], self.pairs[0][j], place.column(1))

            @pl.when(z == 2)
            def _(j=j):
                self.wait(1, j)
                self.down_out[j] = self.cs[j] + self.down[j]

            run.launch_if(z == 2, self.down_out.at[j], self.down.at[j], self.pairs[1][j], place.column(-1))

            @pl.when(z == 2)
            def _(j=j):
                self.slots[c, j] = self.up_out[j] + self.down[j]

        for j in range(4):

            @pl.when(z == 0)
            def _(j=j):
                self.slots[c, j] = self.cs[j]

            @pl.when(z == 1)
            def _(j=j):
                self.wait(1, j)
                self.slots[c, j] = self.cs[j] + self.down[j]

            @pl.when(z == 3)
            def _(j=j):
                self.wait(0, j)
                self.slots[c, j] = self.cs[j] + self.up[j]

        self.near.append(run.launch(self.slots.at[c], self.slots.at[c], place.sibling()))
        for a in self.near:
            a.wait_recv()


class GradChain:
    def __init__(self, run, mine, near, trunk_in, up, down, up_out, down_out, total):
        self.run, self.mine, self.near, self.trunk_in = run, mine, near, trunk_in
        self.up, self.down, self.up_out, self.down_out, self.total = up, down, up_out, down_out, total

    def start(self):
        run, place = self.run, self.run.place
        self.pairs = [[(run.sends.take(), run.recvs.take()) for _ in range(4)] for _ in range(3)]
        self.arrive = []
        self.hand_over(0)

    def hand_over(self, kind):
        run, place = self.run, self.run.place
        self.arrive.append(run.launch(self.mine.at[1 - place.c, kind], self.near.at[kind], place.sibling()))

    def wait(self, which, j):
        dst = (self.trunk_in, self.up, self.down)[which].at[j]
        remote(dst, dst, self.pairs[which][j], self.run.place.column(1)).wait_recv()

    def middle(self):
        run, place = self.run, self.run.place
        z, c = place.z, place.c
        near = self.near
        for kind in range(3):
            self.arrive[kind].wait_recv()
            for j in range(4):
                near[kind, j] = (self.mine[c, kind, j].astype(F32) + near[kind, j].astype(F32)).astype(BF)
                if kind == 0:
                    run.launch_if(z == 3, near.at[0, j], self.trunk_in.at[j], self.pairs[0][j], place.column(-1))
                elif kind == 1:
                    run.launch_if(z == 1, near.at[1, j], self.up.at[j], self.pairs[1][j], place.column(1))
                    run.launch_if(z == 3, near.at[1, j], self.down.at[j], self.pairs[2][j], place.column(-1))

    def pass_on(self):
        run, place = self.run, self.run.place
        z = place.z
        near = self.near
        for j in range(4):
            cond = jnp.logical_or(z == 1, z == 2)

            @pl.when(cond)
            def _(j=j):
                self.wait(0, j)
                near[0, j] = (near[0, j].astype(F32) + self.trunk_in[j].astype(F32)).astype(BF)

            run.launch_if(cond, near.at[0, j], self.trunk_in.at[j], self.pairs[0][j], place.column(-1))

            @pl.when(z == 2)
            def _(j=j):
                self.wait(1, j)
                self.up_out[j] = (near[1, j].astype(F32) + self.up[j].astype(F32)).astype(BF)

            run.launch_if(z == 2, self.up_out.at[j], self.up.at[j], self.pairs[1][j], place.column(1))
        for j in range(4):

            @pl.when(z == 2)
            def _(j=j):
                self.wait(2, j)
                self.down_out[j] = (near[1, j].astype(F32) + self.down[j].astype(F32)).astype(BF)

            run.launch_if(z == 2, self.down_out.at[j], self.down.at[j], self.pairs[2][j], place.column(-1))

    def finish(self, place_in, store):
        place = self.run.place
        z = place.z
        near = self.near

        @pl.when(z == 0)
        def _():
            for j in range(4):
                self.wait(0, j)
                store(j, near[0, j].astype(F32) + self.trunk_in[j].astype(F32))

        @pl.when(z == 1)
        def _():
            for j in range(4):
                self.wait(2, j)
                self.total[j] = (near[1, j].astype(F32) + self.down[j].astype(F32)).astype(BF)

        @pl.when(z == 2)
        def _():
            for j in range(4):
                self.total[j] = (self.up_out[j].astype(F32) + self.down[j].astype(F32)).astype(BF)

        @pl.when(z == 3)
        def _():
            for j in range(4):
                self.wait(1, j)
                self.total[j] = (near[1, j].astype(F32) + self.up[j].astype(F32)).astype(BF)

        @pl.when(z > 0)
        def _():
            for ft in range(4):
                total = near[2, ft].astype(F32)
                for j in range(4):
                    total = total + self.total[j].astype(F32) * place_in[j, ft]
                store(ft, total)


def pick_parents(kp, slots, choose):
    def one(b, carry):
        for cc in range(2):
            total = slots[cc, 0] * choose[b, 0].astype(BF)
            for j in range(1, 4):
                total = total + slots[cc, j] * choose[b, j].astype(BF)
            kp[b, cc] = total
        return carry

    lax.fori_loop(0, 4, one, 0)


def all_keys(trunk, mine, kp, b, lanes):
    return jnp.concatenate(
        [trunk[:, :, :, lanes].reshape(1024, 128), mine[0, b, :, lanes], mine[1, b, :, lanes], kp[b, 0, :, lanes], kp[b, 1, :, lanes]],
        axis=0,
    )


def flat(ref):
    return ref[...].reshape(-1, ref.shape[-1])


def forward_kernel(*refs):
    run = Run(*refs[-3:])
    run.prepare = lambda: run.greet(False)
    forward_body(True, run, list(refs[:-3]))
    run.close()


def forward_body(first, run, refs):

    def take(n):
        out = refs[:n]
        del refs[:n]
        return out

    x_ref, chunks, rows_o, rows_out, vecs, place_in, choose, pen = take(8)
    if not first:
        qkv_in, o_in = take(2)
    layer = 0 if first else 1
    vec = vecs.at[layer]
    in_c, out_c = chunks.at[layer, :, pl.ds(PACKED, WIDE)], rows_out.at[layer]
    if first:
        qkv_in, o_in = chunks.at[0, :, pl.ds(0, PACKED)], rows_o.at[0]
        qkv_next, o_next = chunks.at[1, :, pl.ds(0, PACKED)], rows_o.at[1]
    xn_ref = take(1)[0]
    if first:
        xb_o, qp_o, trunk_o, mine_o, kp_o, p_o, ctx_o, z1_o, hb_o, gp_o, gl_o, z2_o, win_o, wout_o = take(14)
        wqkv_o, wo_o, wqkv_n, wo_n = take(4)
    xb, qp, trunk, mine, kp, p, ctx, z1, hb, gp, gl, z2, win, wout, wqkv, wo, heads, own, rs1_s, rs1_r, rs2_s, rs2_r = take(22)
    tx, *chain_refs = take(7)
    place = run.place
    z, f, c = place.z, place.f, place.c
    launch = run.launch

    xb[f] = x_ref[...].astype(BF)
    wo[192:256, :] = jnp.zeros((64, WIDE), BF)
    if not first:
        loads = [run.local(qkv_in, wqkv), run.local(o_in, wo.at[pl.ds(0, 192)])]
    run.prepare()
    came = [None] + [launch(xb.at[f], xb.at[f], place.plane(k)) for k in (1, 2, 3)]
    trunk_rows = TrunkRows(run, xb, tx)
    trunk_rows.start()
    m_tasks = [Spread(run, in_c, win), Spread(run, out_c, wout)]
    if first:
        a_tasks = [Spread(run, qkv_in, wqkv), SpreadOutput(run, o_in, wo)]
        for t in a_tasks:
            t.start()
        trunk_rows.pass_on()
        a_tasks[0].relay()
        a_tasks[0].finish()
    else:
        trunk_rows.pass_on()
        for a in loads:
            a.wait()
    lane = lax.broadcasted_iota(jnp.int32, (ROWS, 128), 1)
    for k in range(4):
        g = place.f_at(-k)
        if k:
            came[k].wait_recv()
        qkv = product(xb[g], flat(wqkv)) + vec[0:1, :PACKED]
        rows = pl.ds(pl.multiple_of(g * ROWS, ROWS), ROWS)
        mine[c, g] = qkv[:, 256:].astype(BF)
        scaled = qkv[:, :256] * (HEAD_DIM ** (-0.5))
        front = scaled[:, :128]
        qp[rows, 0:128] = jnp.where(lane < 64, front, 0.0).astype(BF)
        qp[rows, 128:256] = jnp.where(lane < 64, pltpu.roll(front, 64, 1), 0.0).astype(BF)
        qp[rows, 256:384] = scaled[:, 128:].astype(BF)
    chain = KeyChain(run, mine, *chain_refs, place_in)
    chain.start()

    @pl.when(z == 0)
    def _():
        trunk[c] = mine[c]

    @pl.when(z > 0)
    def _():
        for k in range(4):
            g = place.f_at(-k)
            if k:
                trunk_rows.wait(k)
            keys = product(tx[g], flat(wqkv)[:, 256:]) + vec[0:1, 256:PACKED]
            trunk[c, g] = keys.astype(BF)

    trunk_near = launch(trunk.at[c], trunk.at[c], place.sibling())
    if first:
        run.save(xb, xb_o)
    if first:
        run.save(qp, qp_o)
    chain.finish()
    trunk_near.wait_recv()
    late_tasks = m_tasks
    for t in late_tasks:
        t.start(z > 0)
    pick_parents(kp, chain.slots, choose)
    if first:
        run.save(kp, kp_o)
    if first:
        run.save(trunk, trunk_o)
    if first:
        run.save(mine, mine_o)
    if first:
        a_tasks[1].relay()

    def attend(i, carry):
        h, b = i // 4, lax.rem(i, 4)
        lanes = pl.ds(pl.multiple_of(h * 128, 128), 128)
        rows = pl.ds(pl.multiple_of(b * ROWS, ROWS), ROWS)
        keys = all_keys(trunk, mine, kp, b, lanes)
        s = product_nt(qp[rows, lanes], keys)
        s = jnp.concatenate(
            [s[:, :1024], s[:, 1024:1280] + pen[4 + b], s[:, 1280:] + pen[b]], axis=1
        )
        e = jnp.exp(s - jnp.max(s, axis=1, keepdims=True))
        pb = (e * (1.0 / jnp.sum(e, axis=1, keepdims=True))).astype(BF)
        p[h, b] = pb
        heads[h, b] = product(pb, keys)
        return carry

    lax.fori_loop(0, 12, attend, 0, unroll=2)
    if first:
        run.save(p, p_o)
    if first:
        a_tasks[1].finish()
    back = [None]
    for k in (1, 2, 3, 0):
        g = place.f_at(-k)
        ctx[g, :, 0:128] = jnp.where(lane < 64, pltpu.roll(heads[0, g], 64, 1), heads[1, g]).astype(BF)
        ctx[g, :, 128:256] = jnp.where(lane < 64, pltpu.roll(heads[2, g], 64, 1), 0.0).astype(BF)
        part = product(ctx[g], wo[...])
        if k:
            rs1_s[k - 1] = part.astype(BF)
            back.append(launch(rs1_s.at[k - 1], rs1_r.at[k - 1], place.plane(-k)))
        else:
            own[...] = part
    if first:
        run.save(ctx, ctx_o)
    for k in (1, 2, 3):
        back[k].wait_recv()
    for t in late_tasks:
        t.start(z == 0)
    total = own[...] + rs1_r[0].astype(F32) + rs1_r[1].astype(F32) + rs1_r[2].astype(F32)
    zz = x_ref[...].astype(F32) + total + vec[1:2, :]
    z1[...] = zz
    if first:
        run.save(z1, z1_o)
    hidden = norm_rows(zz, vec[2:3, :], vec[3:4, :])
    hb[f] = hidden.astype(BF)
    came = [None] + [launch(hb.at[f], hb.at[f], place.plane(k)) for k in (1, 2, 3)]
    back = [None]
    for t in m_tasks:
        t.relay()
    if first:
        n_tasks = [Spread(run, qkv_next, wqkv_n), SpreadOutput(run, o_next, wo_n)]
        for t in n_tasks:
            t.start()
    for t in m_tasks:
        t.finish()
    for k in range(4):
        g = place.f_at(-k)
        if k:
            came[k].wait_recv()
        u = product(hb[g], flat(win)) + vec[4:5, :]
        cdf = 0.5 * (1.0 + lax.erf(u * (0.5 ** 0.5)))
        gp[g] = cdf + u * jnp.exp(-0.5 * u * u) * 0.3989422804014327
        low = (u * cdf).astype(BF)
        gl[g] = low
        part = product(low, flat(wout))
        if k:
            rs2_s[k - 1] = part.astype(BF)
            back.append(launch(rs2_s.at[k - 1], rs2_r.at[k - 1], place.plane(-k)))
        else:
            own[...] = part
    if first:
        run.save(hb, hb_o)
    if first:
        run.save(gp, gp_o)
    if first:
        run.save(gl, gl_o)
    if first:
        run.save(win, win_o)
    if first:
        run.save(wout, wout_o)
    if first:
        run.save(wqkv, wqkv_o)
        run.save(wo.at[pl.ds(0, 192)], wo_o)
    for k in (1, 2, 3):
        back[k].wait_recv()
    total = own[...] + rs2_r[0].astype(F32) + rs2_r[1].astype(F32) + rs2_r[2].astype(F32)
    zz = norm_rows(z1[...], vec[2:3, :], vec[3:4, :]) + total + vec[5:6, :]
    z2[...] = zz
    if first:
        run.save(z2, z2_o)
    xn_ref[...] = norm_rows(zz, vec[6:7, :], vec[7:8, :]).astype(xn_ref.dtype)
    if first:
        for t in n_tasks:
            t.relay()
        for t in n_tasks:
            t.finish()
    return z2, (wout, gp, win, gl, hb, z1, wo, ctx, trunk, mine, kp, qp, p, xb, wqkv)


def turn_kernel(*refs):
    run = Run(*refs[-3:])
    run.prepare = lambda: run.greet(True)
    refs = list(refs[:-3])
    ahead, dy_ref, xn_ref, outs, kept, rest = refs[:10], refs[10], refs[11], refs[12:19], refs[19:48], refs[48:]
    held = forward_body(False, run, ahead + [xn_ref] + kept)
    backward_body(False, run, [dy_ref] + ahead[4:7] + outs + rest, held)
    run.close()


def backward_kernel(*refs):
    run = Run(*refs[-3:])
    backward_body(True, run, list(refs[:-3]), None)
    run.close()


def backward_body(extra, run, refs, held):

    def take(n):
        out = refs[:n]
        del refs[:n]
        return out

    dy_ref, vecs, place_in, choose = take(4)
    vec = vecs.at[0 if extra else 1]
    if extra:
        z2 = take(1)[0]
        late_in = take(15)
        pq_in, pk_in, dvec_in = take(3)
    dx_ref, din_o, dout_o, do_o = take(4)
    if extra:
        dq_n, dk_n, dq_o, dk_o, sm_o = take(5)
    else:
        pq, pk, dvec_o = take(3)
    if extra:
        late = take(15)
    else:
        z2, late = held
    wout, gp, win, gl, hb, z1, wo, ctx, trunk, mine, kp, qp, p, xb, wqkv = late
    (
        df, du, da, dctx, dqf, dqkv, dz, dz1, dkt, dself, dpar, tgt, own, rs1_s, rs1_r, rs2_s, rs2_r,
    ) = take(17)
    chain_refs = take(7)
    pin, nin, fin, tin, pout, nout, fout, po, no, fo, to = take(11)
    if extra:
        pq, pk, dvec_o = take(3)
        nq, fq, tq, nk, fk, tk, nq2, fq2, tq2, nk2, fk2, tk2, sm, sm_a, sm_b, sm_v = take(16)
    place = run.place
    z, f, c = place.z, place.f, place.c
    launch = run.launch
    loads = []
    if extra:
        for n, (src, dst) in enumerate(zip(late_in, late)):
            loads.append(run.local(src, dst.at[pl.ds(0, 192)] if n == 6 else dst))
        wo[192:256, :] = jnp.zeros((64, WIDE), BF)

    grad, dgain, dshift = norm_rows_back(z2[...], vec[6:7, :], dy_ref[...].astype(F32))
    dvec_o[6:7, :] = dgain
    dvec_o[7:8, :] = dshift
    dz[...] = grad
    low = grad.astype(BF)
    df[f] = low
    dvec_o[5:6, :] = jnp.sum(low.astype(F32), axis=0, keepdims=True)
    if extra:
        run.greet(True)
    came = [None] + [launch(df.at[f], df.at[f], place.plane(k)) for k in (1, 2, 3)]
    a_tasks = []
    if extra:
        a_tasks = [Collect(run, pq_in, nq, fq, tq, dq_n), Collect(run, pk_in, nk, fk, tk, dk_n)]
    for t in a_tasks:
        t.start()
    back = [None]
    bias = jnp.zeros((1, WIDE), F32)
    for a in loads[:3]:
        a.wait()
    for k in range(4):
        g = place.f_at(-k)
        if k:
            came[k].wait_recv()
        low = (product_nt(df[g], flat(wout)) * gp[g]).astype(BF)
        du[g] = low
        bias = bias + jnp.sum(low.astype(F32), axis=0, keepdims=True)
        part = product_nt(low, flat(win))
        if k:
            rs1_s[k - 1] = part.astype(BF)
            back.append(launch(rs1_s.at[k - 1], rs1_r.at[k - 1], place.plane(-k)))
        else:
            own[...] = part
            for t in a_tasks:
                t.middle()
    dvec_o[4:5, :] = bias
    m_tasks = [Collect(run, pin, nin, fin, tin, din_o), Collect(run, pout, nout, fout, None, dout_o)]
    o_task = CollectOutput(run, po, no, fo, to, do_o)

    def split_rows(dst, left, right, i):
        lanes = pl.ds(pl.multiple_of(i * 384, 128), 384)
        value = product_tn(left[:, :, lanes].reshape(512, 384), right).astype(BF)
        for zz in range(2):
            for cc in range(2):
                at = (2 * zz + cc) * 96
                dst[cc, 2 * i + zz] = value[at : at + 96, :]

    def outer_grads(i, carry):
        split_rows(pout, gl, flat(df), i)
        return carry

    def inner_grads(i, carry):
        split_rows(pin, hb, flat(du), i)
        return carry

    for a in loads[3:5]:
        a.wait()
    lax.fori_loop(0, 2, outer_grads, 0)
    m_tasks[1].start()
    lax.fori_loop(0, 2, inner_grads, 0)
    m_tasks[0].start()
    m_tasks[1].middle()
    m_tasks[0].middle()
    for k in (1, 2, 3):
        back[k].wait_recv()
    up = dz[...] + own[...] + rs1_r[0].astype(F32) + rs1_r[1].astype(F32) + rs1_r[2].astype(F32)
    for a in loads[5:6]:
        a.wait()
    grad, dgain, dshift = norm_rows_back(z1[...], vec[2:3, :], up)
    dvec_o[2:3, :] = dgain
    dvec_o[3:4, :] = dshift
    dz1[...] = grad
    low = grad.astype(BF)
    da[f] = low
    dvec_o[1:2, :] = jnp.sum(low.astype(F32), axis=0, keepdims=True)
    came = [None] + [launch(da.at[f], da.at[f], place.plane(k)) for k in (1, 2, 3)]
    for t in a_tasks:
        t.end()
    dkt[...] = jnp.zeros_like(dkt)
    lane = lax.broadcasted_iota(jnp.int32, (ROWS, 128), 1)
    for a in loads[6:]:
        a.wait()
    for k in range(4):
        g = place.f_at(-k)
        rows = pl.ds(pl.multiple_of(g * ROWS, ROWS), ROWS)
        if k:
            came[k].wait_recv()
        packed = product_nt(da[g], wo[...])
        ahead, after = packed[:, :128], packed[:, 128:]
        dctx[rows, 0:128] = jnp.where(lane < 64, 0.0, pltpu.roll(ahead, 64, 1)).astype(BF)
        dctx[rows, 128:256] = jnp.where(lane < 64, 0.0, ahead).astype(BF)
        dctx[rows, 256:384] = jnp.where(lane < 64, 0.0, pltpu.roll(after, 64, 1)).astype(BF)
    value = product_tn(flat(ctx), flat(da)).astype(BF)
    for cc in range(2):
        po[cc] = value[96 * cc : 96 * (cc + 1), :]
    o_task.start()
    o_task.middle()

    def attend(i, carry):
        h, b = i // 4, lax.rem(i, 4)
        lanes = pl.ds(pl.multiple_of(h * 128, 128), 128)
        rows = pl.ds(pl.multiple_of(b * ROWS, ROWS), ROWS)
        keys = all_keys(trunk, mine, kp, b, lanes)
        q, g = qp[rows, lanes], dctx[rows, lanes]
        low = p[h, b]
        pf = low.astype(F32)
        dp = product_nt(g, keys)
        t = pf * dp
        ds = (t - pf * jnp.sum(t, axis=1, keepdims=True)).astype(BF)
        dqf[h, rows, :] = product(ds, keys) * (HEAD_DIM ** (-0.5))
        dkv = product_tn(jnp.concatenate([ds, low], axis=0), jnp.concatenate([q, g], axis=0))
        dkt[:, lanes] += dkv[:1024]
        dself[b, :, lanes] = dkv[1024:1280]
        dpar[b, :, lanes] = dkv[1280:]
        return carry

    lax.fori_loop(0, 12, attend, 0)
    for cc in range(2):
        for j in range(4):
            at = cc * 512 + j * ROWS
            tgt[cc, 0, j] = dkt[at : at + ROWS, :].astype(BF)

    chain = GradChain(run, tgt, *chain_refs)
    chain.start()

    def scatter(j, carry):
        for cc in range(2):
            half = slice(cc * ROWS, (cc + 1) * ROWS)
            total = dpar[0, half, :] * choose[0, j]
            for b in range(1, 4):
                total = total + dpar[b, half, :] * choose[b, j]
            tgt[cc, 1, j] = total.astype(BF)
            tgt[cc, 2, j] = dself[j, half, :].astype(BF)
        return carry

    lax.fori_loop(0, 4, scatter, 0)
    chain.hand_over(1)
    chain.hand_over(2)
    for g in range(4):
        rows = slice(g * ROWS, (g + 1) * ROWS)
        ahead = jnp.where(lane < 64, dqf[0, rows, :], pltpu.roll(dqf[1, rows, :], 64, 1))
        dqkv[g, :, 0:128] = ahead.astype(BF)
        dqkv[g, :, 128:256] = jnp.where(lane < 64, dqf[2, rows, :], 0.0).astype(BF)
    chain.middle()
    for t in m_tasks:
        t.end()
    chain.pass_on()

    def q_grads(i, carry):
        split_rows(pq, xb, dqkv[:, :, :256].reshape(512, 256), i)
        return carry

    lax.fori_loop(0, 2, q_grads, 0)
    end_tasks = []
    if extra:
        end_tasks = [Collect(run, pk, nk2, fk2, tk2, dk_o), Collect(run, pq, nq2, fq2, tq2, dq_o)]
        end_tasks[1].start()

    def store(ft, value):
        dqkv[ft, :, 256:] = value.astype(BF)

    chain.finish(place_in, store)

    def k_grads(i, carry):
        split_rows(pk, xb, dqkv[:, :, 256:].reshape(512, SLICE), i)
        return carry

    lax.fori_loop(0, 2, k_grads, 0)
    if extra:
        end_tasks[0].start()
        end_tasks[1].middle()
        end_tasks[0].middle()
    back = [None]
    for k in (1, 2, 3, 0):
        g = place.f_at(-k)
        part = product_nt(dqkv[g], flat(wqkv))
        if k:
            rs2_s[k - 1] = part.astype(BF)
            back.append(launch(rs2_s.at[k - 1], rs2_r.at[k - 1], place.plane(-k)))
        else:
            own[...] = part

    sums = jnp.sum(flat(dqkv).astype(F32), axis=0, keepdims=True)
    dvec_o[0:1, :] = jnp.concatenate([sums, jnp.zeros((1, WIDE - PACKED), F32)], axis=1)
    if extra:
        sm[0:8, :] = dvec_o[...]
        sm[8:16, :] = dvec_in[...]
        sm_near = launch(sm, sm_a, place.sibling())
        sm_near.wait_recv()
        sm_a[...] = sm[...] + sm_a[...]
        sm_far = [launch(sm_a, sm_b.at[k - 1], place.column(k)) for k in (1, 2, 3)]
    o_task.end()
    for t in a_tasks:
        t.last()
    for k in (1, 2, 3):
        back[k].wait_recv()
    total = dz1[...] + own[...] + rs2_r[0].astype(F32) + rs2_r[1].astype(F32) + rs2_r[2].astype(F32)
    dx_ref[...] = total.astype(dx_ref.dtype)
    if extra:
        for t in end_tasks:
            t.end()
        for a in sm_far:
            a.wait_recv()
        sm_v[...] = sm_a[...] + sm_b[0] + sm_b[1] + sm_b[2]
        sm_last = [launch(sm_v, sm_o.at[f], place.plane(k)) for k in (1, 2, 3)]
        sm_o[f] = sm_v[...]
        for a in sm_last:
            a.wait_recv()
    for t in m_tasks + [o_task] + end_tasks:
        t.last()


ANY = pl.BlockSpec(memory_space=pl.ANY)
VM = pl.BlockSpec(memory_space=pltpu.VMEM)
SM = pl.BlockSpec(memory_space=pltpu.SMEM)
LIMIT = 60 * 1024 * 1024
SEMS = (256, 256, 32)


def shape(*dims, dtype=BF):
    return jax.ShapeDtypeStruct(dims, dtype)


def call(kernel, number, outs, out_specs, in_specs, scratch, args, flops):
    return pl.pallas_call(
        kernel,
        out_shape=tuple(outs),
        in_specs=in_specs,
        out_specs=tuple(out_specs),
        scratch_shapes=[pltpu.VMEM(s.shape, s.dtype) for s in scratch]
        + [pltpu.SemaphoreType.DMA((n,)) for n in SEMS],
        compiler_params=pltpu.CompilerParams(
            collective_id=number, has_side_effects=True, vmem_limit_bytes=LIMIT
        ),
        cost_estimate=pl.CostEstimate(flops=flops, bytes_accessed=20000000, transcendentals=0),
    )(*args)


def column_parts(query, key, value, inner):
    n = query.shape[0] * query.shape[1]
    q = query.reshape(n, 4, 3, 64)
    q = jnp.pad(q, ((0, 0), (0, 0), (0, 1), (0, 0))).reshape(n, 4, 256)
    kv = jnp.stack([key.reshape(n, 4, 3, 64), value.reshape(n, 4, 3, 64)], axis=3).reshape(n, 4, 384)
    up = inner.reshape(n, 4, 4, 192).transpose(0, 2, 1, 3).reshape(n, 4, WIDE)
    return jnp.concatenate([q, kv, up], axis=2).transpose(1, 0, 2)


LOCAL = shape(ROWS, WIDE, dtype=F32)
FULL = shape(4, ROWS, WIDE)
PIECE = shape(3, ROWS, WIDE)
QKV = shape(4, 2, 96, PACKED)
BIG = shape(4, 2, 96, WIDE)
OUTPUT = shape(192, WIDE)
HALVES = shape(2, 4, ROWS, SLICE)
QUARTERS = shape(4, ROWS, SLICE)
SAVED = (
    FULL, shape(512, SLICE), HALVES, HALVES, shape(4, 2, ROWS, SLICE), shape(3, 4, ROWS, NKEYS),
    shape(4, ROWS, 256), LOCAL, FULL, shape(4, ROWS, WIDE, dtype=F32), FULL, LOCAL,
)


FORWARD_SCRATCH = (
    list(SAVED)
    + [BIG, BIG, QKV, shape(256, WIDE), shape(3, 4, ROWS, 128, dtype=F32), LOCAL]
    + [PIECE] * 4 + [FULL, HALVES] + [QUARTERS] * 5
)


def forward_layer(state, chunks, rows_o, rows_out, vecs, place_in, choose, pen):
    outs = (LOCAL,) + SAVED + (BIG, BIG, QKV, OUTPUT, QKV, OUTPUT)
    got = call(
        forward_kernel, 1, outs, (VM,) + (ANY,) * (len(outs) - 1), [VM] + [ANY] * 3 + [VM] + [SM] * 3,
        FORWARD_SCRATCH, (state, chunks, rows_o, rows_out, vecs, place_in, choose, pen), 3 * 10**9,
    )
    return got[0], got[1:13], got[13:]


def collect_scratch(columns, rows):
    return [shape(4, 96, columns), shape(3, 96, columns)] + ([shape(96, columns, dtype=F32)] if rows else [])


OUT_SCRATCH = [shape(96, WIDE), shape(4, 96, WIDE), shape(96, WIDE, dtype=F32)]
PARTS = (shape(2, 4, 96, 256), shape(2, 4, 96, SLICE))
SHARES = (shape(4, 24, 256, dtype=F32), shape(4, 24, SLICE, dtype=F32))


def backward_scratch():
    keys = shape(4, 256, SLICE, dtype=F32)
    part = shape(2, 4, 96, WIDE)
    scratch = [
        FULL, FULL, FULL, shape(512, SLICE), shape(3, 512, 128, dtype=F32), shape(4, ROWS, PACKED), LOCAL, LOCAL,
        shape(1024, SLICE, dtype=F32), keys, keys, shape(2, 3, 4, ROWS, SLICE), LOCAL, PIECE, PIECE, PIECE, PIECE,
        shape(3, 4, ROWS, SLICE),
    ] + [QUARTERS] * 6
    scratch += [part] + collect_scratch(WIDE, True) + [part] + collect_scratch(WIDE, False)
    return scratch + [shape(2, 96, WIDE)] + OUT_SCRATCH


SUMS, SUMS2 = shape(8, WIDE, dtype=F32), shape(16, WIDE, dtype=F32)
GRADS = (shape(4, 24, WIDE, dtype=F32), shape(96, WIDE, dtype=F32), shape(24, WIDE, dtype=F32))


def turn_layer(state, chunks, rows_o, rows_out, vecs, place_in, choose, pen, wqkv, wo, upstream):
    outs = (shape(ROWS, WIDE), LOCAL) + GRADS + PARTS + (SUMS,)
    return call(
        turn_kernel, 2, outs, (VM,) * len(outs), [VM] + [ANY] * 3 + [VM] + [SM] * 3 + [ANY] * 2 + [VM],
        FORWARD_SCRATCH + backward_scratch(),
        (state, chunks, rows_o, rows_out, vecs, place_in, choose, pen, wqkv, wo, upstream), 9 * 10**9,
    )


def backward_layer(upstream, weights, vecs, place_in, choose, saved, before):
    wqkv, wo, win, wout = weights
    xb, qp, trunk, mine, kp, p, ctx, z1, hb, gp, gl, z2 = saved
    outs = (shape(ROWS, WIDE),) + GRADS + SHARES + SHARES + (shape(4, 16, WIDE, dtype=F32),)
    scratch = [
        BIG, SAVED[9], BIG, FULL, FULL, LOCAL, shape(256, WIDE), SAVED[6], HALVES, HALVES, SAVED[4], SAVED[1], SAVED[5],
        FULL, QKV,
    ] + backward_scratch()
    scratch += list(PARTS) + [SUMS]
    scratch += (collect_scratch(256, True) + collect_scratch(SLICE, True)) * 2
    scratch += [SUMS2, SUMS2, shape(3, 16, WIDE, dtype=F32), SUMS2]
    return call(
        backward_kernel, 4, outs, (VM,) * len(outs), [VM] * 2 + [SM] * 2 + [VM] + [ANY] * 15 + [VM] * 3, scratch,
        (upstream, vecs, place_in, choose, z2, wout, gp, win, gl, hb, z1, wo, ctx, trunk, mine, kp, qp, p, xb, wqkv)
        + tuple(before),
        6 * 10**9,
    )


def slice_body(
    activations, query_weight, query_bias, key_weight, value_weight, value_bias, output_weight, output_bias,
    first_gain, first_shift, inner_weight, inner_bias, outer_weight, outer_bias, second_gain, second_shift,
    cotangent, parents, segments,
):
    place = Place()
    z, f, c = place.z, place.f, place.c
    col = column_parts(query_weight, key_weight, value_weight, inner_weight)
    vectors = (query_bias, value_bias, output_bias, first_gain, first_shift, outer_bias, second_gain, second_shift)
    label = jnp.broadcast_to(segments[:1].astype(BF)[None], (2, 1))
    small = jnp.concatenate(vectors + (inner_bias, label), axis=1)
    small = jnp.pad(small, ((0, 14), (0, 384 - small.shape[1])))
    colp, op, smallg = call(
        exchange_kernel, 0, (shape(4, 48, 1408), shape(4, 48, WIDE), shape(4, 2, 4, 16, 384)), (ANY,) * 3, [ANY] * 3,
        [], (col, output_weight.reshape(48, WIDE), small), 1000,
    )
    colp = colp.reshape(4, 2, 24, 1408).transpose(1, 0, 2, 3).reshape(2, 96, 1408)
    op = op.reshape(4, 2, 24, WIDE).transpose(1, 0, 2, 3).reshape(2, 96, WIDE)
    small = smallg[:, :, :, :2].transpose(3, 0, 2, 1, 4).astype(F32)
    parts = [small[..., i * 24 : (i + 1) * 24].reshape(2, WIDE) for i in range(8)]
    q_all, v_all, o_all, g1, s1, out_all, g2, s2 = parts
    in_mine = lax.dynamic_index_in_dim(small[..., 192:288], f, 2, keepdims=False).reshape(2, WIDE)
    q_mine = lax.dynamic_slice_in_dim(q_all, 192 * f, 192, 1)
    v_mine = lax.dynamic_slice_in_dim(v_all, 192 * f, 192, 1).reshape(2, 3, 64)
    kv_mine = jnp.pad(v_mine, ((0, 0), (0, 0), (64, 0))).reshape(2, SLICE)
    qkv_mine = jnp.pad(jnp.concatenate([q_mine, jnp.zeros((2, 64), F32), kv_mine], axis=1), ((0, 0), (0, WIDE - PACKED)))
    vecs = jnp.stack([qkv_mine, o_all, g1, s1, in_mine, out_all, g2, s2], axis=1)

    labels = small[0, :, :, 0, 288].reshape(16).astype(jnp.int32)
    above = lookup_rows(labels, parents)
    order = jnp.arange(16, dtype=jnp.int32)
    branch = jnp.logical_and(above == labels[0], order >= 4)
    slot = jnp.where(branch, jnp.sum((branch[:, None] & (order[:, None] < order[None, :])).astype(jnp.int32), axis=0), 4)
    in_slot = slot[None, :] == jnp.arange(4, dtype=jnp.int32)[:, None]
    place_in = lax.dynamic_slice_in_dim(in_slot.astype(F32), 4 * z, 4, 1)
    parent = lax.dynamic_slice_in_dim(above, 4 * z, 4, 0)
    match = parent[:, None, None] == jnp.where(in_slot, labels[None, :], -1)[None]
    choose = jnp.any(match, axis=2).astype(F32)
    pen = jnp.concatenate(
        [jnp.where(jnp.any(match, axis=(1, 2)), 0.0, MASKED), jnp.where(z > 0, jnp.zeros((4,), F32), MASKED)]
    ).astype(F32)

    shared = (colp, op, outer_weight, vecs, place_in, choose, pen)
    state, kept0, (win0, wout0, wqkv0, wo0, wqkv1, wo1) = forward_layer(activations, *shared)
    outcome, upstream, din1, dout1, do1, pq, pk, dvec1 = turn_layer(state, *shared, wqkv1, wo1, cotangent)
    upstream, din0, dout0, do0, dq1, dk1, dq0, dk0, rsm = backward_layer(
        upstream, (wqkv0, wo0, win0, wout0), vecs, place_in, choose, kept0, (pq, pk, dvec1)
    )
    dq = jnp.stack([dq0, dq1]).transpose(0, 2, 1, 3)[..., :192].reshape(2, 24, WIDE)
    dkv = jnp.stack([dk0, dk1]).transpose(0, 2, 1, 3).reshape(2, 24, 4, 3, 2, 64)
    dk = dkv[..., 0, :].reshape(2, 24, WIDE)
    dv = dkv[..., 1, :].reshape(2, 24, WIDE)
    dinner = jnp.stack([din0, din1]).reshape(2, 4, 24, 4, 192).transpose(0, 2, 3, 1, 4).reshape(2, 24, 3072)
    rsm = rsm.reshape(4, 2, 8, WIDE)
    sums = jnp.sum(rsm, axis=0)
    dqb = rsm[:, :, 0, :192].transpose(1, 0, 2).reshape(2, WIDE)
    dvb = rsm[:, :, 0, 256:640].reshape(4, 2, 3, 2, 64)[:, :, :, 1].transpose(1, 0, 2, 3).reshape(2, WIDE)
    rows = jnp.stack([dqb, dvb, sums[:, 1], sums[:, 2], sums[:, 3], sums[:, 5], sums[:, 6], sums[:, 7]])
    rows = lax.dynamic_slice_in_dim(rows, 24 * (8 * z + 2 * f + c), 24, 2)
    dib = lax.dynamic_index_in_dim(rsm[:, :, 4], f, 0, keepdims=False)
    dib = lax.dynamic_slice_in_dim(dib, 96 * (2 * z + c), 96, 1)
    return (
        outcome, upstream, dq, rows[0], dk, dv, rows[1], jnp.stack([do0, do1]), rows[2], rows[3], rows[4],
        dinner, dib, jnp.stack([dout0, dout1]), rows[5], rows[6], rows[7],
    )


def solution(mesh):
    placed = (
        P("fsdp", None),
        P(None, "fsdp", None),
        P(None, "fsdp"),
        P(None, "fsdp", None),
        P(None, "fsdp", None),
        P(None, "fsdp"),
        P(None, "fsdp", None),
        P(None, "fsdp"),
        P(None, "fsdp"),
        P(None, "fsdp"),
        P(None, "fsdp", None),
        P(None, "fsdp"),
        P(None, "fsdp", None),
        P(None, "fsdp"),
        P(None, "fsdp"),
        P(None, "fsdp"),
        P("fsdp", None),
        P(),
        P("fsdp"),
    )
    return jax.shard_map(
        slice_body if mesh.shape["fsdp"] == 32 else body,
        mesh=mesh,
        in_specs=placed,
        out_specs=(
            P("fsdp", None),
            P("fsdp", None),
            P(None, "fsdp", None),
            P(None, "fsdp"),
            P(None, "fsdp", None),
            P(None, "fsdp", None),
            P(None, "fsdp"),
            P(None, "fsdp", None),
            P(None, "fsdp"),
            P(None, "fsdp"),
            P(None, "fsdp"),
            P(None, "fsdp", None),
            P(None, "fsdp"),
            P(None, "fsdp", None),
            P(None, "fsdp"),
            P(None, "fsdp"),
            P(None, "fsdp"),
        ),
        check_vma=False,
    )
```
